32 devices in a mesh: groups: 2 (over y), dp: 16 (over z, x, core).
Axes of the slice: x: 2, y: 2, z: 4, core: 2. Of those that a mesh axis runs over, the one named last changes fastest.
Arguments:
- tile_values: float32 [4096, 128, 128], P(('groups', 'dp')), parts along dimension 0, may hold values from 0.0001 to 1
- tile_row: int32 [4096], P(('groups', 'dp')), parts along dimension 0, may hold values from 0 to 31, as said below
- tile_owner: int32 [4096, 1], P(('groups', 'dp')), parts along dimension 0, may hold values from 0 to 15; in each aligned block of 128 rows (0 to 127, 128 to 255, ...) at most 16 rows name the same one
- tile_sub: int32 [4096], P(('groups', 'dp')), parts along dimension 0, may hold values from 0 to 15
- labels: int32 [8192], P(('groups', 'dp')), parts along dimension 0, may hold values from 0 to 511
Outputs:
- centroids: bfloat16 [1024, 32768], P('groups', 'dp'), parts along dimension 0
- similarity: float32 [8192], P(('groups', 'dp')), parts along dimension 0
The draws below stay inside these ranges and needn't reach their ends.
There are 2 independent parts, one for each index of `groups`. The reference program is written for one: setup_inputs(seed, part) draws one part's arguments, and reference() takes and returns one part's arrays. A program takes and returns all parts, laid end to end along the dimension named above; each array names one. Nothing has to cross between parts.
Inputs may be any that keep to these rules, and one draw needn't show every extreme that they name: `tile_owner`: among the 128 tiles of one index of dp (aligned blocks), at most 16 name the same column group, a bound that some block reaches. `tile_row`: most tiles belong to a row block of their own index of dp; others to any row block.
All inputs are finite; a program needn't handle non-finite values.
Results may differ from the reference program's by a relative error of at most 0.0038.
Values may be sent and summed in bfloat16 or wider, within the bound.
No kernel may reach another device: no remote copies, remote signals or barrier semaphores. Data moves between devices by JAX's collectives and lax.ppermute only.
A program may use at most 128 MiB of HBM per device.

```python
import math
import jax
import jax.numpy as jnp
import numpy as np
from jax import lax

K = 512
TB_OWN = 16
TPB = 64
RB_DEV = 2
VB = 256
V = 32768
TILES_DEV = 128
TILES_ALL = 2048
RB_ALL = 32
DOCS = 4096
CAP = 16
N_DP = 16


def draw_tile_values(key, part):
    key = jax.random.fold_in(key, 11)
    profile_key, value_key = jax.random.split(key, 2)
    low_level = math.log(0.01)
    profile = jnp.exp(jax.random.uniform(profile_key, (128,), jnp.float32, low_level, 0.0))
    entries = jnp.exp(jax.random.uniform(value_key, (TILES_ALL, 128, 128), jnp.float32, low_level, 0.0))
    return (entries * profile[None, None, :]).astype(jnp.float32)


def draw_tile_row(key, part):
    key = jax.random.fold_in(key, 7)
    shed_key, offset_key, other_key, block_key = jax.random.split(key, 4)
    positions = jnp.arange(TILES_ALL, dtype=jnp.int32)
    device_of = positions // TILES_DEV
    home_block = device_of * RB_DEV + positions % RB_DEV
    shed_mask = jax.random.randint(shed_key, (TILES_ALL,), 0, 4) == 0
    offset_kind = jax.random.randint(offset_key, (TILES_ALL,), 0, 4)
    random_device = jax.random.randint(other_key, (TILES_ALL,), 0, N_DP)
    offsets = jnp.where(offset_kind == 0, 1, jnp.where(offset_kind == 1, N_DP // 2, N_DP - 1))
    target = jnp.where(offset_kind == 3, random_device, (device_of + offsets) % N_DP)
    forced_far = positions == 0
    forced_near = positions == TILES_DEV
    target = jnp.where(forced_far, N_DP // 2, target)
    target = jnp.where(forced_near, 2 % N_DP, target)
    shed_mask = jnp.logical_or(shed_mask, jnp.logical_or(forced_far, forced_near))
    foreign = target * RB_DEV + jax.random.randint(block_key, (TILES_ALL,), 0, RB_DEV)
    return jnp.where(shed_mask, foreign, home_block).astype(jnp.int32)


def set_ends(values, stream_key, least, high):
    shape = values.shape
    index_at = [jax.random.randint(jax.random.fold_in(stream_key, axis), (), 0, shape[axis]) for axis in range(len(shape))]
    values = values.at[tuple(index_at)].set(least)
    longest = shape.index(max(shape))
    index_at[longest] = (index_at[longest] + 1) % shape[longest]
    return values.at[tuple(index_at)].set(high)


def assign_block(own_key, own, number, rows, amount, top, most, lean):
    ranking = jax.random.permutation(own_key, amount)
    heavy_load, ordinary = load_shares(amount, rows * top, most, lean, True), load_shares(amount, rows * top, most, lean, False)
    places = jnp.arange(amount)

    def named(lengths, rotation):
        used = int((lengths > 0).sum())
        fixed = max(1, used // 4)
        shifted = fixed + (places - fixed + rotation * (used - fixed)) % max(1, amount - fixed)
        return jnp.zeros((amount,), jnp.int32).at[ranking[jnp.where(places < fixed, places, shifted)]].set(jnp.asarray(lengths, jnp.int32))

    lengths = jnp.where(number % 4 == 0, named(heavy_load, number // 4), named(ordinary, number - number // 4 - 1))
    mixed = jax.random.permutation(jax.random.fold_in(own, 3), amount)
    donor, receiver = mixed[0:amount // 2 * 2:2], mixed[1:amount // 2 * 2:2]
    room = jnp.minimum(lengths[donor] - 1, most - lengths[receiver]) // 2
    room = jnp.where((donor == ranking[0]) | (receiver == ranking[0]) | (lengths[receiver] == 0), 0, jnp.maximum(room, 0))
    shifted = jax.random.randint(jax.random.fold_in(own, 4), (amount // 2,), 0, 1 << 20) % (room + 1)
    lengths = lengths.at[donor].add(-shifted).at[receiver].add(shifted)
    items = jnp.searchsorted(jnp.cumsum(lengths), jnp.arange(rows * top), side="right").astype(jnp.int32)
    listing = items.reshape(top, rows).T
    listing = listing[jax.random.permutation(jax.random.fold_in(own, 1), rows)]
    rotation = jax.random.randint(jax.random.fold_in(own, 2), (rows, 1), 0, top)
    return jnp.take_along_axis(listing, (jnp.arange(top)[None, :] + rotation) % top, axis=1)


def load_shares(count, total, limit, skew, full):
    weights = [(1 << 20) // math.isqrt(rank ** skew) + 1 for rank in range(1, count + 1)]
    largest = limit if full else min(limit, max(-(-total // count), total * weights[0] // sum(weights)))
    least = 1 if total - largest >= count - 1 else 0
    counts, spare = [largest] + [least] * (count - 1), total - largest - least * (count - 1)
    while spare > 0:
        movable = [i for i in range(1, count) if counts[i] < largest] or [i for i in range(1, count) if counts[i] < limit]
        pool, left = sum([weights[i] for i in movable]), spare
        for i in movable:
            more = min(limit - counts[i], max(1, left * weights[i] // pool), spare)
            counts[i] = counts[i] + more
            spare = spare - more
    return np.array(counts)


def setup_inputs(seed: int = 0, part: int = 0) -> dict:
    key_list = jax.random.split(jax.random.key(seed), 6)
    part_keys = jax.random.split(jax.random.fold_in(key_list[5], part), 6)
    tile_values = draw_tile_values(jax.random.fold_in(jax.random.fold_in(key_list[5], part), 71), part)
    tile_row = draw_tile_row(jax.random.fold_in(jax.random.fold_in(key_list[5], part), 71), part)
    tile_owner_keys = jax.random.split(jax.random.fold_in(part_keys[2], 1), TILES_ALL // (TPB * RB_DEV))
    tile_owner_turns = jax.random.permutation(jax.random.fold_in(part_keys[2], 3), TILES_ALL // (TPB * RB_DEV))
    tile_owner = jax.vmap(lambda own, number: assign_block(jax.random.fold_in(part_keys[2], 2), own, number, TPB * RB_DEV, N_DP, 1, CAP, 2))(tile_owner_keys, tile_owner_turns).reshape((TILES_ALL, 1))
    tile_sub = set_ends(jax.random.randint(part_keys[3], (TILES_ALL,), 0, TB_OWN), jax.random.fold_in(part_keys[3], 1), 0, TB_OWN - 1).astype(jnp.int32)
    labels = set_ends(jax.random.randint(part_keys[4], (DOCS,), 0, K), jax.random.fold_in(part_keys[4], 1), 0, K - 1).astype(jnp.int32)
    return dict(tile_values=tile_values, tile_row=tile_row, tile_owner=tile_owner, tile_sub=tile_sub, labels=labels)


EPSILON = 1e-06

def reference(tile_values, tile_row, tile_owner, tile_sub, labels):
    squares = lax.optimization_barrier(jnp.sum(tile_values * tile_values, axis=2))
    row_squares = jax.ops.segment_sum(squares, tile_row, num_segments=RB_ALL)
    inverse = lax.rsqrt(row_squares + EPSILON)
    normed = (tile_values * inverse[tile_row][:, :, None]).astype(jnp.bfloat16)
    row_labels = labels.reshape(RB_ALL, 128)[tile_row]
    column_block = tile_owner[:, 0] * TB_OWN + tile_sub
    segment_ids = (row_labels * VB + column_block[:, None]).reshape(-1).astype(jnp.int32)
    flat_rows = normed.reshape(-1, 128).astype(jnp.float32)
    cluster_sums = jax.ops.segment_sum(flat_rows, segment_ids, num_segments=K * VB)
    wide_sums = cluster_sums.reshape(K, VB * 128)
    cluster_sq = lax.optimization_barrier(jnp.sum(wide_sums * wide_sums, axis=1))
    centroid = wide_sums * lax.rsqrt(cluster_sq + EPSILON)[:, None]
    centroids = (centroid * math.sqrt(V)).astype(jnp.bfloat16)
    picked = centroid.reshape(K * VB, 128)[segment_ids]
    tile_score = lax.optimization_barrier(jnp.sum(flat_rows * picked, axis=1)).reshape(-1, 128)
    similarity = jax.ops.segment_sum(tile_score, tile_row, num_segments=RB_ALL).reshape(DOCS)
    return (centroids, similarity)
```

```python
import functools
import math

import jax
import jax.numpy as jnp
from jax import lax
from jax.experimental import pallas as pl
from jax.experimental.pallas import tpu as pltpu
from jax.sharding import PartitionSpec as P

K = 512
TB_OWN = 16
LANES = 128
EPSILON = 1e-06
CODE_TOP = 65535.0
CODE_SHIFT = 32768
VMEM_BYTES = 56 * 1024 * 1024
STEP_TILES = 16
GROUPS = 4


def split_sum(values, left):
    high = values.astype(jnp.bfloat16)
    low = (values - high.astype(jnp.float32)).astype(jnp.bfloat16)
    dims = (((1,), (1,)), ((), ()))
    return lax.dot_general(left, high, dims, preferred_element_type=jnp.float32) + lax.dot_general(
        left, low, dims, preferred_element_type=jnp.float32
    )


def pack_kernel(cap, owner_ref, row_ref, me_ref, x_ref, *refs):
    count = len(refs) - 6
    outs, sq_ref = refs[:count], refs[count]
    coded, square, used, place, sems = refs[count + 1 :]
    step = pl.program_id(0)
    tiles = x_ref.shape[0]
    me = me_ref[0]

    @pl.when(step == 0)
    def _():
        square[...] = jnp.zeros_like(square)

        def clear(d, carry):
            used[d] = 0
            return carry

        lax.fori_loop(0, count, clear, 0)

    def one_tile(i, carry):
        t = step * tiles + i
        x = x_ref[i]
        square[row_ref[t]] += x * x
        code = jnp.floor(jnp.sqrt(x) * CODE_TOP + 0.5).astype(jnp.int32) - CODE_SHIFT
        coded[t] = code.astype(jnp.int16)
        d = owner_ref[t] ^ me
        rank = used[d]
        place[d * cap + rank] = t
        used[d] = rank + 1
        return carry

    lax.fori_loop(0, tiles, one_tile, 0)

    @pl.when(step == pl.num_programs(0) - 1)
    def _():
        def copy(d, s):
            return pltpu.make_async_copy(
                coded.at[place[d * cap + s]], outs[d].at[s], sems.at[d, s]
            )

        for d in range(count):

            def send(s, carry, d=d):
                copy(d, s).start()
                return carry

            lax.fori_loop(0, used[d], send, 0)
        ones = jnp.ones((8, LANES), jnp.bfloat16)

        def reduce_block(r, carry):
            sq_ref[pl.ds(r, 1), :] = split_sum(square[r], ones)[:1]
            return carry

        lax.fori_loop(0, square.shape[0], reduce_block, 0)
        for d in range(count):

            def finish(s, carry, d=d):
                copy(d, s).wait()
                return carry

            lax.fori_loop(0, used[d], finish, 0)


def pack(tile_values, tile_row, owner, me, devices, cap, blocks):
    tiles = tile_values.shape[0]
    step = math.gcd(STEP_TILES, tiles)
    return pl.pallas_call(
        functools.partial(pack_kernel, cap),
        grid=(tiles // step,),
        in_specs=[pl.BlockSpec(memory_space=pltpu.SMEM)] * 3
        + [pl.BlockSpec((step, LANES, LANES), lambda i: (i, 0, 0))],
        out_specs=[pl.BlockSpec(memory_space=pl.ANY)] * devices
        + [pl.BlockSpec((blocks, LANES), lambda i: (0, 0))],
        out_shape=[jax.ShapeDtypeStruct((cap, LANES, LANES), jnp.int16)] * devices
        + [jax.ShapeDtypeStruct((blocks, LANES), jnp.float32)],
        scratch_shapes=[
            pltpu.VMEM((tiles, LANES, LANES), jnp.int16),
            pltpu.VMEM((blocks, LANES, LANES), jnp.float32),
            pltpu.SMEM((devices,), jnp.int32),
            pltpu.SMEM((devices * cap,), jnp.int32),
            pltpu.SemaphoreType.DMA((devices, cap)),
        ],
        compiler_params=pltpu.CompilerParams(vmem_limit_bytes=VMEM_BYTES),
        cost_estimate=pl.CostEstimate(
            flops=4 * tile_values.size,
            bytes_accessed=6 * tile_values.size,
            transcendentals=tile_values.size,
        ),
        name="pack",
    )(owner, tile_row, me, tile_values)


def hot(labels_ref, row):
    cluster = lax.broadcasted_iota(jnp.int32, (K, LANES), 0)
    return cluster == labels_ref[pl.ds(row, 1), :]


def fold_kernel(shifts, cap, first, last, meta_ref, held_ref, me_ref, labels_ref, inv_ref, *refs):
    width = len(shifts)
    xs = refs[:width]
    rest = refs[width + (0 if first else 1) :]
    normed, sums = rest[:width], rest[width]
    me = me_ref[0]
    if first:
        sums[...] = jnp.zeros_like(sums)
    else:
        pltpu.sync_copy(refs[width], sums)
    for d, x_ref, n_ref in zip(shifts, xs, normed):
        source = me ^ d

        def one_tile(s, carry, source=source, x_ref=x_ref, n_ref=n_ref):
            code = meta_ref[source * cap + s]
            row, sub = code // TB_OWN, code % TB_OWN
            root = x_ref[s].astype(jnp.int32).astype(jnp.float32) + float(CODE_SHIFT)
            tile = (root * root * inv_ref[row]).astype(jnp.bfloat16)
            n_ref[s] = tile
            pick = jnp.where(hot(labels_ref, row), 1.0, 0.0).astype(jnp.bfloat16)
            at = (slice(None), pl.ds(pl.multiple_of(sub * LANES, LANES), LANES))
            sums[at] += jnp.dot(pick, tile, preferred_element_type=jnp.float32)
            return carry

        lax.fori_loop(0, held_ref[source], one_tile, 0)
    if last:
        total = jnp.zeros((K, LANES), jnp.float32)
        for sub in range(TB_OWN):
            part = sums[:, sub * LANES : (sub + 1) * LANES]
            total = total + part * part
        rest[width + 1][...] = split_sum(total, jnp.ones((8, LANES), jnp.bfloat16))


def fold(shifts, cap, meta, held, me, labels, inverse, blocks, sums, last):
    first = sums is None
    vmem = pl.BlockSpec(memory_space=pltpu.VMEM)
    out_shape = [jax.ShapeDtypeStruct((cap, LANES, LANES), jnp.bfloat16)] * len(shifts)
    out_shape += [jax.ShapeDtypeStruct((K, TB_OWN * LANES), jnp.float32)]
    if last:
        out_shape += [jax.ShapeDtypeStruct((8, K), jnp.float32)]
    tiles = len(shifts) * cap // 2
    return pl.pallas_call(
        functools.partial(fold_kernel, shifts, cap, first, last),
        in_specs=[pl.BlockSpec(memory_space=pltpu.SMEM)] * 3
        + [vmem] * (2 + len(shifts))
        + ([] if first else [pl.BlockSpec(memory_space=pl.ANY)]),
        out_specs=[vmem] * len(out_shape),
        out_shape=out_shape,
        compiler_params=pltpu.CompilerParams(vmem_limit_bytes=VMEM_BYTES),
        cost_estimate=pl.CostEstimate(
            flops=tiles * 2 * K * LANES * LANES * 8,
            bytes_accessed=tiles * 8 * LANES * LANES + 4 * inverse.size + 8 * K * TB_OWN * LANES,
            transcendentals=0,
        ),
        name="fold",
    )(meta, held, me, labels, inverse, *blocks, *([] if first else [sums]))


def score_kernel(devices, cap, meta_ref, held_ref, me_ref, labels_ref, sums_ref, *refs):
    normed, out_ref, narrow = refs[:devices], refs[devices], refs[devices + 1]
    me = me_ref[0]
    out_ref[...] = jnp.zeros_like(out_ref)
    narrow[...] = sums_ref[...].astype(jnp.bfloat16)
    for d in range(devices):
        source = me ^ d

        def one_tile(s, carry, source=source, n_ref=normed[d]):
            code = meta_ref[source * cap + s]
            row, sub = code // TB_OWN, code % TB_OWN
            at = (slice(None), pl.ds(pl.multiple_of(sub * LANES, LANES), LANES))
            every = lax.dot_general(
                narrow[at], n_ref[s], (((1,), (1,)), ((), ())), preferred_element_type=jnp.float32
            )
            own = jnp.where(hot(labels_ref, row), every, 0.0)
            out_ref[pl.ds(row, 1), :] += jnp.sum(own, axis=0, keepdims=True)
            return carry

        lax.fori_loop(0, held_ref[source], one_tile, 0)


def score(cap, meta, held, me, labels, sums, normed):
    vmem = pl.BlockSpec(memory_space=pltpu.VMEM)
    tiles = len(normed) * cap // 2
    return pl.pallas_call(
        functools.partial(score_kernel, len(normed), cap),
        in_specs=[pl.BlockSpec(memory_space=pltpu.SMEM)] * 3 + [vmem] * (2 + len(normed)),
        out_specs=vmem,
        out_shape=jax.ShapeDtypeStruct(labels.shape, jnp.float32),
        scratch_shapes=[pltpu.VMEM(sums.shape, jnp.bfloat16)],
        compiler_params=pltpu.CompilerParams(vmem_limit_bytes=VMEM_BYTES),
        cost_estimate=pl.CostEstimate(
            flops=tiles * 2 * K * LANES * LANES * 8,
            bytes_accessed=tiles * 4 * LANES * LANES + 4 * sums.size,
            transcendentals=0,
        ),
        name="score",
    )(meta, held, me, labels, sums, *normed)


def shards(tile_values, tile_row, tile_owner, tile_sub, labels):
    devices = lax.axis_size("dp")
    tiles = tile_values.shape[0]
    home = labels.shape[0]
    blocks = home // LANES * devices
    cap = max(2, 2 * tiles // devices)
    here = lax.axis_index("dp").astype(jnp.int32)
    me = here.reshape(1)
    owner = tile_owner[:, 0]

    described = jnp.concatenate([labels, owner, tile_row * TB_OWN + tile_sub])
    all_described = lax.all_gather(described, "dp", axis=0)
    packed = pack(tile_values, tile_row, owner, me, devices, cap, blocks)
    outgoing, partial_sq = packed[:devices], packed[devices]
    row_sq = lax.psum(partial_sq, "dp")

    incoming = [outgoing[0]] + [
        lax.ppermute(outgoing[d], "dp", [(i, i ^ d) for i in range(devices)])
        for d in range(1, devices)
    ]

    all_labels = all_described[:, :home].reshape(blocks, LANES)
    mine = all_described[:, home : home + tiles] == here
    code = all_described[:, home + tiles :]
    earlier = jnp.arange(tiles)[:, None] < jnp.arange(tiles)[None, :]
    rank = jnp.dot(
        mine.astype(jnp.bfloat16), earlier.astype(jnp.bfloat16), preferred_element_type=jnp.float32
    ).astype(jnp.int32)
    chosen = mine[:, None, :] & (rank[:, None, :] == jnp.arange(cap)[None, :, None])
    meta = jnp.sum(jnp.where(chosen, code[:, None, :], 0), axis=2).reshape(-1)
    held = jnp.sum(mine.astype(jnp.int32), axis=1)

    inverse = lax.rsqrt(row_sq + EPSILON)
    scale = jnp.broadcast_to(
        (inverse * (1.0 / CODE_TOP**2))[:, :, None], (blocks, LANES, LANES)
    )
    per = devices // GROUPS
    sums, normed = None, []
    for g in range(GROUPS):
        shifts = tuple(range(g * per, (g + 1) * per))
        got = fold(
            shifts, cap, meta, held, me, all_labels, scale,
            [incoming[d] for d in shifts], sums, g == GROUPS - 1,
        )
        normed += got[:per]
        sums = got[per]
    cluster_sq = lax.psum(got[per + 1][0], "dp")
    own_scale = lax.rsqrt(cluster_sq + EPSILON)
    vocab_size = TB_OWN * LANES * devices
    centroid = sums * own_scale[:, None]
    centroids = (centroid * math.sqrt(vocab_size)).astype(jnp.bfloat16)
    partial = score(cap, meta, held, me, all_labels, sums, normed)
    gathered = lax.psum_scatter(partial, "dp", scatter_dimension=0, tiled=True).reshape(-1)
    is_label = labels[:, None] == jnp.arange(K, dtype=jnp.int32)[None, :]
    doc_scale = jnp.sum(jnp.where(is_label, own_scale[None, :], 0.0), axis=1)
    return (centroids, gathered * doc_scale)


def solution(mesh):
    return jax.shard_map(
        shards,
        mesh=mesh,
        in_specs=(
            P(("groups", "dp"), None, None),
            P(("groups", "dp")),
            P(("groups", "dp"), None),
            P(("groups", "dp")),
            P(("groups", "dp")),
        ),
        out_specs=(P("groups", "dp"), P(("groups", "dp"))),
        check_vma=False,
    )
```

```python
import functools
import math

import jax
import jax.numpy as jnp
import numpy as np
from jax import lax
from jax.experimental import pallas as pl
from jax.experimental.pallas import tpu as pltpu
from jax.sharding import PartitionSpec as P

K = 512
TB_OWN = 16
LANES = 128
EPSILON = 1e-06
CODE_TOP = 65535.0
CODE_SHIFT = 32768
VMEM_BYTES = 56 * 1024 * 1024
STEP_TILES = 16
PARTS = (0.0, 5 / 16, 10 / 16, 14 / 16, 1.0)
CACHED_BLOCKS = 64
QUAD = 4
NT = (((1,), (1,)), ((), ()))


def lane_sums(values):
    ones = jnp.ones((8, LANES), jnp.bfloat16)
    high = values.astype(jnp.bfloat16)
    low = (values - high.astype(jnp.float32)).astype(jnp.bfloat16)
    return lax.dot_general(ones, high, NT, preferred_element_type=jnp.float32) + lax.dot_general(
        ones, low, NT, preferred_element_type=jnp.float32
    )


def params():
    return pltpu.CompilerParams(vmem_limit_bytes=VMEM_BYTES)


SMEM = pl.BlockSpec(memory_space=pltpu.SMEM)
VMEM = pl.BlockSpec(memory_space=pltpu.VMEM)
ANY = pl.BlockSpec(memory_space=pl.ANY)


def pack_kernel(cuts, owner_ref, x_ref, *refs):
    parts = len(cuts) - 1
    outs = refs[:parts]
    coded, used, place, sems = refs[parts:]
    step = pl.program_id(0)
    tiles = x_ref.shape[0]
    devices = used.shape[0]

    @pl.when(step == 0)
    def _():
        def clear(d, carry):
            used[d] = 0
            return carry

        lax.fori_loop(0, devices, clear, 0)

    def act(t, what):
        spot = place[t]
        owner, rank = spot // cuts[-1], spot % cuts[-1]
        for q in range(parts):

            @pl.when((rank >= cuts[q]) & (rank < cuts[q + 1]))
            def _(q=q):
                copy = pltpu.make_async_copy(
                    coded.at[t], outs[q].at[owner, rank - cuts[q]], sems.at[t]
                )
                what(copy)

    def one_tile(i, carry):
        t = step * tiles + i
        x = x_ref[i]
        root = x * lax.rsqrt(x)
        code = (root * CODE_TOP + 0.5).astype(jnp.int32) - CODE_SHIFT
        coded[t] = code.astype(jnp.int16)
        owner = owner_ref[t]
        rank = used[owner]
        used[owner] = rank + 1
        place[t] = owner * cuts[-1] + rank
        act(t, lambda copy: copy.start())
        return carry

    lax.fori_loop(0, tiles, one_tile, 0)

    @pl.when(step == pl.num_programs(0) - 1)
    def _():
        def finish(t, carry):
            act(t, lambda copy: copy.wait())
            return carry

        lax.fori_loop(0, coded.shape[0], finish, 0)


def pack(tile_values, owner, devices, cuts):
    tiles = tile_values.shape[0]
    step = math.gcd(STEP_TILES, tiles)
    return pl.pallas_call(
        functools.partial(pack_kernel, cuts),
        grid=(tiles // step,),
        in_specs=[SMEM, pl.BlockSpec((step, LANES, LANES), lambda i: (i, 0, 0))],
        out_specs=[ANY] * (len(cuts) - 1),
        out_shape=[
            jax.ShapeDtypeStruct((devices, high - low, LANES, LANES), jnp.int16)
            for low, high in zip(cuts, cuts[1:])
        ],
        scratch_shapes=[
            pltpu.VMEM((tiles, LANES, LANES), jnp.int16),
            pltpu.SMEM((devices,), jnp.int32),
            pltpu.SMEM((tiles,), jnp.int32),
            pltpu.SemaphoreType.DMA((tiles,)),
        ],
        compiler_params=params(),
        cost_estimate=pl.CostEstimate(
            flops=8 * tile_values.size,
            bytes_accessed=6 * tile_values.size,
            transcendentals=tile_values.size,
        ),
        name="pack",
    )(owner, tile_values)


def norms_kernel(row_ref, x_ref, sq_ref, square):
    step = pl.program_id(0)
    tiles = x_ref.shape[0]

    @pl.when(step == 0)
    def _():
        square[...] = jnp.zeros_like(square)

    def one_tile(i, carry):
        x = x_ref[i]
        square[row_ref[step * tiles + i]] += x * x
        return carry

    lax.fori_loop(0, tiles, one_tile, 0)

    @pl.when(step == pl.num_programs(0) - 1)
    def _():
        def reduce_block(r, carry):
            sq_ref[pl.ds(r, 1), :] = lane_sums(square[r])[:1]
            return carry

        lax.fori_loop(0, square.shape[0], reduce_block, 0)


def norms(tile_values, tile_row, blocks):
    tiles = tile_values.shape[0]
    step = math.gcd(STEP_TILES, tiles)
    return pl.pallas_call(
        norms_kernel,
        grid=(tiles // step,),
        in_specs=[SMEM, pl.BlockSpec((step, LANES, LANES), lambda i: (i, 0, 0))],
        out_specs=pl.BlockSpec((blocks, LANES), lambda i: (0, 0)),
        out_shape=jax.ShapeDtypeStruct((blocks, LANES), jnp.float32),
        scratch_shapes=[pltpu.VMEM((blocks, LANES, LANES), jnp.float32)],
        compiler_params=params(),
        cost_estimate=pl.CostEstimate(
            flops=8 * tile_values.size, bytes_accessed=4 * tile_values.size, transcendentals=0
        ),
        name="norms",
    )(tile_row, tile_values)


def fold_kernel(cap, low, part, first, last, order_ref, bound_ref, meta_ref, labels_ref, inv_ref,
                x_ref, *refs):
    normed, sums = refs[0 if first else 1], refs[1 if first else 2]
    if first:
        sums[...] = jnp.zeros_like(sums)
    else:
        pltpu.sync_copy(refs[0], sums)
    cluster = lax.broadcasted_iota(jnp.int32, (K, LANES), 0)

    def decoded(slot, row):
        at = (slot // cap, slot % cap - low)
        root = x_ref[at].astype(jnp.int32).astype(jnp.float32) + float(CODE_SHIFT)
        tile = (root * root * inv_ref[row]).astype(jnp.bfloat16)
        normed[at] = tile
        return tile

    def picked(row):
        hot = cluster == labels_ref[pl.ds(row, 1), :]
        return jnp.where(hot, 1.0, 0.0).astype(jnp.bfloat16)

    def one_sub(sub, carry):
        start = bound_ref[part * (TB_OWN + 1) + sub]
        end = bound_ref[part * (TB_OWN + 1) + sub + 1]
        at = (slice(None), pl.ds(pl.multiple_of(sub * LANES, LANES), LANES))

        def one_pair(p, carry):
            place = start + 2 * p
            more = place + 1 < end
            slot_a = order_ref[place]
            slot_b = order_ref[jnp.where(more, place + 1, place)]
            row_a, row_b = meta_ref[slot_a] // TB_OWN, meta_ref[slot_b] // TB_OWN
            tiles = jnp.concatenate([decoded(slot_a, row_a), decoded(slot_b, row_b)], axis=0)
            none = labels_ref.shape[0] - 1
            pick = jnp.concatenate([picked(row_a), picked(jnp.where(more, row_b, none))], axis=1)
            sums[at] += jnp.dot(pick, tiles, preferred_element_type=jnp.float32)
            return carry

        lax.fori_loop(0, (end - start + 1) // 2, one_pair, 0)
        return carry

    lax.fori_loop(0, TB_OWN, one_sub, 0)
    if last:
        total = jnp.zeros((K, LANES), jnp.float32)
        for sub in range(TB_OWN):
            part = sums[:, sub * LANES : (sub + 1) * LANES]
            total = total + part * part
        refs[-1][...] = lane_sums(total)


def fold(cap, low, part, order, bounds, meta, labels, inverse, x, sums, last):
    first = sums is None
    out_shape = [
        jax.ShapeDtypeStruct(x.shape, jnp.bfloat16),
        jax.ShapeDtypeStruct((K, TB_OWN * LANES), jnp.float32),
    ]
    if last:
        out_shape += [jax.ShapeDtypeStruct((8, K), jnp.float32)]
    return pl.pallas_call(
        functools.partial(fold_kernel, cap, low, part, first, last),
        in_specs=[SMEM] * 3 + [VMEM] * 3 + ([] if first else [ANY]),
        out_specs=[VMEM] * len(out_shape),
        out_shape=out_shape,
        compiler_params=params(),
        cost_estimate=pl.CostEstimate(
            flops=x.size * K * 8,
            bytes_accessed=4 * x.size + 4 * inverse.size + 8 * K * TB_OWN * LANES,
            transcendentals=0,
        ),
        name="fold",
    )(order, bounds, meta, labels, inverse, x, *([] if first else [sums]))


def score_kernel(parts, cached, order_ref, bound_ref, meta_ref, place_ref, hot_ref, sums_ref, *refs):
    normed, out_ref = refs[:parts], refs[parts]
    narrow, tiles, products, hot_some, sems = refs[parts + 1 :]
    copies, base = [], 0
    for q, n_ref in enumerate(normed):
        count = n_ref.shape[0]
        copies.append(pltpu.make_async_copy(n_ref, tiles.at[pl.ds(base, count)], sems.at[q]))
        base += count
    for copy in copies:
        copy.start()
    products[...] = jnp.zeros_like(products)
    narrow[...] = sums_ref[...].astype(jnp.bfloat16)
    for copy in copies:
        copy.wait()
    none = products.shape[0] - 1

    def one_sub(sub, carry):
        start, end = bound_ref[sub], bound_ref[sub + 1]
        at = (slice(None), pl.ds(pl.multiple_of(sub * LANES, LANES), LANES))

        def one_quad(p, carry):
            rows, spots = [], []
            for j in range(QUAD):
                place = start + QUAD * p + j
                held = place < end
                slot = order_ref[jnp.where(held, place, start)]
                rows.append(jnp.where(held, meta_ref[slot] // TB_OWN, none))
                spots.append(place_ref[slot])
            if cached:
                hots = [hot_ref[row] for row in rows]
            else:
                for j, row in enumerate(rows):
                    pltpu.sync_copy(hot_ref.at[row], hot_some.at[j])
                hots = [hot_some[j] for j in range(QUAD)]
            pick = jnp.concatenate(hots, axis=0)
            chosen = jnp.dot(pick, narrow[at], preferred_element_type=jnp.float32)
            for j in range(QUAD):
                part = chosen[j * LANES : (j + 1) * LANES]
                products[rows[j]] += part * tiles[spots[j]].astype(jnp.float32)
            return carry

        lax.fori_loop(0, (end - start + QUAD - 1) // QUAD, one_quad, 0)
        return carry

    lax.fori_loop(0, TB_OWN, one_sub, 0)

    def reduce_block(r, carry):
        out_ref[pl.ds(r, 1), :] = lane_sums(products[r])[:1]
        return carry

    lax.fori_loop(0, none, reduce_block, 0)


def score(order, bounds, meta, place, hot, sums, normed):
    blocks = hot.shape[0] - 1
    cached = blocks <= CACHED_BLOCKS
    flat = [x.reshape((-1, LANES, LANES)) for x in normed]
    slots = sum(x.shape[0] for x in flat)
    return pl.pallas_call(
        functools.partial(score_kernel, len(flat), cached),
        in_specs=[SMEM] * 4 + [VMEM if cached else ANY, VMEM] + [ANY] * len(flat),
        out_specs=VMEM,
        out_shape=jax.ShapeDtypeStruct((blocks, LANES), jnp.float32),
        scratch_shapes=[
            pltpu.VMEM(sums.shape, jnp.bfloat16),
            pltpu.VMEM((slots, LANES, LANES), jnp.bfloat16),
            pltpu.VMEM((blocks + 1, LANES, LANES), jnp.float32),
            pltpu.VMEM((QUAD, LANES, K), jnp.bfloat16),
            pltpu.SemaphoreType.DMA((len(flat),)),
        ],
        compiler_params=params(),
        cost_estimate=pl.CostEstimate(
            flops=slots * LANES * LANES * K * 2,
            bytes_accessed=slots * 2 * LANES * LANES + 4 * sums.size,
            transcendentals=0,
        ),
        name="score",
    )(order, bounds, meta, place, hot, sums, *flat)


def to_all(values):
    devices = lax.axis_size("dp")
    rows = jnp.broadcast_to(values[None], (devices, *values.shape))
    return lax.all_to_all(rows, "dp", split_axis=0, concat_axis=0, tiled=True)


def sorted_slots(key, top):
    slots = jnp.arange(key.shape[0], dtype=jnp.int32)
    ahead = (key[None, :] < key[:, None]) | (
        (key[None, :] == key[:, None]) & (slots[None, :] < slots[:, None])
    )
    position = jnp.sum(ahead.astype(jnp.int32), axis=1)
    here = position[None, :] == slots[:, None]
    order = jnp.sum(jnp.where(here, slots[None, :], 0), axis=1)
    levels = jnp.arange(top + 1, dtype=jnp.int32)
    bounds = jnp.sum((key[None, :] < levels[:, None]).astype(jnp.int32), axis=1)
    return order, bounds


def shards(tile_values, tile_row, tile_owner, tile_sub, labels):
    devices = lax.axis_size("dp")
    tiles = tile_values.shape[0]
    home = labels.shape[0]
    blocks = home // LANES * devices
    cap = max(2, 2 * tiles // devices)
    cuts = tuple(sorted({int(cap * share) for share in PARTS}))
    parts = len(cuts) - 1
    here = lax.axis_index("dp").astype(jnp.int32)
    owner = tile_owner[:, 0]

    described = jnp.concatenate([labels, owner, tile_row * TB_OWN + tile_sub])
    all_described = to_all(described)
    outgoing = pack(tile_values, owner, devices, cuts)
    incoming = [
        lax.all_to_all(x, "dp", split_axis=0, concat_axis=0, tiled=True) for x in outgoing
    ]
    after, unused = lax.optimization_barrier((tile_values, outgoing[0]))
    partial_sq = norms(after, tile_row, blocks)
    row_sq = jnp.sum(to_all(partial_sq), axis=0)

    all_labels = all_described[:, :home].reshape(blocks, LANES)
    padded_labels = jnp.concatenate([all_labels, jnp.full((1, LANES), -1, jnp.int32)])
    hot = (padded_labels[:, :, None] == jnp.arange(K, dtype=jnp.int32)).astype(jnp.bfloat16)
    mine = all_described[:, home : home + tiles] == here
    code = all_described[:, home + tiles :]
    earlier = jnp.arange(tiles)[:, None] < jnp.arange(tiles)[None, :]
    rank = jnp.dot(
        mine.astype(jnp.bfloat16), earlier.astype(jnp.bfloat16), preferred_element_type=jnp.float32
    ).astype(jnp.int32)
    chosen = mine[:, None, :] & (rank[:, None, :] == jnp.arange(cap)[None, :, None])
    meta = jnp.sum(jnp.where(chosen, code[:, None, :] + 1, 0), axis=2).reshape(-1) - 1
    sub = jnp.where(meta < 0, TB_OWN, meta % TB_OWN)
    slot_rank = np.arange(devices * cap) % cap
    slot_part = np.searchsorted(np.array(cuts), slot_rank, side="right") - 1
    low, high = np.array(cuts)[slot_part], np.array(cuts)[slot_part + 1]
    place = (devices * low + np.arange(devices * cap) // cap * (high - low) + slot_rank - low)
    place = jnp.asarray(place, jnp.int32)
    fold_key = jnp.asarray(slot_part * (TB_OWN + 1), jnp.int32) + sub
    fold_order, fold_bounds = sorted_slots(fold_key, parts * (TB_OWN + 1))
    score_order, score_bounds = sorted_slots(sub, TB_OWN)

    inverse = lax.rsqrt(row_sq + EPSILON)
    scale = jnp.broadcast_to((inverse * (1.0 / CODE_TOP**2))[:, :, None], (blocks, LANES, LANES))
    sums, normed = None, []
    for q in range(parts):
        got = fold(
            cap, cuts[q], q, fold_order, fold_bounds, meta, padded_labels, scale,
            incoming[q], sums, q == parts - 1,
        )
        normed.append(got[0])
        sums = got[1]
    cluster_sq = jnp.sum(to_all(got[2][0]), axis=0)
    own_scale = lax.rsqrt(cluster_sq + EPSILON)
    partial = score(score_order, score_bounds, meta, place, hot, sums, normed)
    returned = lax.all_to_all(
        partial.reshape(devices, home), "dp", split_axis=0, concat_axis=0, tiled=True
    )
    vocab_size = TB_OWN * LANES * devices
    centroid = sums * own_scale[:, None]
    centroids = (centroid * math.sqrt(vocab_size)).astype(jnp.bfloat16)
    is_label = labels[:, None] == jnp.arange(K, dtype=jnp.int32)[None, :]
    doc_scale = jnp.sum(jnp.where(is_label, own_scale[None, :], 0.0), axis=1)
    return (centroids, jnp.sum(returned, axis=0) * doc_scale)


def solution(mesh):
    return jax.shard_map(
        shards,
        mesh=mesh,
        in_specs=(
            P(("groups", "dp"), None, None),
            P(("groups", "dp")),
            P(("groups", "dp"), None),
            P(("groups", "dp")),
            P(("groups", "dp")),
        ),
        out_specs=(P("groups", "dp"), P(("groups", "dp"))),
        check_vma=False,
    )
```

```python
import functools
import math

import jax
import jax.numpy as jnp
import numpy as np
from jax import lax
from jax.experimental import pallas as pl
from jax.experimental.pallas import tpu as pltpu
from jax.sharding import PartitionSpec as P

K = 512
TB_OWN = 16
LANES = 128
EPSILON = 1e-06
CODE_TOP = 65535.0
CODE_SHIFT = 32768
VMEM_BYTES = 56 * 1024 * 1024
STEP_TILES = 16
PARTS = (0.0, 8 / 16, 13 / 16, 1.0)
CACHED_BLOCKS = 64
QUAD = 4
BATCH = 8
NT = (((1,), (1,)), ((), ()))
SMEM = pl.BlockSpec(memory_space=pltpu.SMEM)
VMEM = pl.BlockSpec(memory_space=pltpu.VMEM)
ANY = pl.BlockSpec(memory_space=pl.ANY)


def lane_sums(values):
    ones = jnp.ones((8, LANES), jnp.bfloat16)
    high = values.astype(jnp.bfloat16)
    low = (values - high.astype(jnp.float32)).astype(jnp.bfloat16)
    return lax.dot_general(ones, high, NT, preferred_element_type=jnp.float32) + lax.dot_general(
        ones, low, NT, preferred_element_type=jnp.float32
    )


def block_sums(square, out_ref, count):
    batch = math.gcd(BATCH, count)

    def one_batch(c, carry):
        some = square[pl.ds(c * batch, batch)].reshape((batch * LANES, LANES))
        sums = lane_sums(some)
        for j in range(batch):
            out_ref[pl.ds(c * batch + j, 1), :] += sums[:1, j * LANES : (j + 1) * LANES]
        return carry

    lax.fori_loop(0, count // batch, one_batch, 0)


def params():
    return pltpu.CompilerParams(vmem_limit_bytes=VMEM_BYTES)


def pack_kernel(cuts, place_ref, x_ref, *refs):
    parts = len(cuts) - 1
    outs = refs[:parts]
    coded, sems = refs[parts:]
    step = pl.program_id(0)
    tiles = x_ref.shape[0]

    def some_tiles(i, carry):
        first = step * tiles + i * QUAD
        for j in range(QUAD):
            x = x_ref[i * QUAD + j]
            root = x * lax.rsqrt(x)
            code = (root * CODE_TOP + 0.5).astype(jnp.int32) - CODE_SHIFT
            coded[first + j] = code.astype(jnp.int16)
        for j in range(QUAD):
            spot = place_ref[first + j]
            owner, rank = spot // cuts[-1], spot % cuts[-1]
            for q in range(parts):

                @pl.when((rank >= cuts[q]) & (rank < cuts[q + 1]))
                def _(q=q, t=first + j, owner=owner, rank=rank):
                    pltpu.make_async_copy(
                        coded.at[t], outs[q].at[owner, rank - cuts[q]], sems.at[t]
                    ).start()

        return carry

    lax.fori_loop(0, tiles // QUAD, some_tiles, 0)

    @pl.when(step == pl.num_programs(0) - 1)
    def _():
        def finish(t, carry):
            pltpu.make_async_copy(coded.at[t], outs[0].at[0, 0], sems.at[t]).wait()
            return carry

        lax.fori_loop(0, coded.shape[0], finish, 0)


def pack(tile_values, place, devices, cuts):
    tiles = tile_values.shape[0]
    step = math.gcd(STEP_TILES, tiles)
    return pl.pallas_call(
        functools.partial(pack_kernel, cuts),
        grid=(tiles // step,),
        in_specs=[SMEM, pl.BlockSpec((step, LANES, LANES), lambda i: (i, 0, 0))],
        out_specs=[ANY] * (len(cuts) - 1),
        out_shape=[
            jax.ShapeDtypeStruct((devices, high - low, LANES, LANES), jnp.int16)
            for low, high in zip(cuts, cuts[1:])
        ],
        scratch_shapes=[
            pltpu.VMEM((tiles, LANES, LANES), jnp.int16),
            pltpu.SemaphoreType.DMA((tiles,)),
        ],
        compiler_params=params(),
        cost_estimate=pl.CostEstimate(
            flops=8 * tile_values.size,
            bytes_accessed=6 * tile_values.size,
            transcendentals=tile_values.size,
        ),
        name="pack",
    )(place, tile_values)


def norms_kernel(row_ref, x_ref, sq_ref, square):
    step = pl.program_id(0)
    tiles = x_ref.shape[0]

    @pl.when(step == 0)
    def _():
        square[...] = jnp.zeros_like(square)

    def some_tiles(i, carry):
        for j in range(QUAD):
            x = x_ref[i * QUAD + j]
            square[row_ref[step * tiles + i * QUAD + j]] += x * x
        return carry

    lax.fori_loop(0, tiles // QUAD, some_tiles, 0)

    @pl.when(step == pl.num_programs(0) - 1)
    def _():
        sq_ref[...] = jnp.zeros_like(sq_ref)
        block_sums(square, sq_ref, square.shape[0])


def norms(tile_values, tile_row, blocks):
    tiles = tile_values.shape[0]
    step = math.gcd(STEP_TILES, tiles)
    return pl.pallas_call(
        norms_kernel,
        grid=(tiles // step,),
        in_specs=[SMEM, pl.BlockSpec((step, LANES, LANES), lambda i: (i, 0, 0))],
        out_specs=pl.BlockSpec((blocks, LANES), lambda i: (0, 0)),
        out_shape=jax.ShapeDtypeStruct((blocks, LANES), jnp.float32),
        scratch_shapes=[pltpu.VMEM((blocks, LANES, LANES), jnp.float32)],
        compiler_params=params(),
        cost_estimate=pl.CostEstimate(
            flops=8 * tile_values.size, bytes_accessed=4 * tile_values.size, transcendentals=0
        ),
        name="norms",
    )(tile_row, tile_values)


def stage_kernel(q, base, last, cached, fold_order, fold_bound, score_order, score_bound, meta,
                 place, done, labels, before, inv_hbm, x_hbm, hot_hbm, *refs):
    earlier, refs = refs[:q], refs[q:]
    sums_in, refs = (refs[0], refs[1:]) if q else (None, refs)
    part, sums_out, extra = refs[:3]
    inv, x, hot, sums, narrow, tiles, products, sems = refs[3:]
    fresh = tiles.at[pl.ds(base, x.shape[0])]
    needed = [
        pltpu.make_async_copy(x_hbm, x, sems.at[0]),
        pltpu.make_async_copy(inv_hbm, inv, sems.at[1]),
    ]
    if q:
        needed.append(pltpu.make_async_copy(sums_in, sums, sems.at[2]))
    later = [pltpu.make_async_copy(hot_hbm, hot, sems.at[3])] if cached else []
    spot = 0
    for e, e_hbm in enumerate(earlier):
        held = tiles.at[pl.ds(spot, e_hbm.shape[0])]
        later.append(pltpu.make_async_copy(e_hbm, held, sems.at[6 + e]))
        spot += e_hbm.shape[0]
    for copy in needed + later:
        copy.start()
    products[...] = jnp.zeros_like(products)
    part[...] = before[...]
    if not q:
        sums[...] = jnp.zeros_like(sums)
    for copy in needed:
        copy.wait()
    none = products.shape[0] - 1
    cluster = lax.broadcasted_iota(jnp.int32, (K, LANES), 0)

    def columns(sub):
        return (slice(None), pl.ds(pl.multiple_of(sub * LANES, LANES), LANES))

    def quad(order, start, end, p):
        rows, spots = [], []
        for j in range(QUAD):
            at = start + QUAD * p + j
            slot = order[jnp.where(at < end, at, start)]
            rows.append((meta[slot] // TB_OWN, at < end))
            spots.append(place[slot])
        return rows, spots

    def fold_sub(sub, carry):
        start = fold_bound[q * (TB_OWN + 1) + sub]
        end = fold_bound[q * (TB_OWN + 1) + sub + 1]

        def one_quad(p, carry):
            rows, spots = quad(fold_order, start, end, p)
            folded, picks = [], []
            for (row, held), spot in zip(rows, spots):
                root = x[spot - base].astype(jnp.int32).astype(jnp.float32) + float(CODE_SHIFT)
                tile = (root * root * inv[row]).astype(jnp.bfloat16)
                tiles[spot] = tile
                folded.append(tile)
                own = cluster == labels[pl.ds(jnp.where(held, row, none), 1), :]
                picks.append(jnp.where(own, 1.0, 0.0).astype(jnp.bfloat16))
            pick = jnp.concatenate(picks, axis=1)
            sums[columns(sub)] += jnp.dot(
                pick, jnp.concatenate(folded, axis=0), preferred_element_type=jnp.float32
            )
            return carry

        lax.fori_loop(0, (end - start + QUAD - 1) // QUAD, one_quad, 0)
        return carry

    lax.fori_loop(0, TB_OWN, fold_sub, 0)
    results = [pltpu.make_async_copy(sums, sums_out, sems.at[4])]
    if not last:
        results.append(pltpu.make_async_copy(fresh, extra, sems.at[5]))
    for copy in results:
        copy.start()
    if last:
        total = jnp.zeros((K, LANES), jnp.float32)
        for sub in range(TB_OWN):
            some = sums[:, sub * LANES : (sub + 1) * LANES]
            total = total + some * some
        extra[...] = lane_sums(total)
    for copy in later:
        copy.wait()

    def score_sub(sub, carry):
        start, end = score_bound[sub], score_bound[sub + 1]
        narrow[...] = sums[columns(sub)].astype(jnp.bfloat16)

        def one_quad(p, carry):
            rows, spots = quad(score_order, start, end, p)
            rows = [jnp.where(held, row, none) for row, held in rows]
            if cached:
                hots = [hot[row] for row in rows]
            else:
                for j, row in enumerate(rows):
                    pltpu.sync_copy(hot_hbm.at[row], hot.at[j])
                hots = [hot[j] for j in range(QUAD)]
            chosen = jnp.dot(
                jnp.concatenate(hots, axis=0), narrow[...], preferred_element_type=jnp.float32
            )
            for j in range(QUAD):
                own = chosen[j * LANES : (j + 1) * LANES]
                products[rows[j]] += own * tiles[spots[j]].astype(jnp.float32)
            return carry

        lax.fori_loop(0, (end - start + QUAD - 1) // QUAD, one_quad, 0)
        return carry

    lax.fori_loop(done[q], done[q + 1], score_sub, 0)
    block_sums(products, part, none)
    for copy in results:
        copy.wait()


def stage(q, cuts, scalars, labels, before, inverse, x, hot, normed, sums):
    devices, width = x.shape[:2]
    last = q == len(cuts) - 2
    blocks = inverse.shape[0]
    cached = blocks <= CACHED_BLOCKS
    flat = x.reshape((devices * width, LANES, LANES))
    tile_rows = devices * cuts[-1]
    wide = jax.ShapeDtypeStruct((K, TB_OWN * LANES), jnp.float32)
    return pl.pallas_call(
        functools.partial(stage_kernel, q, devices * cuts[q], last, cached),
        in_specs=[SMEM] * len(scalars) + [VMEM] * 2 + [ANY] * (3 + q + (q > 0)),
        out_specs=[VMEM, ANY, VMEM if last else ANY],
        out_shape=[
            jax.ShapeDtypeStruct((blocks, LANES), jnp.float32),
            wide,
            jax.ShapeDtypeStruct((8, K), jnp.float32)
            if last
            else jax.ShapeDtypeStruct(flat.shape, jnp.bfloat16),
        ],
        scratch_shapes=[
            pltpu.VMEM(inverse.shape, jnp.float32),
            pltpu.VMEM(flat.shape, jnp.int16),
            pltpu.VMEM(hot.shape if cached else (QUAD, LANES, K), jnp.bfloat16),
            pltpu.VMEM(wide.shape, jnp.float32),
            pltpu.VMEM((K, LANES), jnp.bfloat16),
            pltpu.VMEM((tile_rows, LANES, LANES), jnp.bfloat16),
            pltpu.VMEM((blocks + 1, LANES, LANES), jnp.float32),
            pltpu.SemaphoreType.DMA((6 + len(cuts),)),
        ],
        compiler_params=params(),
        cost_estimate=pl.CostEstimate(
            flops=x.size * K * 8,
            bytes_accessed=4 * x.size + 4 * inverse.size + 8 * K * TB_OWN * LANES,
            transcendentals=0,
        ),
        name="stage",
    )(*scalars, labels, before, inverse, flat, hot, *normed, *([sums] if q else []))


def exchange(x):
    return lax.all_to_all(x, "dp", split_axis=0, concat_axis=0, tiled=True)


def after(value, *others):
    return lax.optimization_barrier((value, *others))[0]


def sorted_slots(key, top):
    slots = jnp.arange(key.shape[0], dtype=jnp.int32)
    ahead = (key[None, :] < key[:, None]) | (
        (key[None, :] == key[:, None]) & (slots[None, :] < slots[:, None])
    )
    position = jnp.sum(ahead.astype(jnp.int32), axis=1)
    here = position[None, :] == slots[:, None]
    order = jnp.sum(jnp.where(here, slots[None, :], 0), axis=1)
    levels = jnp.arange(top + 1, dtype=jnp.int32)
    bounds = jnp.sum((key[None, :] < levels[:, None]).astype(jnp.int32), axis=1)
    return order, bounds


def ranks(group, sub):
    index = jnp.arange(sub.shape[-1], dtype=jnp.int32)
    before = (sub[..., None, :] < sub[..., :, None]) | (
        (sub[..., None, :] == sub[..., :, None]) & (index[None, :] < index[:, None])
    )
    same = group[..., None, :] == group[..., :, None]
    return jnp.sum((before & same).astype(jnp.int32), axis=-1)


def shards(tile_values, tile_row, tile_owner, tile_sub, labels):
    devices = lax.axis_size("dp")
    tiles = tile_values.shape[0]
    home = labels.shape[0]
    blocks = home // LANES * devices
    cap = max(2, 2 * tiles // devices)
    cuts = tuple(sorted({int(cap * share) for share in PARTS}))
    parts = len(cuts) - 1
    here = lax.axis_index("dp").astype(jnp.int32)
    owner = tile_owner[:, 0]

    partial_sq = norms(tile_values, tile_row, blocks)
    described = jnp.concatenate([labels, owner, tile_row * TB_OWN + tile_sub])
    told = jnp.concatenate([partial_sq.reshape(-1), described.astype(jnp.float32)])
    heard = exchange(jnp.broadcast_to(told[None], (devices, told.shape[0])))
    put = after(owner * cap + ranks(owner, tile_sub), partial_sq)
    outgoing = pack(tile_values, put, devices, cuts)
    incoming, previous = [], heard
    for x in outgoing:
        previous = exchange(after(x, previous))
        incoming.append(previous)

    row_sq = jnp.sum(heard[:, : blocks * LANES], axis=0).reshape(blocks, LANES)
    all_described = heard[:, blocks * LANES :].astype(jnp.int32)
    all_labels = all_described[:, :home].reshape(blocks, LANES)
    padded_labels = jnp.concatenate([all_labels, jnp.full((1, LANES), -1, jnp.int32)])
    hot = (padded_labels[:, :, None] == jnp.arange(K, dtype=jnp.int32)).astype(jnp.bfloat16)
    mine = all_described[:, home : home + tiles] == here
    code = all_described[:, home + tiles :]
    rank = ranks(mine.astype(jnp.int32), code % TB_OWN)
    chosen = mine[:, None, :] & (rank[:, None, :] == jnp.arange(cap)[None, :, None])
    meta = jnp.sum(jnp.where(chosen, code[:, None, :] + 1, 0), axis=2).reshape(-1) - 1
    sub = jnp.where(meta < 0, TB_OWN, meta % TB_OWN)
    slot_rank = np.arange(devices * cap) % cap
    slot_part = np.searchsorted(np.array(cuts), slot_rank, side="right") - 1
    low, high = np.array(cuts)[slot_part], np.array(cuts)[slot_part + 1]
    place = devices * low + np.arange(devices * cap) // cap * (high - low) + slot_rank - low
    fold_key = jnp.asarray(slot_part * (TB_OWN + 1), jnp.int32) + sub
    fold_order, fold_bounds = sorted_slots(fold_key, parts * (TB_OWN + 1))
    score_order, score_bounds = sorted_slots(sub, TB_OWN)
    left = np.arange(parts)[:, None] < slot_part[None, :]
    done = jnp.min(jnp.where(left, sub[None, :], TB_OWN), axis=1)
    done = jnp.concatenate([jnp.zeros((1,), jnp.int32), done])
    scalars = [
        fold_order, fold_bounds, score_order, score_bounds, meta, jnp.asarray(place, jnp.int32), done
    ]

    inverse = lax.rsqrt(row_sq + EPSILON)
    scale = jnp.broadcast_to((inverse * (1.0 / CODE_TOP**2))[:, :, None], (blocks, LANES, LANES))
    partial, sums, normed = jnp.zeros((blocks, LANES), jnp.float32), None, []
    for q in range(parts):
        partial, sums, extra = stage(
            q, cuts, scalars, padded_labels, partial, scale, incoming[q], hot, normed, sums
        )
        normed.append(extra)
    square = jnp.broadcast_to(extra[:1], (devices, K))
    back = jnp.sum(
        exchange(jnp.concatenate([partial.reshape(devices, home), square], axis=1)), axis=0
    )
    own_scale = lax.rsqrt(back[home:] + EPSILON)
    vocab_size = TB_OWN * LANES * devices
    centroid = sums * own_scale[:, None]
    centroids = (centroid * math.sqrt(vocab_size)).astype(jnp.bfloat16)
    is_label = labels[:, None] == jnp.arange(K, dtype=jnp.int32)[None, :]
    doc_scale = jnp.sum(jnp.where(is_label, own_scale[None, :], 0.0), axis=1)
    return (centroids, back[:home] * doc_scale)


def solution(mesh):
    return jax.shard_map(
        shards,
        mesh=mesh,
        in_specs=(
            P(("groups", "dp"), None, None),
            P(("groups", "dp")),
            P(("groups", "dp"), None),
            P(("groups", "dp")),
            P(("groups", "dp")),
        ),
        out_specs=(P("groups", "dp"), P(("groups", "dp"))),
        check_vma=False,
    )
```

```python
import functools
import math

import jax
import jax.numpy as jnp
import numpy as np
from jax import lax
from jax.experimental import pallas as pl
from jax.experimental.pallas import tpu as pltpu
from jax.sharding import PartitionSpec as P

K = 512
TB_OWN = 16
LANES = 128
EPSILON = 1e-06
CODE_TOP = 65535.0
CODE_SHIFT = 32768
VMEM_BYTES = 56 * 1024 * 1024
STEP_TILES = 16
PARTS = (0.0, 9 / 16, 14 / 16, 1.0)
CACHED_BLOCKS = 64
QUAD = 4
BATCH = 8
NT = (((1,), (1,)), ((), ()))
SMEM = pl.BlockSpec(memory_space=pltpu.SMEM)
VMEM = pl.BlockSpec(memory_space=pltpu.VMEM)
ANY = pl.BlockSpec(memory_space=pl.ANY)


def lane_sums(values):
    ones = jnp.ones((8, LANES), jnp.bfloat16)
    high = values.astype(jnp.bfloat16)
    low = (values - high.astype(jnp.float32)).astype(jnp.bfloat16)
    return lax.dot_general(ones, high, NT, preferred_element_type=jnp.float32) + lax.dot_general(
        ones, low, NT, preferred_element_type=jnp.float32
    )


def block_sums(square, out_ref, count):
    batch = math.gcd(BATCH, count)

    def one_batch(c, carry):
        some = square[pl.ds(c * batch, batch)].reshape((batch * LANES, LANES))
        sums = lane_sums(some)
        for j in range(batch):
            out_ref[pl.ds(c * batch + j, 1), :] += sums[:1, j * LANES : (j + 1) * LANES]
        return carry

    lax.fori_loop(0, count // batch, one_batch, 0)


def params():
    return pltpu.CompilerParams(vmem_limit_bytes=VMEM_BYTES)


def pack_kernel(cuts, place_ref, x_ref, *refs):
    parts = len(cuts) - 1
    outs = refs[:parts]
    coded, sems = refs[parts:]
    step = pl.program_id(0)
    tiles = x_ref.shape[0]

    def some_tiles(i, carry):
        first = step * tiles + i * QUAD
        for j in range(QUAD):
            x = x_ref[i * QUAD + j]
            root = x * lax.rsqrt(x)
            code = (root * CODE_TOP + 0.5).astype(jnp.int32) - CODE_SHIFT
            coded[first + j] = code.astype(jnp.int16)
        for j in range(QUAD):
            spot = place_ref[first + j]
            owner, rank = spot // cuts[-1], spot % cuts[-1]
            for q in range(parts):

                @pl.when((rank >= cuts[q]) & (rank < cuts[q + 1]))
                def _(q=q, t=first + j, owner=owner, rank=rank):
                    pltpu.make_async_copy(
                        coded.at[t], outs[q].at[owner, rank - cuts[q]], sems.at[t]
                    ).start()

        return carry

    lax.fori_loop(0, tiles // QUAD, some_tiles, 0)

    @pl.when(step == pl.num_programs(0) - 1)
    def _():
        def finish(t, carry):
            pltpu.make_async_copy(coded.at[t], outs[0].at[0, 0], sems.at[t]).wait()
            return carry

        lax.fori_loop(0, coded.shape[0], finish, 0)


def pack(tile_values, place, devices, cuts):
    tiles = tile_values.shape[0]
    step = math.gcd(STEP_TILES, tiles)
    return pl.pallas_call(
        functools.partial(pack_kernel, cuts),
        grid=(tiles // step,),
        in_specs=[SMEM, pl.BlockSpec((step, LANES, LANES), lambda i: (i, 0, 0))],
        out_specs=[ANY] * (len(cuts) - 1),
        out_shape=[
            jax.ShapeDtypeStruct((devices, high - low, LANES, LANES), jnp.int16)
            for low, high in zip(cuts, cuts[1:])
        ],
        scratch_shapes=[
            pltpu.VMEM((tiles, LANES, LANES), jnp.int16),
            pltpu.SemaphoreType.DMA((tiles,)),
        ],
        compiler_params=params(),
        cost_estimate=pl.CostEstimate(
            flops=8 * tile_values.size,
            bytes_accessed=6 * tile_values.size,
            transcendentals=tile_values.size,
        ),
        name="pack",
    )(place, tile_values)


def norms_kernel(row_ref, x_ref, sq_ref, square):
    step = pl.program_id(0)
    tiles = x_ref.shape[0]

    @pl.when(step == 0)
    def _():
        square[...] = jnp.zeros_like(square)

    def some_tiles(i, carry):
        for j in range(QUAD):
            x = x_ref[i * QUAD + j]
            square[row_ref[step * tiles + i * QUAD + j]] += x * x
        return carry

    lax.fori_loop(0, tiles // QUAD, some_tiles, 0)

    @pl.when(step == pl.num_programs(0) - 1)
    def _():
        sq_ref[...] = jnp.zeros_like(sq_ref)
        block_sums(square, sq_ref, square.shape[0])


def norms(tile_values, tile_row, blocks):
    tiles = tile_values.shape[0]
    step = math.gcd(STEP_TILES, tiles)
    return pl.pallas_call(
        norms_kernel,
        grid=(tiles // step,),
        in_specs=[SMEM, pl.BlockSpec((step, LANES, LANES), lambda i: (i, 0, 0))],
        out_specs=pl.BlockSpec((blocks, LANES), lambda i: (0, 0)),
        out_shape=jax.ShapeDtypeStruct((blocks, LANES), jnp.float32),
        scratch_shapes=[pltpu.VMEM((blocks, LANES, LANES), jnp.float32)],
        compiler_params=params(),
        cost_estimate=pl.CostEstimate(
            flops=8 * tile_values.size, bytes_accessed=4 * tile_values.size, transcendentals=0
        ),
        name="norms",
    )(tile_row, tile_values)


def stage_kernel(q, base, last, cached, fold_order, fold_bound, score_order, score_bound, meta,
                 place, done, labels, before, inv_hbm, x_hbm, hot_hbm, *refs):
    earlier, refs = refs[:q], refs[q:]
    sums_in, refs = (refs[0], refs[1:]) if q else (None, refs)
    part, sums_out, extra = refs[:3]
    inv, x, hot, sums, narrow, tiles, products, sems = refs[3:]
    fresh = tiles.at[pl.ds(base, x.shape[0])]
    needed = [
        pltpu.make_async_copy(x_hbm, x, sems.at[0]),
        pltpu.make_async_copy(inv_hbm, inv, sems.at[1]),
    ]
    if q:
        needed.append(pltpu.make_async_copy(sums_in, sums, sems.at[2]))
    later = [pltpu.make_async_copy(hot_hbm, hot, sems.at[3])] if cached else []
    spot = 0
    for e, e_hbm in enumerate(earlier):
        held = tiles.at[pl.ds(spot, e_hbm.shape[0])]
        later.append(pltpu.make_async_copy(e_hbm, held, sems.at[6 + e]))
        spot += e_hbm.shape[0]
    for copy in needed + later:
        copy.start()
    products[...] = jnp.zeros_like(products)
    part[...] = before[...]
    if not q:
        sums[...] = jnp.zeros_like(sums)
    for copy in needed:
        copy.wait()
    none = products.shape[0] - 1
    cluster = lax.broadcasted_iota(jnp.int32, (K, LANES), 0)

    def columns(sub):
        return (slice(None), pl.ds(pl.multiple_of(sub * LANES, LANES), LANES))

    def quad(order, start, end, p):
        rows, spots = [], []
        for j in range(QUAD):
            at = start + QUAD * p + j
            slot = order[jnp.where(at < end, at, start)]
            rows.append((meta[slot] // TB_OWN, at < end))
            spots.append(place[slot])
        return rows, spots

    def fold_sub(sub, carry):
        start = fold_bound[q * (TB_OWN + 1) + sub]
        end = fold_bound[q * (TB_OWN + 1) + sub + 1]

        def one_quad(p, carry):
            rows, spots = quad(fold_order, start, end, p)
            folded, picks = [], []
            for (row, held), spot in zip(rows, spots):
                root = x[spot - base].astype(jnp.int32).astype(jnp.float32) + float(CODE_SHIFT)
                tile = (root * root * inv[row]).astype(jnp.bfloat16)
                tiles[spot] = tile
                folded.append(tile)
                own = cluster == labels[pl.ds(jnp.where(held, row, none), 1), :]
                picks.append(jnp.where(own, 1.0, 0.0).astype(jnp.bfloat16))
            pick = jnp.concatenate(picks, axis=1)
            sums[columns(sub)] += jnp.dot(
                pick, jnp.concatenate(folded, axis=0), preferred_element_type=jnp.float32
            )
            return carry

        lax.fori_loop(0, (end - start + QUAD - 1) // QUAD, one_quad, 0)
        return carry

    lax.fori_loop(0, TB_OWN, fold_sub, 0)
    results = [pltpu.make_async_copy(sums, sums_out, sems.at[4])]
    if not last:
        results.append(pltpu.make_async_copy(fresh, extra, sems.at[5]))
    for copy in results:
        copy.start()
    if last:
        total = jnp.zeros((K, LANES), jnp.float32)
        for sub in range(TB_OWN):
            some = sums[:, sub * LANES : (sub + 1) * LANES]
            total = total + some * some
        extra[...] = lane_sums(total)
    for copy in later:
        copy.wait()

    def score_sub(sub, carry):
        start, end = score_bound[sub], score_bound[sub + 1]
        narrow[...] = sums[columns(sub)].astype(jnp.bfloat16)

        def one_quad(p, carry):
            rows, spots = quad(score_order, start, end, p)
            rows = [jnp.where(held, row, none) for row, held in rows]
            if cached:
                hots = [hot[row] for row in rows]
            else:
                for j, row in enumerate(rows):
                    pltpu.sync_copy(hot_hbm.at[row], hot.at[j])
                hots = [hot[j] for j in range(QUAD)]
            chosen = jnp.dot(
                jnp.concatenate(hots, axis=0), narrow[...], preferred_element_type=jnp.float32
            )
            for j in range(QUAD):
                own = chosen[j * LANES : (j + 1) * LANES]
                products[rows[j]] += own * tiles[spots[j]].astype(jnp.float32)
            return carry

        lax.fori_loop(0, (end - start + QUAD - 1) // QUAD, one_quad, 0)
        return carry

    lax.fori_loop(done[q], done[q + 1], score_sub, 0)
    block_sums(products, part, none)
    for copy in results:
        copy.wait()


def stage(q, cuts, scalars, labels, before, inverse, x, hot, normed, sums):
    devices, width = x.shape[:2]
    last = q == len(cuts) - 2
    blocks = inverse.shape[0]
    cached = blocks <= CACHED_BLOCKS
    flat = x.reshape((devices * width, LANES, LANES))
    tile_rows = devices * cuts[-1]
    wide = jax.ShapeDtypeStruct((K, TB_OWN * LANES), jnp.float32)
    return pl.pallas_call(
        functools.partial(stage_kernel, q, devices * cuts[q], last, cached),
        in_specs=[SMEM] * len(scalars) + [VMEM] * 2 + [ANY] * (3 + q + (q > 0)),
        out_specs=[VMEM, ANY, VMEM if last else ANY],
        out_shape=[
            jax.ShapeDtypeStruct((blocks, LANES), jnp.float32),
            wide,
            jax.ShapeDtypeStruct((8, K), jnp.float32)
            if last
            else jax.ShapeDtypeStruct(flat.shape, jnp.bfloat16),
        ],
        scratch_shapes=[
            pltpu.VMEM(inverse.shape, jnp.float32),
            pltpu.VMEM(flat.shape, jnp.int16),
            pltpu.VMEM(hot.shape if cached else (QUAD, LANES, K), jnp.bfloat16),
            pltpu.VMEM(wide.shape, jnp.float32),
            pltpu.VMEM((K, LANES), jnp.bfloat16),
            pltpu.VMEM((tile_rows, LANES, LANES), jnp.bfloat16),
            pltpu.VMEM((blocks + 1, LANES, LANES), jnp.float32),
            pltpu.SemaphoreType.DMA((6 + len(cuts),)),
        ],
        compiler_params=params(),
        cost_estimate=pl.CostEstimate(
            flops=x.size * K * 8,
            bytes_accessed=4 * x.size + 4 * inverse.size + 8 * K * TB_OWN * LANES,
            transcendentals=0,
        ),
        name="stage",
    )(*scalars, labels, before, inverse, flat, hot, *normed, *([sums] if q else []))


def exchange(x):
    return lax.all_to_all(x, "dp", split_axis=0, concat_axis=0, tiled=True)


def after(value, *others):
    return lax.optimization_barrier((value, *others))[0]


def sorted_slots(key, top):
    slots = jnp.arange(key.shape[0], dtype=jnp.int32)
    ahead = (key[None, :] < key[:, None]) | (
        (key[None, :] == key[:, None]) & (slots[None, :] < slots[:, None])
    )
    position = jnp.sum(ahead.astype(jnp.int32), axis=1)
    here = position[None, :] == slots[:, None]
    order = jnp.sum(jnp.where(here, slots[None, :], 0), axis=1)
    levels = jnp.arange(top + 1, dtype=jnp.int32)
    bounds = jnp.sum((key[None, :] < levels[:, None]).astype(jnp.int32), axis=1)
    return order, bounds


def ranks(group, sub):
    index = jnp.arange(sub.shape[-1], dtype=jnp.int32)
    before = (sub[..., None, :] < sub[..., :, None]) | (
        (sub[..., None, :] == sub[..., :, None]) & (index[None, :] < index[:, None])
    )
    same = group[..., None, :] == group[..., :, None]
    return jnp.sum((before & same).astype(jnp.int32), axis=-1)


def shards(tile_values, tile_row, tile_owner, tile_sub, labels):
    devices = lax.axis_size("dp")
    tiles = tile_values.shape[0]
    home = labels.shape[0]
    blocks = home // LANES * devices
    cap = max(2, 2 * tiles // devices)
    cuts = tuple(sorted({int(cap * share) for share in PARTS}))
    parts = len(cuts) - 1
    here = lax.axis_index("dp").astype(jnp.int32)
    owner = tile_owner[:, 0]

    outgoing = pack(tile_values, owner * cap + ranks(owner, tile_sub), devices, cuts)
    incoming = [exchange(outgoing[0])]
    partial_sq = norms(after(tile_values, outgoing[0]), tile_row, blocks)
    described = jnp.concatenate([labels, owner, tile_row * TB_OWN + tile_sub])
    told = jnp.concatenate([partial_sq.reshape(-1), described.astype(jnp.float32)])
    heard = exchange(jnp.broadcast_to(told[None], (devices, told.shape[0])))

    row_sq = jnp.sum(heard[:, : blocks * LANES], axis=0).reshape(blocks, LANES)
    all_described = heard[:, blocks * LANES :].astype(jnp.int32)
    all_labels = all_described[:, :home].reshape(blocks, LANES)
    padded_labels = jnp.concatenate([all_labels, jnp.full((1, LANES), -1, jnp.int32)])
    hot = (padded_labels[:, :, None] == jnp.arange(K, dtype=jnp.int32)).astype(jnp.bfloat16)
    mine = all_described[:, home : home + tiles] == here
    code = all_described[:, home + tiles :]
    rank = ranks(mine.astype(jnp.int32), code % TB_OWN)
    chosen = mine[:, None, :] & (rank[:, None, :] == jnp.arange(cap)[None, :, None])
    meta = jnp.sum(jnp.where(chosen, code[:, None, :] + 1, 0), axis=2).reshape(-1) - 1
    sub = jnp.where(meta < 0, TB_OWN, meta % TB_OWN)
    slot_rank = np.arange(devices * cap) % cap
    slot_part = np.searchsorted(np.array(cuts), slot_rank, side="right") - 1
    low, high = np.array(cuts)[slot_part], np.array(cuts)[slot_part + 1]
    place = devices * low + np.arange(devices * cap) // cap * (high - low) + slot_rank - low
    fold_key = jnp.asarray(slot_part * (TB_OWN + 1), jnp.int32) + sub
    fold_order, fold_bounds = sorted_slots(fold_key, parts * (TB_OWN + 1))
    score_order, score_bounds = sorted_slots(sub, TB_OWN)
    left = np.arange(parts)[:, None] < slot_part[None, :]
    done = jnp.min(jnp.where(left, sub[None, :], TB_OWN), axis=1)
    done = jnp.concatenate([jnp.zeros((1,), jnp.int32), done])
    scalars = [
        fold_order, fold_bounds, score_order, score_bounds, meta, jnp.asarray(place, jnp.int32), done
    ]

    inverse = lax.rsqrt(row_sq + EPSILON)
    scale = jnp.broadcast_to((inverse * (1.0 / CODE_TOP**2))[:, :, None], (blocks, LANES, LANES))
    partial, sums, normed = jnp.zeros((blocks, LANES), jnp.float32), None, []
    beside = (*scalars, padded_labels, hot, scale)
    for q in range(parts):
        if q + 1 < parts:
            incoming.append(exchange(after(outgoing[q + 1], incoming[q], *beside)))
        partial, sums, extra = stage(
            q, cuts, scalars, padded_labels, partial, scale, incoming[q], hot, normed, sums
        )
        beside = (partial, sums, extra)
        normed.append(extra)
    square = jnp.broadcast_to(extra[:1], (devices, K))
    back = jnp.sum(
        exchange(jnp.concatenate([partial.reshape(devices, home), square], axis=1)), axis=0
    )
    own_scale = lax.rsqrt(back[home:] + EPSILON)
    vocab_size = TB_OWN * LANES * devices
    centroid = sums * own_scale[:, None]
    centroids = (centroid * math.sqrt(vocab_size)).astype(jnp.bfloat16)
    is_label = labels[:, None] == jnp.arange(K, dtype=jnp.int32)[None, :]
    doc_scale = jnp.sum(jnp.where(is_label, own_scale[None, :], 0.0), axis=1)
    return (centroids, back[:home] * doc_scale)


def solution(mesh):
    return jax.shard_map(
        shards,
        mesh=mesh,
        in_specs=(
            P(("groups", "dp"), None, None),
            P(("groups", "dp")),
            P(("groups", "dp"), None),
            P(("groups", "dp")),
            P(("groups", "dp")),
        ),
        out_specs=(P("groups", "dp"), P(("groups", "dp"))),
        check_vma=False,
    )
```

```python
import functools
import math

import jax
import jax.numpy as jnp
import numpy as np
from jax import lax
from jax.experimental import pallas as pl
from jax.experimental.pallas import tpu as pltpu
from jax.sharding import PartitionSpec as P

K = 512
TB_OWN = 16
LANES = 128
EPSILON = 1e-06
CODE_TOP = 65535.0
CODE_SHIFT = 32768
VMEM_BYTES = 56 * 1024 * 1024
STEP_TILES = 32
PARTS = (0.0, 12 / 16, 1.0)
FLIGHT = 6
GROUPS = (6 / 30, 11 / 30, 15 / 30, 24 / 30, 1.0)
CACHED_BLOCKS = 64
QUAD = 4
BATCH = 8
NT = (((1,), (1,)), ((), ()))
SMEM = pl.BlockSpec(memory_space=pltpu.SMEM)
VMEM = pl.BlockSpec(memory_space=pltpu.VMEM)
ANY = pl.BlockSpec(memory_space=pl.ANY)


def lane_sums(values):
    ones = jnp.ones((8, LANES), jnp.bfloat16)
    high = values.astype(jnp.bfloat16)
    low = (values - high.astype(jnp.float32)).astype(jnp.bfloat16)
    return lax.dot_general(ones, high, NT, preferred_element_type=jnp.float32) + lax.dot_general(
        ones, low, NT, preferred_element_type=jnp.float32
    )


def block_sums(square, out_ref, count):
    batch = math.gcd(BATCH, count)

    def one_batch(c, carry):
        some = square[pl.ds(c * batch, batch)].reshape((batch * LANES, LANES))
        sums = lane_sums(some)
        for j in range(batch):
            out_ref[pl.ds(c * batch + j, 1), :] += sums[:1, j * LANES : (j + 1) * LANES]
        return carry

    lax.fori_loop(0, count // batch, one_batch, 0)


def params():
    return pltpu.CompilerParams(vmem_limit_bytes=VMEM_BYTES)


def pack_kernel(cuts, put_ref, used_ref, x_ref, *refs):
    parts = len(cuts) - 1
    devices = used_ref.shape[0]
    outs = refs[: devices * parts]
    coded, sems = refs[devices * parts :]
    step = pl.program_id(0)
    tiles = x_ref.shape[0]

    def some_tiles(i, carry):
        for j in range(QUAD):
            x = x_ref[i * QUAD + j]
            root = x * lax.rsqrt(x)
            code = (root * CODE_TOP + 0.5).astype(jnp.int32) - CODE_SHIFT
            coded[put_ref[step * tiles + i * QUAD + j]] = code.astype(jnp.int16)
        return carry

    lax.fori_loop(0, tiles // QUAD, some_tiles, 0)

    def each(what):
        for q in range(parts):
            for d in range(devices):

                @pl.when(used_ref[d] > cuts[q])
                def _(q=q, d=d):
                    some = coded.at[pl.ds(d * cuts[-1] + cuts[q], cuts[q + 1] - cuts[q])]
                    spot = q * devices + d
                    what(pltpu.make_async_copy(some, outs[spot], sems.at[spot]))

    @pl.when(step == pl.num_programs(0) - 1)
    def _():
        each(lambda copy: copy.start())
        each(lambda copy: copy.wait())


def pack(tile_values, put, used, cuts):
    tiles = tile_values.shape[0]
    devices = used.shape[0]
    step = math.gcd(STEP_TILES, tiles)
    count = devices * (len(cuts) - 1)
    return pl.pallas_call(
        functools.partial(pack_kernel, cuts),
        grid=(tiles // step,),
        in_specs=[SMEM, SMEM, pl.BlockSpec((step, LANES, LANES), lambda i: (i, 0, 0))],
        out_specs=[ANY] * count,
        out_shape=[
            jax.ShapeDtypeStruct((high - low, LANES, LANES), jnp.int16)
            for low, high in zip(cuts, cuts[1:])
            for d in range(devices)
        ],
        scratch_shapes=[
            pltpu.VMEM((devices * cuts[-1], LANES, LANES), jnp.int16),
            pltpu.SemaphoreType.DMA((count,)),
        ],
        compiler_params=params(),
        cost_estimate=pl.CostEstimate(
            flops=8 * tile_values.size,
            bytes_accessed=6 * tile_values.size,
            transcendentals=tile_values.size,
        ),
        name="pack",
    )(put, used, tile_values)


def norms_kernel(row_ref, x_ref, sq_ref, square):
    step = pl.program_id(0)
    tiles = x_ref.shape[0]

    @pl.when(step == 0)
    def _():
        square[...] = jnp.zeros_like(square)

    def some_tiles(i, carry):
        for j in range(QUAD):
            x = x_ref[i * QUAD + j]
            square[row_ref[step * tiles + i * QUAD + j]] += x * x
        return carry

    lax.fori_loop(0, tiles // QUAD, some_tiles, 0)

    @pl.when(step == pl.num_programs(0) - 1)
    def _():
        sq_ref[...] = jnp.zeros_like(sq_ref)
        block_sums(square, sq_ref, square.shape[0])


def norms(tile_values, tile_row, blocks):
    tiles = tile_values.shape[0]
    step = math.gcd(STEP_TILES, tiles)
    return pl.pallas_call(
        norms_kernel,
        grid=(tiles // step,),
        in_specs=[SMEM, pl.BlockSpec((step, LANES, LANES), lambda i: (i, 0, 0))],
        out_specs=pl.BlockSpec((blocks, LANES), lambda i: (0, 0)),
        out_shape=jax.ShapeDtypeStruct((blocks, LANES), jnp.float32),
        scratch_shapes=[pltpu.VMEM((blocks, LANES, LANES), jnp.float32)],
        compiler_params=params(),
        cost_estimate=pl.CostEstimate(
            flops=8 * tile_values.size, bytes_accessed=4 * tile_values.size, transcendentals=0
        ),
        name="norms",
    )(tile_row, tile_values)


def stage_kernel(q, base, width, last, cached, fold_order, fold_bound, score_order, score_bound,
                 meta, place, done, labels, before, inv_hbm, hot_hbm, *refs):
    x_hbms, earlier, refs = refs[:width], refs[width : width + q], refs[width + q :]
    sums_in, refs = (refs[0], refs[1:]) if q else (None, refs)
    part, sums_out, extra = refs[:3]
    inv, x, hot, sums, narrow, tiles, products, sems = refs[3:]
    fresh = tiles.at[pl.ds(base, x.shape[0])]
    needed = [pltpu.make_async_copy(inv_hbm, inv, sems.at[1])]
    if q:
        needed.append(pltpu.make_async_copy(sums_in, sums, sems.at[2]))
    spot = 0
    for e, x_hbm in enumerate(x_hbms):
        held = x.at[pl.ds(spot, x_hbm.shape[0])]
        needed.append(pltpu.make_async_copy(x_hbm, held, sems.at[6 + e]))
        spot += x_hbm.shape[0]
    later = [pltpu.make_async_copy(hot_hbm, hot, sems.at[3])] if cached else []
    spot = 0
    for e, e_hbm in enumerate(earlier):
        held = tiles.at[pl.ds(spot, e_hbm.shape[0])]
        later.append(pltpu.make_async_copy(e_hbm, held, sems.at[6 + width + e]))
        spot += e_hbm.shape[0]
    for copy in needed + later:
        copy.start()
    products[...] = jnp.zeros_like(products)
    part[...] = before[...]
    if not q:
        sums[...] = jnp.zeros_like(sums)
    for copy in needed:
        copy.wait()
    none = products.shape[0] - 1
    cluster = lax.broadcasted_iota(jnp.int32, (K, LANES), 0)

    def columns(sub):
        return (slice(None), pl.ds(pl.multiple_of(sub * LANES, LANES), LANES))

    def quad(order, start, end, p):
        rows, spots = [], []
        for j in range(QUAD):
            at = start + QUAD * p + j
            slot = order[jnp.where(at < end, at, start)]
            rows.append((meta[slot] // TB_OWN, at < end))
            spots.append(place[slot])
        return rows, spots

    def fold_sub(sub, carry):
        start = fold_bound[q * (TB_OWN + 1) + sub]
        end = fold_bound[q * (TB_OWN + 1) + sub + 1]

        def one_quad(p, carry):
            rows, spots = quad(fold_order, start, end, p)
            folded, picks = [], []
            for (row, held), spot in zip(rows, spots):
                root = x[spot - base].astype(jnp.int32).astype(jnp.float32) + float(CODE_SHIFT)
                tile = (root * root * inv[row]).astype(jnp.bfloat16)
                tiles[spot] = tile
                folded.append(tile)
                own = cluster == labels[pl.ds(jnp.where(held, row, none), 1), :]
                picks.append(jnp.where(own, 1.0, 0.0).astype(jnp.bfloat16))
            pick = jnp.concatenate(picks, axis=1)
            sums[columns(sub)] += jnp.dot(
                pick, jnp.concatenate(folded, axis=0), preferred_element_type=jnp.float32
            )
            return carry

        lax.fori_loop(0, (end - start + QUAD - 1) // QUAD, one_quad, 0)
        return carry

    lax.fori_loop(0, TB_OWN, fold_sub, 0)
    results = [pltpu.make_async_copy(sums, sums_out, sems.at[4])]
    if not last:
        results.append(pltpu.make_async_copy(fresh, extra, sems.at[5]))
    for copy in results:
        copy.start()
    if last:
        total = jnp.zeros((K, LANES), jnp.float32)
        for sub in range(TB_OWN):
            some = sums[:, sub * LANES : (sub + 1) * LANES]
            total = total + some * some
        extra[...] = lane_sums(total)
    for copy in later:
        copy.wait()

    def score_sub(sub, carry):
        start, end = score_bound[sub], score_bound[sub + 1]
        narrow[...] = sums[columns(sub)].astype(jnp.bfloat16)

        def one_quad(p, carry):
            rows, spots = quad(score_order, start, end, p)
            rows = [jnp.where(held, row, none) for row, held in rows]
            if cached:
                hots = [hot[row] for row in rows]
            else:
                for j, row in enumerate(rows):
                    pltpu.sync_copy(hot_hbm.at[row], hot.at[j])
                hots = [hot[j] for j in range(QUAD)]
            chosen = jnp.dot(
                jnp.concatenate(hots, axis=0), narrow[...], preferred_element_type=jnp.float32
            )
            for j in range(QUAD):
                own = chosen[j * LANES : (j + 1) * LANES]
                products[rows[j]] += own * tiles[spots[j]].astype(jnp.float32)
            return carry

        lax.fori_loop(0, (end - start + QUAD - 1) // QUAD, one_quad, 0)
        return carry

    lax.fori_loop(done[q], done[q + 1], score_sub, 0)
    block_sums(products, part, none)
    for copy in results:
        copy.wait()


def stage(q, base, slots, last, scalars, labels, before, inverse, hot, xs, normed, sums):
    blocks = inverse.shape[0]
    cached = blocks <= CACHED_BLOCKS
    fresh = sum(x.shape[0] for x in xs)
    wide = jax.ShapeDtypeStruct((K, TB_OWN * LANES), jnp.float32)
    return pl.pallas_call(
        functools.partial(stage_kernel, q, base, len(xs), last, cached),
        in_specs=[SMEM] * len(scalars) + [VMEM] * 2 + [ANY] * (2 + len(xs) + q + (q > 0)),
        out_specs=[VMEM, ANY, VMEM if last else ANY],
        out_shape=[
            jax.ShapeDtypeStruct((blocks, LANES), jnp.float32),
            wide,
            jax.ShapeDtypeStruct((8, K), jnp.float32)
            if last
            else jax.ShapeDtypeStruct((fresh, LANES, LANES), jnp.bfloat16),
        ],
        scratch_shapes=[
            pltpu.VMEM(inverse.shape, jnp.float32),
            pltpu.VMEM((fresh, LANES, LANES), jnp.int16),
            pltpu.VMEM(hot.shape if cached else (QUAD, LANES, K), jnp.bfloat16),
            pltpu.VMEM(wide.shape, jnp.float32),
            pltpu.VMEM((K, LANES), jnp.bfloat16),
            pltpu.VMEM((slots, LANES, LANES), jnp.bfloat16),
            pltpu.VMEM((blocks + 1, LANES, LANES), jnp.float32),
            pltpu.SemaphoreType.DMA((6 + len(xs) + q,)),
        ],
        compiler_params=params(),
        cost_estimate=pl.CostEstimate(
            flops=fresh * LANES * LANES * K * 8,
            bytes_accessed=4 * fresh * LANES * LANES + 4 * inverse.size + 8 * K * TB_OWN * LANES,
            transcendentals=0,
        ),
        name="stage",
    )(*scalars, labels, before, inverse, hot, *xs, *normed, *([sums] if q else []))


def exchange(x):
    return lax.all_to_all(x, "dp", split_axis=0, concat_axis=0, tiled=True)


def after(value, *others):
    return lax.optimization_barrier((value, *others))[0]


def sorted_slots(key, top):
    slots = jnp.arange(key.shape[0], dtype=jnp.int32)
    ahead = (key[None, :] < key[:, None]) | (
        (key[None, :] == key[:, None]) & (slots[None, :] < slots[:, None])
    )
    position = jnp.sum(ahead.astype(jnp.int32), axis=1)
    here = position[None, :] == slots[:, None]
    order = jnp.sum(jnp.where(here, slots[None, :], 0), axis=1)
    levels = jnp.arange(top + 1, dtype=jnp.int32)
    bounds = jnp.sum((key[None, :] < levels[:, None]).astype(jnp.int32), axis=1)
    return order, bounds


def ranks(group, sub):
    index = jnp.arange(sub.shape[-1], dtype=jnp.int32)
    before = (sub[..., None, :] < sub[..., :, None]) | (
        (sub[..., None, :] == sub[..., :, None]) & (index[None, :] < index[:, None])
    )
    same = group[..., None, :] == group[..., :, None]
    return jnp.sum((before & same).astype(jnp.int32), axis=-1)


def schedule(devices, parts):
    far, near = list(range(devices // 2, devices)), list(range(1, devices // 2))
    order = [d for pair in zip(far, near) for d in pair] + far[len(near) :]
    route = [(d, q) for q in range(parts) for d in [0, *order]]
    groups, moved = {}, 0
    for d, q in route:
        moved += d > 0
        share = max(moved, 1) / (parts * (devices - 1))
        groups[d, q] = sum(share > end + 1e-9 for end in GROUPS)
    return route, groups


def shards(tile_values, tile_row, tile_owner, tile_sub, labels):
    devices = lax.axis_size("dp")
    tiles = tile_values.shape[0]
    home = labels.shape[0]
    blocks = home // LANES * devices
    cap = max(2, 2 * tiles // devices)
    cuts = tuple(sorted({int(cap * share) for share in PARTS})) if cap >= 8 else (0, cap)
    parts = len(cuts) - 1
    here = lax.axis_index("dp").astype(jnp.int32)
    owner = tile_owner[:, 0]

    partial_sq = norms(tile_values, tile_row, blocks)
    described = jnp.concatenate([labels, owner, tile_row * TB_OWN + tile_sub])
    told = jnp.concatenate([partial_sq.reshape(-1), described.astype(jnp.float32)])
    heard = exchange(jnp.broadcast_to(told[None], (devices, told.shape[0])))
    shift = owner ^ here
    put = after(shift * cap + ranks(owner, tile_sub), partial_sq)
    every = jnp.arange(devices, dtype=jnp.int32)
    used = jnp.sum((shift[None, :] == every[:, None]).astype(jnp.int32), axis=1)
    outgoing = pack(tile_values, put, used, cuts)

    row_sq = jnp.sum(heard[:, : blocks * LANES], axis=0).reshape(blocks, LANES)
    all_described = heard[:, blocks * LANES :].astype(jnp.int32)
    all_labels = all_described[:, :home].reshape(blocks, LANES)
    padded_labels = jnp.concatenate([all_labels, jnp.full((1, LANES), -1, jnp.int32)])
    hot = (padded_labels[:, :, None] == jnp.arange(K, dtype=jnp.int32)).astype(jnp.bfloat16)
    mine = all_described[:, home : home + tiles] == here
    code = all_described[:, home + tiles :]
    rank = ranks(mine.astype(jnp.int32), code % TB_OWN)
    chosen = mine[:, None, :] & (rank[:, None, :] == jnp.arange(cap)[None, :, None])
    meta = jnp.sum(jnp.where(chosen, code[:, None, :] + 1, 0), axis=2) - 1
    from_shift = (every[None, :] == (every ^ here)[:, None]).astype(jnp.int32)
    meta = jnp.sum(from_shift[:, :, None] * meta[None], axis=1).reshape(-1)
    sub = jnp.where(meta < 0, TB_OWN, meta % TB_OWN)
    route, groups = schedule(devices, parts)
    stages = max(groups.values()) + 1
    place, slot_group, bases, spot = np.zeros((devices, cap)), np.zeros((devices, cap), int), [], 0
    for g in range(stages):
        bases.append(spot)
        for d, q in route:
            if groups[d, q] == g:
                some = slice(cuts[q], cuts[q + 1])
                place[d, some] = spot + np.arange(cuts[q + 1] - cuts[q])
                slot_group[d, some] = g
                spot += cuts[q + 1] - cuts[q]
    place, slot_group = place.reshape(-1), slot_group.reshape(-1)
    fold_key = jnp.asarray(slot_group * (TB_OWN + 1), jnp.int32) + sub
    fold_order, fold_bounds = sorted_slots(fold_key, stages * (TB_OWN + 1))
    score_order, score_bounds = sorted_slots(sub, TB_OWN)
    left = np.arange(stages)[:, None] < slot_group[None, :]
    done = jnp.min(jnp.where(left, sub[None, :], TB_OWN), axis=1)
    done = jnp.concatenate([jnp.zeros((1,), jnp.int32), done])
    scalars = [
        fold_order, fold_bounds, score_order, score_bounds, meta, jnp.asarray(place, jnp.int32), done
    ]

    inverse = lax.rsqrt(row_sq + EPSILON)
    scale = jnp.broadcast_to((inverse * (1.0 / CODE_TOP**2))[:, :, None], (blocks, LANES, LANES))
    partial, sums, normed = jnp.zeros((blocks, LANES), jnp.float32), None, []
    sent, incoming, beside = [], {}, {FLIGHT: (*scalars, padded_labels, hot, scale)}
    moves = [key for key in route if key[0]]
    ends = [max(i for i, key in enumerate(moves) if groups[key] == g) for g in range(stages)]
    for g in range(stages):
        for i, (d, q) in enumerate(moves):
            if groups[d, q] != g:
                continue
            ahead = beside.get(i, ())
            if i >= FLIGHT:
                ahead = (sent[i - FLIGHT], *ahead)
            x = outgoing[q * devices + d]
            x = after(x, *ahead) if ahead else after(x, heard)
            sent.append(lax.ppermute(x, "dp", [(j, j ^ d) for j in range(devices)]))
            incoming[d, q] = sent[-1]
        for q in range(parts):
            incoming[0, q] = outgoing[q * devices]
        xs = [incoming[key] for key in route if groups[key] == g]
        partial, sums, extra = stage(
            g, bases[g], devices * cap, g == stages - 1,
            scalars, padded_labels, partial, scale, hot, xs, normed, sums,
        )
        if g + 1 < stages:
            at = ends[g + 1]
            beside[at] = beside.get(at, ()) + (partial, sums, extra)
        normed.append(extra)
    square = jnp.broadcast_to(extra[:1], (devices, K))
    back = jnp.sum(
        exchange(jnp.concatenate([partial.reshape(devices, home), square], axis=1)), axis=0
    )
    own_scale = lax.rsqrt(back[home:] + EPSILON)
    vocab_size = TB_OWN * LANES * devices
    centroid = sums * own_scale[:, None]
    centroids = (centroid * math.sqrt(vocab_size)).astype(jnp.bfloat16)
    is_label = labels[:, None] == jnp.arange(K, dtype=jnp.int32)[None, :]
    doc_scale = jnp.sum(jnp.where(is_label, own_scale[None, :], 0.0), axis=1)
    return (centroids, back[:home] * doc_scale)


def solution(mesh):
    return jax.shard_map(
        shards,
        mesh=mesh,
        in_specs=(
            P(("groups", "dp"), None, None),
            P(("groups", "dp")),
            P(("groups", "dp"), None),
            P(("groups", "dp")),
            P(("groups", "dp")),
        ),
        out_specs=(P("groups", "dp"), P(("groups", "dp"))),
        check_vma=False,
    )
```

```python
import functools
import math

import jax
import jax.numpy as jnp
import numpy as np
from jax import lax
from jax.experimental import pallas as pl
from jax.experimental.pallas import tpu as pltpu
from jax.sharding import PartitionSpec as P

K = 512
TB_OWN = 16
LANES = 128
EPSILON = 1e-06
CODE_TOP = 65535.0
CODE_SHIFT = 32768
VMEM_BYTES = 56 * 1024 * 1024
STEP_TILES = 32
PARTS = (0.0, 13 / 16, 1.0)
LOG_STEPS = 1800.0
LOG_MIDDLE = -3.0
CACHED_BLOCKS = 64
QUAD = 4
BATCH = 8
NT = (((1,), (1,)), ((), ()))
SMEM = pl.BlockSpec(memory_space=pltpu.SMEM)
VMEM = pl.BlockSpec(memory_space=pltpu.VMEM)
ANY = pl.BlockSpec(memory_space=pl.ANY)


def lane_sums(values):
    ones = jnp.ones((8, LANES), jnp.bfloat16)
    high = values.astype(jnp.bfloat16)
    low = (values - high.astype(jnp.float32)).astype(jnp.bfloat16)
    return lax.dot_general(ones, high, NT, preferred_element_type=jnp.float32) + lax.dot_general(
        ones, low, NT, preferred_element_type=jnp.float32
    )


def block_sums(square, out_ref, count):
    batch = math.gcd(BATCH, count)

    def one_batch(c, carry):
        some = square[pl.ds(c * batch, batch)].reshape((batch * LANES, LANES))
        sums = lane_sums(some)
        for j in range(batch):
            out_ref[pl.ds(c * batch + j, 1), :] += sums[:1, j * LANES : (j + 1) * LANES]
        return carry

    lax.fori_loop(0, count // batch, one_batch, 0)


def params():
    return pltpu.CompilerParams(vmem_limit_bytes=VMEM_BYTES)


def pack_kernel(cuts, put_ref, row_ref, told_ref, x_ref, *refs):
    parts = len(cuts) - 1
    outs = refs[:parts]
    coded, square, sums, notes, held, sems = refs[parts:]
    step = pl.program_id(0)
    tiles = x_ref.shape[0]
    devices = held.shape[0]
    blocks = square.shape[0]

    @pl.when(step == 0)
    def _():
        square[...] = jnp.zeros_like(square)

        def clear(d, carry):
            held[d] = 0
            return carry

        lax.fori_loop(0, devices, clear, 0)

    def some_tiles(i, carry):
        for j in range(QUAD):
            t = step * tiles + i * QUAD + j
            x = x_ref[i * QUAD + j]
            root = x * lax.rsqrt(x)
            code = (root * CODE_TOP + 0.5).astype(jnp.int32) - CODE_SHIFT
            put = put_ref[t]
            coded[pl.ds(pl.multiple_of(put * LANES, LANES), LANES), :] = code.astype(jnp.int16)
            square[row_ref[t]] += x * x
            owner = put // cuts[-1]
            held[owner] = jnp.maximum(held[owner], put % cuts[-1] + 1)
        return carry

    lax.fori_loop(0, tiles // QUAD, some_tiles, 0)

    def slots(q, d):
        some = pl.ds((d * cuts[-1] + cuts[q]) * LANES, (cuts[q + 1] - cuts[q]) * LANES)
        into = outs[q].at[d, pl.ds(0, (cuts[q + 1] - cuts[q]) * LANES)]
        return pltpu.make_async_copy(coded.at[some], into, sems.at[q * devices + d])

    def note(d):
        into = outs[0].at[d, pl.ds((cuts[1] - cuts[0]) * LANES, notes.shape[0])]
        return pltpu.make_async_copy(notes, into, sems.at[parts * devices + d])

    def each(what):
        for q in range(parts):
            for d in range(devices):
                pl.when(held[d] > cuts[q])(lambda q=q, d=d: what(slots(q, d)))

    @pl.when(step == pl.num_programs(0) - 1)
    def _():
        each(lambda copy: copy.start())
        sums[...] = jnp.zeros_like(sums)
        block_sums(square, sums, blocks)
        total = sums[...]
        level = (jnp.log2(jnp.maximum(total, 1e-30)) - LOG_MIDDLE) * LOG_STEPS
        level = jnp.where(total > 0.0, jnp.clip(level, -32700.0, 32700.0), -32768.0)
        level = (level + 32768.5).astype(jnp.int32) - 32768
        notes[...] = jnp.concatenate([level, told_ref[...]], axis=0).astype(jnp.int16)
        for d in range(devices):
            note(d).start()
        each(lambda copy: copy.wait())
        for d in range(devices):
            note(d).wait()


def pack(tile_values, put, tile_row, told, devices, blocks, cuts):
    tiles = tile_values.shape[0]
    step = math.gcd(STEP_TILES, tiles)
    noted = blocks + told.shape[0]
    rows = [(high - low) * LANES for low, high in zip(cuts, cuts[1:])]
    rows[0] += noted
    return pl.pallas_call(
        functools.partial(pack_kernel, cuts),
        grid=(tiles // step,),
        in_specs=[SMEM, SMEM, pl.BlockSpec(told.shape, lambda i: (0, 0))]
        + [pl.BlockSpec((step, LANES, LANES), lambda i: (i, 0, 0))],
        out_specs=[ANY] * len(rows),
        out_shape=[jax.ShapeDtypeStruct((devices, some, LANES), jnp.int16) for some in rows],
        scratch_shapes=[
            pltpu.VMEM((devices * cuts[-1] * LANES, LANES), jnp.int16),
            pltpu.VMEM((blocks, LANES, LANES), jnp.float32),
            pltpu.VMEM((blocks, LANES), jnp.float32),
            pltpu.VMEM((noted, LANES), jnp.int16),
            pltpu.SMEM((devices,), jnp.int32),
            pltpu.SemaphoreType.DMA(((len(rows) + 1) * devices,)),
        ],
        compiler_params=params(),
        cost_estimate=pl.CostEstimate(
            flops=8 * tile_values.size,
            bytes_accessed=6 * tile_values.size,
            transcendentals=tile_values.size,
        ),
        name="pack",
    )(put, tile_row, told, tile_values)


def stage_kernel(q, base, last, cached, fold_order, fold_bound, score_order, score_bound, meta,
                 place, done, labels, before, inv_hbm, x_hbm, hot_hbm, *refs):
    earlier, refs = refs[:q], refs[q:]
    sums_in, refs = (refs[0], refs[1:]) if q else (None, refs)
    part, sums_out, extra = (*refs[:2], None) if last else refs[:3]
    refs = refs[2:] if last else refs[3:]
    inv, x, hot, sums, narrow, tiles, products, scores, sems = refs
    devices, width = x.shape[0], x.shape[1] // LANES
    fresh = tiles.at[pl.ds(base, devices * width)]
    from_hbm = x_hbm.at[:, pl.ds(0, width * LANES)]
    needed = [
        pltpu.make_async_copy(from_hbm, x, sems.at[0]),
        pltpu.make_async_copy(inv_hbm, inv, sems.at[1]),
    ]
    if q:
        needed.append(pltpu.make_async_copy(sums_in, sums, sems.at[2]))
    later = [pltpu.make_async_copy(hot_hbm, hot, sems.at[3])] if cached else []
    spot = 0
    for e, e_hbm in enumerate(earlier):
        held = tiles.at[pl.ds(spot, e_hbm.shape[0])]
        later.append(pltpu.make_async_copy(e_hbm, held, sems.at[6 + e]))
        spot += e_hbm.shape[0]
    for copy in needed + later:
        copy.start()
    products[...] = jnp.zeros_like(products)
    scores[...] = before[...]
    if not q:
        sums[...] = jnp.zeros_like(sums)
    for copy in needed:
        copy.wait()
    none = products.shape[0] - 1
    cluster = lax.broadcasted_iota(jnp.int32, (K, LANES), 0)

    def columns(sub):
        return (slice(None), pl.ds(pl.multiple_of(sub * LANES, LANES), LANES))

    def quad(order, start, end, p):
        rows, spots = [], []
        for j in range(QUAD):
            at = start + QUAD * p + j
            slot = order[jnp.where(at < end, at, start)]
            rows.append((meta[slot] // TB_OWN, at < end))
            spots.append(place[slot])
        return rows, spots

    def fold_sub(sub, carry):
        start = fold_bound[q * (TB_OWN + 1) + sub]
        end = fold_bound[q * (TB_OWN + 1) + sub + 1]

        def one_quad(p, carry):
            rows, spots = quad(fold_order, start, end, p)
            folded, picks = [], []
            for (row, held), spot in zip(rows, spots):
                source, slot = (spot - base) // width, (spot - base) % width
                raw = x[source, pl.ds(pl.multiple_of(slot * LANES, LANES), LANES), :]
                root = raw.astype(jnp.int32).astype(jnp.float32) + float(CODE_SHIFT)
                tile = (root * root * inv[row]).astype(jnp.bfloat16)
                tiles[spot] = tile
                folded.append(tile)
                own = cluster == labels[pl.ds(jnp.where(held, row, none), 1), :]
                picks.append(jnp.where(own, 1.0, 0.0).astype(jnp.bfloat16))
            pick = jnp.concatenate(picks, axis=1)
            sums[columns(sub)] += jnp.dot(
                pick, jnp.concatenate(folded, axis=0), preferred_element_type=jnp.float32
            )
            return carry

        lax.fori_loop(0, (end - start + QUAD - 1) // QUAD, one_quad, 0)
        return carry

    lax.fori_loop(0, TB_OWN, fold_sub, 0)
    results = [pltpu.make_async_copy(sums, sums_out, sems.at[4])]
    if not last:
        results.append(pltpu.make_async_copy(fresh, extra, sems.at[5]))
    for copy in results:
        copy.start()
    if last:
        total = jnp.zeros((K, LANES), jnp.float32)
        for sub in range(TB_OWN):
            some = sums[:, sub * LANES : (sub + 1) * LANES]
            total = total + some * some
        square = lane_sums(total)[:1]
        for d in range(devices):
            part[d, :, part.shape[2] - K :] = square
    for copy in later:
        copy.wait()

    def score_sub(sub, carry):
        start, end = score_bound[sub], score_bound[sub + 1]
        narrow[...] = sums[columns(sub)].astype(jnp.bfloat16)

        def one_quad(p, carry):
            rows, spots = quad(score_order, start, end, p)
            rows = [jnp.where(held, row, none) for row, held in rows]
            if cached:
                hots = [hot[row] for row in rows]
            else:
                for j, row in enumerate(rows):
                    pltpu.sync_copy(hot_hbm.at[row], hot.at[j])
                hots = [hot[j] for j in range(QUAD)]
            chosen = jnp.dot(
                jnp.concatenate(hots, axis=0), narrow[...], preferred_element_type=jnp.float32
            )
            for j in range(QUAD):
                own = chosen[j * LANES : (j + 1) * LANES]
                products[rows[j]] += own * tiles[spots[j]].astype(jnp.float32)
            return carry

        lax.fori_loop(0, (end - start + QUAD - 1) // QUAD, one_quad, 0)
        return carry

    lax.fori_loop(done[q], done[q + 1], score_sub, 0)
    block_sums(products, scores, none)
    if last:
        own = none // devices
        for d in range(devices):
            for b in range(own):
                at = d * own + b
                part[d, :, b * LANES : (b + 1) * LANES] = scores[at : at + 1, :]
    else:
        part[...] = scores[...]
    for copy in results:
        copy.wait()


def stage(q, cuts, scalars, labels, before, inverse, x, hot, normed, sums):
    devices = x.shape[0]
    last = q == len(cuts) - 2
    blocks = inverse.shape[0]
    cached = blocks <= CACHED_BLOCKS
    width = cuts[q + 1] - cuts[q]
    home = blocks // devices * LANES
    wide = jax.ShapeDtypeStruct((K, TB_OWN * LANES), jnp.float32)
    if last:
        out_shape = [jax.ShapeDtypeStruct((devices, 1, home + K), jnp.float32), wide]
    else:
        out_shape = [
            jax.ShapeDtypeStruct((blocks, LANES), jnp.float32),
            wide,
            jax.ShapeDtypeStruct((devices * width, LANES, LANES), jnp.bfloat16),
        ]
    return pl.pallas_call(
        functools.partial(stage_kernel, q, devices * cuts[q], last, cached),
        in_specs=[SMEM] * len(scalars) + [VMEM] * 2 + [ANY] * (3 + q + (q > 0)),
        out_specs=[VMEM, ANY, ANY][: len(out_shape)],
        out_shape=out_shape,
        scratch_shapes=[
            pltpu.VMEM(inverse.shape, jnp.float32),
            pltpu.VMEM((devices, width * LANES, LANES), jnp.int16),
            pltpu.VMEM(hot.shape if cached else (QUAD, LANES, K), jnp.bfloat16),
            pltpu.VMEM(wide.shape, jnp.float32),
            pltpu.VMEM((K, LANES), jnp.bfloat16),
            pltpu.VMEM((devices * cuts[-1], LANES, LANES), jnp.bfloat16),
            pltpu.VMEM((blocks + 1, LANES, LANES), jnp.float32),
            pltpu.VMEM((blocks, LANES), jnp.float32),
            pltpu.SemaphoreType.DMA((6 + len(cuts),)),
        ],
        compiler_params=params(),
        cost_estimate=pl.CostEstimate(
            flops=devices * width * LANES * LANES * K * 8,
            bytes_accessed=4 * devices * width * LANES * LANES + 8 * K * TB_OWN * LANES,
            transcendentals=0,
        ),
        name="stage",
    )(*scalars, labels, before, inverse, x, hot, *normed, *([sums] if q else []))


def exchange(x):
    return lax.all_to_all(x, "dp", split_axis=0, concat_axis=0, tiled=True)


def after(value, *others):
    return lax.optimization_barrier((value, *others))[0]


def sorted_slots(key, top):
    slots = jnp.arange(key.shape[0], dtype=jnp.int32)
    ahead = (key[None, :] < key[:, None]) | (
        (key[None, :] == key[:, None]) & (slots[None, :] < slots[:, None])
    )
    position = jnp.sum(ahead.astype(jnp.int32), axis=1)
    here = position[None, :] == slots[:, None]
    order = jnp.sum(jnp.where(here, slots[None, :], 0), axis=1)
    levels = jnp.arange(top + 1, dtype=jnp.int32)
    bounds = jnp.sum((key[None, :] < levels[:, None]).astype(jnp.int32), axis=1)
    return order, bounds


def ranks(group, sub):
    index = jnp.arange(sub.shape[-1], dtype=jnp.int32)
    before = (sub[..., None, :] < sub[..., :, None]) | (
        (sub[..., None, :] == sub[..., :, None]) & (index[None, :] < index[:, None])
    )
    same = group[..., None, :] == group[..., :, None]
    return jnp.sum((before & same).astype(jnp.int32), axis=-1)


def shards(tile_values, tile_row, tile_owner, tile_sub, labels):
    devices = lax.axis_size("dp")
    tiles = tile_values.shape[0]
    home = labels.shape[0]
    blocks = home // LANES * devices
    cap = max(2, 2 * tiles // devices)
    cuts = tuple(sorted({int(cap * share) for share in PARTS})) if cap >= 8 else (0, cap)
    parts = len(cuts) - 1
    here = lax.axis_index("dp").astype(jnp.int32)
    owner = tile_owner[:, 0]

    put = owner * cap + ranks(owner, tile_sub)
    told = jnp.concatenate([labels, owner, tile_row * TB_OWN + tile_sub]).reshape(-1, LANES)
    told = jnp.pad(told, ((0, -(blocks + told.shape[0]) % 16), (0, 0)))
    outgoing = pack(tile_values, put, tile_row, told, devices, blocks, cuts)
    incoming = [exchange(outgoing[0])]
    heard = incoming[0][:, (cuts[1] - cuts[0]) * LANES :].astype(jnp.int32)
    level = heard[:, :blocks]
    partial_sq = jnp.exp2(level.astype(jnp.float32) * (1.0 / LOG_STEPS) + LOG_MIDDLE)
    row_sq = jnp.sum(jnp.where(level > -32768, partial_sq, 0.0), axis=0)
    all_described = heard[:, blocks:].reshape(devices, -1)
    all_labels = all_described[:, :home].reshape(blocks, LANES)
    padded_labels = jnp.concatenate([all_labels, jnp.full((1, LANES), -1, jnp.int32)])
    hot = (padded_labels[:, :, None] == jnp.arange(K, dtype=jnp.int32)).astype(jnp.bfloat16)
    mine = all_described[:, home : home + tiles] == here
    code = all_described[:, home + tiles : home + 2 * tiles]
    rank = ranks(mine.astype(jnp.int32), code % TB_OWN)
    chosen = mine[:, None, :] & (rank[:, None, :] == jnp.arange(cap)[None, :, None])
    meta = jnp.sum(jnp.where(chosen, code[:, None, :] + 1, 0), axis=2).reshape(-1) - 1
    sub = jnp.where(meta < 0, TB_OWN, meta % TB_OWN)
    slot_rank = np.arange(devices * cap) % cap
    slot_part = np.searchsorted(np.array(cuts), slot_rank, side="right") - 1
    low, high = np.array(cuts)[slot_part], np.array(cuts)[slot_part + 1]
    place = devices * low + np.arange(devices * cap) // cap * (high - low) + slot_rank - low
    fold_key = jnp.asarray(slot_part * (TB_OWN + 1), jnp.int32) + sub
    fold_order, fold_bounds = sorted_slots(fold_key, parts * (TB_OWN + 1))
    score_order, score_bounds = sorted_slots(sub, TB_OWN)
    left = np.arange(parts)[:, None] < slot_part[None, :]
    done = jnp.min(jnp.where(left, sub[None, :], TB_OWN), axis=1)
    done = jnp.concatenate([jnp.zeros((1,), jnp.int32), done])
    scalars = [
        fold_order, fold_bounds, score_order, score_bounds, meta, jnp.asarray(place, jnp.int32), done
    ]

    inverse = lax.rsqrt(row_sq + EPSILON)
    scale = jnp.broadcast_to((inverse * (1.0 / CODE_TOP**2))[:, :, None], (blocks, LANES, LANES))
    partial, sums, normed = jnp.zeros((blocks, LANES), jnp.float32), None, []
    beside = (*scalars, padded_labels, hot, scale)
    for q in range(parts):
        if q + 1 < parts:
            ahead = (incoming[q], *beside) if q else (incoming[q],)
            incoming.append(exchange(after(outgoing[q + 1], *ahead)))
        partial, sums, *extra = stage(
            q, cuts, scalars, padded_labels, partial, scale, incoming[q], hot, normed, sums
        )
        beside = (partial, sums)
        normed += extra
    back = jnp.sum(exchange(partial), axis=(0, 1))
    own_scale = lax.rsqrt(back[home:] + EPSILON)
    vocab_size = TB_OWN * LANES * devices
    centroid = sums * own_scale[:, None]
    centroids = (centroid * math.sqrt(vocab_size)).astype(jnp.bfloat16)
    is_label = labels[:, None] == jnp.arange(K, dtype=jnp.int32)[None, :]
    doc_scale = jnp.sum(jnp.where(is_label, own_scale[None, :], 0.0), axis=1)
    return (centroids, back[:home] * doc_scale)


def solution(mesh):
    return jax.shard_map(
        shards,
        mesh=mesh,
        in_specs=(
            P(("groups", "dp"), None, None),
            P(("groups", "dp")),
            P(("groups", "dp"), None),
            P(("groups", "dp")),
            P(("groups", "dp")),
        ),
        out_specs=(P("groups", "dp"), P(("groups", "dp"))),
        check_vma=False,
    )
```

```python
import functools
import math

import jax
import jax.numpy as jnp
import numpy as np
from jax import lax
from jax.experimental import pallas as pl
from jax.experimental.pallas import tpu as pltpu
from jax.sharding import PartitionSpec as P

K = 512
TB_OWN = 16
LANES = 128
EPSILON = 1e-06
CODE_TOP = 65535.0
CODE_SHIFT = 32768
VMEM_BYTES = 56 * 1024 * 1024
STEP_TILES = 32
PARTS = (0.0, 12 / 16, 1.0)
LOG_STEPS = 1800.0
LOG_MIDDLE = -3.0
CACHED_BLOCKS = 64
QUAD = 4
EIGHT = 8
BATCH = 8
NT = (((1,), (1,)), ((), ()))
SMEM = pl.BlockSpec(memory_space=pltpu.SMEM)
VMEM = pl.BlockSpec(memory_space=pltpu.VMEM)
ANY = pl.BlockSpec(memory_space=pl.ANY)


def lane_sums(values):
    ones = jnp.ones((8, LANES), jnp.bfloat16)
    high = values.astype(jnp.bfloat16)
    low = (values - high.astype(jnp.float32)).astype(jnp.bfloat16)
    return lax.dot_general(ones, high, NT, preferred_element_type=jnp.float32) + lax.dot_general(
        ones, low, NT, preferred_element_type=jnp.float32
    )


def block_sums(square, out_ref, count):
    batch = math.gcd(BATCH, count)

    def one_batch(c, carry):
        some = square[pl.ds(c * batch, batch)].reshape((batch * LANES, LANES))
        sums = lane_sums(some)
        for j in range(batch):
            out_ref[pl.ds(c * batch + j, 1), :] += sums[:1, j * LANES : (j + 1) * LANES]
        return carry

    lax.fori_loop(0, count // batch, one_batch, 0)


def params():
    return pltpu.CompilerParams(vmem_limit_bytes=VMEM_BYTES)


def pack_kernel(cuts, put_ref, row_ref, *refs):
    parts = len(cuts) - 1
    (*told_refs, x_ref), refs = refs[:5], refs[5:]
    outs = refs[:parts]
    coded, square, sums, words, notes, held, sems = refs[parts:]
    step = pl.program_id(0)
    tiles = x_ref.shape[0]
    devices = held.shape[0]
    blocks = square.shape[0]

    @pl.when(step == 0)
    def _():
        square[...] = jnp.zeros_like(square)

        def clear(d, carry):
            held[d] = 0
            return carry

        lax.fori_loop(0, devices, clear, 0)

    def some_tiles(i, carry):
        for j in range(QUAD):
            t = step * tiles + i * QUAD + j
            x = x_ref[i * QUAD + j]
            root = x * lax.rsqrt(x)
            code = (root * CODE_TOP + 0.5).astype(jnp.int32) - CODE_SHIFT
            put = put_ref[t]
            coded[pl.ds(pl.multiple_of(put * LANES, LANES), LANES), :] = code.astype(jnp.int16)
            square[row_ref[t]] += x * x
            owner = put // cuts[-1]
            held[owner] = jnp.maximum(held[owner], put % cuts[-1] + 1)
        return carry

    lax.fori_loop(0, tiles // QUAD, some_tiles, 0)

    def slots(q, d):
        some = pl.ds((d * cuts[-1] + cuts[q]) * LANES, (cuts[q + 1] - cuts[q]) * LANES)
        into = outs[q].at[d, pl.ds(0, (cuts[q + 1] - cuts[q]) * LANES)]
        return pltpu.make_async_copy(coded.at[some], into, sems.at[q * devices + d])

    def note(d):
        into = outs[0].at[d, pl.ds((cuts[1] - cuts[0]) * LANES, notes.shape[0])]
        return pltpu.make_async_copy(notes, into, sems.at[parts * devices + d])

    def each(what):
        for q in range(parts):
            for d in range(devices):
                pl.when(held[d] > cuts[q])(lambda q=q, d=d: what(slots(q, d)))

    @pl.when(step == pl.num_programs(0) - 1)
    def _():
        each(lambda copy: copy.start())
        sums[...] = jnp.zeros_like(sums)
        block_sums(square, sums, blocks)
        total = sums[...]
        level = (jnp.log2(jnp.maximum(total, 1e-30)) - LOG_MIDDLE) * LOG_STEPS
        level = jnp.where(total > 0.0, jnp.clip(level, -32700.0, 32700.0), -32768.0)
        level = (level + 32768.5).astype(jnp.int32) - 32768
        labels, owner, row, sub = [ref[...] for ref in told_refs]
        words[...] = jnp.zeros_like(words)
        words[:blocks, :] = level
        at = blocks
        for told in (labels, owner, row * TB_OWN + sub):
            words[at : at + told.shape[0], :] = told
            at += told.shape[0]
        notes[...] = words[...].astype(jnp.int16)
        for d in range(devices):
            note(d).start()
        each(lambda copy: copy.wait())
        for d in range(devices):
            note(d).wait()


def pack(tile_values, put, tile_row, told, devices, blocks, cuts):
    tiles = tile_values.shape[0]
    step = math.gcd(STEP_TILES, tiles)
    told = [x.reshape(-1, LANES) for x in told]
    noted = -(-(blocks + sum(x.shape[0] for x in told[:3])) // 16) * 16
    rows = [(high - low) * LANES for low, high in zip(cuts, cuts[1:])]
    rows[0] += noted
    return pl.pallas_call(
        functools.partial(pack_kernel, cuts),
        grid=(tiles // step,),
        in_specs=[SMEM, SMEM]
        + [pl.BlockSpec(x.shape, lambda i: (0, 0)) for x in told]
        + [pl.BlockSpec((step, LANES, LANES), lambda i: (i, 0, 0))],
        out_specs=[ANY] * len(rows),
        out_shape=[jax.ShapeDtypeStruct((devices, some, LANES), jnp.int16) for some in rows],
        scratch_shapes=[
            pltpu.VMEM((devices * cuts[-1] * LANES, LANES), jnp.int16),
            pltpu.VMEM((blocks, LANES, LANES), jnp.float32),
            pltpu.VMEM((blocks, LANES), jnp.float32),
            pltpu.VMEM((noted, LANES), jnp.int32),
            pltpu.VMEM((noted, LANES), jnp.int16),
            pltpu.SMEM((devices,), jnp.int32),
            pltpu.SemaphoreType.DMA(((len(rows) + 1) * devices,)),
        ],
        compiler_params=params(),
        cost_estimate=pl.CostEstimate(
            flops=8 * tile_values.size,
            bytes_accessed=6 * tile_values.size,
            transcendentals=tile_values.size,
        ),
        name="pack",
    )(put, tile_row, *told, tile_values)


def stage_kernel(q, base, last, cached, fold_order, fold_bound, score_order, score_bound, meta,
                 place, done, labels, before, inv_hbm, x_hbm, hot_hbm, *refs):
    earlier, refs = refs[:q], refs[q:]
    sums_in, refs = (refs[0], refs[1:]) if q else (None, refs)
    part, sums_out, extra = (*refs[:2], None) if last else refs[:3]
    refs = refs[2:] if last else refs[3:]
    inv, x, hot, sums, narrow, tiles, products, scores, sems = refs
    devices, width = x.shape[0], x.shape[1] // LANES
    fresh = tiles.at[pl.ds(base, devices * width)]
    from_hbm = x_hbm.at[:, pl.ds(0, width * LANES)]
    needed = [
        pltpu.make_async_copy(from_hbm, x, sems.at[0]),
        pltpu.make_async_copy(inv_hbm, inv, sems.at[1]),
    ]
    if q:
        needed.append(pltpu.make_async_copy(sums_in, sums, sems.at[2]))
    later = [pltpu.make_async_copy(hot_hbm, hot, sems.at[3])] if cached else []
    spot = 0
    for e, e_hbm in enumerate(earlier):
        held = tiles.at[pl.ds(spot, e_hbm.shape[0])]
        later.append(pltpu.make_async_copy(e_hbm, held, sems.at[6 + e]))
        spot += e_hbm.shape[0]
    for copy in needed + later:
        copy.start()
    products[...] = jnp.zeros_like(products)
    scores[...] = before[...]
    if not q:
        sums[...] = jnp.zeros_like(sums)
    for copy in needed:
        copy.wait()
    none = products.shape[0] - 1
    cluster = lax.broadcasted_iota(jnp.int32, (K, LANES), 0)

    def columns(sub):
        return (slice(None), pl.ds(pl.multiple_of(sub * LANES, LANES), LANES))

    def eight(order, start, end, p):
        rows, spots = [], []
        for j in range(EIGHT):
            at = start + EIGHT * p + j
            slot = order[jnp.where(at < end, at, start)]
            rows.append((meta[slot] // TB_OWN, at < end))
            spots.append(place[slot])
        return rows, spots

    def fold_sub(sub, carry):
        start = fold_bound[q * (TB_OWN + 1) + sub]
        end = fold_bound[q * (TB_OWN + 1) + sub + 1]

        def one_eight(p, carry):
            rows, spots = eight(fold_order, start, end, p)
            folded, picks = [], []
            for (row, held), spot in zip(rows, spots):
                source, slot = (spot - base) // width, (spot - base) % width
                raw = x[source, pl.ds(pl.multiple_of(slot * LANES, LANES), LANES), :]
                root = raw.astype(jnp.int32).astype(jnp.float32) + float(CODE_SHIFT)
                tile = (root * root * inv[row]).astype(jnp.bfloat16)
                tiles[spot] = tile
                folded.append(tile)
                own = cluster == labels[pl.ds(jnp.where(held, row, none), 1), :]
                picks.append(jnp.where(own, 1.0, 0.0).astype(jnp.bfloat16))
            pick = jnp.concatenate(picks, axis=1)
            sums[columns(sub)] += jnp.dot(
                pick, jnp.concatenate(folded, axis=0), preferred_element_type=jnp.float32
            )
            return carry

        lax.fori_loop(0, (end - start + EIGHT - 1) // EIGHT, one_eight, 0)
        return carry

    lax.fori_loop(0, TB_OWN, fold_sub, 0)
    results = [pltpu.make_async_copy(sums, sums_out, sems.at[4])]
    if not last:
        results.append(pltpu.make_async_copy(fresh, extra, sems.at[5]))
    for copy in results:
        copy.start()
    if last:
        total = jnp.zeros((K, LANES), jnp.float32)
        for sub in range(TB_OWN):
            some = sums[:, sub * LANES : (sub + 1) * LANES]
            total = total + some * some
        square = lane_sums(total)[:1]
        for d in range(devices):
            part[d, :, part.shape[2] - K :] = square
    for copy in later:
        copy.wait()

    def score_sub(sub, carry):
        start, end = score_bound[sub], score_bound[sub + 1]
        narrow[...] = sums[columns(sub)].astype(jnp.bfloat16)

        def one_eight(p, carry):
            rows, spots = eight(score_order, start, end, p)
            rows = [jnp.where(held, row, none) for row, held in rows]
            if cached:
                hots = [hot[row] for row in rows]
            else:
                for j, row in enumerate(rows):
                    pltpu.sync_copy(hot_hbm.at[row], hot.at[j])
                hots = [hot[j] for j in range(EIGHT)]
            chosen = jnp.dot(
                jnp.concatenate(hots, axis=0), narrow[...], preferred_element_type=jnp.float32
            )
            for j in range(EIGHT):
                own = chosen[j * LANES : (j + 1) * LANES]
                products[rows[j]] += own * tiles[spots[j]].astype(jnp.float32)
            return carry

        lax.fori_loop(0, (end - start + EIGHT - 1) // EIGHT, one_eight, 0)
        return carry

    lax.fori_loop(done[q], done[q + 1], score_sub, 0)
    block_sums(products, scores, none)
    if last:
        own = none // devices
        for d in range(devices):
            for b in range(own):
                at = d * own + b
                part[d, :, b * LANES : (b + 1) * LANES] = scores[at : at + 1, :]
    else:
        part[...] = scores[...]
    for copy in results:
        copy.wait()


def stage(q, cuts, scalars, labels, before, inverse, x, hot, normed, sums):
    devices = x.shape[0]
    last = q == len(cuts) - 2
    blocks = inverse.shape[0]
    cached = blocks <= CACHED_BLOCKS
    width = cuts[q + 1] - cuts[q]
    home = blocks // devices * LANES
    wide = jax.ShapeDtypeStruct((K, TB_OWN * LANES), jnp.float32)
    if last:
        out_shape = [jax.ShapeDtypeStruct((devices, 1, home + K), jnp.float32), wide]
    else:
        out_shape = [
            jax.ShapeDtypeStruct((blocks, LANES), jnp.float32),
            wide,
            jax.ShapeDtypeStruct((devices * width, LANES, LANES), jnp.bfloat16),
        ]
    return pl.pallas_call(
        functools.partial(stage_kernel, q, devices * cuts[q], last, cached),
        in_specs=[SMEM] * len(scalars) + [VMEM] * 2 + [ANY] * (3 + q + (q > 0)),
        out_specs=[VMEM, ANY, ANY][: len(out_shape)],
        out_shape=out_shape,
        scratch_shapes=[
            pltpu.VMEM(inverse.shape, jnp.float32),
            pltpu.VMEM((devices, width * LANES, LANES), jnp.int16),
            pltpu.VMEM(hot.shape if cached else (EIGHT, LANES, K), jnp.bfloat16),
            pltpu.VMEM(wide.shape, jnp.float32),
            pltpu.VMEM((K, LANES), jnp.bfloat16),
            pltpu.VMEM((devices * cuts[-1], LANES, LANES), jnp.bfloat16),
            pltpu.VMEM((blocks + 1, LANES, LANES), jnp.float32),
            pltpu.VMEM((blocks, LANES), jnp.float32),
            pltpu.SemaphoreType.DMA((6 + len(cuts),)),
        ],
        compiler_params=params(),
        cost_estimate=pl.CostEstimate(
            flops=devices * width * LANES * LANES * K * 8,
            bytes_accessed=4 * devices * width * LANES * LANES + 8 * K * TB_OWN * LANES,
            transcendentals=0,
        ),
        name="stage",
    )(*scalars, labels, before, inverse, x, hot, *normed, *([sums] if q else []))


def exchange(x):
    return lax.all_to_all(x, "dp", split_axis=0, concat_axis=0, tiled=True)


def after(value, *others):
    return lax.optimization_barrier((value, *others))[0]


def sorted_slots(key, top):
    slots = jnp.arange(key.shape[0], dtype=jnp.int32)
    ahead = (key[None, :] < key[:, None]) | (
        (key[None, :] == key[:, None]) & (slots[None, :] < slots[:, None])
    )
    position = jnp.sum(ahead.astype(jnp.int32), axis=1)
    here = position[None, :] == slots[:, None]
    order = jnp.sum(jnp.where(here, slots[None, :], 0), axis=1)
    levels = jnp.arange(top + 1, dtype=jnp.int32)
    bounds = jnp.sum((key[None, :] < levels[:, None]).astype(jnp.int32), axis=1)
    return order, bounds


def ranks(group, sub):
    index = jnp.arange(sub.shape[-1], dtype=jnp.int32)
    before = (sub[..., None, :] < sub[..., :, None]) | (
        (sub[..., None, :] == sub[..., :, None]) & (index[None, :] < index[:, None])
    )
    same = group[..., None, :] == group[..., :, None]
    return jnp.sum((before & same).astype(jnp.int32), axis=-1)


def shards(tile_values, tile_row, tile_owner, tile_sub, labels):
    devices = lax.axis_size("dp")
    tiles = tile_values.shape[0]
    home = labels.shape[0]
    blocks = home // LANES * devices
    cap = max(2, 2 * tiles // devices)
    cuts = tuple(sorted({int(cap * share) for share in PARTS})) if cap >= 8 else (0, cap)
    parts = len(cuts) - 1
    here = lax.axis_index("dp").astype(jnp.int32)
    owner = tile_owner[:, 0]

    put = owner * cap + ranks(owner, tile_sub)
    told = (labels, owner, tile_row, tile_sub)
    outgoing = pack(tile_values, put, tile_row, told, devices, blocks, cuts)
    incoming = [exchange(outgoing[0])]
    heard = incoming[0][:, (cuts[1] - cuts[0]) * LANES :].astype(jnp.int32)
    level = heard[:, :blocks]
    partial_sq = jnp.exp2(level.astype(jnp.float32) * (1.0 / LOG_STEPS) + LOG_MIDDLE)
    row_sq = jnp.sum(jnp.where(level > -32768, partial_sq, 0.0), axis=0)
    all_described = heard[:, blocks:].reshape(devices, -1)
    all_labels = all_described[:, :home].reshape(blocks, LANES)
    padded_labels = jnp.concatenate([all_labels, jnp.full((1, LANES), -1, jnp.int32)])
    hot = (padded_labels[:, :, None] == jnp.arange(K, dtype=jnp.int32)).astype(jnp.bfloat16)
    mine = all_described[:, home : home + tiles] == here
    code = all_described[:, home + tiles : home + 2 * tiles]
    rank = ranks(mine.astype(jnp.int32), code % TB_OWN)
    chosen = mine[:, None, :] & (rank[:, None, :] == jnp.arange(cap)[None, :, None])
    meta = jnp.sum(jnp.where(chosen, code[:, None, :] + 1, 0), axis=2).reshape(-1) - 1
    sub = jnp.where(meta < 0, TB_OWN, meta % TB_OWN)
    slot_rank = np.arange(devices * cap) % cap
    slot_part = np.searchsorted(np.array(cuts), slot_rank, side="right") - 1
    low, high = np.array(cuts)[slot_part], np.array(cuts)[slot_part + 1]
    place = devices * low + np.arange(devices * cap) // cap * (high - low) + slot_rank - low
    fold_key = jnp.asarray(slot_part * (TB_OWN + 1), jnp.int32) + sub
    fold_order, fold_bounds = sorted_slots(fold_key, parts * (TB_OWN + 1))
    score_order, score_bounds = sorted_slots(sub, TB_OWN)
    left = np.arange(parts)[:, None] < slot_part[None, :]
    done = jnp.min(jnp.where(left, sub[None, :], TB_OWN), axis=1)
    done = jnp.concatenate([jnp.zeros((1,), jnp.int32), done])
    scalars = [
        fold_order, fold_bounds, score_order, score_bounds, meta, jnp.asarray(place, jnp.int32), done
    ]

    inverse = lax.rsqrt(row_sq + EPSILON)
    scale = jnp.broadcast_to((inverse * (1.0 / CODE_TOP**2))[:, :, None], (blocks, LANES, LANES))
    partial, sums, normed = jnp.zeros((blocks, LANES), jnp.float32), None, []
    beside = (*scalars, padded_labels, hot, scale)
    for q in range(parts):
        if q + 1 < parts:
            ahead = (incoming[q], *beside) if q else (incoming[q],)
            incoming.append(exchange(after(outgoing[q + 1], *ahead)))
        partial, sums, *extra = stage(
            q, cuts, scalars, padded_labels, partial, scale, incoming[q], hot, normed, sums
        )
        beside = (partial, sums)
        normed += extra
    back = jnp.sum(exchange(partial), axis=(0, 1))
    own_scale = lax.rsqrt(back[home:] + EPSILON)
    vocab_size = TB_OWN * LANES * devices
    centroid = sums * own_scale[:, None]
    centroids = (centroid * math.sqrt(vocab_size)).astype(jnp.bfloat16)
    is_label = labels[:, None] == jnp.arange(K, dtype=jnp.int32)[None, :]
    doc_scale = jnp.sum(jnp.where(is_label, own_scale[None, :], 0.0), axis=1)
    return (centroids, back[:home] * doc_scale)


def solution(mesh):
    return jax.shard_map(
        shards,
        mesh=mesh,
        in_specs=(
            P(("groups", "dp"), None, None),
            P(("groups", "dp")),
            P(("groups", "dp"), None),
            P(("groups", "dp")),
            P(("groups", "dp")),
        ),
        out_specs=(P("groups", "dp"), P(("groups", "dp"))),
        check_vma=False,
    )
```

```python
import functools
import math

import jax
import jax.numpy as jnp
import numpy as np
from jax import lax
from jax.experimental import pallas as pl
from jax.experimental.pallas import tpu as pltpu
from jax.sharding import PartitionSpec as P

K = 512
TB_OWN = 16
LANES = 128
EPSILON = 1e-06
CODE_TOP = 65535.0
CODE_SHIFT = 32768
SPARE_BYTES = 6 * 1024 * 1024
STEP_TILES = 32
PARTS = (0.0, 12 / 16, 1.0)
LOG_STEPS = 1800.0
LOG_MIDDLE = -3.0
CACHED_BLOCKS = 64
QUAD = 4
EIGHT = 8
BATCH = 8
NT = (((1,), (1,)), ((), ()))
SMEM = pl.BlockSpec(memory_space=pltpu.SMEM)
VMEM = pl.BlockSpec(memory_space=pltpu.VMEM)
ANY = pl.BlockSpec(memory_space=pl.ANY)


def lane_sums(values):
    ones = jnp.ones((8, LANES), jnp.bfloat16)
    high = values.astype(jnp.bfloat16)
    low = (values - high.astype(jnp.float32)).astype(jnp.bfloat16)
    return lax.dot_general(ones, high, NT, preferred_element_type=jnp.float32) + lax.dot_general(
        ones, low, NT, preferred_element_type=jnp.float32
    )


def block_sums(square, out_ref, count):
    batch = math.gcd(BATCH, count)

    def one_batch(c, carry):
        some = square[pl.ds(c * batch, batch)].reshape((batch * LANES, LANES))
        sums = lane_sums(some)
        for j in range(batch):
            out_ref[pl.ds(c * batch + j, 1), :] += sums[:1, j * LANES : (j + 1) * LANES]
        return carry

    lax.fori_loop(0, count // batch, one_batch, 0)


def params(*held):
    need = sum(math.prod(shape) * jnp.dtype(dtype).itemsize for shape, dtype in held)
    return pltpu.CompilerParams(vmem_limit_bytes=need + SPARE_BYTES)


def pack_kernel(cuts, put_ref, row_ref, *refs):
    parts = len(cuts) - 1
    (*told_refs, x_ref), refs = refs[:5], refs[5:]
    outs = refs[:parts]
    coded, square, sums, words, notes, held, sems = refs[parts:]
    step = pl.program_id(0)
    tiles = x_ref.shape[0]
    devices = held.shape[0]
    blocks = square.shape[0]

    @pl.when(step == 0)
    def _():
        square[...] = jnp.zeros_like(square)

        def clear(d, carry):
            held[d] = 0
            return carry

        lax.fori_loop(0, devices, clear, 0)

    def some_tiles(i, carry):
        for j in range(QUAD):
            t = step * tiles + i * QUAD + j
            x = x_ref[i * QUAD + j]
            root = x * lax.rsqrt(x)
            code = (root * CODE_TOP + 0.5).astype(jnp.int32) - CODE_SHIFT
            put = put_ref[t]
            coded[pl.ds(pl.multiple_of(put * LANES, LANES), LANES), :] = code.astype(jnp.int16)
            square[row_ref[t]] += x * x
            owner = put // cuts[-1]
            held[owner] = jnp.maximum(held[owner], put % cuts[-1] + 1)
        return carry

    lax.fori_loop(0, tiles // QUAD, some_tiles, 0)

    def slots(q, d):
        some = pl.ds((d * cuts[-1] + cuts[q]) * LANES, (cuts[q + 1] - cuts[q]) * LANES)
        into = outs[q].at[d, pl.ds(0, (cuts[q + 1] - cuts[q]) * LANES)]
        return pltpu.make_async_copy(coded.at[some], into, sems.at[q * devices + d])

    def note(d):
        into = outs[0].at[d, pl.ds((cuts[1] - cuts[0]) * LANES, notes.shape[0])]
        return pltpu.make_async_copy(notes, into, sems.at[parts * devices + d])

    def each(what):
        for q in range(parts):
            for d in range(devices):
                pl.when(held[d] > cuts[q])(lambda q=q, d=d: what(slots(q, d)))

    @pl.when(step == pl.num_programs(0) - 1)
    def _():
        each(lambda copy: copy.start())
        sums[...] = jnp.zeros_like(sums)
        block_sums(square, sums, blocks)
        total = sums[...]
        level = (jnp.log2(jnp.maximum(total, 1e-30)) - LOG_MIDDLE) * LOG_STEPS
        level = jnp.where(total > 0.0, jnp.clip(level, -32700.0, 32700.0), -32768.0)
        level = (level + 32768.5).astype(jnp.int32) - 32768
        labels, owner, row, sub = [ref[...] for ref in told_refs]
        words[...] = jnp.zeros_like(words)
        words[:blocks, :] = level
        at = blocks
        for told in (labels, owner, row * TB_OWN + sub):
            words[at : at + told.shape[0], :] = told
            at += told.shape[0]
        notes[...] = words[...].astype(jnp.int16)
        for d in range(devices):
            note(d).start()
        each(lambda copy: copy.wait())
        for d in range(devices):
            note(d).wait()


def pack(tile_values, put, tile_row, told, devices, blocks, cuts):
    tiles = tile_values.shape[0]
    step = math.gcd(STEP_TILES, tiles)
    told = [x.reshape(-1, LANES) for x in told]
    noted = -(-(blocks + sum(x.shape[0] for x in told[:3])) // 16) * 16
    rows = [(high - low) * LANES for low, high in zip(cuts, cuts[1:])]
    rows[0] += noted
    return pl.pallas_call(
        functools.partial(pack_kernel, cuts),
        grid=(tiles // step,),
        in_specs=[SMEM, SMEM]
        + [pl.BlockSpec(x.shape, lambda i: (0, 0)) for x in told]
        + [pl.BlockSpec((step, LANES, LANES), lambda i: (i, 0, 0))],
        out_specs=[ANY] * len(rows),
        out_shape=[jax.ShapeDtypeStruct((devices, some, LANES), jnp.int16) for some in rows],
        scratch_shapes=[
            pltpu.VMEM((devices * cuts[-1] * LANES, LANES), jnp.int16),
            pltpu.VMEM((blocks, LANES, LANES), jnp.float32),
            pltpu.VMEM((blocks, LANES), jnp.float32),
            pltpu.VMEM((noted, LANES), jnp.int32),
            pltpu.VMEM((noted, LANES), jnp.int16),
            pltpu.SMEM((devices,), jnp.int32),
            pltpu.SemaphoreType.DMA(((len(rows) + 1) * devices,)),
        ],
        compiler_params=params(
            ((2 * step, LANES, LANES), jnp.float32),
            ((devices * cuts[-1], LANES, LANES), jnp.int16),
            ((blocks, LANES, LANES), jnp.float32),
        ),
        cost_estimate=pl.CostEstimate(
            flops=8 * tile_values.size,
            bytes_accessed=6 * tile_values.size,
            transcendentals=tile_values.size,
        ),
        name="pack",
    )(put, tile_row, *told, tile_values)


def stage_kernel(q, base, last, cached, fold_order, fold_bound, score_order, score_bound, meta,
                 place, done, labels, before, inv_hbm, x_hbm, hot_hbm, *refs):
    earlier, refs = refs[:q], refs[q:]
    sums_in, refs = (refs[0], refs[1:]) if q else (None, refs)
    part, sums_out, extra = (*refs[:2], None) if last else refs[:3]
    refs = refs[2:] if last else refs[3:]
    inv, x, hot, sums, narrow, tiles, products, scores, sems = refs
    devices, width = x.shape[0], x.shape[1] // LANES
    fresh = tiles.at[pl.ds(base, devices * width)]
    from_hbm = x_hbm.at[:, pl.ds(0, width * LANES)]
    needed = [
        pltpu.make_async_copy(from_hbm, x, sems.at[0]),
        pltpu.make_async_copy(inv_hbm, inv, sems.at[1]),
    ]
    if q:
        needed.append(pltpu.make_async_copy(sums_in, sums, sems.at[2]))
    later = [pltpu.make_async_copy(hot_hbm, hot, sems.at[3])] if cached else []
    spot = 0
    for e, e_hbm in enumerate(earlier):
        held = tiles.at[pl.ds(spot, e_hbm.shape[0])]
        later.append(pltpu.make_async_copy(e_hbm, held, sems.at[6 + e]))
        spot += e_hbm.shape[0]
    for copy in needed + later:
        copy.start()
    products[...] = jnp.zeros_like(products)
    scores[...] = before[...]
    if not q:
        sums[...] = jnp.zeros_like(sums)
    for copy in needed:
        copy.wait()
    none = products.shape[0] - 1
    cluster = lax.broadcasted_iota(jnp.int32, (K, LANES), 0)

    def columns(sub):
        return (slice(None), pl.ds(pl.multiple_of(sub * LANES, LANES), LANES))

    def eight(order, start, end, p):
        rows, spots = [], []
        for j in range(EIGHT):
            at = start + EIGHT * p + j
            slot = order[jnp.where(at < end, at, start)]
            rows.append((meta[slot] // TB_OWN, at < end))
            spots.append(place[slot])
        return rows, spots

    def fold_sub(sub, carry):
        start = fold_bound[q * (TB_OWN + 1) + sub]
        end = fold_bound[q * (TB_OWN + 1) + sub + 1]

        def one_eight(p, carry):
            rows, spots = eight(fold_order, start, end, p)
            folded, picks = [], []
            for (row, held), spot in zip(rows, spots):
                source, slot = (spot - base) // width, (spot - base) % width
                raw = x[source, pl.ds(pl.multiple_of(slot * LANES, LANES), LANES), :]
                root = raw.astype(jnp.int32).astype(jnp.float32) + float(CODE_SHIFT)
                tile = (root * root * inv[row]).astype(jnp.bfloat16)
                tiles[spot] = tile
                folded.append(tile)
                own = cluster == labels[pl.ds(jnp.where(held, row, none), 1), :]
                picks.append(jnp.where(own, 1.0, 0.0).astype(jnp.bfloat16))
            pick = jnp.concatenate(picks, axis=1)
            sums[columns(sub)] += jnp.dot(
                pick, jnp.concatenate(folded, axis=0), preferred_element_type=jnp.float32
            )
            return carry

        lax.fori_loop(0, (end - start + EIGHT - 1) // EIGHT, one_eight, 0)
        return carry

    lax.fori_loop(0, TB_OWN, fold_sub, 0)
    results = [pltpu.make_async_copy(sums, sums_out, sems.at[4])]
    if not last:
        results.append(pltpu.make_async_copy(fresh, extra, sems.at[5]))
    for copy in results:
        copy.start()
    if last:
        total = jnp.zeros((K, LANES), jnp.float32)
        for sub in range(TB_OWN):
            some = sums[:, sub * LANES : (sub + 1) * LANES]
            total = total + some * some
        square = lane_sums(total)[:1]
        for d in range(devices):
            part[d, :, part.shape[2] - K :] = square
    for copy in later:
        copy.wait()

    def score_sub(sub, carry):
        start, end = score_bound[sub], score_bound[sub + 1]
        narrow[...] = sums[columns(sub)].astype(jnp.bfloat16)

        def one_eight(p, carry):
            rows, spots = eight(score_order, start, end, p)
            rows = [jnp.where(held, row, none) for row, held in rows]
            if cached:
                hots = [hot[row] for row in rows]
            else:
                for j, row in enumerate(rows):
                    pltpu.sync_copy(hot_hbm.at[row], hot.at[j])
                hots = [hot[j] for j in range(EIGHT)]
            chosen = jnp.dot(
                jnp.concatenate(hots, axis=0), narrow[...], preferred_element_type=jnp.float32
            )
            for j in range(EIGHT):
                own = chosen[j * LANES : (j + 1) * LANES]
                products[rows[j]] += own * tiles[spots[j]].astype(jnp.float32)
            return carry

        lax.fori_loop(0, (end - start + EIGHT - 1) // EIGHT, one_eight, 0)
        return carry

    lax.fori_loop(done[q], done[q + 1], score_sub, 0)
    block_sums(products, scores, none)
    if last:
        own = none // devices
        for d in range(devices):
            for b in range(own):
                at = d * own + b
                part[d, :, b * LANES : (b + 1) * LANES] = scores[at : at + 1, :]
    else:
        part[...] = scores[...]
    for copy in results:
        copy.wait()


def stage(q, cuts, scalars, labels, before, inverse, x, hot, normed, sums):
    devices = x.shape[0]
    last = q == len(cuts) - 2
    blocks = inverse.shape[0]
    cached = blocks <= CACHED_BLOCKS
    width = cuts[q + 1] - cuts[q]
    home = blocks // devices * LANES
    wide = jax.ShapeDtypeStruct((K, TB_OWN * LANES), jnp.float32)
    if last:
        out_shape = [jax.ShapeDtypeStruct((devices, 1, home + K), jnp.float32), wide]
    else:
        out_shape = [
            jax.ShapeDtypeStruct((blocks, LANES), jnp.float32),
            wide,
            jax.ShapeDtypeStruct((devices * width, LANES, LANES), jnp.bfloat16),
        ]
    return pl.pallas_call(
        functools.partial(stage_kernel, q, devices * cuts[q], last, cached),
        in_specs=[SMEM] * len(scalars) + [VMEM] * 2 + [ANY] * (3 + q + (q > 0)),
        out_specs=[VMEM, ANY, ANY][: len(out_shape)],
        out_shape=out_shape,
        scratch_shapes=[
            pltpu.VMEM(inverse.shape, jnp.float32),
            pltpu.VMEM((devices, width * LANES, LANES), jnp.int16),
            pltpu.VMEM(hot.shape if cached else (EIGHT, LANES, K), jnp.bfloat16),
            pltpu.VMEM(wide.shape, jnp.float32),
            pltpu.VMEM((K, LANES), jnp.bfloat16),
            pltpu.VMEM((devices * cuts[-1], LANES, LANES), jnp.bfloat16),
            pltpu.VMEM((blocks + 1, LANES, LANES), jnp.float32),
            pltpu.VMEM((blocks, LANES), jnp.float32),
            pltpu.SemaphoreType.DMA((6 + len(cuts),)),
        ],
        compiler_params=params(
            (inverse.shape, jnp.float32),
            ((devices * width, LANES, LANES), jnp.int16),
            (hot.shape if cached else (EIGHT, LANES, K), jnp.bfloat16),
            (wide.shape, jnp.float32),
            ((devices * cuts[-1], LANES, LANES), jnp.bfloat16),
            ((blocks + 1, LANES, LANES), jnp.float32),
        ),
        cost_estimate=pl.CostEstimate(
            flops=devices * width * LANES * LANES * K * 8,
            bytes_accessed=4 * devices * width * LANES * LANES + 8 * K * TB_OWN * LANES,
            transcendentals=0,
        ),
        name="stage",
    )(*scalars, labels, before, inverse, x, hot, *normed, *([sums] if q else []))


def exchange(x):
    return lax.all_to_all(x, "dp", split_axis=0, concat_axis=0, tiled=True)


def after(value, *others):
    return lax.optimization_barrier((value, *others))[0]


def sorted_slots(key, top):
    slots = jnp.arange(key.shape[0], dtype=jnp.int32)
    ahead = (key[None, :] < key[:, None]) | (
        (key[None, :] == key[:, None]) & (slots[None, :] < slots[:, None])
    )
    position = jnp.sum(ahead.astype(jnp.int32), axis=1)
    here = position[None, :] == slots[:, None]
    order = jnp.sum(jnp.where(here, slots[None, :], 0), axis=1)
    levels = jnp.arange(top + 1, dtype=jnp.int32)
    bounds = jnp.sum((key[None, :] < levels[:, None]).astype(jnp.int32), axis=1)
    return order, bounds


def ranks(group, sub):
    index = jnp.arange(sub.shape[-1], dtype=jnp.int32)
    before = (sub[..., None, :] < sub[..., :, None]) | (
        (sub[..., None, :] == sub[..., :, None]) & (index[None, :] < index[:, None])
    )
    same = group[..., None, :] == group[..., :, None]
    return jnp.sum((before & same).astype(jnp.int32), axis=-1)


def shards(tile_values, tile_row, tile_owner, tile_sub, labels):
    devices = lax.axis_size("dp")
    tiles = tile_values.shape[0]
    home = labels.shape[0]
    blocks = home // LANES * devices
    cap = max(2, 2 * tiles // devices)
    cuts = tuple(sorted({int(cap * share) for share in PARTS})) if cap >= 8 else (0, cap)
    parts = len(cuts) - 1
    here = lax.axis_index("dp").astype(jnp.int32)
    owner = tile_owner[:, 0]

    put = owner * cap + ranks(owner, tile_sub)
    told = (labels, owner, tile_row, tile_sub)
    outgoing = pack(tile_values, put, tile_row, told, devices, blocks, cuts)
    incoming = [exchange(outgoing[0])]
    heard = incoming[0][:, (cuts[1] - cuts[0]) * LANES :].astype(jnp.int32)
    level = heard[:, :blocks]
    partial_sq = jnp.exp2(level.astype(jnp.float32) * (1.0 / LOG_STEPS) + LOG_MIDDLE)
    row_sq = jnp.sum(jnp.where(level > -32768, partial_sq, 0.0), axis=0)
    all_described = heard[:, blocks:].reshape(devices, -1)
    all_labels = all_described[:, :home].reshape(blocks, LANES)
    padded_labels = jnp.concatenate([all_labels, jnp.full((1, LANES), -1, jnp.int32)])
    hot = (padded_labels[:, :, None] == jnp.arange(K, dtype=jnp.int32)).astype(jnp.bfloat16)
    mine = all_described[:, home : home + tiles] == here
    code = all_described[:, home + tiles : home + 2 * tiles]
    rank = ranks(mine.astype(jnp.int32), code % TB_OWN)
    chosen = mine[:, None, :] & (rank[:, None, :] == jnp.arange(cap)[None, :, None])
    meta = jnp.sum(jnp.where(chosen, code[:, None, :] + 1, 0), axis=2).reshape(-1) - 1
    sub = jnp.where(meta < 0, TB_OWN, meta % TB_OWN)
    slot_rank = np.arange(devices * cap) % cap
    slot_part = np.searchsorted(np.array(cuts), slot_rank, side="right") - 1
    low, high = np.array(cuts)[slot_part], np.array(cuts)[slot_part + 1]
    place = devices * low + np.arange(devices * cap) // cap * (high - low) + slot_rank - low
    fold_key = jnp.asarray(slot_part * (TB_OWN + 1), jnp.int32) + sub
    fold_order, fold_bounds = sorted_slots(fold_key, parts * (TB_OWN + 1))
    score_order, score_bounds = sorted_slots(sub, TB_OWN)
    left = np.arange(parts)[:, None] < slot_part[None, :]
    done = jnp.min(jnp.where(left, sub[None, :], TB_OWN), axis=1)
    done = jnp.concatenate([jnp.zeros((1,), jnp.int32), done])
    scalars = [
        fold_order, fold_bounds, score_order, score_bounds, meta, jnp.asarray(place, jnp.int32), done
    ]

    inverse = lax.rsqrt(row_sq + EPSILON)
    scale = jnp.broadcast_to((inverse * (1.0 / CODE_TOP**2))[:, :, None], (blocks, LANES, LANES))
    partial, sums, normed = jnp.zeros((blocks, LANES), jnp.float32), None, []
    beside = (*scalars, padded_labels, hot, scale)
    for q in range(parts):
        if q + 1 < parts:
            ahead = (incoming[q], *beside) if q else (incoming[q],)
            incoming.append(exchange(after(outgoing[q + 1], *ahead)))
        partial, sums, *extra = stage(
            q, cuts, scalars, padded_labels, partial, scale, incoming[q], hot, normed, sums
        )
        beside = (partial, sums)
        normed += extra
    back = jnp.sum(exchange(partial), axis=(0, 1))
    own_scale = lax.rsqrt(back[home:] + EPSILON)
    vocab_size = TB_OWN * LANES * devices
    centroid = sums * own_scale[:, None]
    centroids = (centroid * math.sqrt(vocab_size)).astype(jnp.bfloat16)
    is_label = labels[:, None] == jnp.arange(K, dtype=jnp.int32)[None, :]
    doc_scale = jnp.sum(jnp.where(is_label, own_scale[None, :], 0.0), axis=1)
    return (centroids, back[:home] * doc_scale)


def solution(mesh):
    return jax.shard_map(
        shards,
        mesh=mesh,
        in_specs=(
            P(("groups", "dp"), None, None),
            P(("groups", "dp")),
            P(("groups", "dp"), None),
            P(("groups", "dp")),
            P(("groups", "dp")),
        ),
        out_specs=(P("groups", "dp"), P(("groups", "dp"))),
        check_vma=False,
    )
```

```python
import functools
import math

import jax
import jax.numpy as jnp
import numpy as np
from jax import lax
from jax.experimental import pallas as pl
from jax.experimental.pallas import tpu as pltpu
from jax.sharding import PartitionSpec as P

K = 512
TB_OWN = 16
LANES = 128
EPSILON = 1e-06
CODE_TOP = 65535.0
CODE_SHIFT = 32768
VMEM_BYTES = 56 * 1024 * 1024
STEP_TILES = 32
PARTS = (0.0, 12 / 16, 1.0)
LOG_STEPS = 1800.0
LOG_MIDDLE = -3.0
CACHED_BLOCKS = 64
QUAD = 4
EIGHT = 8
BATCH = 8
NT = (((1,), (1,)), ((), ()))
SMEM = pl.BlockSpec(memory_space=pltpu.SMEM)
VMEM = pl.BlockSpec(memory_space=pltpu.VMEM)
ANY = pl.BlockSpec(memory_space=pl.ANY)


def lane_sums(values):
    ones = jnp.ones((8, LANES), jnp.bfloat16)
    high = values.astype(jnp.bfloat16)
    low = (values - high.astype(jnp.float32)).astype(jnp.bfloat16)
    return lax.dot_general(ones, high, NT, preferred_element_type=jnp.float32) + lax.dot_general(
        ones, low, NT, preferred_element_type=jnp.float32
    )


def block_sums(square, out_ref, count):
    batch = math.gcd(BATCH, count)

    def one_batch(c, carry):
        some = square[pl.ds(c * batch, batch)].reshape((batch * LANES, LANES))
        sums = lane_sums(some)
        for j in range(batch):
            out_ref[pl.ds(c * batch + j, 1), :] += sums[:1, j * LANES : (j + 1) * LANES]
        return carry

    lax.fori_loop(0, count // batch, one_batch, 0)


def params():
    return pltpu.CompilerParams(vmem_limit_bytes=VMEM_BYTES)


def pack_kernel(cuts, put_ref, row_ref, *refs):
    parts = len(cuts) - 1
    (*told_refs, x_ref), refs = refs[:5], refs[5:]
    outs = refs[:parts]
    coded, square, sums, words, notes, held, sems = refs[parts:]
    step = pl.program_id(0)
    tiles = x_ref.shape[0]
    devices = held.shape[0]
    blocks = square.shape[0]

    @pl.when(step == 0)
    def _():
        square[...] = jnp.zeros_like(square)

        def clear(d, carry):
            held[d] = 0
            return carry

        lax.fori_loop(0, devices, clear, 0)

    def some_tiles(i, carry):
        for j in range(QUAD):
            t = step * tiles + i * QUAD + j
            x = x_ref[i * QUAD + j]
            root = x * lax.rsqrt(x)
            code = (root * CODE_TOP + 0.5).astype(jnp.int32) - CODE_SHIFT
            put = put_ref[t]
            coded[pl.ds(pl.multiple_of(put * LANES, LANES), LANES), :] = code.astype(jnp.int16)
            square[row_ref[t]] += x * x
            owner = put // cuts[-1]
            held[owner] = jnp.maximum(held[owner], put % cuts[-1] + 1)
        return carry

    lax.fori_loop(0, tiles // QUAD, some_tiles, 0)

    def slots(q, d):
        some = pl.ds((d * cuts[-1] + cuts[q]) * LANES, (cuts[q + 1] - cuts[q]) * LANES)
        into = outs[q].at[d, pl.ds(0, (cuts[q + 1] - cuts[q]) * LANES)]
        return pltpu.make_async_copy(coded.at[some], into, sems.at[q * devices + d])

    def note(d):
        into = outs[0].at[d, pl.ds((cuts[1] - cuts[0]) * LANES, notes.shape[0])]
        return pltpu.make_async_copy(notes, into, sems.at[parts * devices + d])

    def each(what):
        for q in range(parts):
            for d in range(devices):
                pl.when(held[d] > cuts[q])(lambda q=q, d=d: what(slots(q, d)))

    @pl.when(step == pl.num_programs(0) - 1)
    def _():
        each(lambda copy: copy.start())
        sums[...] = jnp.zeros_like(sums)
        block_sums(square, sums, blocks)
        total = sums[...]
        level = (jnp.log2(jnp.maximum(total, 1e-30)) - LOG_MIDDLE) * LOG_STEPS
        level = jnp.where(total > 0.0, jnp.clip(level, -32700.0, 32700.0), -32768.0)
        level = (level + 32768.5).astype(jnp.int32) - 32768
        labels, owner, row, sub = [ref[...] for ref in told_refs]
        words[...] = jnp.zeros_like(words)
        words[:blocks, :] = level
        at = blocks
        for told in (labels, owner, row * TB_OWN + sub):
            words[at : at + told.shape[0], :] = told
            at += told.shape[0]
        notes[...] = words[...].astype(jnp.int16)
        for d in range(devices):
            note(d).start()
        each(lambda copy: copy.wait())
        for d in range(devices):
            note(d).wait()


def pack(tile_values, put, tile_row, told, devices, blocks, cuts):
    tiles = tile_values.shape[0]
    step = math.gcd(STEP_TILES, tiles)
    told = [x.reshape(-1, LANES) for x in told]
    noted = -(-(blocks + sum(x.shape[0] for x in told[:3])) // 16) * 16
    rows = [(high - low) * LANES for low, high in zip(cuts, cuts[1:])]
    rows[0] += noted
    return pl.pallas_call(
        functools.partial(pack_kernel, cuts),
        grid=(tiles // step,),
        in_specs=[SMEM, SMEM]
        + [pl.BlockSpec(x.shape, lambda i: (0, 0)) for x in told]
        + [pl.BlockSpec((step, LANES, LANES), lambda i: (i, 0, 0))],
        out_specs=[ANY] * len(rows),
        out_shape=[jax.ShapeDtypeStruct((devices, some, LANES), jnp.int16) for some in rows],
        scratch_shapes=[
            pltpu.VMEM((devices * cuts[-1] * LANES, LANES), jnp.int16),
            pltpu.VMEM((blocks, LANES, LANES), jnp.float32),
            pltpu.VMEM((blocks, LANES), jnp.float32),
            pltpu.VMEM((noted, LANES), jnp.int32),
            pltpu.VMEM((noted, LANES), jnp.int16),
            pltpu.SMEM((devices,), jnp.int32),
            pltpu.SemaphoreType.DMA(((len(rows) + 1) * devices,)),
        ],
        compiler_params=params(),
        cost_estimate=pl.CostEstimate(
            flops=8 * tile_values.size,
            bytes_accessed=6 * tile_values.size,
            transcendentals=tile_values.size,
        ),
        name="pack",
    )(put, tile_row, *told, tile_values)


def stage_kernel(q, bases, last, cached, fold_order, fold_bound, score_order, score_bound, meta,
                 place, done, labels, before, inv_hbm, x_hbm, *refs):
    base = bases[q]
    earlier, refs = refs[:q], refs[q:]
    (sums_in, squares_in), refs = (refs[:2], refs[2:]) if q else ((None, None), refs)
    part, sums_out, refs = refs[0], refs[1], refs[2:]
    (squares_out, fresh_out), refs = ((None, None), refs) if last else (refs[:2], refs[2:])
    inv, x, hot, sums, narrow, tiles, products, scores, squares, sems, sub_sems, tile_sems = refs
    devices, width = x.shape[0], x.shape[1] // LANES
    none = products.shape[0] - 1
    begin, end = done[q], done[q + 1]
    needed = [
        pltpu.make_async_copy(x_hbm.at[:, pl.ds(0, width * LANES)], x, sems.at[0]),
        pltpu.make_async_copy(inv_hbm, inv, sems.at[1]),
    ]
    for copy in needed:
        copy.start()

    def columns(sub):
        return (slice(None), pl.ds(pl.multiple_of(sub * LANES, LANES), LANES))

    def sums_read(sub):
        return pltpu.make_async_copy(
            sums_in.at[columns(sub)], sums.at[columns(sub)], sub_sems.at[0, sub]
        )

    def sums_write(sub):
        return pltpu.make_async_copy(
            sums.at[columns(sub)], sums_out.at[columns(sub)], sub_sems.at[1, sub]
        )

    def each_sub(low, high, what):
        def one(sub, carry):
            what(sub)
            return carry

        lax.fori_loop(low, high, one, 0)

    def each_earlier(what):
        def one(p, carry):
            spot = place[score_order[p]]
            for e, e_hbm in enumerate(earlier):
                inside = (spot >= bases[e]) & (spot < bases[e + 1])
                pl.when(inside)(
                    lambda e=e, e_hbm=e_hbm: what(
                        pltpu.make_async_copy(
                            e_hbm.at[spot - bases[e]], tiles.at[spot], tile_sems.at[spot]
                        )
                    )
                )
            return carry

        lax.fori_loop(score_bound[begin], score_bound[TB_OWN], one, 0)

    if q:
        each_sub(begin, TB_OWN, lambda sub: sums_read(sub).start())
        each_earlier(lambda copy: copy.start())
        squares[...] = squares_in[...]
    else:
        sums[...] = jnp.zeros_like(sums)
        squares[...] = jnp.zeros_like(squares)
    products[...] = jnp.zeros_like(products)
    scores[...] = before[...]
    cluster = lax.broadcasted_iota(jnp.int32, (K, LANES), 0)
    lane = lax.broadcasted_iota(jnp.int32, (LANES, LANES), 1)

    def one_hot(row):
        own = jnp.broadcast_to(labels[pl.ds(row, 1), :].astype(jnp.float32), (LANES, LANES))
        own = jnp.transpose(own).astype(jnp.int32)
        some = [jnp.where(own == lane + g, 1.0, 0.0) for g in range(0, K, LANES)]
        return jnp.concatenate(some, axis=1).astype(jnp.bfloat16)

    if cached:
        batch = math.gcd(none + 1, 3)

        def build(c, carry):
            for j in range(batch):
                hot[c * batch + j] = one_hot(c * batch + j)
            return carry

        lax.fori_loop(0, (none + 1) // batch, build, 0)
    for copy in needed:
        copy.wait()

    def eight(order, start, end, p):
        rows, spots = [], []
        for j in range(EIGHT):
            at = start + EIGHT * p + j
            slot = order[jnp.where(at < end, at, start)]
            rows.append((meta[slot] // TB_OWN, at < end))
            spots.append(place[slot])
        return rows, spots

    def fold_sub(sub):
        start = fold_bound[q * (TB_OWN + 1) + sub]
        end = fold_bound[q * (TB_OWN + 1) + sub + 1]
        if q:
            sums_read(sub).wait()

        def one_eight(p, carry):
            rows, spots = eight(fold_order, start, end, p)
            folded, picks = [], []
            for (row, held), spot in zip(rows, spots):
                source, slot = (spot - base) // width, (spot - base) % width
                raw = x[source, pl.ds(pl.multiple_of(slot * LANES, LANES), LANES), :]
                root = raw.astype(jnp.int32).astype(jnp.float32) + float(CODE_SHIFT)
                tile = (root * root * inv[row]).astype(jnp.bfloat16)
                tiles[spot] = tile
                folded.append(tile)
                own = cluster == labels[pl.ds(jnp.where(held, row, none), 1), :]
                picks.append(jnp.where(own, 1.0, 0.0).astype(jnp.bfloat16))
            pick = jnp.concatenate(picks, axis=1)
            sums[columns(sub)] += jnp.dot(
                pick, jnp.concatenate(folded, axis=0), preferred_element_type=jnp.float32
            )
            return carry

        lax.fori_loop(0, (end - start + EIGHT - 1) // EIGHT, one_eight, 0)
        sums_write(sub).start()

    each_sub(begin, TB_OWN, fold_sub)
    kept = []
    if not last:
        fresh = tiles.at[pl.ds(base, devices * width)]
        kept.append(pltpu.make_async_copy(fresh, fresh_out, sems.at[2]))
    for copy in kept:
        copy.start()
    if q:
        each_earlier(lambda copy: copy.wait())

    def score_sub(sub):
        start, end = score_bound[sub], score_bound[sub + 1]
        some = sums[columns(sub)]
        narrow[...] = some.astype(jnp.bfloat16)
        squares[...] += some * some

        def one_eight(p, carry):
            rows, spots = eight(score_order, start, end, p)
            rows = [jnp.where(held, row, none) for row, held in rows]
            hots = [hot[row] if cached else one_hot(row) for row in rows]
            chosen = jnp.dot(
                jnp.concatenate(hots, axis=0), narrow[...], preferred_element_type=jnp.float32
            )
            for j in range(EIGHT):
                own = chosen[j * LANES : (j + 1) * LANES]
                products[rows[j]] += own * tiles[spots[j]].astype(jnp.float32)
            return carry

        lax.fori_loop(0, (end - start + EIGHT - 1) // EIGHT, one_eight, 0)

    each_sub(begin, end, score_sub)
    block_sums(products, scores, none)
    if last:
        own = none // devices
        square = lane_sums(squares[...])[:1]
        for d in range(devices):
            part[d, :, part.shape[2] - K :] = square
            for b in range(own):
                at = d * own + b
                part[d, :, b * LANES : (b + 1) * LANES] = scores[at : at + 1, :]
    else:
        part[...] = scores[...]
        squares_out[...] = squares[...]
    for copy in kept:
        copy.wait()
    each_sub(begin, TB_OWN, lambda sub: sums_write(sub).wait())


def stage(q, cuts, scalars, labels, before, inverse, x, normed, totals):
    devices = x.shape[0]
    last = q == len(cuts) - 2
    blocks = inverse.shape[0]
    cached = blocks <= CACHED_BLOCKS
    width = cuts[q + 1] - cuts[q]
    home = blocks // devices * LANES
    wide = jax.ShapeDtypeStruct((K, TB_OWN * LANES), jnp.float32)
    if last:
        out_shape = [jax.ShapeDtypeStruct((devices, 1, home + K), jnp.float32), wide]
    else:
        out_shape = [
            jax.ShapeDtypeStruct((blocks, LANES), jnp.float32),
            wide,
            jax.ShapeDtypeStruct((K, LANES), jnp.float32),
            jax.ShapeDtypeStruct((devices * width, LANES, LANES), jnp.bfloat16),
        ]
    slots = devices * cuts[-1]
    operands = [*scalars, labels, before, inverse, x, *normed, *totals]
    return pl.pallas_call(
        functools.partial(stage_kernel, q, [devices * cut for cut in cuts], last, cached),
        in_specs=[SMEM] * len(scalars) + [VMEM] * 2 + [ANY] * (2 + q) + [ANY, VMEM][: len(totals)],
        out_specs=[VMEM, ANY, VMEM, ANY][: len(out_shape)],
        out_shape=out_shape,
        input_output_aliases={len(operands) - 2: 1} if q else {},
        scratch_shapes=[
            pltpu.VMEM(inverse.shape, jnp.float32),
            pltpu.VMEM((devices, width * LANES, LANES), jnp.int16),
            pltpu.VMEM((blocks + 1 if cached else 1, LANES, K), jnp.bfloat16),
            pltpu.VMEM(wide.shape, jnp.float32),
            pltpu.VMEM((K, LANES), jnp.bfloat16),
            pltpu.VMEM((slots, LANES, LANES), jnp.bfloat16),
            pltpu.VMEM((blocks + 1, LANES, LANES), jnp.float32),
            pltpu.VMEM((blocks, LANES), jnp.float32),
            pltpu.VMEM((K, LANES), jnp.float32),
            pltpu.SemaphoreType.DMA((3,)),
            pltpu.SemaphoreType.DMA((2, TB_OWN)),
            pltpu.SemaphoreType.DMA((slots,)),
        ],
        compiler_params=params(),
        cost_estimate=pl.CostEstimate(
            flops=devices * width * LANES * LANES * K * 8,
            bytes_accessed=4 * devices * width * LANES * LANES + 8 * K * TB_OWN * LANES,
            transcendentals=0,
        ),
        name="stage",
    )(*operands)


def exchange(x):
    return lax.all_to_all(x, "dp", split_axis=0, concat_axis=0, tiled=True)


def after(value, *others):
    return lax.optimization_barrier((value, *others))[0]


def sorted_slots(key, top):
    slots = jnp.arange(key.shape[0], dtype=jnp.int32)
    ahead = (key[None, :] < key[:, None]) | (
        (key[None, :] == key[:, None]) & (slots[None, :] < slots[:, None])
    )
    position = jnp.sum(ahead.astype(jnp.int32), axis=1)
    here = position[None, :] == slots[:, None]
    order = jnp.sum(jnp.where(here, slots[None, :], 0), axis=1)
    levels = jnp.arange(top + 1, dtype=jnp.int32)
    bounds = jnp.sum((key[None, :] < levels[:, None]).astype(jnp.int32), axis=1)
    return order, bounds


def ranks(group, sub):
    index = jnp.arange(sub.shape[-1], dtype=jnp.int32)
    before = (sub[..., None, :] < sub[..., :, None]) | (
        (sub[..., None, :] == sub[..., :, None]) & (index[None, :] < index[:, None])
    )
    same = group[..., None, :] == group[..., :, None]
    return jnp.sum((before & same).astype(jnp.int32), axis=-1)


def shards(tile_values, tile_row, tile_owner, tile_sub, labels):
    devices = lax.axis_size("dp")
    tiles = tile_values.shape[0]
    home = labels.shape[0]
    blocks = home // LANES * devices
    cap = max(2, 2 * tiles // devices)
    cuts = tuple(sorted({int(cap * share) for share in PARTS})) if cap >= 8 else (0, cap)
    parts = len(cuts) - 1
    here = lax.axis_index("dp").astype(jnp.int32)
    owner = tile_owner[:, 0]

    put = owner * cap + ranks(owner, tile_sub)
    told = (labels, owner, tile_row, tile_sub)
    outgoing = pack(tile_values, put, tile_row, told, devices, blocks, cuts)
    incoming = [exchange(outgoing[0])]
    heard = incoming[0][:, (cuts[1] - cuts[0]) * LANES :].astype(jnp.int32)
    level = heard[:, :blocks]
    partial_sq = jnp.exp2(level.astype(jnp.float32) * (1.0 / LOG_STEPS) + LOG_MIDDLE)
    row_sq = jnp.sum(jnp.where(level > -32768, partial_sq, 0.0), axis=0)
    all_described = heard[:, blocks:].reshape(devices, -1)
    all_labels = all_described[:, :home].reshape(blocks, LANES)
    padded_labels = jnp.concatenate([all_labels, jnp.full((1, LANES), -1, jnp.int32)])
    mine = all_described[:, home : home + tiles] == here
    code = all_described[:, home + tiles : home + 2 * tiles]
    rank = ranks(mine.astype(jnp.int32), code % TB_OWN)
    chosen = mine[:, None, :] & (rank[:, None, :] == jnp.arange(cap)[None, :, None])
    meta = jnp.sum(jnp.where(chosen, code[:, None, :] + 1, 0), axis=2).reshape(-1) - 1
    sub = jnp.where(meta < 0, TB_OWN, meta % TB_OWN)
    slot_rank = np.arange(devices * cap) % cap
    slot_part = np.searchsorted(np.array(cuts), slot_rank, side="right") - 1
    low, high = np.array(cuts)[slot_part], np.array(cuts)[slot_part + 1]
    place = devices * low + np.arange(devices * cap) // cap * (high - low) + slot_rank - low
    fold_key = jnp.asarray(slot_part * (TB_OWN + 1), jnp.int32) + sub
    fold_order, fold_bounds = sorted_slots(fold_key, parts * (TB_OWN + 1))
    score_order, score_bounds = sorted_slots(sub, TB_OWN)
    left = np.arange(parts)[:, None] < slot_part[None, :]
    done = jnp.min(jnp.where(left, sub[None, :], TB_OWN), axis=1)
    done = jnp.concatenate([jnp.zeros((1,), jnp.int32), done])
    scalars = [
        fold_order, fold_bounds, score_order, score_bounds, meta, jnp.asarray(place, jnp.int32), done
    ]

    inverse = lax.rsqrt(row_sq + EPSILON)
    scale = jnp.broadcast_to((inverse * (1.0 / CODE_TOP**2))[:, :, None], (blocks, LANES, LANES))
    partial, totals, normed = jnp.zeros((blocks, LANES), jnp.float32), (), []
    beside = (*scalars, padded_labels, scale)
    for q in range(parts):
        if q + 1 < parts:
            ahead = (incoming[q], *beside) if q else (incoming[q],)
            incoming.append(exchange(after(outgoing[q + 1], *ahead)))
        partial, sums, *more = stage(
            q, cuts, scalars, padded_labels, partial, scale, incoming[q], normed, totals
        )
        beside = (partial, sums)
        totals, normed = (sums, *more[:1]), normed + more[1:]
    back = jnp.sum(exchange(partial), axis=(0, 1))
    own_scale = lax.rsqrt(back[home:] + EPSILON)
    vocab_size = TB_OWN * LANES * devices
    centroid = sums * own_scale[:, None]
    centroids = (centroid * math.sqrt(vocab_size)).astype(jnp.bfloat16)
    is_label = labels[:, None] == jnp.arange(K, dtype=jnp.int32)[None, :]
    doc_scale = jnp.sum(jnp.where(is_label, own_scale[None, :], 0.0), axis=1)
    return (centroids, back[:home] * doc_scale)


def solution(mesh):
    return jax.shard_map(
        shards,
        mesh=mesh,
        in_specs=(
            P(("groups", "dp"), None, None),
            P(("groups", "dp")),
            P(("groups", "dp"), None),
            P(("groups", "dp")),
            P(("groups", "dp")),
        ),
        out_specs=(P("groups", "dp"), P(("groups", "dp"))),
        check_vma=False,
    )
```

```python
import functools
import math

import jax
import jax.numpy as jnp
import numpy as np
from jax import lax
from jax.experimental import pallas as pl
from jax.experimental.pallas import tpu as pltpu
from jax.sharding import PartitionSpec as P

K = 512
TB_OWN = 16
LANES = 128
EPSILON = 1e-06
CODE_TOP = 65535.0
CODE_SHIFT = 32768
VMEM_BYTES = 56 * 1024 * 1024
STEP_TILES = 32
PARTS = (0.0, 12 / 16, 1.0)
LOG_STEPS = 1800.0
LOG_MIDDLE = -3.0
CACHED_BLOCKS = 64
QUAD = 4
EIGHT = 8
BATCH = 8
NT = (((1,), (1,)), ((), ()))
SMEM = pl.BlockSpec(memory_space=pltpu.SMEM)
VMEM = pl.BlockSpec(memory_space=pltpu.VMEM)
ANY = pl.BlockSpec(memory_space=pl.ANY)


def lane_sums(values):
    ones = jnp.ones((8, LANES), jnp.bfloat16)
    high = values.astype(jnp.bfloat16)
    low = (values - high.astype(jnp.float32)).astype(jnp.bfloat16)
    return lax.dot_general(ones, high, NT, preferred_element_type=jnp.float32) + lax.dot_general(
        ones, low, NT, preferred_element_type=jnp.float32
    )


def block_sums(square, out_ref, count):
    batch = math.gcd(BATCH, count)

    def one_batch(c, carry):
        some = square[pl.ds(c * batch, batch)].reshape((batch * LANES, LANES))
        sums = lane_sums(some)
        for j in range(batch):
            out_ref[pl.ds(c * batch + j, 1), :] += sums[:1, j * LANES : (j + 1) * LANES]
        return carry

    lax.fori_loop(0, count // batch, one_batch, 0)


def params():
    return pltpu.CompilerParams(vmem_limit_bytes=VMEM_BYTES)


def pack_kernel(cuts, put_ref, row_ref, *refs):
    parts = len(cuts) - 1
    (*told_refs, x_ref), refs = refs[:5], refs[5:]
    outs = refs[:parts]
    coded, square, sums, words, notes, held, sems = refs[parts:]
    step = pl.program_id(0)
    tiles = x_ref.shape[0]
    devices = held.shape[0]
    blocks = square.shape[0]

    @pl.when(step == 0)
    def _():
        square[...] = jnp.zeros_like(square)

        def clear(d, carry):
            held[d] = 0
            return carry

        lax.fori_loop(0, devices, clear, 0)

    def some_tiles(i, carry):
        for j in range(QUAD):
            t = step * tiles + i * QUAD + j
            x = x_ref[i * QUAD + j]
            root = x * lax.rsqrt(x)
            code = (root * CODE_TOP + 0.5).astype(jnp.int32) - CODE_SHIFT
            put = put_ref[t]
            coded[pl.ds(pl.multiple_of(put * LANES, LANES), LANES), :] = code.astype(jnp.int16)
            square[row_ref[t]] += x * x
            owner = put // cuts[-1]
            held[owner] = jnp.maximum(held[owner], put % cuts[-1] + 1)
        return carry

    lax.fori_loop(0, tiles // QUAD, some_tiles, 0)

    def slots(q, d):
        some = pl.ds((d * cuts[-1] + cuts[q]) * LANES, (cuts[q + 1] - cuts[q]) * LANES)
        into = outs[q].at[d, pl.ds(0, (cuts[q + 1] - cuts[q]) * LANES)]
        return pltpu.make_async_copy(coded.at[some], into, sems.at[q * devices + d])

    def note(d):
        into = outs[0].at[d, pl.ds((cuts[1] - cuts[0]) * LANES, notes.shape[0])]
        return pltpu.make_async_copy(notes, into, sems.at[parts * devices + d])

    def each(what):
        for q in range(parts):
            for d in range(devices):
                pl.when(held[d] > cuts[q])(lambda q=q, d=d: what(slots(q, d)))

    @pl.when(step == pl.num_programs(0) - 1)
    def _():
        each(lambda copy: copy.start())
        sums[...] = jnp.zeros_like(sums)
        block_sums(square, sums, blocks)
        total = sums[...]
        level = (jnp.log2(jnp.maximum(total, 1e-30)) - LOG_MIDDLE) * LOG_STEPS
        level = jnp.where(total > 0.0, jnp.clip(level, -32700.0, 32700.0), -32768.0)
        level = (level + 32768.5).astype(jnp.int32) - 32768
        labels, owner, row, sub = [ref[...] for ref in told_refs]
        words[...] = jnp.zeros_like(words)
        words[:blocks, :] = level
        at = blocks
        for told in (labels, owner, row * TB_OWN + sub):
            words[at : at + told.shape[0], :] = told
            at += told.shape[0]
        notes[...] = words[...].astype(jnp.int16)
        for d in range(devices):
            note(d).start()
        each(lambda copy: copy.wait())
        for d in range(devices):
            note(d).wait()


def pack(tile_values, put, tile_row, told, devices, blocks, cuts):
    tiles = tile_values.shape[0]
    step = math.gcd(STEP_TILES, tiles)
    told = [x.reshape(-1, LANES) for x in told]
    noted = -(-(blocks + sum(x.shape[0] for x in told[:3])) // 16) * 16
    rows = [(high - low) * LANES for low, high in zip(cuts, cuts[1:])]
    rows[0] += noted
    return pl.pallas_call(
        functools.partial(pack_kernel, cuts),
        grid=(tiles // step,),
        in_specs=[SMEM, SMEM]
        + [pl.BlockSpec(x.shape, lambda i: (0, 0)) for x in told]
        + [pl.BlockSpec((step, LANES, LANES), lambda i: (i, 0, 0))],
        out_specs=[ANY] * len(rows),
        out_shape=[jax.ShapeDtypeStruct((devices, some, LANES), jnp.int16) for some in rows],
        scratch_shapes=[
            pltpu.VMEM((devices * cuts[-1] * LANES, LANES), jnp.int16),
            pltpu.VMEM((blocks, LANES, LANES), jnp.float32),
            pltpu.VMEM((blocks, LANES), jnp.float32),
            pltpu.VMEM((noted, LANES), jnp.int32),
            pltpu.VMEM((noted, LANES), jnp.int16),
            pltpu.SMEM((devices,), jnp.int32),
            pltpu.SemaphoreType.DMA(((len(rows) + 1) * devices,)),
        ],
        compiler_params=params(),
        cost_estimate=pl.CostEstimate(
            flops=8 * tile_values.size,
            bytes_accessed=6 * tile_values.size,
            transcendentals=tile_values.size,
        ),
        name="pack",
    )(put, tile_row, *told, tile_values)


def stage_kernel(q, bases, last, cached, fold_order, fold_bound, score_order, score_bound, meta,
                 place, done, labels, before, inv_hbm, x_hbm, *refs):
    base = bases[q]
    earlier, refs = refs[:q], refs[q:]
    (sums_in, squares_in), refs = (refs[:2], refs[2:]) if q else ((None, None), refs)
    part, sums_out, refs = refs[0], refs[1], refs[2:]
    (squares_out, fresh_out), refs = ((None, None), refs) if last else (refs[:2], refs[2:])
    inv, x, hot, sums, narrow, tiles, products, scores, squares, sems, sub_sems, tile_sems = refs
    devices, width = x.shape[0], x.shape[1] // LANES
    none = products.shape[0] - 1
    begin, end = done[q], done[q + 1]
    needed = [
        pltpu.make_async_copy(x_hbm.at[:, pl.ds(0, width * LANES)], x, sems.at[0]),
        pltpu.make_async_copy(inv_hbm, inv, sems.at[1]),
    ]
    for copy in needed:
        copy.start()

    def columns(sub):
        return (slice(None), pl.ds(pl.multiple_of(sub * LANES, LANES), LANES))

    def sums_read(sub):
        return pltpu.make_async_copy(
            sums_in.at[columns(sub)], sums.at[columns(sub)], sub_sems.at[0, sub]
        )

    def sums_write(sub):
        return pltpu.make_async_copy(
            sums.at[columns(sub)], sums_out.at[columns(sub)], sub_sems.at[1, sub]
        )

    def each_sub(low, high, what):
        def one(sub, carry):
            what(sub)
            return carry

        lax.fori_loop(low, high, one, 0)

    if q:
        each_sub(begin, TB_OWN, lambda sub: sums_read(sub).start())
        squares[...] = squares_in[...]
    else:
        sums[...] = jnp.zeros_like(sums)
        squares[...] = jnp.zeros_like(squares)
    later = []
    for e, e_hbm in enumerate(earlier):
        held = tiles.at[pl.ds(bases[e], e_hbm.shape[0])]
        later.append(pltpu.make_async_copy(e_hbm, held, tile_sems.at[e]))
        later[e].start()
    products[...] = jnp.zeros_like(products)
    scores[...] = before[...]
    cluster = lax.broadcasted_iota(jnp.int32, (K, LANES), 0)
    lane = lax.broadcasted_iota(jnp.int32, (LANES, LANES), 1)

    def one_hot(row):
        own = jnp.broadcast_to(labels[pl.ds(row, 1), :].astype(jnp.float32), (LANES, LANES))
        own = jnp.transpose(own).astype(jnp.int32)
        some = [jnp.where(own == lane + g, 1.0, 0.0) for g in range(0, K, LANES)]
        return jnp.concatenate(some, axis=1).astype(jnp.bfloat16)

    if cached:
        batch = math.gcd(none + 1, 3)

        def build(c, carry):
            for j in range(batch):
                hot[c * batch + j] = one_hot(c * batch + j)
            return carry

        lax.fori_loop(0, (none + 1) // batch, build, 0)
    for copy in needed:
        copy.wait()

    def eight(order, start, end, p):
        rows, spots = [], []
        for j in range(EIGHT):
            at = start + EIGHT * p + j
            slot = order[jnp.where(at < end, at, start)]
            rows.append((meta[slot] // TB_OWN, at < end))
            spots.append(place[slot])
        return rows, spots

    def fold_sub(sub):
        start = fold_bound[q * (TB_OWN + 1) + sub]
        end = fold_bound[q * (TB_OWN + 1) + sub + 1]
        if q:
            sums_read(sub).wait()

        def one_eight(p, carry):
            rows, spots = eight(fold_order, start, end, p)
            folded, picks = [], []
            for (row, held), spot in zip(rows, spots):
                source, slot = (spot - base) // width, (spot - base) % width
                raw = x[source, pl.ds(pl.multiple_of(slot * LANES, LANES), LANES), :]
                root = raw.astype(jnp.int32).astype(jnp.float32) + float(CODE_SHIFT)
                tile = (root * root * inv[row]).astype(jnp.bfloat16)
                tiles[spot] = tile
                folded.append(tile)
                own = cluster == labels[pl.ds(jnp.where(held, row, none), 1), :]
                picks.append(jnp.where(own, 1.0, 0.0).astype(jnp.bfloat16))
            pick = jnp.concatenate(picks, axis=1)
            sums[columns(sub)] += jnp.dot(
                pick, jnp.concatenate(folded, axis=0), preferred_element_type=jnp.float32
            )
            return carry

        lax.fori_loop(0, (end - start + EIGHT - 1) // EIGHT, one_eight, 0)
        sums_write(sub).start()

    each_sub(begin, TB_OWN, fold_sub)
    kept = []
    if not last:
        fresh = tiles.at[pl.ds(base, devices * width)]
        kept.append(pltpu.make_async_copy(fresh, fresh_out, sems.at[2]))
    for copy in kept:
        copy.start()
    for copy in later:
        copy.wait()

    def score_sub(sub):
        start, end = score_bound[sub], score_bound[sub + 1]
        some = sums[columns(sub)]
        narrow[...] = some.astype(jnp.bfloat16)
        squares[...] += some * some

        def one_eight(p, carry):
            rows, spots = eight(score_order, start, end, p)
            rows = [jnp.where(held, row, none) for row, held in rows]
            hots = [hot[row] if cached else one_hot(row) for row in rows]
            chosen = jnp.dot(
                jnp.concatenate(hots, axis=0), narrow[...], preferred_element_type=jnp.float32
            )
            for j in range(EIGHT):
                own = chosen[j * LANES : (j + 1) * LANES]
                products[rows[j]] += own * tiles[spots[j]].astype(jnp.float32)
            return carry

        lax.fori_loop(0, (end - start + EIGHT - 1) // EIGHT, one_eight, 0)

    each_sub(begin, end, score_sub)
    block_sums(products, scores, none)
    if last:
        own = none // devices
        square = lane_sums(squares[...])[:1]
        for d in range(devices):
            part[d, :, part.shape[2] - K :] = square
            for b in range(own):
                at = d * own + b
                part[d, :, b * LANES : (b + 1) * LANES] = scores[at : at + 1, :]
    else:
        part[...] = scores[...]
        squares_out[...] = squares[...]
    for copy in kept:
        copy.wait()
    each_sub(begin, TB_OWN, lambda sub: sums_write(sub).wait())


def stage(q, cuts, scalars, labels, before, inverse, x, normed, totals):
    devices = x.shape[0]
    last = q == len(cuts) - 2
    blocks = inverse.shape[0]
    cached = blocks <= CACHED_BLOCKS
    width = cuts[q + 1] - cuts[q]
    home = blocks // devices * LANES
    wide = jax.ShapeDtypeStruct((K, TB_OWN * LANES), jnp.float32)
    if last:
        out_shape = [jax.ShapeDtypeStruct((devices, 1, home + K), jnp.float32), wide]
    else:
        out_shape = [
            jax.ShapeDtypeStruct((blocks, LANES), jnp.float32),
            wide,
            jax.ShapeDtypeStruct((K, LANES), jnp.float32),
            jax.ShapeDtypeStruct((devices * width, LANES, LANES), jnp.bfloat16),
        ]
    slots = devices * cuts[-1]
    operands = [*scalars, labels, before, inverse, x, *normed, *totals]
    return pl.pallas_call(
        functools.partial(stage_kernel, q, [devices * cut for cut in cuts], last, cached),
        in_specs=[SMEM] * len(scalars) + [VMEM] * 2 + [ANY] * (2 + q) + [ANY, VMEM][: len(totals)],
        out_specs=[VMEM, ANY, VMEM, ANY][: len(out_shape)],
        out_shape=out_shape,
        input_output_aliases={len(operands) - 2: 1} if q else {},
        scratch_shapes=[
            pltpu.VMEM(inverse.shape, jnp.float32),
            pltpu.VMEM((devices, width * LANES, LANES), jnp.int16),
            pltpu.VMEM((blocks + 1 if cached else 1, LANES, K), jnp.bfloat16),
            pltpu.VMEM(wide.shape, jnp.float32),
            pltpu.VMEM((K, LANES), jnp.bfloat16),
            pltpu.VMEM((slots, LANES, LANES), jnp.bfloat16),
            pltpu.VMEM((blocks + 1, LANES, LANES), jnp.float32),
            pltpu.VMEM((blocks, LANES), jnp.float32),
            pltpu.VMEM((K, LANES), jnp.float32),
            pltpu.SemaphoreType.DMA((3,)),
            pltpu.SemaphoreType.DMA((2, TB_OWN)),
            pltpu.SemaphoreType.DMA((len(cuts),)),
        ],
        compiler_params=params(),
        cost_estimate=pl.CostEstimate(
            flops=devices * width * LANES * LANES * K * 8,
            bytes_accessed=4 * devices * width * LANES * LANES + 8 * K * TB_OWN * LANES,
            transcendentals=0,
        ),
        name="stage",
    )(*operands)


def exchange(x):
    return lax.all_to_all(x, "dp", split_axis=0, concat_axis=0, tiled=True)


def after(value, *others):
    return lax.optimization_barrier((value, *others))[0]


def sorted_slots(key, top):
    slots = jnp.arange(key.shape[0], dtype=jnp.int32)
    ahead = (key[None, :] < key[:, None]) | (
        (key[None, :] == key[:, None]) & (slots[None, :] < slots[:, None])
    )
    position = jnp.sum(ahead.astype(jnp.int32), axis=1)
    here = position[None, :] == slots[:, None]
    order = jnp.sum(jnp.where(here, slots[None, :], 0), axis=1)
    levels = jnp.arange(top + 1, dtype=jnp.int32)
    bounds = jnp.sum((key[None, :] < levels[:, None]).astype(jnp.int32), axis=1)
    return order, bounds


def ranks(group, sub):
    index = jnp.arange(sub.shape[-1], dtype=jnp.int32)
    before = (sub[..., None, :] < sub[..., :, None]) | (
        (sub[..., None, :] == sub[..., :, None]) & (index[None, :] < index[:, None])
    )
    same = group[..., None, :] == group[..., :, None]
    return jnp.sum((before & same).astype(jnp.int32), axis=-1)


def shards(tile_values, tile_row, tile_owner, tile_sub, labels):
    devices = lax.axis_size("dp")
    tiles = tile_values.shape[0]
    home = labels.shape[0]
    blocks = home // LANES * devices
    cap = max(2, 2 * tiles // devices)
    cuts = tuple(sorted({int(cap * share) for share in PARTS})) if cap >= 8 else (0, cap)
    parts = len(cuts) - 1
    here = lax.axis_index("dp").astype(jnp.int32)
    owner = tile_owner[:, 0]

    put = owner * cap + ranks(owner, tile_sub)
    told = (labels, owner, tile_row, tile_sub)
    outgoing = pack(tile_values, put, tile_row, told, devices, blocks, cuts)
    incoming = [exchange(outgoing[0])]
    heard = incoming[0][:, (cuts[1] - cuts[0]) * LANES :].astype(jnp.int32)
    level = heard[:, :blocks]
    partial_sq = jnp.exp2(level.astype(jnp.float32) * (1.0 / LOG_STEPS) + LOG_MIDDLE)
    row_sq = jnp.sum(jnp.where(level > -32768, partial_sq, 0.0), axis=0)
    all_described = heard[:, blocks:].reshape(devices, -1)
    all_labels = all_described[:, :home].reshape(blocks, LANES)
    padded_labels = jnp.concatenate([all_labels, jnp.full((1, LANES), -1, jnp.int32)])
    mine = all_described[:, home : home + tiles] == here
    code = all_described[:, home + tiles : home + 2 * tiles]
    rank = ranks(mine.astype(jnp.int32), code % TB_OWN)
    chosen = mine[:, None, :] & (rank[:, None, :] == jnp.arange(cap)[None, :, None])
    meta = jnp.sum(jnp.where(chosen, code[:, None, :] + 1, 0), axis=2).reshape(-1) - 1
    sub = jnp.where(meta < 0, TB_OWN, meta % TB_OWN)
    slot_rank = np.arange(devices * cap) % cap
    slot_part = np.searchsorted(np.array(cuts), slot_rank, side="right") - 1
    low, high = np.array(cuts)[slot_part], np.array(cuts)[slot_part + 1]
    place = devices * low + np.arange(devices * cap) // cap * (high - low) + slot_rank - low
    fold_key = jnp.asarray(slot_part * (TB_OWN + 1), jnp.int32) + sub
    fold_order, fold_bounds = sorted_slots(fold_key, parts * (TB_OWN + 1))
    score_order, score_bounds = sorted_slots(sub, TB_OWN)
    left = np.arange(parts)[:, None] < slot_part[None, :]
    done = jnp.min(jnp.where(left, sub[None, :], TB_OWN), axis=1)
    done = jnp.concatenate([jnp.zeros((1,), jnp.int32), done])
    scalars = [
        fold_order, fold_bounds, score_order, score_bounds, meta, jnp.asarray(place, jnp.int32), done
    ]

    inverse = lax.rsqrt(row_sq + EPSILON)
    scale = jnp.broadcast_to((inverse * (1.0 / CODE_TOP**2))[:, :, None], (blocks, LANES, LANES))
    partial, totals, normed = jnp.zeros((blocks, LANES), jnp.float32), (), []
    beside = (*scalars, padded_labels, scale)
    for q in range(parts):
        if q + 1 < parts:
            ahead = (incoming[q], *beside) if q else (incoming[q],)
            incoming.append(exchange(after(outgoing[q + 1], *ahead)))
        partial, sums, *more = stage(
            q, cuts, scalars, padded_labels, partial, scale, incoming[q], normed, totals
        )
        beside = (partial, sums)
        totals, normed = (sums, *more[:1]), normed + more[1:]
    back = jnp.sum(exchange(partial), axis=(0, 1))
    own_scale = lax.rsqrt(back[home:] + EPSILON)
    vocab_size = TB_OWN * LANES * devices
    centroid = sums * own_scale[:, None]
    centroids = (centroid * math.sqrt(vocab_size)).astype(jnp.bfloat16)
    is_label = labels[:, None] == jnp.arange(K, dtype=jnp.int32)[None, :]
    doc_scale = jnp.sum(jnp.where(is_label, own_scale[None, :], 0.0), axis=1)
    return (centroids, back[:home] * doc_scale)


def solution(mesh):
    return jax.shard_map(
        shards,
        mesh=mesh,
        in_specs=(
            P(("groups", "dp"), None, None),
            P(("groups", "dp")),
            P(("groups", "dp"), None),
            P(("groups", "dp")),
            P(("groups", "dp")),
        ),
        out_specs=(P("groups", "dp"), P(("groups", "dp"))),
        check_vma=False,
    )
```

```python
import functools
import math

import jax
import jax.numpy as jnp
import numpy as np
from jax import lax
from jax.experimental import pallas as pl
from jax.experimental.pallas import tpu as pltpu
from jax.sharding import PartitionSpec as P

K = 512
HALF = K // 2
TB_OWN = 16
LANES = 128
EPSILON = 1e-06
CODE_TOP = 65535.0
CODE_SHIFT = 32768
VMEM_BYTES = 56 * 1024 * 1024
STEP_TILES = 32
PARTS = (0.0, 12 / 16, 1.0)
LOG_STEPS = 1800.0
LOG_MIDDLE = -3.0
CACHED_BLOCKS = 64
QUAD = 4
EIGHT = 8
BATCH = 8
NT = (((1,), (1,)), ((), ()))
SMEM = pl.BlockSpec(memory_space=pltpu.SMEM)
VMEM = pl.BlockSpec(memory_space=pltpu.VMEM)
ANY = pl.BlockSpec(memory_space=pl.ANY)


def lane_sums(values):
    ones = jnp.ones((8, LANES), jnp.bfloat16)
    high = values.astype(jnp.bfloat16)
    low = (values - high.astype(jnp.float32)).astype(jnp.bfloat16)
    return lax.dot_general(ones, high, NT, preferred_element_type=jnp.float32) + lax.dot_general(
        ones, low, NT, preferred_element_type=jnp.float32
    )


def block_sums(square, out_ref, count):
    batch = math.gcd(BATCH, count)

    def one_batch(c, carry):
        some = square[pl.ds(c * batch, batch)].reshape((batch * LANES, LANES))
        sums = lane_sums(some)
        for j in range(batch):
            out_ref[pl.ds(c * batch + j, 1), :] += sums[:1, j * LANES : (j + 1) * LANES]
        return carry

    lax.fori_loop(0, count // batch, one_batch, 0)


def params():
    return pltpu.CompilerParams(vmem_limit_bytes=VMEM_BYTES)


def pack_kernel(cuts, put_ref, row_ref, *refs):
    parts = len(cuts) - 1
    (*told_refs, x_ref), refs = refs[:5], refs[5:]
    outs = refs[:parts]
    coded, square, sums, words, notes, held, sems = refs[parts:]
    step = pl.program_id(0)
    tiles = x_ref.shape[0]
    devices = held.shape[0]
    blocks = square.shape[0]

    @pl.when(step == 0)
    def _():
        square[...] = jnp.zeros_like(square)

        def clear(d, carry):
            held[d] = 0
            return carry

        lax.fori_loop(0, devices, clear, 0)

    def some_tiles(i, carry):
        for j in range(QUAD):
            t = step * tiles + i * QUAD + j
            x = x_ref[i * QUAD + j]
            root = x * lax.rsqrt(x)
            code = (root * CODE_TOP + 0.5).astype(jnp.int32) - CODE_SHIFT
            put = put_ref[t]
            coded[pl.ds(pl.multiple_of(put * LANES, LANES), LANES), :] = code.astype(jnp.int16)
            square[row_ref[t]] += x * x
            owner = put // cuts[-1]
            held[owner] = jnp.maximum(held[owner], put % cuts[-1] + 1)
        return carry

    lax.fori_loop(0, tiles // QUAD, some_tiles, 0)

    def slots(q, d):
        some = pl.ds((d * cuts[-1] + cuts[q]) * LANES, (cuts[q + 1] - cuts[q]) * LANES)
        into = outs[q].at[d, pl.ds(0, (cuts[q + 1] - cuts[q]) * LANES)]
        return pltpu.make_async_copy(coded.at[some], into, sems.at[q * devices + d])

    def note(d):
        into = outs[0].at[d, pl.ds((cuts[1] - cuts[0]) * LANES, notes.shape[0])]
        return pltpu.make_async_copy(notes, into, sems.at[parts * devices + d])

    def each(what):
        for q in range(parts):
            for d in range(devices):
                pl.when(held[d] > cuts[q])(lambda q=q, d=d: what(slots(q, d)))

    @pl.when(step == pl.num_programs(0) - 1)
    def _():
        each(lambda copy: copy.start())
        sums[...] = jnp.zeros_like(sums)
        block_sums(square, sums, blocks)
        total = sums[...]
        level = (jnp.log2(jnp.maximum(total, 1e-30)) - LOG_MIDDLE) * LOG_STEPS
        level = jnp.where(total > 0.0, jnp.clip(level, -32700.0, 32700.0), -32768.0)
        level = (level + 32768.5).astype(jnp.int32) - 32768
        labels, owner, row, sub = [ref[...] for ref in told_refs]
        words[...] = jnp.zeros_like(words)
        words[:blocks, :] = level
        at = blocks
        for told in (labels, owner, row * TB_OWN + sub):
            words[at : at + told.shape[0], :] = told
            at += told.shape[0]
        notes[...] = words[...].astype(jnp.int16)
        for d in range(devices):
            note(d).start()
        each(lambda copy: copy.wait())
        for d in range(devices):
            note(d).wait()


def pack(tile_values, put, tile_row, told, devices, blocks, cuts):
    tiles = tile_values.shape[0]
    step = math.gcd(STEP_TILES, tiles)
    told = [x.reshape(-1, LANES) for x in told]
    noted = -(-(blocks + sum(x.shape[0] for x in told[:3])) // 16) * 16
    rows = [(high - low) * LANES for low, high in zip(cuts, cuts[1:])]
    rows[0] += noted
    return pl.pallas_call(
        functools.partial(pack_kernel, cuts),
        grid=(tiles // step,),
        in_specs=[SMEM, SMEM]
        + [pl.BlockSpec(x.shape, lambda i: (0, 0)) for x in told]
        + [pl.BlockSpec((step, LANES, LANES), lambda i: (i, 0, 0))],
        out_specs=[ANY] * len(rows),
        out_shape=[jax.ShapeDtypeStruct((devices, some, LANES), jnp.int16) for some in rows],
        scratch_shapes=[
            pltpu.VMEM((devices * cuts[-1] * LANES, LANES), jnp.int16),
            pltpu.VMEM((blocks, LANES, LANES), jnp.float32),
            pltpu.VMEM((blocks, LANES), jnp.float32),
            pltpu.VMEM((noted, LANES), jnp.int32),
            pltpu.VMEM((noted, LANES), jnp.int16),
            pltpu.SMEM((devices,), jnp.int32),
            pltpu.SemaphoreType.DMA(((len(rows) + 1) * devices,)),
        ],
        compiler_params=params(),
        cost_estimate=pl.CostEstimate(
            flops=8 * tile_values.size,
            bytes_accessed=6 * tile_values.size,
            transcendentals=tile_values.size,
        ),
        name="pack",
    )(put, tile_row, *told, tile_values)


def stage_kernel(q, bases, last, cached, fold_order, fold_bound, score_order, score_bound, meta,
                 place, done, mods, signed, before, x_hbm, *refs):
    base = bases[q]
    earlier, refs = refs[:q], refs[q:]
    (sums_in, squares_in), refs = (refs[:2], refs[2:]) if q else ((None, None), refs)
    part, sums_out, refs = refs[0], refs[1], refs[2:]
    (squares_out, fresh_out), refs = ((None, None), refs) if last else (refs[:2], refs[2:])
    spread, x, hot, sums, narrow, tiles, products, scores, squares, sems, sub_sems, tile_sems = refs
    devices, width = x.shape[0], x.shape[1] // LANES
    none = products.shape[0] - 1
    begin, end = done[q], done[q + 1]
    needed = pltpu.make_async_copy(x_hbm.at[:, pl.ds(0, width * LANES)], x, sems.at[0])
    needed.start()

    def columns(sub):
        return (slice(None), pl.ds(pl.multiple_of(sub * 2 * LANES, 2 * LANES), 2 * LANES))

    def sums_read(sub):
        return pltpu.make_async_copy(
            sums_in.at[columns(sub)], sums.at[columns(sub)], sub_sems.at[0, sub]
        )

    def sums_write(sub):
        return pltpu.make_async_copy(
            sums.at[columns(sub)], sums_out.at[columns(sub)], sub_sems.at[1, sub]
        )

    def each_sub(low, high, what):
        def one(sub, carry):
            what(sub)
            return carry

        lax.fori_loop(low, high, one, 0)

    if q:
        each_sub(begin, TB_OWN, lambda sub: sums_read(sub).start())
        squares[...] = squares_in[...]
    else:
        sums[...] = jnp.zeros_like(sums)
        squares[...] = jnp.zeros_like(squares)
    later = []
    for e, e_hbm in enumerate(earlier):
        held = tiles.at[pl.ds(bases[e], e_hbm.shape[0])]
        later.append(pltpu.make_async_copy(e_hbm, held, tile_sems.at[e]))
        later[e].start()
    products[...] = jnp.zeros_like(products)
    scores[...] = before[...]
    cluster = lax.broadcasted_iota(jnp.int32, (HALF, LANES), 0)
    lane = lax.broadcasted_iota(jnp.int32, (LANES, LANES), 1)

    def column(ref, row):
        return jnp.transpose(jnp.broadcast_to(ref[pl.ds(row, 1), :], (LANES, LANES)))

    def one_hot(row):
        own = column(mods, row).astype(jnp.int32)
        some = [jnp.where(own == lane + g, 1.0, 0.0) for g in range(0, HALF, LANES)]
        return jnp.concatenate(some, axis=1).astype(jnp.bfloat16)

    batch = math.gcd(none + 1, 3)

    def build(c, carry):
        for j in range(batch):
            spread[c * batch + j] = column(signed, c * batch + j)
            if cached:
                hot[c * batch + j] = one_hot(c * batch + j)
        return carry

    lax.fori_loop(0, (none + 1) // batch, build, 0)
    needed.wait()

    def eight(order, start, end, p):
        rows, spots = [], []
        for j in range(EIGHT):
            at = start + EIGHT * p + j
            slot = order[jnp.where(at < end, at, start)]
            rows.append((meta[slot] // TB_OWN, at < end))
            spots.append(place[slot])
        return rows, spots

    def fold_sub(sub):
        start = fold_bound[q * (TB_OWN + 1) + sub]
        end = fold_bound[q * (TB_OWN + 1) + sub + 1]
        if q:
            sums_read(sub).wait()

        def one_eight(p, carry):
            rows, spots = eight(fold_order, start, end, p)
            folded, picks = [], []
            for (row, held), spot in zip(rows, spots):
                source, slot = (spot - base) // width, (spot - base) % width
                raw = x[source, pl.ds(pl.multiple_of(slot * LANES, LANES), LANES), :]
                root = raw.astype(jnp.int32).astype(jnp.float32) + float(CODE_SHIFT)
                scale = spread[row]
                tile = root * root * jnp.abs(scale)
                tiles[spot] = tile.astype(jnp.bfloat16)
                halves = [jnp.where(scale > 0.0, tile, 0.0), jnp.where(scale < 0.0, tile, 0.0)]
                folded.append(jnp.concatenate(halves, axis=1).astype(jnp.bfloat16))
                own = mods[pl.ds(jnp.where(held, row, none), 1), :].astype(jnp.int32)
                picks.append(jnp.where(cluster == own, 1.0, 0.0).astype(jnp.bfloat16))
            pick = jnp.concatenate(picks, axis=1)
            sums[columns(sub)] += jnp.dot(
                pick, jnp.concatenate(folded, axis=0), preferred_element_type=jnp.float32
            )
            return carry

        lax.fori_loop(0, (end - start + EIGHT - 1) // EIGHT, one_eight, 0)
        sums_write(sub).start()

    each_sub(begin, TB_OWN, fold_sub)
    kept = []
    if not last:
        fresh = tiles.at[pl.ds(base, devices * width)]
        kept.append(pltpu.make_async_copy(fresh, fresh_out, sems.at[2]))
    for copy in kept:
        copy.start()
    for copy in later:
        copy.wait()

    def score_sub(sub):
        start, end = score_bound[sub], score_bound[sub + 1]
        some = sums[columns(sub)]
        narrow[...] = some.astype(jnp.bfloat16)
        squares[...] += some * some

        def one_eight(p, carry):
            rows, spots = eight(score_order, start, end, p)
            rows = [jnp.where(held, row, none) for row, held in rows]
            hots = [hot[row] if cached else one_hot(row) for row in rows]
            chosen = jnp.dot(
                jnp.concatenate(hots, axis=0), narrow[...], preferred_element_type=jnp.float32
            )
            for j in range(EIGHT):
                both = chosen[j * LANES : (j + 1) * LANES]
                own = jnp.where(spread[rows[j]] < 0.0, both[:, LANES:], both[:, :LANES])
                products[rows[j]] += own * tiles[spots[j]].astype(jnp.float32)
            return carry

        lax.fori_loop(0, (end - start + EIGHT - 1) // EIGHT, one_eight, 0)

    each_sub(begin, end, score_sub)
    block_sums(products, scores, none)
    if last:
        own = none // devices
        square = [lane_sums(squares[:, h : h + LANES])[:1] for h in (0, LANES)]
        square = jnp.concatenate(square, axis=1)
        for d in range(devices):
            part[d, :, part.shape[2] - K :] = square
            for b in range(own):
                at = d * own + b
                part[d, :, b * LANES : (b + 1) * LANES] = scores[at : at + 1, :]
    else:
        part[...] = scores[...]
        squares_out[...] = squares[...]
    for copy in kept:
        copy.wait()
    each_sub(begin, TB_OWN, lambda sub: sums_write(sub).wait())


def stage(q, cuts, scalars, mods, signed, before, x, normed, totals):
    devices = x.shape[0]
    last = q == len(cuts) - 2
    blocks = before.shape[0]
    cached = blocks <= CACHED_BLOCKS
    width = cuts[q + 1] - cuts[q]
    home = blocks // devices * LANES
    wide = jax.ShapeDtypeStruct((HALF, TB_OWN * 2 * LANES), jnp.float32)
    square = jax.ShapeDtypeStruct((HALF, 2 * LANES), jnp.float32)
    if last:
        out_shape = [jax.ShapeDtypeStruct((devices, 1, home + K), jnp.float32), wide]
    else:
        out_shape = [
            jax.ShapeDtypeStruct((blocks, LANES), jnp.float32),
            wide,
            square,
            jax.ShapeDtypeStruct((devices * width, LANES, LANES), jnp.bfloat16),
        ]
    slots = devices * cuts[-1]
    operands = [*scalars, mods, signed, before, x, *normed, *totals]
    return pl.pallas_call(
        functools.partial(stage_kernel, q, [devices * cut for cut in cuts], last, cached),
        in_specs=[SMEM] * len(scalars) + [VMEM] * 3 + [ANY] * (1 + q) + [ANY, VMEM][: len(totals)],
        out_specs=[VMEM, ANY, VMEM, ANY][: len(out_shape)],
        out_shape=out_shape,
        input_output_aliases={len(operands) - 2: 1} if q else {},
        scratch_shapes=[
            pltpu.VMEM((blocks + 1, LANES, LANES), jnp.float32),
            pltpu.VMEM((devices, width * LANES, LANES), jnp.int16),
            pltpu.VMEM((blocks + 1 if cached else 1, LANES, HALF), jnp.bfloat16),
            pltpu.VMEM(wide.shape, jnp.float32),
            pltpu.VMEM(square.shape, jnp.bfloat16),
            pltpu.VMEM((slots, LANES, LANES), jnp.bfloat16),
            pltpu.VMEM((blocks + 1, LANES, LANES), jnp.float32),
            pltpu.VMEM((blocks, LANES), jnp.float32),
            pltpu.VMEM(square.shape, jnp.float32),
            pltpu.SemaphoreType.DMA((3,)),
            pltpu.SemaphoreType.DMA((2, TB_OWN)),
            pltpu.SemaphoreType.DMA((len(cuts),)),
        ],
        compiler_params=params(),
        cost_estimate=pl.CostEstimate(
            flops=devices * width * LANES * LANES * K * 8,
            bytes_accessed=4 * devices * width * LANES * LANES + 8 * K * TB_OWN * LANES,
            transcendentals=0,
        ),
        name="stage",
    )(*operands)


def close_kernel(root, groups, labels_ref, got_ref, sums_hbm, out_hbm, similarity, sums, out, sems):
    width = TB_OWN // groups
    reads, writes = [], []
    for g in range(groups):
        some = (slice(None), pl.ds(g * width * 2 * LANES, width * 2 * LANES))
        reads.append(pltpu.make_async_copy(sums_hbm.at[some], sums.at[some], sems.at[0, g]))
        some = (slice(None), pl.ds(g * width * LANES, width * LANES))
        writes.append(pltpu.make_async_copy(out.at[some], out_hbm.at[some], sems.at[1, g]))
        reads[g].start()
    total = jnp.sum(got_ref[...], axis=0)
    home = total.shape[1] - K
    own = lax.rsqrt(total[:, home:] + EPSILON)
    columns = [
        jnp.transpose(jnp.broadcast_to(own[:, k : k + LANES], (LANES, LANES)))
        for k in range(0, K, LANES)
    ]
    cluster = lax.broadcasted_iota(jnp.int32, (LANES, LANES), 0)
    for b in range(home // LANES):
        found = jnp.zeros((LANES, LANES), jnp.float32)
        for i, column in enumerate(columns):
            found += jnp.where(cluster + i * LANES == labels_ref[b : b + 1, :], column, 0.0)
        found = jnp.sum(found, axis=0, keepdims=True)
        similarity[b : b + 1, :] = total[:, b * LANES : (b + 1) * LANES] * found
    for g in range(groups):
        reads[g].wait()
        for sub in range(g * width, (g + 1) * width):
            for i, column in enumerate(columns):
                half, row = divmod(i * LANES, HALF)
                at = (2 * sub + half) * LANES
                some = sums[row : row + LANES, at : at + LANES]
                done = (some * column * root).astype(jnp.bfloat16)
                out[i * LANES : (i + 1) * LANES, sub * LANES : (sub + 1) * LANES] = done
        writes[g].start()
    for write in writes:
        write.wait()


def close(labels, got, sums, vocab_size):
    groups = 4
    labels = labels.reshape(-1, LANES)
    wide = jax.ShapeDtypeStruct((K, TB_OWN * LANES), jnp.bfloat16)
    centroids, similarity = pl.pallas_call(
        functools.partial(close_kernel, math.sqrt(vocab_size), groups),
        in_specs=[VMEM, VMEM, ANY],
        out_specs=[ANY, VMEM],
        out_shape=[wide, jax.ShapeDtypeStruct(labels.shape, jnp.float32)],
        scratch_shapes=[
            pltpu.VMEM(sums.shape, jnp.float32),
            pltpu.VMEM(wide.shape, jnp.bfloat16),
            pltpu.SemaphoreType.DMA((2, groups)),
        ],
        compiler_params=params(),
        cost_estimate=pl.CostEstimate(
            flops=2 * sums.size, bytes_accessed=6 * sums.size, transcendentals=0
        ),
        name="close",
    )(labels, got, sums)
    return centroids, similarity.reshape(-1)


def exchange(x):
    return lax.all_to_all(x, "dp", split_axis=0, concat_axis=0, tiled=True)


def after(value, *others):
    return lax.optimization_barrier((value, *others))[0]


def sorted_slots(key, top):
    slots = jnp.arange(key.shape[0], dtype=jnp.int32)
    ahead = (key[None, :] < key[:, None]) | (
        (key[None, :] == key[:, None]) & (slots[None, :] < slots[:, None])
    )
    position = jnp.sum(ahead.astype(jnp.int32), axis=1)
    here = position[None, :] == slots[:, None]
    order = jnp.sum(jnp.where(here, slots[None, :], 0), axis=1)
    levels = jnp.arange(top + 1, dtype=jnp.int32)
    bounds = jnp.sum((key[None, :] < levels[:, None]).astype(jnp.int32), axis=1)
    return order, bounds


def ranks(group, sub):
    index = jnp.arange(sub.shape[-1], dtype=jnp.int32)
    before = (sub[..., None, :] < sub[..., :, None]) | (
        (sub[..., None, :] == sub[..., :, None]) & (index[None, :] < index[:, None])
    )
    same = group[..., None, :] == group[..., :, None]
    return jnp.sum((before & same).astype(jnp.int32), axis=-1)


def shards(tile_values, tile_row, tile_owner, tile_sub, labels):
    devices = lax.axis_size("dp")
    tiles = tile_values.shape[0]
    home = labels.shape[0]
    blocks = home // LANES * devices
    cap = max(2, 2 * tiles // devices)
    cuts = tuple(sorted({int(cap * share) for share in PARTS})) if cap >= 8 else (0, cap)
    parts = len(cuts) - 1
    here = lax.axis_index("dp").astype(jnp.int32)
    owner = tile_owner[:, 0]

    put = owner * cap + ranks(owner, tile_sub)
    told = (labels, owner, tile_row, tile_sub)
    outgoing = pack(tile_values, put, tile_row, told, devices, blocks, cuts)
    incoming = [exchange(outgoing[0])]
    heard = incoming[0][:, (cuts[1] - cuts[0]) * LANES :].astype(jnp.int32)
    level = heard[:, :blocks]
    partial_sq = jnp.exp2(level.astype(jnp.float32) * (1.0 / LOG_STEPS) + LOG_MIDDLE)
    row_sq = jnp.sum(jnp.where(level > -32768, partial_sq, 0.0), axis=0)
    all_described = heard[:, blocks:].reshape(devices, -1)
    all_labels = all_described[:, :home].reshape(blocks, LANES)
    mine = all_described[:, home : home + tiles] == here
    code = all_described[:, home + tiles : home + 2 * tiles]
    rank = ranks(mine.astype(jnp.int32), code % TB_OWN)
    chosen = mine[:, None, :] & (rank[:, None, :] == jnp.arange(cap)[None, :, None])
    meta = jnp.sum(jnp.where(chosen, code[:, None, :] + 1, 0), axis=2).reshape(-1) - 1
    sub = jnp.where(meta < 0, TB_OWN, meta % TB_OWN)
    slot_rank = np.arange(devices * cap) % cap
    slot_part = np.searchsorted(np.array(cuts), slot_rank, side="right") - 1
    low, high = np.array(cuts)[slot_part], np.array(cuts)[slot_part + 1]
    place = devices * low + np.arange(devices * cap) // cap * (high - low) + slot_rank - low
    fold_key = jnp.asarray(slot_part * (TB_OWN + 1), jnp.int32) + sub
    fold_order, fold_bounds = sorted_slots(fold_key, parts * (TB_OWN + 1))
    score_order, score_bounds = sorted_slots(sub, TB_OWN)
    left = np.arange(parts)[:, None] < slot_part[None, :]
    done = jnp.min(jnp.where(left, sub[None, :], TB_OWN), axis=1)
    done = jnp.concatenate([jnp.zeros((1,), jnp.int32), done])
    scalars = [
        fold_order, fold_bounds, score_order, score_bounds, meta, jnp.asarray(place, jnp.int32), done
    ]

    scale = lax.rsqrt(row_sq + EPSILON) * (1.0 / CODE_TOP**2)
    signed = jnp.pad(jnp.where(all_labels < HALF, scale, -scale), ((0, 1), (0, 0)))
    mods = (all_labels % HALF).astype(jnp.float32)
    mods = jnp.pad(mods, ((0, 1), (0, 0)), constant_values=-1.0)
    partial, totals, normed = jnp.zeros((blocks, LANES), jnp.float32), (), []
    beside = (*scalars, mods, signed)
    for q in range(parts):
        if q + 1 < parts:
            ahead = (incoming[q], *beside) if q else (incoming[q],)
            incoming.append(exchange(after(outgoing[q + 1], *ahead)))
        partial, sums, *more = stage(
            q, cuts, scalars, mods, signed, partial, incoming[q], normed, totals
        )
        beside = (partial, sums)
        totals, normed = (sums, *more[:1]), normed + more[1:]
    return close(labels, exchange(partial), sums, TB_OWN * LANES * devices)


def solution(mesh):
    return jax.shard_map(
        shards,
        mesh=mesh,
        in_specs=(
            P(("groups", "dp"), None, None),
            P(("groups", "dp")),
            P(("groups", "dp"), None),
            P(("groups", "dp")),
            P(("groups", "dp")),
        ),
        out_specs=(P("groups", "dp"), P(("groups", "dp"))),
        check_vma=False,
    )
```

```python
import functools
import math

import jax
import jax.numpy as jnp
import numpy as np
from jax import lax
from jax.experimental import pallas as pl
from jax.experimental.pallas import tpu as pltpu
from jax.sharding import PartitionSpec as P

K = 512
HALF = K // 2
TB_OWN = 16
LANES = 128
EPSILON = 1e-06
CODE_TOP = 65535.0
CODE_SHIFT = 32768
VMEM_BYTES = 60 * 1024 * 1024
STEP_TILES = 32
PARTS = (0.0, 13 / 16, 1.0)
LOG_STEPS = 1800.0
LOG_MIDDLE = -3.0
CACHED_BLOCKS = 64
QUAD = 4
EIGHT = 8
BATCH = 8
NT = (((1,), (1,)), ((), ()))
SMEM = pl.BlockSpec(memory_space=pltpu.SMEM)
VMEM = pl.BlockSpec(memory_space=pltpu.VMEM)
ANY = pl.BlockSpec(memory_space=pl.ANY)


def lane_sums(values):
    ones = jnp.ones((8, LANES), jnp.bfloat16)
    high = values.astype(jnp.bfloat16)
    low = (values - high.astype(jnp.float32)).astype(jnp.bfloat16)
    return lax.dot_general(ones, high, NT, preferred_element_type=jnp.float32) + lax.dot_general(
        ones, low, NT, preferred_element_type=jnp.float32
    )


def block_sums(square, out_ref, count):
    batch = math.gcd(BATCH, count)

    def one_batch(c, carry):
        some = square[pl.ds(c * batch, batch)].reshape((batch * LANES, LANES))
        sums = lane_sums(some)
        for j in range(batch):
            out_ref[pl.ds(c * batch + j, 1), :] += sums[:1, j * LANES : (j + 1) * LANES]
        return carry

    lax.fori_loop(0, count // batch, one_batch, 0)


def params():
    return pltpu.CompilerParams(vmem_limit_bytes=VMEM_BYTES)


def pack_kernel(cuts, put_ref, row_ref, *refs):
    parts = len(cuts) - 1
    (*told_refs, x_ref), refs = refs[:5], refs[5:]
    outs = refs[:parts]
    coded, square, sums, words, notes, held, sems = refs[parts:]
    step = pl.program_id(0)
    tiles = x_ref.shape[0]
    devices = held.shape[0]
    blocks = square.shape[0]

    @pl.when(step == 0)
    def _():
        square[...] = jnp.zeros_like(square)

        def clear(d, carry):
            held[d] = 0
            return carry

        lax.fori_loop(0, devices, clear, 0)

    def some_tiles(i, carry):
        for j in range(QUAD):
            t = step * tiles + i * QUAD + j
            x = x_ref[i * QUAD + j]
            root = x * lax.rsqrt(x)
            code = (root * CODE_TOP + 0.5).astype(jnp.int32) - CODE_SHIFT
            put = put_ref[t]
            coded[pl.ds(pl.multiple_of(put * LANES, LANES), LANES), :] = code.astype(jnp.int16)
            square[row_ref[t]] += x * x
            owner = put // cuts[-1]
            held[owner] = jnp.maximum(held[owner], put % cuts[-1] + 1)
        return carry

    lax.fori_loop(0, tiles // QUAD, some_tiles, 0)

    def slots(q, d):
        some = pl.ds((d * cuts[-1] + cuts[q]) * LANES, (cuts[q + 1] - cuts[q]) * LANES)
        into = outs[q].at[d, pl.ds(0, (cuts[q + 1] - cuts[q]) * LANES)]
        return pltpu.make_async_copy(coded.at[some], into, sems.at[q * devices + d])

    def note(d):
        into = outs[0].at[d, pl.ds((cuts[1] - cuts[0]) * LANES, notes.shape[0])]
        return pltpu.make_async_copy(notes, into, sems.at[parts * devices + d])

    def each(what):
        for q in range(parts):
            for d in range(devices):
                pl.when(held[d] > cuts[q])(lambda q=q, d=d: what(slots(q, d)))

    @pl.when(step == pl.num_programs(0) - 1)
    def _():
        each(lambda copy: copy.start())
        sums[...] = jnp.zeros_like(sums)
        block_sums(square, sums, blocks)
        total = sums[...]
        level = (jnp.log2(jnp.maximum(total, 1e-30)) - LOG_MIDDLE) * LOG_STEPS
        level = jnp.where(total > 0.0, jnp.clip(level, -32700.0, 32700.0), -32768.0)
        level = (level + 32768.5).astype(jnp.int32) - 32768
        labels, owner, row, sub = [ref[...] for ref in told_refs]
        words[...] = jnp.zeros_like(words)
        words[:blocks, :] = level
        at = blocks
        for told in (labels, owner, row * TB_OWN + sub):
            words[at : at + told.shape[0], :] = told
            at += told.shape[0]
        notes[...] = words[...].astype(jnp.int16)
        for d in range(devices):
            note(d).start()
        each(lambda copy: copy.wait())
        for d in range(devices):
            note(d).wait()


def pack(tile_values, put, tile_row, told, devices, blocks, cuts):
    tiles = tile_values.shape[0]
    step = math.gcd(STEP_TILES, tiles)
    told = [x.reshape(-1, LANES) for x in told]
    noted = -(-(blocks + sum(x.shape[0] for x in told[:3])) // 16) * 16
    rows = [(high - low) * LANES for low, high in zip(cuts, cuts[1:])]
    rows[0] += noted
    return pl.pallas_call(
        functools.partial(pack_kernel, cuts),
        grid=(tiles // step,),
        in_specs=[SMEM, SMEM]
        + [pl.BlockSpec(x.shape, lambda i: (0, 0)) for x in told]
        + [pl.BlockSpec((step, LANES, LANES), lambda i: (i, 0, 0))],
        out_specs=[ANY] * len(rows),
        out_shape=[jax.ShapeDtypeStruct((devices, some, LANES), jnp.int16) for some in rows],
        scratch_shapes=[
            pltpu.VMEM((devices * cuts[-1] * LANES, LANES), jnp.int16),
            pltpu.VMEM((blocks, LANES, LANES), jnp.float32),
            pltpu.VMEM((blocks, LANES), jnp.float32),
            pltpu.VMEM((noted, LANES), jnp.int32),
            pltpu.VMEM((noted, LANES), jnp.int16),
            pltpu.SMEM((devices,), jnp.int32),
            pltpu.SemaphoreType.DMA(((len(rows) + 1) * devices,)),
        ],
        compiler_params=params(),
        cost_estimate=pl.CostEstimate(
            flops=8 * tile_values.size,
            bytes_accessed=6 * tile_values.size,
            transcendentals=tile_values.size,
        ),
        name="pack",
    )(put, tile_row, *told, tile_values)


def stage_kernel(q, bases, last, cached, fold_order, fold_bound, score_order, score_bound, meta,
                 place, done, mods, signed, before, x_hbm, *refs):
    base = bases[q]
    earlier, refs = refs[:q], refs[q:]
    (sums_in, squares_in, *made_in), refs = (refs[:4], refs[4:]) if q else ((None,) * 4, refs)
    part, sums_out, refs = refs[0], refs[1], refs[2:]
    (squares_out, *made_out, fresh_out), refs = ((None,) * 4, refs) if last else (refs[:4], refs[4:])
    spread, x, hot, sums, narrow, tiles, products, scores, squares, sems, sub_sems, tile_sems = refs
    devices, width = x.shape[0], x.shape[1] // LANES
    none = products.shape[0] - 1
    begin, end = done[q], done[q + 1]
    needed = [pltpu.make_async_copy(x_hbm.at[:, pl.ds(0, width * LANES)], x, sems.at[0])]
    if q:
        needed.append(pltpu.make_async_copy(made_in[0], spread, sems.at[1]))
    for copy in needed:
        copy.start()

    def columns(sub):
        return (slice(None), pl.ds(pl.multiple_of(sub * 2 * LANES, 2 * LANES), 2 * LANES))

    def sums_read(sub):
        return pltpu.make_async_copy(
            sums_in.at[columns(sub)], sums.at[columns(sub)], sub_sems.at[0, sub]
        )

    def sums_write(sub):
        return pltpu.make_async_copy(
            sums.at[columns(sub)], sums_out.at[columns(sub)], sub_sems.at[1, sub]
        )

    def each_sub(low, high, what):
        def one(sub, carry):
            what(sub)
            return carry

        lax.fori_loop(low, high, one, 0)

    if q:
        each_sub(begin, TB_OWN, lambda sub: sums_read(sub).start())
        squares[...] = squares_in[...]
    else:
        sums[...] = jnp.zeros_like(sums)
        squares[...] = jnp.zeros_like(squares)
    later = [pltpu.make_async_copy(made_in[1], hot, sems.at[3])] if q and cached else []
    for e, e_hbm in enumerate(earlier):
        held = tiles.at[pl.ds(bases[e], e_hbm.shape[0])]
        later.append(pltpu.make_async_copy(e_hbm, held, tile_sems.at[e]))
    for copy in later:
        copy.start()
    products[...] = jnp.zeros_like(products)
    scores[...] = before[...]
    cluster = lax.broadcasted_iota(jnp.int32, (HALF, LANES), 0)
    lane = lax.broadcasted_iota(jnp.int32, (LANES, LANES), 1)

    def column(ref, row):
        return jnp.transpose(jnp.broadcast_to(ref[pl.ds(row, 1), :], (LANES, LANES)))

    def one_hot(row):
        own = column(mods, row).astype(jnp.int32)
        some = [jnp.where(own == lane + g, 1.0, 0.0) for g in range(0, HALF, LANES)]
        return jnp.concatenate(some, axis=1).astype(jnp.bfloat16)

    batch = math.gcd(none + 1, 3)

    def build(c, carry):
        for j in range(batch):
            spread[c * batch + j] = column(signed, c * batch + j)
            if cached:
                hot[c * batch + j] = one_hot(c * batch + j)
        return carry

    if not q:
        lax.fori_loop(0, (none + 1) // batch, build, 0)
    for copy in needed:
        copy.wait()

    def eight(order, start, end, p):
        rows, spots = [], []
        for j in range(EIGHT):
            at = start + EIGHT * p + j
            slot = order[jnp.where(at < end, at, start)]
            rows.append((meta[slot] // TB_OWN, at < end))
            spots.append(place[slot])
        return rows, spots

    def fold_sub(sub):
        start = fold_bound[q * (TB_OWN + 1) + sub]
        end = fold_bound[q * (TB_OWN + 1) + sub + 1]
        if q:
            sums_read(sub).wait()

        def one_eight(p, carry):
            rows, spots = eight(fold_order, start, end, p)
            folded, picks = [], []
            for (row, held), spot in zip(rows, spots):
                source, slot = (spot - base) // width, (spot - base) % width
                raw = x[source, pl.ds(pl.multiple_of(slot * LANES, LANES), LANES), :]
                root = raw.astype(jnp.int32).astype(jnp.float32) + float(CODE_SHIFT)
                scale = spread[row]
                tile = root * root * jnp.abs(scale)
                tiles[spot] = tile.astype(jnp.bfloat16)
                halves = [jnp.where(scale > 0.0, tile, 0.0), jnp.where(scale < 0.0, tile, 0.0)]
                folded.append(jnp.concatenate(halves, axis=1).astype(jnp.bfloat16))
                own = mods[pl.ds(jnp.where(held, row, none), 1), :].astype(jnp.int32)
                picks.append(jnp.where(cluster == own, 1.0, 0.0).astype(jnp.bfloat16))
            pick = jnp.concatenate(picks, axis=1)
            sums[columns(sub)] += jnp.dot(
                pick, jnp.concatenate(folded, axis=0), preferred_element_type=jnp.float32
            )
            return carry

        lax.fori_loop(0, (end - start + EIGHT - 1) // EIGHT, one_eight, 0)
        sums_write(sub).start()

    each_sub(begin, TB_OWN, fold_sub)
    kept = []
    if not last:
        fresh = tiles.at[pl.ds(base, devices * width)]
        kept.append(pltpu.make_async_copy(fresh, fresh_out, sems.at[2]))
        kept.append(pltpu.make_async_copy(spread, made_out[0], sems.at[4]))
        kept.append(pltpu.make_async_copy(hot, made_out[1], sems.at[5]))
    for copy in kept:
        copy.start()
    for copy in later:
        copy.wait()

    def score_sub(sub):
        start, end = score_bound[sub], score_bound[sub + 1]
        some = sums[columns(sub)]
        narrow[...] = some.astype(jnp.bfloat16)
        squares[...] += some * some

        def one_eight(p, carry):
            rows, spots = eight(score_order, start, end, p)
            rows = [jnp.where(held, row, none) for row, held in rows]
            hots = [hot[row] if cached else one_hot(row) for row in rows]
            chosen = jnp.dot(
                jnp.concatenate(hots, axis=0), narrow[...], preferred_element_type=jnp.float32
            )
            for j in range(EIGHT):
                both = chosen[j * LANES : (j + 1) * LANES]
                own = jnp.where(spread[rows[j]] < 0.0, both[:, LANES:], both[:, :LANES])
                products[rows[j]] += own * tiles[spots[j]].astype(jnp.float32)
            return carry

        lax.fori_loop(0, (end - start + EIGHT - 1) // EIGHT, one_eight, 0)

    each_sub(begin, end, score_sub)
    block_sums(products, scores, none)
    if last:
        own = none // devices
        square = [lane_sums(squares[:, h : h + LANES])[:1] for h in (0, LANES)]
        square = jnp.concatenate(square, axis=1)
        for d in range(devices):
            part[d, :, part.shape[2] - K :] = square
            for b in range(own):
                at = d * own + b
                part[d, :, b * LANES : (b + 1) * LANES] = scores[at : at + 1, :]
    else:
        part[...] = scores[...]
        squares_out[...] = squares[...]
    for copy in kept:
        copy.wait()
    each_sub(begin, TB_OWN, lambda sub: sums_write(sub).wait())


def stage(q, cuts, scalars, mods, signed, before, x, normed, totals):
    devices = x.shape[0]
    last = q == len(cuts) - 2
    blocks = before.shape[0]
    cached = blocks <= CACHED_BLOCKS
    width = cuts[q + 1] - cuts[q]
    home = blocks // devices * LANES
    wide = jax.ShapeDtypeStruct((HALF, TB_OWN * 2 * LANES), jnp.float32)
    square = jax.ShapeDtypeStruct((HALF, 2 * LANES), jnp.float32)
    if last:
        out_shape = [jax.ShapeDtypeStruct((devices, 1, home + K), jnp.float32), wide]
    else:
        out_shape = [
            jax.ShapeDtypeStruct((blocks, LANES), jnp.float32),
            wide,
            square,
            jax.ShapeDtypeStruct((blocks + 1, LANES, LANES), jnp.float32),
            jax.ShapeDtypeStruct((blocks + 1 if cached else 1, LANES, HALF), jnp.bfloat16),
            jax.ShapeDtypeStruct((devices * width, LANES, LANES), jnp.bfloat16),
        ]
    slots = devices * cuts[-1]
    operands = [*scalars, mods, signed, before, x, *normed, *totals]
    return pl.pallas_call(
        functools.partial(stage_kernel, q, [devices * cut for cut in cuts], last, cached),
        in_specs=[SMEM] * len(scalars) + [VMEM] * 3 + [ANY] * (1 + q) + [ANY, VMEM, ANY, ANY][: len(totals)],
        out_specs=[VMEM, ANY, VMEM, ANY, ANY, ANY][: len(out_shape)],
        out_shape=out_shape,
        input_output_aliases={len(operands) - len(totals): 1} if q else {},
        scratch_shapes=[
            pltpu.VMEM((blocks + 1, LANES, LANES), jnp.float32),
            pltpu.VMEM((devices, width * LANES, LANES), jnp.int16),
            pltpu.VMEM((blocks + 1 if cached else 1, LANES, HALF), jnp.bfloat16),
            pltpu.VMEM(wide.shape, jnp.float32),
            pltpu.VMEM(square.shape, jnp.bfloat16),
            pltpu.VMEM((slots, LANES, LANES), jnp.bfloat16),
            pltpu.VMEM((blocks + 1, LANES, LANES), jnp.float32),
            pltpu.VMEM((blocks, LANES), jnp.float32),
            pltpu.VMEM(square.shape, jnp.float32),
            pltpu.SemaphoreType.DMA((6,)),
            pltpu.SemaphoreType.DMA((2, TB_OWN)),
            pltpu.SemaphoreType.DMA((len(cuts),)),
        ],
        compiler_params=params(),
        cost_estimate=pl.CostEstimate(
            flops=devices * width * LANES * LANES * K * 8,
            bytes_accessed=4 * devices * width * LANES * LANES + 8 * K * TB_OWN * LANES,
            transcendentals=0,
        ),
        name="stage",
    )(*operands)


def close_kernel(root, groups, labels_ref, got_ref, sums_hbm, out_hbm, similarity, sums, out, sems):
    width = TB_OWN // groups
    reads, writes = [], []
    for g in range(groups):
        some = (slice(None), pl.ds(g * width * 2 * LANES, width * 2 * LANES))
        reads.append(pltpu.make_async_copy(sums_hbm.at[some], sums.at[some], sems.at[0, g]))
        some = (slice(None), pl.ds(g * width * LANES, width * LANES))
        writes.append(pltpu.make_async_copy(out.at[some], out_hbm.at[some], sems.at[1, g]))
        reads[g].start()
    total = jnp.sum(got_ref[...], axis=0)
    home = total.shape[1] - K
    own = lax.rsqrt(total[:, home:] + EPSILON)
    columns = [
        jnp.transpose(jnp.broadcast_to(own[:, k : k + LANES], (LANES, LANES)))
        for k in range(0, K, LANES)
    ]
    cluster = lax.broadcasted_iota(jnp.int32, (LANES, LANES), 0)
    for b in range(home // LANES):
        found = jnp.zeros((LANES, LANES), jnp.float32)
        for i, column in enumerate(columns):
            found += jnp.where(cluster + i * LANES == labels_ref[b : b + 1, :], column, 0.0)
        found = jnp.sum(found, axis=0, keepdims=True)
        similarity[b : b + 1, :] = total[:, b * LANES : (b + 1) * LANES] * found
    for g in range(groups):
        reads[g].wait()
        for sub in range(g * width, (g + 1) * width):
            for i, column in enumerate(columns):
                half, row = divmod(i * LANES, HALF)
                at = (2 * sub + half) * LANES
                some = sums[row : row + LANES, at : at + LANES]
                done = (some * column * root).astype(jnp.bfloat16)
                out[i * LANES : (i + 1) * LANES, sub * LANES : (sub + 1) * LANES] = done
        writes[g].start()
    for write in writes:
        write.wait()


def close(labels, got, sums, vocab_size):
    groups = 4
    labels = labels.reshape(-1, LANES)
    wide = jax.ShapeDtypeStruct((K, TB_OWN * LANES), jnp.bfloat16)
    centroids, similarity = pl.pallas_call(
        functools.partial(close_kernel, math.sqrt(vocab_size), groups),
        in_specs=[VMEM, VMEM, ANY],
        out_specs=[ANY, VMEM],
        out_shape=[wide, jax.ShapeDtypeStruct(labels.shape, jnp.float32)],
        scratch_shapes=[
            pltpu.VMEM(sums.shape, jnp.float32),
            pltpu.VMEM(wide.shape, jnp.bfloat16),
            pltpu.SemaphoreType.DMA((2, groups)),
        ],
        compiler_params=params(),
        cost_estimate=pl.CostEstimate(
            flops=2 * sums.size, bytes_accessed=6 * sums.size, transcendentals=0
        ),
        name="close",
    )(labels, got, sums)
    return centroids, similarity.reshape(-1)


def exchange(x):
    return lax.all_to_all(x, "dp", split_axis=0, concat_axis=0, tiled=True)


def after(value, *others):
    return lax.optimization_barrier((value, *others))[0]


def sorted_slots(key, top):
    slots = jnp.arange(key.shape[0], dtype=jnp.int32)
    ahead = (key[None, :] < key[:, None]) | (
        (key[None, :] == key[:, None]) & (slots[None, :] < slots[:, None])
    )
    position = jnp.sum(ahead.astype(jnp.int32), axis=1)
    here = position[None, :] == slots[:, None]
    order = jnp.sum(jnp.where(here, slots[None, :], 0), axis=1)
    levels = jnp.arange(top + 1, dtype=jnp.int32)
    bounds = jnp.sum((key[None, :] < levels[:, None]).astype(jnp.int32), axis=1)
    return order, bounds


def ranks(group, sub):
    index = jnp.arange(sub.shape[-1], dtype=jnp.int32)
    before = (sub[..., None, :] < sub[..., :, None]) | (
        (sub[..., None, :] == sub[..., :, None]) & (index[None, :] < index[:, None])
    )
    same = group[..., None, :] == group[..., :, None]
    return jnp.sum((before & same).astype(jnp.int32), axis=-1)


def shards(tile_values, tile_row, tile_owner, tile_sub, labels):
    devices = lax.axis_size("dp")
    tiles = tile_values.shape[0]
    home = labels.shape[0]
    blocks = home // LANES * devices
    cap = max(2, 2 * tiles // devices)
    cuts = tuple(sorted({int(cap * share) for share in PARTS})) if cap >= 8 else (0, cap)
    parts = len(cuts) - 1
    here = lax.axis_index("dp").astype(jnp.int32)
    owner = tile_owner[:, 0]

    put = owner * cap + ranks(owner, tile_sub)
    told = (labels, owner, tile_row, tile_sub)
    outgoing = pack(tile_values, put, tile_row, told, devices, blocks, cuts)
    incoming = [exchange(outgoing[0])]
    heard = incoming[0][:, (cuts[1] - cuts[0]) * LANES :].astype(jnp.int32)
    level = heard[:, :blocks]
    partial_sq = jnp.exp2(level.astype(jnp.float32) * (1.0 / LOG_STEPS) + LOG_MIDDLE)
    row_sq = jnp.sum(jnp.where(level > -32768, partial_sq, 0.0), axis=0)
    all_described = heard[:, blocks:].reshape(devices, -1)
    all_labels = all_described[:, :home].reshape(blocks, LANES)
    mine = all_described[:, home : home + tiles] == here
    code = all_described[:, home + tiles : home + 2 * tiles]
    rank = ranks(mine.astype(jnp.int32), code % TB_OWN)
    chosen = mine[:, None, :] & (rank[:, None, :] == jnp.arange(cap)[None, :, None])
    meta = jnp.sum(jnp.where(chosen, code[:, None, :] + 1, 0), axis=2).reshape(-1) - 1
    sub = jnp.where(meta < 0, TB_OWN, meta % TB_OWN)
    slot_rank = np.arange(devices * cap) % cap
    slot_part = np.searchsorted(np.array(cuts), slot_rank, side="right") - 1
    low, high = np.array(cuts)[slot_part], np.array(cuts)[slot_part + 1]
    place = devices * low + np.arange(devices * cap) // cap * (high - low) + slot_rank - low
    fold_key = jnp.asarray(slot_part * (TB_OWN + 1), jnp.int32) + sub
    fold_order, fold_bounds = sorted_slots(fold_key, parts * (TB_OWN + 1))
    score_order, score_bounds = sorted_slots(sub, TB_OWN)
    left = np.arange(parts)[:, None] < slot_part[None, :]
    done = jnp.min(jnp.where(left, sub[None, :], TB_OWN), axis=1)
    done = jnp.concatenate([jnp.zeros((1,), jnp.int32), done])
    scalars = [
        fold_order, fold_bounds, score_order, score_bounds, meta, jnp.asarray(place, jnp.int32), done
    ]

    scale = lax.rsqrt(row_sq + EPSILON) * (1.0 / CODE_TOP**2)
    signed = jnp.pad(jnp.where(all_labels < HALF, scale, -scale), ((0, 1), (0, 0)))
    mods = (all_labels % HALF).astype(jnp.float32)
    mods = jnp.pad(mods, ((0, 1), (0, 0)), constant_values=-1.0)
    partial, totals, normed = jnp.zeros((blocks, LANES), jnp.float32), (), []
    beside = (*scalars, mods, signed)
    for q in range(parts):
        if q + 1 < parts:
            ahead = (incoming[q], *beside) if q else (incoming[q],)
            incoming.append(exchange(after(outgoing[q + 1], *ahead)))
        partial, sums, *more = stage(
            q, cuts, scalars, mods, signed, partial, incoming[q], normed, totals
        )
        beside = (partial, sums)
        totals, normed = (sums, *more[:3]), normed + more[3:]
    return close(labels, exchange(partial), sums, TB_OWN * LANES * devices)


def solution(mesh):
    return jax.shard_map(
        shards,
        mesh=mesh,
        in_specs=(
            P(("groups", "dp"), None, None),
            P(("groups", "dp")),
            P(("groups", "dp"), None),
            P(("groups", "dp")),
            P(("groups", "dp")),
        ),
        out_specs=(P("groups", "dp"), P(("groups", "dp"))),
        check_vma=False,
    )
```

```python
import functools
import math

import jax
import jax.numpy as jnp
import numpy as np
from jax import lax
from jax.experimental import pallas as pl
from jax.experimental.pallas import tpu as pltpu
from jax.sharding import PartitionSpec as P

K = 512
HALF = K // 2
TB_OWN = 16
LANES = 128
EPSILON = 1e-06
CODE_TOP = 65535.0
CODE_SHIFT = 32768
VMEM_BYTES = 60 * 1024 * 1024
STEP_TILES = 16
PARTS = (0.0, 13 / 16, 1.0)
LOG_STEPS = 1800.0
LOG_MIDDLE = -3.0
CACHED_BLOCKS = 64
QUAD = 4
PAIR = 2
EIGHT = 8
BATCH = 8
NT = (((1,), (1,)), ((), ()))
SMEM = pl.BlockSpec(memory_space=pltpu.SMEM)
VMEM = pl.BlockSpec(memory_space=pltpu.VMEM)
ANY = pl.BlockSpec(memory_space=pl.ANY)


def lane_sums(values):
    ones = jnp.ones((8, LANES), jnp.bfloat16)
    high = values.astype(jnp.bfloat16)
    low = (values - high.astype(jnp.float32)).astype(jnp.bfloat16)
    return lax.dot_general(ones, high, NT, preferred_element_type=jnp.float32) + lax.dot_general(
        ones, low, NT, preferred_element_type=jnp.float32
    )


def block_sums(square, out_ref, count):
    batch = math.gcd(BATCH, count)

    def one_batch(c, carry):
        some = square[pl.ds(c * batch, batch)].reshape((batch * LANES, LANES))
        sums = lane_sums(some)
        for j in range(batch):
            out_ref[pl.ds(c * batch + j, 1), :] += sums[:1, j * LANES : (j + 1) * LANES]
        return carry

    lax.fori_loop(0, count // batch, one_batch, 0)


def params():
    return pltpu.CompilerParams(vmem_limit_bytes=VMEM_BYTES)


def pack_kernel(cuts, owner_ref, rank_ref, row_ref, *refs):
    parts = len(cuts) - 1
    (*told_refs, x_hbm), refs = refs[:5], refs[5:]
    outs = refs[:parts]
    x, coded, square, sums, words, notes, held, tile_at, sems, x_sems = refs[parts:]
    tiles = x.shape[0]
    devices = held.shape[0]
    blocks = square.shape[0]
    step = math.gcd(STEP_TILES, tiles)
    reads = [
        pltpu.make_async_copy(x_hbm.at[pl.ds(i, step)], x.at[pl.ds(i, step)], x_sems.at[i // step])
        for i in range(0, tiles, step)
    ]
    for read in reads:
        read.start()

    def clear(d, carry):
        held[d] = 0
        return carry

    def list_tile(t, carry):
        owner, rank = owner_ref[t], rank_ref[t]
        tile_at[owner * cuts[-1] + rank] = t
        held[owner] = jnp.maximum(held[owner], rank + 1)
        return carry

    lax.fori_loop(0, devices, clear, 0)
    lax.fori_loop(0, tiles, list_tile, 0)
    square[...] = jnp.zeros_like(square)
    for i, read in enumerate(reads):
        read.wait()

        def some_squares(c, carry, first=i * step):
            for j in range(QUAD):
                t = first + c * QUAD + j
                square[row_ref[t]] += x[t] * x[t]
            return carry

        lax.fori_loop(0, step // QUAD, some_squares, 0)

    def slots(q, d):
        some = pl.ds((d * cuts[-1] + cuts[q]) * LANES, (cuts[q + 1] - cuts[q]) * LANES)
        into = outs[q].at[d, pl.ds(0, (cuts[q + 1] - cuts[q]) * LANES)]
        return pltpu.make_async_copy(coded.at[some], into, sems.at[q, d])

    def note(d):
        into = outs[0].at[d, pl.ds((cuts[1] - cuts[0]) * LANES, notes.shape[0])]
        return pltpu.make_async_copy(notes, into, sems.at[parts, d])

    def one_owner(d, carry):
        count = held[d]

        def some_codes(c, carry):
            for j in range(PAIR):
                slot = d * cuts[-1] + jnp.minimum(c * PAIR + j, count - 1)
                some = x[tile_at[slot]]
                root = some * lax.rsqrt(some)
                code = (root * CODE_TOP + 0.5).astype(jnp.int32) - CODE_SHIFT
                at = pl.ds(pl.multiple_of(slot * LANES, LANES), LANES)
                coded[at, :] = code.astype(jnp.int16)
            return carry

        lax.fori_loop(0, (count + PAIR - 1) // PAIR, some_codes, 0)
        for q in range(parts):
            pl.when(count > cuts[q])(lambda q=q: slots(q, d).start())
        return carry

    lax.fori_loop(0, devices, one_owner, 0)
    sums[...] = jnp.zeros_like(sums)
    block_sums(square, sums, blocks)
    total = sums[...]
    level = (jnp.log2(jnp.maximum(total, 1e-30)) - LOG_MIDDLE) * LOG_STEPS
    level = jnp.where(total > 0.0, jnp.clip(level, -32700.0, 32700.0), -32768.0)
    level = (level + 32768.5).astype(jnp.int32) - 32768
    labels, owner, row, sub = [ref[...] for ref in told_refs]
    words[...] = jnp.zeros_like(words)
    words[:blocks, :] = level
    at = blocks
    for told in (labels, owner, row * TB_OWN + sub):
        words[at : at + told.shape[0], :] = told
        at += told.shape[0]
    notes[...] = words[...].astype(jnp.int16)

    def finish(d, carry):
        for q in range(parts):
            pl.when(held[d] > cuts[q])(lambda q=q: slots(q, d).wait())
        return carry

    for d in range(devices):
        note(d).start()
    lax.fori_loop(0, devices, finish, 0)
    for d in range(devices):
        note(d).wait()


def pack(tile_values, owner, rank, tile_row, told, devices, blocks, cuts):
    tiles = tile_values.shape[0]
    told = [x.reshape(-1, LANES) for x in told]
    noted = -(-(blocks + sum(x.shape[0] for x in told[:3])) // 16) * 16
    rows = [(high - low) * LANES for low, high in zip(cuts, cuts[1:])]
    rows[0] += noted
    return pl.pallas_call(
        functools.partial(pack_kernel, cuts),
        in_specs=[SMEM] * 3 + [VMEM] * 4 + [ANY],
        out_specs=[ANY] * len(rows),
        out_shape=[jax.ShapeDtypeStruct((devices, some, LANES), jnp.int16) for some in rows],
        scratch_shapes=[
            pltpu.VMEM(tile_values.shape, jnp.float32),
            pltpu.VMEM((devices * cuts[-1] * LANES, LANES), jnp.int16),
            pltpu.VMEM((blocks, LANES, LANES), jnp.float32),
            pltpu.VMEM((blocks, LANES), jnp.float32),
            pltpu.VMEM((noted, LANES), jnp.int32),
            pltpu.VMEM((noted, LANES), jnp.int16),
            pltpu.SMEM((devices,), jnp.int32),
            pltpu.SMEM((devices * cuts[-1],), jnp.int32),
            pltpu.SemaphoreType.DMA((len(rows) + 1, devices)),
            pltpu.SemaphoreType.DMA((tiles,)),
        ],
        compiler_params=params(),
        cost_estimate=pl.CostEstimate(
            flops=8 * tile_values.size,
            bytes_accessed=6 * tile_values.size,
            transcendentals=tile_values.size,
        ),
        name="pack",
    )(owner, rank, tile_row, *told, tile_values)


def stage_kernel(q, bases, last, cached, fold_order, fold_bound, score_order, score_bound, meta,
                 place, done, mods_in, signed_in, x_hbm, *refs):
    base = bases[q]
    earlier, refs = refs[:q], refs[q:]
    before, sums_in, squares_in, *made_in = refs[:5] if q else (None,) * 5
    refs = refs[5:] if q else refs
    part, sums_out, refs = refs[0], refs[1], refs[2:]
    (squares_out, *made_out, fresh_out), refs = ((None,) * 4, refs) if last else (refs[:4], refs[4:])
    spread, x, hot, sums, narrow, tiles, products, scores, squares, mods, signed, *refs = refs
    sems, sub_sems, tile_sems = refs
    devices, width = x.shape[0], x.shape[1] // LANES
    none = products.shape[0] - 1
    begin, end = done[q - 1] if q else 0, done[q]
    needed = [pltpu.make_async_copy(x_hbm.at[:, pl.ds(0, width * LANES)], x, sems.at[0])]
    if q:
        needed.append(pltpu.make_async_copy(made_in[0], spread, sems.at[1]))
    for copy in needed:
        copy.start()

    def columns(sub):
        return (slice(None), pl.ds(pl.multiple_of(sub * 2 * LANES, 2 * LANES), 2 * LANES))

    def sums_read(sub):
        return pltpu.make_async_copy(
            sums_in.at[columns(sub)], sums.at[columns(sub)], sub_sems.at[0, sub]
        )

    def sums_write(sub):
        return pltpu.make_async_copy(
            sums.at[columns(sub)], sums_out.at[columns(sub)], sub_sems.at[1, sub]
        )

    def each_sub(low, high, what):
        def one(sub, carry):
            what(sub)
            return carry

        lax.fori_loop(low, high, one, 0)

    if q:
        each_sub(begin, TB_OWN, lambda sub: sums_read(sub).start())
        squares[...] = squares_in[...]
    else:
        sums[...] = jnp.zeros_like(sums)
        squares[...] = jnp.zeros_like(squares)
    later = [pltpu.make_async_copy(made_in[1], hot, sems.at[3])] if q and cached else []
    for e, e_hbm in enumerate(earlier):
        held = tiles.at[pl.ds(bases[e], e_hbm.shape[0])]
        later.append(pltpu.make_async_copy(e_hbm, held, tile_sems.at[e]))
    for copy in later:
        copy.start()
    products[...] = jnp.zeros_like(products)
    scores[...] = before[...] if q else jnp.zeros_like(scores)
    for held, given, empty in ((mods, mods_in, -1.0), (signed, signed_in, 0.0)):
        held[:none, :] = given[...]
        held[none : none + 1, :] = jnp.full((1, LANES), empty, jnp.float32)
    cluster = lax.broadcasted_iota(jnp.int32, (HALF, LANES), 0)
    lane = lax.broadcasted_iota(jnp.int32, (LANES, LANES), 1)

    def column(ref, row):
        return jnp.transpose(jnp.broadcast_to(ref[pl.ds(row, 1), :], (LANES, LANES)))

    def one_hot(row):
        own = column(mods, row).astype(jnp.int32)
        some = [jnp.where(own == lane + g, 1.0, 0.0) for g in range(0, HALF, LANES)]
        return jnp.concatenate(some, axis=1).astype(jnp.bfloat16)

    batch = math.gcd(none + 1, 3)

    def build(c, carry):
        for j in range(batch):
            spread[c * batch + j] = column(signed, c * batch + j)
            if cached:
                hot[c * batch + j] = one_hot(c * batch + j)
        return carry

    if not q:
        lax.fori_loop(0, (none + 1) // batch, build, 0)
    for copy in needed:
        copy.wait()

    def eight(order, start, end, p):
        rows, spots = [], []
        for j in range(EIGHT):
            at = start + EIGHT * p + j
            slot = order[jnp.where(at < end, at, start)]
            rows.append((meta[slot] // TB_OWN, at < end))
            spots.append(place[slot])
        return rows, spots

    def fold_sub(sub):
        start = fold_bound[q * (TB_OWN + 1) + sub]
        end = fold_bound[q * (TB_OWN + 1) + sub + 1]
        if q:
            sums_read(sub).wait()

        def one_eight(p, carry):
            rows, spots = eight(fold_order, start, end, p)
            folded, picks = [], []
            for (row, held), spot in zip(rows, spots):
                source, slot = (spot - base) // width, (spot - base) % width
                raw = x[source, pl.ds(pl.multiple_of(slot * LANES, LANES), LANES), :]
                root = raw.astype(jnp.int32).astype(jnp.float32) + float(CODE_SHIFT)
                scale = spread[row]
                tile = root * root * jnp.abs(scale)
                tiles[spot] = tile.astype(jnp.bfloat16)
                halves = [jnp.where(scale > 0.0, tile, 0.0), jnp.where(scale < 0.0, tile, 0.0)]
                folded.append(jnp.concatenate(halves, axis=1).astype(jnp.bfloat16))
                own = mods[pl.ds(jnp.where(held, row, none), 1), :].astype(jnp.int32)
                picks.append(jnp.where(cluster == own, 1.0, 0.0).astype(jnp.bfloat16))
            pick = jnp.concatenate(picks, axis=1)
            sums[columns(sub)] += jnp.dot(
                pick, jnp.concatenate(folded, axis=0), preferred_element_type=jnp.float32
            )
            return carry

        lax.fori_loop(0, (end - start + EIGHT - 1) // EIGHT, one_eight, 0)
        sums_write(sub).start()

    each_sub(begin, TB_OWN, fold_sub)
    kept = []
    if not last:
        fresh = tiles.at[pl.ds(base, devices * width)]
        kept.append(pltpu.make_async_copy(fresh, fresh_out, sems.at[2]))
        kept.append(pltpu.make_async_copy(spread, made_out[0], sems.at[4]))
        kept.append(pltpu.make_async_copy(hot, made_out[1], sems.at[5]))
    for copy in kept:
        copy.start()
    for copy in later:
        copy.wait()

    def score_sub(sub):
        start, end = score_bound[sub], score_bound[sub + 1]
        some = sums[columns(sub)]
        narrow[...] = some.astype(jnp.bfloat16)
        squares[...] += some * some

        def one_eight(p, carry):
            rows, spots = eight(score_order, start, end, p)
            rows = [jnp.where(held, row, none) for row, held in rows]
            hots = [hot[row] if cached else one_hot(row) for row in rows]
            chosen = jnp.dot(
                jnp.concatenate(hots, axis=0), narrow[...], preferred_element_type=jnp.float32
            )
            for j in range(EIGHT):
                both = chosen[j * LANES : (j + 1) * LANES]
                own = jnp.where(spread[rows[j]] < 0.0, both[:, LANES:], both[:, :LANES])
                products[rows[j]] += own * tiles[spots[j]].astype(jnp.float32)
            return carry

        lax.fori_loop(0, (end - start + EIGHT - 1) // EIGHT, one_eight, 0)

    each_sub(begin, end, score_sub)
    block_sums(products, scores, none)
    if last:
        own = none // devices
        square = [lane_sums(squares[:, h : h + LANES])[:1] for h in (0, LANES)]
        square = jnp.concatenate(square, axis=1)
        for d in range(devices):
            part[d, :, part.shape[2] - K :] = square
            for b in range(own):
                at = d * own + b
                part[d, :, b * LANES : (b + 1) * LANES] = scores[at : at + 1, :]
    else:
        part[...] = scores[...]
        squares_out[...] = squares[...]
    for copy in kept:
        copy.wait()
    each_sub(begin, TB_OWN, lambda sub: sums_write(sub).wait())


def stage(q, cuts, scalars, mods, signed, x, normed, totals):
    devices = x.shape[0]
    last = q == len(cuts) - 2
    blocks = mods.shape[0]
    cached = blocks <= CACHED_BLOCKS
    width = cuts[q + 1] - cuts[q]
    home = blocks // devices * LANES
    wide = jax.ShapeDtypeStruct((HALF, TB_OWN * 2 * LANES), jnp.float32)
    square = jax.ShapeDtypeStruct((HALF, 2 * LANES), jnp.float32)
    if last:
        out_shape = [jax.ShapeDtypeStruct((devices, 1, home + K), jnp.float32), wide]
    else:
        out_shape = [
            jax.ShapeDtypeStruct((blocks, LANES), jnp.float32),
            wide,
            square,
            jax.ShapeDtypeStruct((blocks + 1, LANES, LANES), jnp.float32),
            jax.ShapeDtypeStruct((blocks + 1 if cached else 1, LANES, HALF), jnp.bfloat16),
            jax.ShapeDtypeStruct((devices * width, LANES, LANES), jnp.bfloat16),
        ]
    slots = devices * cuts[-1]
    operands = [*scalars, mods, signed, x, *normed, *totals]
    return pl.pallas_call(
        functools.partial(stage_kernel, q, [devices * cut for cut in cuts], last, cached),
        in_specs=[SMEM] * len(scalars) + [VMEM] * 2 + [ANY] * (1 + q) + [VMEM, ANY, VMEM, ANY, ANY][: len(totals)],
        out_specs=[VMEM, ANY, VMEM, ANY, ANY, ANY][: len(out_shape)],
        out_shape=out_shape,
        input_output_aliases={len(operands) - len(totals) + 1: 1} if q else {},
        scratch_shapes=[
            pltpu.VMEM((blocks + 1, LANES, LANES), jnp.float32),
            pltpu.VMEM((devices, width * LANES, LANES), jnp.int16),
            pltpu.VMEM((blocks + 1 if cached else 1, LANES, HALF), jnp.bfloat16),
            pltpu.VMEM(wide.shape, jnp.float32),
            pltpu.VMEM(square.shape, jnp.bfloat16),
            pltpu.VMEM((slots, LANES, LANES), jnp.bfloat16),
            pltpu.VMEM((blocks + 1, LANES, LANES), jnp.float32),
            pltpu.VMEM((blocks, LANES), jnp.float32),
            pltpu.VMEM(square.shape, jnp.float32),
            pltpu.VMEM((blocks + 1, LANES), jnp.float32),
            pltpu.VMEM((blocks + 1, LANES), jnp.float32),
            pltpu.SemaphoreType.DMA((6,)),
            pltpu.SemaphoreType.DMA((2, TB_OWN)),
            pltpu.SemaphoreType.DMA((len(cuts),)),
        ],
        compiler_params=params(),
        cost_estimate=pl.CostEstimate(
            flops=devices * width * LANES * LANES * K * 8,
            bytes_accessed=4 * devices * width * LANES * LANES + 8 * K * TB_OWN * LANES,
            transcendentals=0,
        ),
        name="stage",
    )(*operands)


def close_kernel(root, groups, labels_ref, got_ref, sums_hbm, out_hbm, similarity, sums, out, sems):
    width = TB_OWN // groups
    reads, writes = [], []
    for g in range(groups):
        some = (slice(None), pl.ds(g * width * 2 * LANES, width * 2 * LANES))
        reads.append(pltpu.make_async_copy(sums_hbm.at[some], sums.at[some], sems.at[0, g]))
        some = (slice(None), pl.ds(g * width * LANES, width * LANES))
        writes.append(pltpu.make_async_copy(out.at[some], out_hbm.at[some], sems.at[1, g]))
        reads[g].start()
    total = jnp.sum(got_ref[...], axis=0)
    home = total.shape[1] - K
    own = lax.rsqrt(total[:, home:] + EPSILON)
    columns = [
        jnp.transpose(jnp.broadcast_to(own[:, k : k + LANES], (LANES, LANES)))
        for k in range(0, K, LANES)
    ]
    cluster = lax.broadcasted_iota(jnp.int32, (LANES, LANES), 0)
    for b in range(home // LANES):
        found = jnp.zeros((LANES, LANES), jnp.float32)
        for i, column in enumerate(columns):
            found += jnp.where(cluster + i * LANES == labels_ref[b : b + 1, :], column, 0.0)
        found = jnp.sum(found, axis=0, keepdims=True)
        similarity[b : b + 1, :] = total[:, b * LANES : (b + 1) * LANES] * found
    for g in range(groups):
        reads[g].wait()
        for sub in range(g * width, (g + 1) * width):
            for i, column in enumerate(columns):
                half, row = divmod(i * LANES, HALF)
                at = (2 * sub + half) * LANES
                some = sums[row : row + LANES, at : at + LANES]
                done = (some * column * root).astype(jnp.bfloat16)
                out[i * LANES : (i + 1) * LANES, sub * LANES : (sub + 1) * LANES] = done
        writes[g].start()
    for write in writes:
        write.wait()


def close(labels, got, sums, vocab_size):
    groups = 4
    labels = labels.reshape(-1, LANES)
    wide = jax.ShapeDtypeStruct((K, TB_OWN * LANES), jnp.bfloat16)
    centroids, similarity = pl.pallas_call(
        functools.partial(close_kernel, math.sqrt(vocab_size), groups),
        in_specs=[VMEM, VMEM, ANY],
        out_specs=[ANY, VMEM],
        out_shape=[wide, jax.ShapeDtypeStruct(labels.shape, jnp.float32)],
        scratch_shapes=[
            pltpu.VMEM(sums.shape, jnp.float32),
            pltpu.VMEM(wide.shape, jnp.bfloat16),
            pltpu.SemaphoreType.DMA((2, groups)),
        ],
        compiler_params=params(),
        cost_estimate=pl.CostEstimate(
            flops=2 * sums.size, bytes_accessed=6 * sums.size, transcendentals=0
        ),
        name="close",
    )(labels, got, sums)
    return centroids, similarity.reshape(-1)


def exchange(x):
    return lax.all_to_all(x, "dp", split_axis=0, concat_axis=0, tiled=True)


def after(value, *others):
    return lax.optimization_barrier((value, *others))[0]


def sorted_slots(key, top):
    slots = jnp.arange(key.shape[0], dtype=jnp.int32)
    ahead = (key[None, :] < key[:, None]) | (
        (key[None, :] == key[:, None]) & (slots[None, :] < slots[:, None])
    )
    position = jnp.sum(ahead.astype(jnp.int32), axis=1)
    here = position[None, :] == slots[:, None]
    order = jnp.sum(jnp.where(here, slots[None, :], 0), axis=1)
    levels = jnp.arange(top + 1, dtype=jnp.int32)
    bounds = jnp.sum((key[None, :] < levels[:, None]).astype(jnp.int32), axis=1)
    return order, bounds


def ranks(group, sub):
    index = jnp.arange(sub.shape[-1], dtype=jnp.int32)
    before = (sub[..., None, :] < sub[..., :, None]) | (
        (sub[..., None, :] == sub[..., :, None]) & (index[None, :] < index[:, None])
    )
    same = group[..., None, :] == group[..., :, None]
    return jnp.sum((before & same).astype(jnp.int32), axis=-1)


def shards(tile_values, tile_row, tile_owner, tile_sub, labels):
    devices = lax.axis_size("dp")
    tiles = tile_values.shape[0]
    home = labels.shape[0]
    blocks = home // LANES * devices
    cap = max(2, 2 * tiles // devices)
    cuts = tuple(sorted({int(cap * share) for share in PARTS})) if cap >= 8 else (0, cap)
    parts = len(cuts) - 1
    here = lax.axis_index("dp").astype(jnp.int32)
    owner = tile_owner[:, 0]

    told = (labels, owner, tile_row, tile_sub)
    rank = ranks(owner, tile_sub)
    outgoing = pack(tile_values, owner, rank, tile_row, told, devices, blocks, cuts)
    incoming = [exchange(outgoing[0])]
    heard = incoming[0][:, (cuts[1] - cuts[0]) * LANES :].astype(jnp.int32)
    level = heard[:, :blocks]
    partial_sq = jnp.exp2(level.astype(jnp.float32) * (1.0 / LOG_STEPS) + LOG_MIDDLE)
    row_sq = jnp.sum(jnp.where(level > -32768, partial_sq, 0.0), axis=0)
    all_described = heard[:, blocks:].reshape(devices, -1)
    all_labels = all_described[:, :home].reshape(blocks, LANES)
    mine = all_described[:, home : home + tiles] == here
    code = all_described[:, home + tiles : home + 2 * tiles]
    rank = ranks(mine.astype(jnp.int32), code % TB_OWN)
    chosen = mine[:, None, :] & (rank[:, None, :] == jnp.arange(cap)[None, :, None])
    meta = jnp.sum(jnp.where(chosen, code[:, None, :] + 1, 0), axis=2).reshape(-1) - 1
    sub = jnp.where(meta < 0, TB_OWN, meta % TB_OWN)
    slot_rank = np.arange(devices * cap) % cap
    slot_part = np.searchsorted(np.array(cuts), slot_rank, side="right") - 1
    low, high = np.array(cuts)[slot_part], np.array(cuts)[slot_part + 1]
    place = devices * low + np.arange(devices * cap) // cap * (high - low) + slot_rank - low
    fold_key = jnp.asarray(slot_part * (TB_OWN + 1), jnp.int32) + sub
    fold_order, fold_bounds = sorted_slots(fold_key, parts * (TB_OWN + 1))
    score_order, score_bounds = sorted_slots(sub, TB_OWN)
    left = np.arange(parts)[:, None] < slot_part[None, :]
    done = jnp.min(jnp.where(left, sub[None, :], TB_OWN), axis=1)
    scalars = [
        fold_order, fold_bounds, score_order, score_bounds, meta, jnp.asarray(place, jnp.int32), done
    ]

    scale = lax.rsqrt(row_sq + EPSILON) * (1.0 / CODE_TOP**2)
    signed = jnp.where(all_labels < HALF, scale, -scale)
    mods = (all_labels % HALF).astype(jnp.float32)
    totals, normed = (), []
    beside = (*scalars, mods, signed)
    for q in range(parts):
        if q + 1 < parts:
            ahead = (incoming[q], *beside) if q else (incoming[q],)
            incoming.append(exchange(after(outgoing[q + 1], *ahead)))
        partial, sums, *more = stage(
            q, cuts, scalars, mods, signed, incoming[q], normed, totals
        )
        beside = (partial, sums)
        totals, normed = (partial, sums, *more[:3]), normed + more[3:]
    return close(labels, exchange(partial), sums, TB_OWN * LANES * devices)


def solution(mesh):
    return jax.shard_map(
        shards,
        mesh=mesh,
        in_specs=(
            P(("groups", "dp"), None, None),
            P(("groups", "dp")),
            P(("groups", "dp"), None),
            P(("groups", "dp")),
            P(("groups", "dp")),
        ),
        out_specs=(P("groups", "dp"), P(("groups", "dp"))),
        check_vma=False,
    )
```

```python
import functools
import math

import jax
import jax.numpy as jnp
import numpy as np
from jax import lax
from jax.experimental import pallas as pl
from jax.experimental.pallas import tpu as pltpu
from jax.sharding import PartitionSpec as P

K = 512
HALF = K // 2
TB_OWN = 16
LANES = 128
EPSILON = 1e-06
CODE_TOP = 65535.0
CODE_SHIFT = 32768
VMEM_BYTES = 60 * 1024 * 1024
STEP_TILES = 16
PARTS = (0.0, 12 / 16, 1.0)
LOG_STEPS = 1800.0
LOG_MIDDLE = -3.0
CACHED_BLOCKS = 64
QUAD = 4
EIGHT = 8
BATCH = 8
NT = (((1,), (1,)), ((), ()))
SMEM = pl.BlockSpec(memory_space=pltpu.SMEM)
VMEM = pl.BlockSpec(memory_space=pltpu.VMEM)
ANY = pl.BlockSpec(memory_space=pl.ANY)


def lane_sums(values):
    ones = jnp.ones((8, LANES), jnp.bfloat16)
    high = values.astype(jnp.bfloat16)
    low = (values - high.astype(jnp.float32)).astype(jnp.bfloat16)
    return lax.dot_general(ones, high, NT, preferred_element_type=jnp.float32) + lax.dot_general(
        ones, low, NT, preferred_element_type=jnp.float32
    )


def block_sums(square, out_ref, count):
    batch = math.gcd(BATCH, count)

    def one_batch(c, carry):
        some = square[pl.ds(c * batch, batch)].reshape((batch * LANES, LANES))
        sums = lane_sums(some)
        for j in range(batch):
            out_ref[pl.ds(c * batch + j, 1), :] += sums[:1, j * LANES : (j + 1) * LANES]
        return carry

    lax.fori_loop(0, count // batch, one_batch, 0)


def params():
    return pltpu.CompilerParams(vmem_limit_bytes=VMEM_BYTES)


def pack_kernel(cuts, owner_ref, rank_ref, row_ref, *refs):
    parts = len(cuts) - 1
    (*told_refs, x_hbm), refs = refs[:5], refs[5:]
    outs = refs[:parts]
    x, coded, square, sums, words, notes, held, sems, x_sems = refs[parts:]
    tiles = x.shape[0]
    devices = held.shape[0]
    blocks = square.shape[0]
    step = math.gcd(STEP_TILES, tiles)

    def read(c):
        some = pl.ds(c * step, step)
        return pltpu.make_async_copy(x_hbm.at[some], x.at[some], x_sems.at[c])

    def clear(d, carry):
        held[d] = 0
        return carry

    for c in range(tiles // step):
        read(c).start()
    lax.fori_loop(0, devices, clear, 0)
    square[...] = jnp.zeros_like(square)

    def some_tiles(i, carry):
        pl.when(i % (step // QUAD) == 0)(lambda: read(i // (step // QUAD)).wait())
        for j in range(QUAD):
            t = i * QUAD + j
            some = x[t]
            root = some * lax.rsqrt(some)
            code = (root * CODE_TOP + 0.5).astype(jnp.int32) - CODE_SHIFT
            owner, rank = owner_ref[t], rank_ref[t]
            at = pl.ds(pl.multiple_of((owner * cuts[-1] + rank) * LANES, LANES), LANES)
            coded[at, :] = code.astype(jnp.int16)
            square[row_ref[t]] += some * some
            held[owner] = jnp.maximum(held[owner], rank + 1)
        return carry

    lax.fori_loop(0, tiles // QUAD, some_tiles, 0)

    def slots(q, d):
        some = pl.ds((d * cuts[-1] + cuts[q]) * LANES, (cuts[q + 1] - cuts[q]) * LANES)
        into = outs[q].at[d, pl.ds(0, (cuts[q + 1] - cuts[q]) * LANES)]
        return pltpu.make_async_copy(coded.at[some], into, sems.at[q, d])

    def note(d):
        into = outs[0].at[d, pl.ds((cuts[1] - cuts[0]) * LANES, notes.shape[0])]
        return pltpu.make_async_copy(notes, into, sems.at[parts, d])

    def each(what):
        def one(d, carry):
            for q in range(parts):
                pl.when(held[d] > cuts[q])(lambda q=q: what(slots(q, d)))
            return carry

        lax.fori_loop(0, devices, one, 0)

    each(lambda copy: copy.start())
    sums[...] = jnp.zeros_like(sums)
    block_sums(square, sums, blocks)
    total = sums[...]
    level = (jnp.log2(jnp.maximum(total, 1e-30)) - LOG_MIDDLE) * LOG_STEPS
    level = jnp.where(total > 0.0, jnp.clip(level, -32700.0, 32700.0), -32768.0)
    level = (level + 32768.5).astype(jnp.int32) - 32768
    labels, owner, row, sub = [ref[...] for ref in told_refs]
    words[...] = jnp.zeros_like(words)
    words[:blocks, :] = level
    at = blocks
    for told in (labels, owner, row * TB_OWN + sub):
        words[at : at + told.shape[0], :] = told
        at += told.shape[0]
    notes[...] = words[...].astype(jnp.int16)

    for d in range(devices):
        note(d).start()
    each(lambda copy: copy.wait())
    for d in range(devices):
        note(d).wait()


def pack(tile_values, owner, rank, tile_row, told, devices, blocks, cuts):
    tiles = tile_values.shape[0]
    told = [x.reshape(-1, LANES) for x in told]
    noted = -(-(blocks + sum(x.shape[0] for x in told[:3])) // 16) * 16
    rows = [(high - low) * LANES for low, high in zip(cuts, cuts[1:])]
    rows[0] += noted
    return pl.pallas_call(
        functools.partial(pack_kernel, cuts),
        in_specs=[SMEM] * 3 + [VMEM] * 4 + [ANY],
        out_specs=[ANY] * len(rows),
        out_shape=[jax.ShapeDtypeStruct((devices, some, LANES), jnp.int16) for some in rows],
        scratch_shapes=[
            pltpu.VMEM(tile_values.shape, jnp.float32),
            pltpu.VMEM((devices * cuts[-1] * LANES, LANES), jnp.int16),
            pltpu.VMEM((blocks, LANES, LANES), jnp.float32),
            pltpu.VMEM((blocks, LANES), jnp.float32),
            pltpu.VMEM((noted, LANES), jnp.int32),
            pltpu.VMEM((noted, LANES), jnp.int16),
            pltpu.SMEM((devices,), jnp.int32),
            pltpu.SemaphoreType.DMA((len(rows) + 1, devices)),
            pltpu.SemaphoreType.DMA((tiles,)),
        ],
        compiler_params=params(),
        cost_estimate=pl.CostEstimate(
            flops=8 * tile_values.size,
            bytes_accessed=6 * tile_values.size,
            transcendentals=tile_values.size,
        ),
        name="pack",
    )(owner, rank, tile_row, *told, tile_values)


def stage_kernel(q, bases, last, cached, fold_order, fold_bound, score_order, score_bound, meta,
                 place, done, mods_in, signed_in, x_hbm, *refs):
    base = bases[q]
    earlier, refs = refs[:q], refs[q:]
    before, sums_in, squares_in, *made_in = refs[:5] if q else (None,) * 5
    refs = refs[5:] if q else refs
    part, sums_out, refs = refs[0], refs[1], refs[2:]
    (squares_out, *made_out, fresh_out), refs = ((None,) * 4, refs) if last else (refs[:4], refs[4:])
    spread, x, hot, sums, narrow, tiles, products, scores, squares, mods, signed, *refs = refs
    sems, sub_sems, tile_sems = refs
    devices, width = x.shape[0], x.shape[1] // LANES
    none = products.shape[0] - 1
    begin, end = done[q - 1] if q else 0, done[q]
    needed = [pltpu.make_async_copy(x_hbm.at[:, pl.ds(0, width * LANES)], x, sems.at[0])]
    if q:
        needed.append(pltpu.make_async_copy(made_in[0], spread, sems.at[1]))
    for copy in needed:
        copy.start()

    def columns(sub):
        return (slice(None), pl.ds(pl.multiple_of(sub * 2 * LANES, 2 * LANES), 2 * LANES))

    def sums_read(sub):
        return pltpu.make_async_copy(
            sums_in.at[columns(sub)], sums.at[columns(sub)], sub_sems.at[0, sub]
        )

    def sums_write(sub):
        return pltpu.make_async_copy(
            sums.at[columns(sub)], sums_out.at[columns(sub)], sub_sems.at[1, sub]
        )

    def each_sub(low, high, what):
        def one(sub, carry):
            what(sub)
            return carry

        lax.fori_loop(low, high, one, 0)

    if q:
        each_sub(begin, TB_OWN, lambda sub: sums_read(sub).start())
        squares[...] = squares_in[...]
    else:
        sums[...] = jnp.zeros_like(sums)
        squares[...] = jnp.zeros_like(squares)
    later = [pltpu.make_async_copy(made_in[1], hot, sems.at[3])] if q and cached else []
    for e, e_hbm in enumerate(earlier):
        held = tiles.at[pl.ds(bases[e], e_hbm.shape[0])]
        later.append(pltpu.make_async_copy(e_hbm, held, tile_sems.at[e]))
    for copy in later:
        copy.start()
    products[...] = jnp.zeros_like(products)
    scores[...] = before[...] if q else jnp.zeros_like(scores)
    for held, given, empty in ((mods, mods_in, -1.0), (signed, signed_in, 0.0)):
        held[:none, :] = given[...]
        held[none : none + 1, :] = jnp.full((1, LANES), empty, jnp.float32)
    cluster = lax.broadcasted_iota(jnp.int32, (HALF, LANES), 0)
    lane = lax.broadcasted_iota(jnp.int32, (LANES, LANES), 1)

    def column(ref, row):
        return jnp.transpose(jnp.broadcast_to(ref[pl.ds(row, 1), :], (LANES, LANES)))

    def one_hot(row):
        own = column(mods, row).astype(jnp.int32)
        some = [jnp.where(own == lane + g, 1.0, 0.0) for g in range(0, HALF, LANES)]
        return jnp.concatenate(some, axis=1).astype(jnp.bfloat16)

    batch = math.gcd(none + 1, 3)

    def build(c, carry):
        for j in range(batch):
            spread[c * batch + j] = column(signed, c * batch + j)
            if cached:
                hot[c * batch + j] = one_hot(c * batch + j)
        return carry

    if not q:
        lax.fori_loop(0, (none + 1) // batch, build, 0)
    for copy in needed:
        copy.wait()

    def eight(order, start, end, p):
        rows, spots = [], []
        for j in range(EIGHT):
            at = start + EIGHT * p + j
            slot = order[jnp.where(at < end, at, start)]
            rows.append((meta[slot] // TB_OWN, at < end))
            spots.append(place[slot])
        return rows, spots

    def fold_sub(sub):
        start = fold_bound[q * (TB_OWN + 1) + sub]
        end = fold_bound[q * (TB_OWN + 1) + sub + 1]
        if q:
            sums_read(sub).wait()

        def one_eight(p, carry):
            rows, spots = eight(fold_order, start, end, p)
            folded, picks = [], []
            for (row, held), spot in zip(rows, spots):
                source, slot = (spot - base) // width, (spot - base) % width
                raw = x[source, pl.ds(pl.multiple_of(slot * LANES, LANES), LANES), :]
                root = raw.astype(jnp.int32).astype(jnp.float32) + float(CODE_SHIFT)
                scale = spread[row]
                tile = root * root * jnp.abs(scale)
                tiles[spot] = tile.astype(jnp.bfloat16)
                halves = [jnp.where(scale > 0.0, tile, 0.0), jnp.where(scale < 0.0, tile, 0.0)]
                folded.append(jnp.concatenate(halves, axis=1).astype(jnp.bfloat16))
                own = mods[pl.ds(jnp.where(held, row, none), 1), :].astype(jnp.int32)
                picks.append(jnp.where(cluster == own, 1.0, 0.0).astype(jnp.bfloat16))
            pick = jnp.concatenate(picks, axis=1)
            sums[columns(sub)] += jnp.dot(
                pick, jnp.concatenate(folded, axis=0), preferred_element_type=jnp.float32
            )
            return carry

        lax.fori_loop(0, (end - start + EIGHT - 1) // EIGHT, one_eight, 0)
        sums_write(sub).start()

    each_sub(begin, TB_OWN, fold_sub)
    kept = []
    if not last:
        fresh = tiles.at[pl.ds(base, devices * width)]
        kept.append(pltpu.make_async_copy(fresh, fresh_out, sems.at[2]))
        kept.append(pltpu.make_async_copy(spread, made_out[0], sems.at[4]))
        kept.append(pltpu.make_async_copy(hot, made_out[1], sems.at[5]))
    for copy in kept:
        copy.start()
    for copy in later:
        copy.wait()

    def score_sub(sub):
        start, end = score_bound[sub], score_bound[sub + 1]
        some = sums[columns(sub)]
        narrow[...] = some.astype(jnp.bfloat16)
        squares[...] += some * some

        def one_eight(p, carry):
            rows, spots = eight(score_order, start, end, p)
            rows = [jnp.where(held, row, none) for row, held in rows]
            hots = [hot[row] if cached else one_hot(row) for row in rows]
            chosen = jnp.dot(
                jnp.concatenate(hots, axis=0), narrow[...], preferred_element_type=jnp.float32
            )
            for j in range(EIGHT):
                both = chosen[j * LANES : (j + 1) * LANES]
                own = jnp.where(spread[rows[j]] < 0.0, both[:, LANES:], both[:, :LANES])
                products[rows[j]] += own * tiles[spots[j]].astype(jnp.float32)
            return carry

        lax.fori_loop(0, (end - start + EIGHT - 1) // EIGHT, one_eight, 0)

    each_sub(begin, end, score_sub)
    block_sums(products, scores, none)
    if last:
        own = none // devices
        square = [lane_sums(squares[:, h : h + LANES])[:1] for h in (0, LANES)]
        square = jnp.concatenate(square, axis=1)
        for d in range(devices):
            part[d, :, part.shape[2] - K :] = square
            for b in range(own):
                at = d * own + b
                part[d, :, b * LANES : (b + 1) * LANES] = scores[at : at + 1, :]
    else:
        part[...] = scores[...]
        squares_out[...] = squares[...]
    for copy in kept:
        copy.wait()
    each_sub(begin, TB_OWN, lambda sub: sums_write(sub).wait())


def stage(q, cuts, scalars, mods, signed, x, normed, totals):
    devices = x.shape[0]
    last = q == len(cuts) - 2
    blocks = mods.shape[0]
    cached = blocks <= CACHED_BLOCKS
    width = cuts[q + 1] - cuts[q]
    home = blocks // devices * LANES
    wide = jax.ShapeDtypeStruct((HALF, TB_OWN * 2 * LANES), jnp.float32)
    square = jax.ShapeDtypeStruct((HALF, 2 * LANES), jnp.float32)
    if last:
        out_shape = [jax.ShapeDtypeStruct((devices, 1, home + K), jnp.float32), wide]
    else:
        out_shape = [
            jax.ShapeDtypeStruct((blocks, LANES), jnp.float32),
            wide,
            square,
            jax.ShapeDtypeStruct((blocks + 1, LANES, LANES), jnp.float32),
            jax.ShapeDtypeStruct((blocks + 1 if cached else 1, LANES, HALF), jnp.bfloat16),
            jax.ShapeDtypeStruct((devices * width, LANES, LANES), jnp.bfloat16),
        ]
    slots = devices * cuts[-1]
    operands = [*scalars, mods, signed, x, *normed, *totals]
    return pl.pallas_call(
        functools.partial(stage_kernel, q, [devices * cut for cut in cuts], last, cached),
        in_specs=[SMEM] * len(scalars) + [VMEM] * 2 + [ANY] * (1 + q) + [VMEM, ANY, VMEM, ANY, ANY][: len(totals)],
        out_specs=[VMEM, ANY, VMEM, ANY, ANY, ANY][: len(out_shape)],
        out_shape=out_shape,
        input_output_aliases={len(operands) - len(totals) + 1: 1} if q else {},
        scratch_shapes=[
            pltpu.VMEM((blocks + 1, LANES, LANES), jnp.float32),
            pltpu.VMEM((devices, width * LANES, LANES), jnp.int16),
            pltpu.VMEM((blocks + 1 if cached else 1, LANES, HALF), jnp.bfloat16),
            pltpu.VMEM(wide.shape, jnp.float32),
            pltpu.VMEM(square.shape, jnp.bfloat16),
            pltpu.VMEM((slots, LANES, LANES), jnp.bfloat16),
            pltpu.VMEM((blocks + 1, LANES, LANES), jnp.float32),
            pltpu.VMEM((blocks, LANES), jnp.float32),
            pltpu.VMEM(square.shape, jnp.float32),
            pltpu.VMEM((blocks + 1, LANES), jnp.float32),
            pltpu.VMEM((blocks + 1, LANES), jnp.float32),
            pltpu.SemaphoreType.DMA((6,)),
            pltpu.SemaphoreType.DMA((2, TB_OWN)),
            pltpu.SemaphoreType.DMA((len(cuts),)),
        ],
        compiler_params=params(),
        cost_estimate=pl.CostEstimate(
            flops=devices * width * LANES * LANES * K * 8,
            bytes_accessed=4 * devices * width * LANES * LANES + 8 * K * TB_OWN * LANES,
            transcendentals=0,
        ),
        name="stage",
    )(*operands)


def close_kernel(root, groups, labels_ref, got_ref, sums_hbm, out_hbm, similarity, sums, out, sems):
    width = TB_OWN // groups
    reads, writes = [], []
    for g in range(groups):
        some = (slice(None), pl.ds(g * width * 2 * LANES, width * 2 * LANES))
        reads.append(pltpu.make_async_copy(sums_hbm.at[some], sums.at[some], sems.at[0, g]))
        some = (slice(None), pl.ds(g * width * LANES, width * LANES))
        writes.append(pltpu.make_async_copy(out.at[some], out_hbm.at[some], sems.at[1, g]))
        reads[g].start()
    total = jnp.sum(got_ref[...], axis=0)
    home = total.shape[1] - K
    own = lax.rsqrt(total[:, home:] + EPSILON)
    columns = [
        jnp.transpose(jnp.broadcast_to(own[:, k : k + LANES], (LANES, LANES)))
        for k in range(0, K, LANES)
    ]
    cluster = lax.broadcasted_iota(jnp.int32, (LANES, LANES), 0)
    for b in range(home // LANES):
        found = jnp.zeros((LANES, LANES), jnp.float32)
        for i, column in enumerate(columns):
            found += jnp.where(cluster + i * LANES == labels_ref[b : b + 1, :], column, 0.0)
        found = jnp.sum(found, axis=0, keepdims=True)
        similarity[b : b + 1, :] = total[:, b * LANES : (b + 1) * LANES] * found
    for g in range(groups):
        reads[g].wait()

        def one_sub(sub, carry):
            to = pl.ds(pl.multiple_of(sub * LANES, LANES), LANES)
            for i, column in enumerate(columns):
                half, row = divmod(i * LANES, HALF)
                at = pl.ds(pl.multiple_of((2 * sub + half) * LANES, LANES), LANES)
                done = sums[row : row + LANES, at] * column * root
                out[i * LANES : (i + 1) * LANES, to] = done.astype(jnp.bfloat16)
            return carry

        lax.fori_loop(g * width, (g + 1) * width, one_sub, 0)
        writes[g].start()
    for write in writes:
        write.wait()


def close(labels, got, sums, vocab_size):
    groups = 4
    labels = labels.reshape(-1, LANES)
    wide = jax.ShapeDtypeStruct((K, TB_OWN * LANES), jnp.bfloat16)
    centroids, similarity = pl.pallas_call(
        functools.partial(close_kernel, math.sqrt(vocab_size), groups),
        in_specs=[VMEM, VMEM, ANY],
        out_specs=[ANY, VMEM],
        out_shape=[wide, jax.ShapeDtypeStruct(labels.shape, jnp.float32)],
        scratch_shapes=[
            pltpu.VMEM(sums.shape, jnp.float32),
            pltpu.VMEM(wide.shape, jnp.bfloat16),
            pltpu.SemaphoreType.DMA((2, groups)),
        ],
        compiler_params=params(),
        cost_estimate=pl.CostEstimate(
            flops=2 * sums.size, bytes_accessed=6 * sums.size, transcendentals=0
        ),
        name="close",
    )(labels, got, sums)
    return centroids, similarity.reshape(-1)


def exchange(x):
    return lax.all_to_all(x, "dp", split_axis=0, concat_axis=0, tiled=True)


def after(value, *others):
    return lax.optimization_barrier((value, *others))[0]


def sorted_slots(key, top):
    slots = jnp.arange(key.shape[0], dtype=jnp.int32)
    ahead = (key[None, :] < key[:, None]) | (
        (key[None, :] == key[:, None]) & (slots[None, :] < slots[:, None])
    )
    position = jnp.sum(ahead.astype(jnp.int32), axis=1)
    here = position[None, :] == slots[:, None]
    order = jnp.sum(jnp.where(here, slots[None, :], 0), axis=1)
    levels = jnp.arange(top + 1, dtype=jnp.int32)
    bounds = jnp.sum((key[None, :] < levels[:, None]).astype(jnp.int32), axis=1)
    return order, bounds


def ranks(group, sub):
    index = jnp.arange(sub.shape[-1], dtype=jnp.int32)
    before = (sub[..., None, :] < sub[..., :, None]) | (
        (sub[..., None, :] == sub[..., :, None]) & (index[None, :] < index[:, None])
    )
    same = group[..., None, :] == group[..., :, None]
    return jnp.sum((before & same).astype(jnp.int32), axis=-1)


def shards(tile_values, tile_row, tile_owner, tile_sub, labels):
    devices = lax.axis_size("dp")
    tiles = tile_values.shape[0]
    home = labels.shape[0]
    blocks = home // LANES * devices
    cap = max(2, 2 * tiles // devices)
    cuts = tuple(sorted({int(cap * share) for share in PARTS})) if cap >= 8 else (0, cap)
    parts = len(cuts) - 1
    here = lax.axis_index("dp").astype(jnp.int32)
    owner = tile_owner[:, 0]

    told = (labels, owner, tile_row, tile_sub)
    rank = ranks(owner, tile_sub)
    outgoing = pack(tile_values, owner, rank, tile_row, told, devices, blocks, cuts)
    incoming = [exchange(outgoing[0])]
    heard = incoming[0][:, (cuts[1] - cuts[0]) * LANES :].astype(jnp.int32)
    level = heard[:, :blocks]
    partial_sq = jnp.exp2(level.astype(jnp.float32) * (1.0 / LOG_STEPS) + LOG_MIDDLE)
    row_sq = jnp.sum(jnp.where(level > -32768, partial_sq, 0.0), axis=0)
    all_described = heard[:, blocks:].reshape(devices, -1)
    all_labels = all_described[:, :home].reshape(blocks, LANES)
    mine = all_described[:, home : home + tiles] == here
    code = all_described[:, home + tiles : home + 2 * tiles]
    rank = ranks(mine.astype(jnp.int32), code % TB_OWN)
    chosen = mine[:, None, :] & (rank[:, None, :] == jnp.arange(cap)[None, :, None])
    meta = jnp.sum(jnp.where(chosen, code[:, None, :] + 1, 0), axis=2).reshape(-1) - 1
    sub = jnp.where(meta < 0, TB_OWN, meta % TB_OWN)
    slot_rank = np.arange(devices * cap) % cap
    slot_part = np.searchsorted(np.array(cuts), slot_rank, side="right") - 1
    low, high = np.array(cuts)[slot_part], np.array(cuts)[slot_part + 1]
    place = devices * low + np.arange(devices * cap) // cap * (high - low) + slot_rank - low
    fold_key = jnp.asarray(slot_part * (TB_OWN + 1), jnp.int32) + sub
    fold_order, fold_bounds = sorted_slots(fold_key, parts * (TB_OWN + 1))
    score_order, score_bounds = sorted_slots(sub, TB_OWN)
    left = np.arange(parts)[:, None] < slot_part[None, :]
    done = jnp.min(jnp.where(left, sub[None, :], TB_OWN), axis=1)
    scalars = [
        fold_order, fold_bounds, score_order, score_bounds, meta, jnp.asarray(place, jnp.int32), done
    ]

    scale = lax.rsqrt(row_sq + EPSILON) * (1.0 / CODE_TOP**2)
    signed = jnp.where(all_labels < HALF, scale, -scale)
    mods = (all_labels % HALF).astype(jnp.float32)
    totals, normed = (), []
    beside = (*scalars, mods, signed)
    for q in range(parts):
        if q + 1 < parts:
            ahead = (incoming[q], *beside) if q else (incoming[q],)
            incoming.append(exchange(after(outgoing[q + 1], *ahead)))
        partial, sums, *more = stage(
            q, cuts, scalars, mods, signed, incoming[q], normed, totals
        )
        beside = (partial, sums)
        totals, normed = (partial, sums, *more[:3]), normed + more[3:]
    return close(labels, exchange(partial), sums, TB_OWN * LANES * devices)


def solution(mesh):
    return jax.shard_map(
        shards,
        mesh=mesh,
        in_specs=(
            P(("groups", "dp"), None, None),
            P(("groups", "dp")),
            P(("groups", "dp"), None),
            P(("groups", "dp")),
            P(("groups", "dp")),
        ),
        out_specs=(P("groups", "dp"), P(("groups", "dp"))),
        check_vma=False,
    )
```

```python
import functools
import math

import jax
import jax.numpy as jnp
import numpy as np
from jax import lax
from jax.experimental import pallas as pl
from jax.experimental.pallas import tpu as pltpu
from jax.sharding import PartitionSpec as P

K = 512
HALF = K // 2
TB_OWN = 16
LANES = 128
EPSILON = 1e-06
CODE_TOP = 65535.0
CODE_SHIFT = 32768
VMEM_BYTES = 60 * 1024 * 1024
STEP_TILES = 16
PARTS = (0.0, 13 / 16, 1.0)
LOG_STEPS = 1800.0
LOG_MIDDLE = -3.0
CACHED_BLOCKS = 64
QUAD = 4
EIGHT = 8
BATCH = 8
NT = (((1,), (1,)), ((), ()))
SMEM = pl.BlockSpec(memory_space=pltpu.SMEM)
VMEM = pl.BlockSpec(memory_space=pltpu.VMEM)
ANY = pl.BlockSpec(memory_space=pl.ANY)


def lane_sums(values):
    ones = jnp.ones((8, LANES), jnp.bfloat16)
    high = values.astype(jnp.bfloat16)
    low = (values - high.astype(jnp.float32)).astype(jnp.bfloat16)
    return lax.dot_general(ones, high, NT, preferred_element_type=jnp.float32) + lax.dot_general(
        ones, low, NT, preferred_element_type=jnp.float32
    )


def block_sums(square, out_ref, count):
    batch = math.gcd(BATCH, count)

    def one_batch(c, carry):
        some = square[pl.ds(c * batch, batch)].reshape((batch * LANES, LANES))
        sums = lane_sums(some)
        for j in range(batch):
            out_ref[pl.ds(c * batch + j, 1), :] += sums[:1, j * LANES : (j + 1) * LANES]
        return carry

    lax.fori_loop(0, count // batch, one_batch, 0)


def params():
    return pltpu.CompilerParams(vmem_limit_bytes=VMEM_BYTES)


def pack_kernel(cuts, owner_ref, rank_ref, row_ref, *refs):
    parts = len(cuts) - 1
    (*told_refs, x_hbm), refs = refs[:5], refs[5:]
    outs = refs[:parts]
    x, coded, square, sums, words, notes, held, sems, x_sems = refs[parts:]
    tiles = x.shape[0]
    devices = held.shape[0]
    blocks = square.shape[0]
    step = math.gcd(STEP_TILES, tiles)

    def read(c):
        some = pl.ds(c * step, step)
        return pltpu.make_async_copy(x_hbm.at[some], x.at[some], x_sems.at[c])

    def clear(d, carry):
        held[d] = 0
        return carry

    for c in range(tiles // step):
        read(c).start()
    lax.fori_loop(0, devices, clear, 0)
    square[...] = jnp.zeros_like(square)

    def some_tiles(i, carry):
        pl.when(i % (step // QUAD) == 0)(lambda: read(i // (step // QUAD)).wait())
        for j in range(QUAD):
            t = i * QUAD + j
            some = x[t]
            root = some * lax.rsqrt(some)
            code = (root * CODE_TOP + 0.5).astype(jnp.int32) - CODE_SHIFT
            owner, rank = owner_ref[t], rank_ref[t]
            at = pl.ds(pl.multiple_of((owner * cuts[-1] + rank) * LANES, LANES), LANES)
            coded[at, :] = code.astype(jnp.int16)
            square[row_ref[t]] += some * some
            held[owner] = jnp.maximum(held[owner], rank + 1)
        return carry

    lax.fori_loop(0, tiles // QUAD, some_tiles, 0)

    def slots(q, d):
        some = pl.ds((d * cuts[-1] + cuts[q]) * LANES, (cuts[q + 1] - cuts[q]) * LANES)
        into = outs[q].at[d, pl.ds(0, (cuts[q + 1] - cuts[q]) * LANES)]
        return pltpu.make_async_copy(coded.at[some], into, sems.at[q, d])

    def note(d):
        into = outs[0].at[d, pl.ds((cuts[1] - cuts[0]) * LANES, notes.shape[0])]
        return pltpu.make_async_copy(notes, into, sems.at[parts, d])

    def each(what):
        def one(d, carry):
            for q in range(parts):
                pl.when(held[d] > cuts[q])(lambda q=q: what(slots(q, d)))
            return carry

        lax.fori_loop(0, devices, one, 0)

    each(lambda copy: copy.start())
    sums[...] = jnp.zeros_like(sums)
    block_sums(square, sums, blocks)
    total = sums[...]
    level = (jnp.log2(jnp.maximum(total, 1e-30)) - LOG_MIDDLE) * LOG_STEPS
    level = jnp.where(total > 0.0, jnp.clip(level, -32700.0, 32700.0), -32768.0)
    level = (level + 32768.5).astype(jnp.int32) - 32768
    labels, owner, row, sub = [ref[...] for ref in told_refs]
    words[...] = jnp.zeros_like(words)
    words[:blocks, :] = level
    at = blocks
    for told in (labels, owner, row * TB_OWN + sub):
        words[at : at + told.shape[0], :] = told
        at += told.shape[0]
    notes[...] = words[...].astype(jnp.int16)

    for d in range(devices):
        note(d).start()
    each(lambda copy: copy.wait())
    for d in range(devices):
        note(d).wait()


def pack(tile_values, owner, rank, tile_row, told, devices, blocks, cuts):
    tiles = tile_values.shape[0]
    told = [x.reshape(-1, LANES) for x in told]
    noted = -(-(blocks + sum(x.shape[0] for x in told[:3])) // 16) * 16
    rows = [(high - low) * LANES for low, high in zip(cuts, cuts[1:])]
    rows[0] += noted
    return pl.pallas_call(
        functools.partial(pack_kernel, cuts),
        in_specs=[SMEM] * 3 + [VMEM] * 4 + [ANY],
        out_specs=[ANY] * len(rows),
        out_shape=[jax.ShapeDtypeStruct((devices, some, LANES), jnp.int16) for some in rows],
        scratch_shapes=[
            pltpu.VMEM(tile_values.shape, jnp.float32),
            pltpu.VMEM((devices * cuts[-1] * LANES, LANES), jnp.int16),
            pltpu.VMEM((blocks, LANES, LANES), jnp.float32),
            pltpu.VMEM((blocks, LANES), jnp.float32),
            pltpu.VMEM((noted, LANES), jnp.int32),
            pltpu.VMEM((noted, LANES), jnp.int16),
            pltpu.SMEM((devices,), jnp.int32),
            pltpu.SemaphoreType.DMA((len(rows) + 1, devices)),
            pltpu.SemaphoreType.DMA((tiles,)),
        ],
        compiler_params=params(),
        cost_estimate=pl.CostEstimate(
            flops=8 * tile_values.size,
            bytes_accessed=6 * tile_values.size,
            transcendentals=tile_values.size,
        ),
        name="pack",
    )(owner, rank, tile_row, *told, tile_values)


def stage_kernel(q, bases, last, cached, fold_order, fold_bound, score_order, score_bound, meta,
                 place, done, mods_in, signed_in, x_hbm, *refs):
    base = bases[q]
    earlier, refs = refs[:q], refs[q:]
    before, sums_in, squares_in, *made_in = refs[:5] if q else (None,) * 5
    refs = refs[5:] if q else refs
    part, sums_out, refs = refs[0], refs[1], refs[2:]
    (squares_out, *made_out, fresh_out), refs = ((None,) * 4, refs) if last else (refs[:4], refs[4:])
    spread, x, hot, sums, narrow, tiles, products, scores, squares, mods, signed, *refs = refs
    sems, sub_sems, tile_sems = refs
    devices, width = x.shape[0], x.shape[1] // LANES
    none = products.shape[0] - 1
    begin, end = done[q - 1] if q else 0, done[q]
    needed = [pltpu.make_async_copy(x_hbm.at[:, pl.ds(0, width * LANES)], x, sems.at[0])]
    if q:
        needed.append(pltpu.make_async_copy(made_in[0], spread, sems.at[1]))
    for copy in needed:
        copy.start()

    def columns(sub):
        return (slice(None), pl.ds(pl.multiple_of(sub * 2 * LANES, 2 * LANES), 2 * LANES))

    def sums_read(sub):
        return pltpu.make_async_copy(
            sums_in.at[columns(sub)], sums.at[columns(sub)], sub_sems.at[0, sub]
        )

    def sums_write(sub):
        return pltpu.make_async_copy(
            sums.at[columns(sub)], sums_out.at[columns(sub)], sub_sems.at[1, sub]
        )

    def each_sub(low, high, what):
        def one(sub, carry):
            what(sub)
            return carry

        lax.fori_loop(low, high, one, 0)

    if q:
        each_sub(begin, TB_OWN, lambda sub: sums_read(sub).start())
        squares[...] = squares_in[...]
    else:
        sums[...] = jnp.zeros_like(sums)
        squares[...] = jnp.zeros_like(squares)
    later = [pltpu.make_async_copy(made_in[1], hot, sems.at[3])] if q and cached else []
    for e, e_hbm in enumerate(earlier):
        held = tiles.at[pl.ds(bases[e], e_hbm.shape[0])]
        later.append(pltpu.make_async_copy(e_hbm, held, tile_sems.at[e]))
    for copy in later:
        copy.start()
    products[...] = jnp.zeros_like(products)
    scores[...] = before[...] if q else jnp.zeros_like(scores)
    for held, given, empty in ((mods, mods_in, -1.0), (signed, signed_in, 0.0)):
        held[:none, :] = given[...]
        held[none : none + 1, :] = jnp.full((1, LANES), empty, jnp.float32)
    cluster = lax.broadcasted_iota(jnp.int32, (HALF, LANES), 0).astype(jnp.float32)
    cluster = cluster.astype(jnp.bfloat16).reshape(HALF // 16, 16, LANES)
    one, zero = jnp.ones((), jnp.bfloat16), jnp.zeros((), jnp.bfloat16)
    lane = lax.broadcasted_iota(jnp.int32, (LANES, LANES), 1)

    def column(ref, row):
        return jnp.transpose(jnp.broadcast_to(ref[pl.ds(row, 1), :], (LANES, LANES)))

    def one_hot(row):
        own = column(mods, row).astype(jnp.int32)
        some = [jnp.where(own == lane + g, 1.0, 0.0) for g in range(0, HALF, LANES)]
        return jnp.concatenate(some, axis=1).astype(jnp.bfloat16)

    batch = math.gcd(none + 1, 3)

    def build(c, carry):
        for j in range(batch):
            spread[c * batch + j] = column(signed, c * batch + j)
            if cached:
                hot[c * batch + j] = one_hot(c * batch + j)
        return carry

    if not q:
        lax.fori_loop(0, (none + 1) // batch, build, 0)
    for copy in needed:
        copy.wait()

    def eight(order, start, end, p):
        rows, spots = [], []
        for j in range(EIGHT):
            at = start + EIGHT * p + j
            slot = order[jnp.where(at < end, at, start)]
            rows.append((meta[slot] // TB_OWN, at < end))
            spots.append(place[slot])
        return rows, spots

    def fold_sub(sub):
        start = fold_bound[q * (TB_OWN + 1) + sub]
        end = fold_bound[q * (TB_OWN + 1) + sub + 1]
        if q:
            sums_read(sub).wait()

        def one_eight(p, carry):
            rows, spots = eight(fold_order, start, end, p)
            folded, picks = [], []
            for (row, held), spot in zip(rows, spots):
                source, slot = (spot - base) // width, (spot - base) % width
                raw = x[source, pl.ds(pl.multiple_of(slot * LANES, LANES), LANES), :]
                root = raw.astype(jnp.int32).astype(jnp.float32) + float(CODE_SHIFT)
                scale = spread[row]
                square = root * root
                tile = square * jnp.abs(scale)
                lower = square * jnp.maximum(scale, 0.0)
                tiles[spot] = tile.astype(jnp.bfloat16)
                halves = [lower.astype(jnp.bfloat16), (tile - lower).astype(jnp.bfloat16)]
                folded.append(jnp.concatenate(halves, axis=1))
                own = jnp.broadcast_to(mods[pl.ds(jnp.where(held, row, none), 1), :], (16, LANES))
                own = jnp.where(cluster == own.astype(jnp.bfloat16)[None], one, zero)
                picks.append(own.reshape(HALF, LANES))
            pick = jnp.concatenate(picks, axis=1)
            sums[columns(sub)] += jnp.dot(
                pick, jnp.concatenate(folded, axis=0), preferred_element_type=jnp.float32
            )
            return carry

        lax.fori_loop(0, (end - start + EIGHT - 1) // EIGHT, one_eight, 0)
        sums_write(sub).start()

    each_sub(begin, TB_OWN, fold_sub)
    kept = []
    if not last:
        fresh = tiles.at[pl.ds(base, devices * width)]
        kept.append(pltpu.make_async_copy(fresh, fresh_out, sems.at[2]))
        kept.append(pltpu.make_async_copy(spread, made_out[0], sems.at[4]))
        kept.append(pltpu.make_async_copy(hot, made_out[1], sems.at[5]))
    for copy in kept:
        copy.start()
    for copy in later:
        copy.wait()

    def score_sub(sub):
        start, end = score_bound[sub], score_bound[sub + 1]
        some = sums[columns(sub)]
        narrow[...] = some.astype(jnp.bfloat16)
        squares[...] += some * some

        def one_eight(p, carry):
            rows, spots = eight(score_order, start, end, p)
            rows = [jnp.where(held, row, none) for row, held in rows]
            hots = [hot[row] if cached else one_hot(row) for row in rows]
            chosen = jnp.dot(
                jnp.concatenate(hots, axis=0), narrow[...], preferred_element_type=jnp.float32
            )
            for j in range(EIGHT):
                both = chosen[j * LANES : (j + 1) * LANES]
                own = jnp.where(spread[rows[j]] < 0.0, both[:, LANES:], both[:, :LANES])
                products[rows[j]] += own * tiles[spots[j]].astype(jnp.float32)
            return carry

        lax.fori_loop(0, (end - start + EIGHT - 1) // EIGHT, one_eight, 0)

    each_sub(begin, end, score_sub)
    block_sums(products, scores, none)
    if last:
        own = none // devices
        square = [lane_sums(squares[:, h : h + LANES])[:1] for h in (0, LANES)]
        square = jnp.concatenate(square, axis=1)
        for d in range(devices):
            part[d, :, part.shape[2] - K :] = square
            for b in range(own):
                at = d * own + b
                part[d, :, b * LANES : (b + 1) * LANES] = scores[at : at + 1, :]
    else:
        part[...] = scores[...]
        squares_out[...] = squares[...]
    for copy in kept:
        copy.wait()
    each_sub(begin, TB_OWN, lambda sub: sums_write(sub).wait())


def stage(q, cuts, scalars, mods, signed, x, normed, totals):
    devices = x.shape[0]
    last = q == len(cuts) - 2
    blocks = mods.shape[0]
    cached = blocks <= CACHED_BLOCKS
    width = cuts[q + 1] - cuts[q]
    home = blocks // devices * LANES
    wide = jax.ShapeDtypeStruct((HALF, TB_OWN * 2 * LANES), jnp.float32)
    square = jax.ShapeDtypeStruct((HALF, 2 * LANES), jnp.float32)
    if last:
        out_shape = [jax.ShapeDtypeStruct((devices, 1, home + K), jnp.float32), wide]
    else:
        out_shape = [
            jax.ShapeDtypeStruct((blocks, LANES), jnp.float32),
            wide,
            square,
            jax.ShapeDtypeStruct((blocks + 1, LANES, LANES), jnp.float32),
            jax.ShapeDtypeStruct((blocks + 1 if cached else 1, LANES, HALF), jnp.bfloat16),
            jax.ShapeDtypeStruct((devices * width, LANES, LANES), jnp.bfloat16),
        ]
    slots = devices * cuts[-1]
    operands = [*scalars, mods, signed, x, *normed, *totals]
    return pl.pallas_call(
        functools.partial(stage_kernel, q, [devices * cut for cut in cuts], last, cached),
        in_specs=[SMEM] * len(scalars) + [VMEM] * 2 + [ANY] * (1 + q) + [VMEM, ANY, VMEM, ANY, ANY][: len(totals)],
        out_specs=[VMEM, ANY, VMEM, ANY, ANY, ANY][: len(out_shape)],
        out_shape=out_shape,
        input_output_aliases={len(operands) - len(totals) + 1: 1} if q else {},
        scratch_shapes=[
            pltpu.VMEM((blocks + 1, LANES, LANES), jnp.float32),
            pltpu.VMEM((devices, width * LANES, LANES), jnp.int16),
            pltpu.VMEM((blocks + 1 if cached else 1, LANES, HALF), jnp.bfloat16),
            pltpu.VMEM(wide.shape, jnp.float32),
            pltpu.VMEM(square.shape, jnp.bfloat16),
            pltpu.VMEM((slots, LANES, LANES), jnp.bfloat16),
            pltpu.VMEM((blocks + 1, LANES, LANES), jnp.float32),
            pltpu.VMEM((blocks, LANES), jnp.float32),
            pltpu.VMEM(square.shape, jnp.float32),
            pltpu.VMEM((blocks + 1, LANES), jnp.float32),
            pltpu.VMEM((blocks + 1, LANES), jnp.float32),
            pltpu.SemaphoreType.DMA((6,)),
            pltpu.SemaphoreType.DMA((2, TB_OWN)),
            pltpu.SemaphoreType.DMA((len(cuts),)),
        ],
        compiler_params=params(),
        cost_estimate=pl.CostEstimate(
            flops=devices * width * LANES * LANES * K * 8,
            bytes_accessed=4 * devices * width * LANES * LANES + 8 * K * TB_OWN * LANES,
            transcendentals=0,
        ),
        name="stage",
    )(*operands)


def close_kernel(root, groups, labels_ref, got_ref, sums_hbm, out_hbm, similarity, sums, out, sems):
    width = TB_OWN // groups
    reads, writes = [], []
    for g in range(groups):
        some = (slice(None), pl.ds(g * width * 2 * LANES, width * 2 * LANES))
        reads.append(pltpu.make_async_copy(sums_hbm.at[some], sums.at[some], sems.at[0, g]))
        some = (slice(None), pl.ds(g * width * LANES, width * LANES))
        writes.append(pltpu.make_async_copy(out.at[some], out_hbm.at[some], sems.at[1, g]))
        reads[g].start()
    total = jnp.sum(got_ref[...], axis=0)
    home = total.shape[1] - K
    own = lax.rsqrt(total[:, home:] + EPSILON)
    columns = [
        jnp.transpose(jnp.broadcast_to(own[:, k : k + LANES], (LANES, LANES)))
        for k in range(0, K, LANES)
    ]
    cluster = lax.broadcasted_iota(jnp.int32, (LANES, LANES), 0)
    for b in range(home // LANES):
        found = jnp.zeros((LANES, LANES), jnp.float32)
        for i, column in enumerate(columns):
            found += jnp.where(cluster + i * LANES == labels_ref[b : b + 1, :], column, 0.0)
        found = jnp.sum(found, axis=0, keepdims=True)
        similarity[b : b + 1, :] = total[:, b * LANES : (b + 1) * LANES] * found
    for g in range(groups):
        reads[g].wait()

        def one_sub(sub, carry):
            to = pl.ds(pl.multiple_of(sub * LANES, LANES), LANES)
            for i, column in enumerate(columns):
                half, row = divmod(i * LANES, HALF)
                at = pl.ds(pl.multiple_of((2 * sub + half) * LANES, LANES), LANES)
                done = sums[row : row + LANES, at] * column * root
                out[i * LANES : (i + 1) * LANES, to] = done.astype(jnp.bfloat16)
            return carry

        lax.fori_loop(g * width, (g + 1) * width, one_sub, 0)
        writes[g].start()
    for write in writes:
        write.wait()


def close(labels, got, sums, vocab_size):
    groups = 4
    labels = labels.reshape(-1, LANES)
    wide = jax.ShapeDtypeStruct((K, TB_OWN * LANES), jnp.bfloat16)
    centroids, similarity = pl.pallas_call(
        functools.partial(close_kernel, math.sqrt(vocab_size), groups),
        in_specs=[VMEM, VMEM, ANY],
        out_specs=[ANY, VMEM],
        out_shape=[wide, jax.ShapeDtypeStruct(labels.shape, jnp.float32)],
        scratch_shapes=[
            pltpu.VMEM(sums.shape, jnp.float32),
            pltpu.VMEM(wide.shape, jnp.bfloat16),
            pltpu.SemaphoreType.DMA((2, groups)),
        ],
        compiler_params=params(),
        cost_estimate=pl.CostEstimate(
            flops=2 * sums.size, bytes_accessed=6 * sums.size, transcendentals=0
        ),
        name="close",
    )(labels, got, sums)
    return centroids, similarity.reshape(-1)


def exchange(x):
    return lax.all_to_all(x, "dp", split_axis=0, concat_axis=0, tiled=True)


def after(value, *others):
    return lax.optimization_barrier((value, *others))[0]


def sorted_slots(key, top):
    slots = jnp.arange(key.shape[0], dtype=jnp.int32)
    ahead = (key[None, :] < key[:, None]) | (
        (key[None, :] == key[:, None]) & (slots[None, :] < slots[:, None])
    )
    position = jnp.sum(ahead.astype(jnp.int32), axis=1)
    here = position[None, :] == slots[:, None]
    order = jnp.sum(jnp.where(here, slots[None, :], 0), axis=1)
    levels = jnp.arange(top + 1, dtype=jnp.int32)
    bounds = jnp.sum((key[None, :] < levels[:, None]).astype(jnp.int32), axis=1)
    return order, bounds


def ranks(group, sub):
    index = jnp.arange(sub.shape[-1], dtype=jnp.int32)
    before = (sub[..., None, :] < sub[..., :, None]) | (
        (sub[..., None, :] == sub[..., :, None]) & (index[None, :] < index[:, None])
    )
    same = group[..., None, :] == group[..., :, None]
    return jnp.sum((before & same).astype(jnp.int32), axis=-1)


def shards(tile_values, tile_row, tile_owner, tile_sub, labels):
    devices = lax.axis_size("dp")
    tiles = tile_values.shape[0]
    home = labels.shape[0]
    blocks = home // LANES * devices
    cap = max(2, 2 * tiles // devices)
    cuts = tuple(sorted({int(cap * share) for share in PARTS})) if cap >= 8 else (0, cap)
    parts = len(cuts) - 1
    here = lax.axis_index("dp").astype(jnp.int32)
    owner = tile_owner[:, 0]

    told = (labels, owner, tile_row, tile_sub)
    rank = ranks(owner, tile_sub)
    outgoing = pack(tile_values, owner, rank, tile_row, told, devices, blocks, cuts)
    incoming = [exchange(outgoing[0])]
    heard = incoming[0][:, (cuts[1] - cuts[0]) * LANES :].astype(jnp.int32)
    level = heard[:, :blocks]
    partial_sq = jnp.exp2(level.astype(jnp.float32) * (1.0 / LOG_STEPS) + LOG_MIDDLE)
    row_sq = jnp.sum(jnp.where(level > -32768, partial_sq, 0.0), axis=0)
    all_described = heard[:, blocks:].reshape(devices, -1)
    all_labels = all_described[:, :home].reshape(blocks, LANES)
    mine = all_described[:, home : home + tiles] == here
    code = all_described[:, home + tiles : home + 2 * tiles]
    rank = ranks(mine.astype(jnp.int32), code % TB_OWN)
    chosen = mine[:, None, :] & (rank[:, None, :] == jnp.arange(cap)[None, :, None])
    meta = jnp.sum(jnp.where(chosen, code[:, None, :] + 1, 0), axis=2).reshape(-1) - 1
    sub = jnp.where(meta < 0, TB_OWN, meta % TB_OWN)
    slot_rank = np.arange(devices * cap) % cap
    slot_part = np.searchsorted(np.array(cuts), slot_rank, side="right") - 1
    low, high = np.array(cuts)[slot_part], np.array(cuts)[slot_part + 1]
    place = devices * low + np.arange(devices * cap) // cap * (high - low) + slot_rank - low
    fold_key = jnp.asarray(slot_part * (TB_OWN + 1), jnp.int32) + sub
    fold_order, fold_bounds = sorted_slots(fold_key, parts * (TB_OWN + 1))
    score_order, score_bounds = sorted_slots(sub, TB_OWN)
    left = np.arange(parts)[:, None] < slot_part[None, :]
    done = jnp.min(jnp.where(left, sub[None, :], TB_OWN), axis=1)
    scalars = [
        fold_order, fold_bounds, score_order, score_bounds, meta, jnp.asarray(place, jnp.int32), done
    ]

    scale = lax.rsqrt(row_sq + EPSILON) * (1.0 / CODE_TOP**2)
    signed = jnp.where(all_labels < HALF, scale, -scale)
    mods = (all_labels % HALF).astype(jnp.float32)
    totals, normed = (), []
    beside = (*scalars, mods, signed)
    for q in range(parts):
        if q + 1 < parts:
            ahead = (incoming[q], *beside) if q else (incoming[q],)
            incoming.append(exchange(after(outgoing[q + 1], *ahead)))
        partial, sums, *more = stage(
            q, cuts, scalars, mods, signed, incoming[q], normed, totals
        )
        beside = (partial, sums)
        totals, normed = (partial, sums, *more[:3]), normed + more[3:]
    return close(labels, exchange(partial), sums, TB_OWN * LANES * devices)


def solution(mesh):
    return jax.shard_map(
        shards,
        mesh=mesh,
        in_specs=(
            P(("groups", "dp"), None, None),
            P(("groups", "dp")),
            P(("groups", "dp"), None),
            P(("groups", "dp")),
            P(("groups", "dp")),
        ),
        out_specs=(P("groups", "dp"), P(("groups", "dp"))),
        check_vma=False,
    )
```

```python
import functools
import math

import jax
import jax.numpy as jnp
import numpy as np
from jax import lax
from jax.experimental import pallas as pl
from jax.experimental.pallas import tpu as pltpu
from jax.sharding import PartitionSpec as P

K = 512
HALF = K // 2
TB_OWN = 16
LANES = 128
EPSILON = 1e-06
CODE_TOP = 65535.0
CODE_SHIFT = 32768
VMEM_BYTES = 60 * 1024 * 1024
STEP_TILES = 16
PARTS = (0.0, 13 / 16, 1.0)
LOG_STEPS = 1800.0
LOG_MIDDLE = -3.0
CACHED_BLOCKS = 64
QUAD = 4
EIGHT = 8
ROW_SHIFT, SOURCE_SHIFT = 16, 8
PLACE_MASK, SOURCE_MASK, SLOT_MASK = 0xFFFF, 0xFF, 0xFF
BATCH = 8
NT = (((1,), (1,)), ((), ()))
SMEM = pl.BlockSpec(memory_space=pltpu.SMEM)
VMEM = pl.BlockSpec(memory_space=pltpu.VMEM)
ANY = pl.BlockSpec(memory_space=pl.ANY)


def lane_sums(values):
    ones = jnp.ones((8, LANES), jnp.bfloat16)
    high = values.astype(jnp.bfloat16)
    low = (values - high.astype(jnp.float32)).astype(jnp.bfloat16)
    return lax.dot_general(ones, high, NT, preferred_element_type=jnp.float32) + lax.dot_general(
        ones, low, NT, preferred_element_type=jnp.float32
    )


def block_sums(square, out_ref, count):
    batch = math.gcd(BATCH, count)

    def one_batch(c, carry):
        some = square[pl.ds(c * batch, batch)].reshape((batch * LANES, LANES))
        sums = lane_sums(some)
        for j in range(batch):
            out_ref[pl.ds(c * batch + j, 1), :] += sums[:1, j * LANES : (j + 1) * LANES]
        return carry

    lax.fori_loop(0, count // batch, one_batch, 0)


def params():
    return pltpu.CompilerParams(vmem_limit_bytes=VMEM_BYTES)


def pack_kernel(cuts, owner_ref, rank_ref, row_ref, *refs):
    parts = len(cuts) - 1
    (*told_refs, x_hbm), refs = refs[:5], refs[5:]
    outs = refs[:parts]
    x, coded, square, sums, words, notes, held, sems, x_sems = refs[parts:]
    tiles = x.shape[0]
    devices = held.shape[0]
    blocks = square.shape[0]
    step = math.gcd(STEP_TILES, tiles)

    def read(c):
        some = pl.ds(c * step, step)
        return pltpu.make_async_copy(x_hbm.at[some], x.at[some], x_sems.at[c])

    def clear(d, carry):
        held[d] = 0
        return carry

    for c in range(tiles // step):
        read(c).start()
    lax.fori_loop(0, devices, clear, 0)
    square[...] = jnp.zeros_like(square)

    def some_tiles(i, carry):
        pl.when(i % (step // QUAD) == 0)(lambda: read(i // (step // QUAD)).wait())
        for j in range(QUAD):
            t = i * QUAD + j
            some = x[t]
            root = some * lax.rsqrt(some)
            code = (root * CODE_TOP + 0.5).astype(jnp.int32) - CODE_SHIFT
            owner, rank = owner_ref[t], rank_ref[t]
            at = pl.ds(pl.multiple_of((owner * cuts[-1] + rank) * LANES, LANES), LANES)
            coded[at, :] = code.astype(jnp.int16)
            square[row_ref[t]] += some * some
            held[owner] = jnp.maximum(held[owner], rank + 1)
        return carry

    lax.fori_loop(0, tiles // QUAD, some_tiles, 0)

    def slots(q, d):
        some = pl.ds((d * cuts[-1] + cuts[q]) * LANES, (cuts[q + 1] - cuts[q]) * LANES)
        into = outs[q].at[d, pl.ds(0, (cuts[q + 1] - cuts[q]) * LANES)]
        return pltpu.make_async_copy(coded.at[some], into, sems.at[q, d])

    def note(d):
        into = outs[0].at[d, pl.ds((cuts[1] - cuts[0]) * LANES, notes.shape[0])]
        return pltpu.make_async_copy(notes, into, sems.at[parts, d])

    def each(what):
        def one(d, carry):
            for q in range(parts):
                pl.when(held[d] > cuts[q])(lambda q=q: what(slots(q, d)))
            return carry

        lax.fori_loop(0, devices, one, 0)

    each(lambda copy: copy.start())
    sums[...] = jnp.zeros_like(sums)
    block_sums(square, sums, blocks)
    total = sums[...]
    level = (jnp.log2(jnp.maximum(total, 1e-30)) - LOG_MIDDLE) * LOG_STEPS
    level = jnp.where(total > 0.0, jnp.clip(level, -32700.0, 32700.0), -32768.0)
    level = (level + 32768.5).astype(jnp.int32) - 32768
    labels, owner, row, sub = [ref[...] for ref in told_refs]
    words[...] = jnp.zeros_like(words)
    words[:blocks, :] = level
    at = blocks
    for told in (labels, owner, row * TB_OWN + sub):
        words[at : at + told.shape[0], :] = told
        at += told.shape[0]
    notes[...] = words[...].astype(jnp.int16)

    for d in range(devices):
        note(d).start()
    each(lambda copy: copy.wait())
    for d in range(devices):
        note(d).wait()


def pack(tile_values, owner, rank, tile_row, told, devices, blocks, cuts):
    tiles = tile_values.shape[0]
    told = [x.reshape(-1, LANES) for x in told]
    noted = -(-(blocks + sum(x.shape[0] for x in told[:3])) // 16) * 16
    rows = [(high - low) * LANES for low, high in zip(cuts, cuts[1:])]
    rows[0] += noted
    return pl.pallas_call(
        functools.partial(pack_kernel, cuts),
        in_specs=[SMEM] * 3 + [VMEM] * 4 + [ANY],
        out_specs=[ANY] * len(rows),
        out_shape=[jax.ShapeDtypeStruct((devices, some, LANES), jnp.int16) for some in rows],
        scratch_shapes=[
            pltpu.VMEM(tile_values.shape, jnp.float32),
            pltpu.VMEM((devices * cuts[-1] * LANES, LANES), jnp.int16),
            pltpu.VMEM((blocks, LANES, LANES), jnp.float32),
            pltpu.VMEM((blocks, LANES), jnp.float32),
            pltpu.VMEM((noted, LANES), jnp.int32),
            pltpu.VMEM((noted, LANES), jnp.int16),
            pltpu.SMEM((devices,), jnp.int32),
            pltpu.SemaphoreType.DMA((len(rows) + 1, devices)),
            pltpu.SemaphoreType.DMA((tiles,)),
        ],
        compiler_params=params(),
        cost_estimate=pl.CostEstimate(
            flops=8 * tile_values.size,
            bytes_accessed=6 * tile_values.size,
            transcendentals=tile_values.size,
        ),
        name="pack",
    )(owner, rank, tile_row, *told, tile_values)


def stage_kernel(q, bases, last, cached, fold_list, fold_bound, score_list, score_bound, done,
                 mods_in, signed_in, x_hbm, *refs):
    base = bases[q]
    earlier, refs = refs[:q], refs[q:]
    before, sums_in, squares_in, *made_in = refs[:5] if q else (None,) * 5
    refs = refs[5:] if q else refs
    part, sums_out, refs = refs[0], refs[1], refs[2:]
    (squares_out, *made_out, fresh_out), refs = ((None,) * 4, refs) if last else (refs[:4], refs[4:])
    spread, x, hot, sums, narrow, tiles, products, scores, squares, mods, signed, *refs = refs
    sems, sub_sems, tile_sems = refs
    devices, width = x.shape[0], x.shape[1] // LANES
    none = products.shape[0] - 1
    begin, end = done[q - 1] if q else 0, done[q]
    needed = [pltpu.make_async_copy(x_hbm.at[:, pl.ds(0, width * LANES)], x, sems.at[0])]
    if q:
        needed.append(pltpu.make_async_copy(made_in[0], spread, sems.at[1]))
    for copy in needed:
        copy.start()

    def columns(sub):
        return (slice(None), pl.ds(pl.multiple_of(sub * 2 * LANES, 2 * LANES), 2 * LANES))

    def sums_read(sub):
        return pltpu.make_async_copy(
            sums_in.at[columns(sub)], sums.at[columns(sub)], sub_sems.at[0, sub]
        )

    def sums_write(sub):
        return pltpu.make_async_copy(
            sums.at[columns(sub)], sums_out.at[columns(sub)], sub_sems.at[1, sub]
        )

    def each_sub(low, high, what):
        def one(sub, carry):
            what(sub)
            return carry

        lax.fori_loop(low, high, one, 0)

    if q:
        each_sub(begin, TB_OWN, lambda sub: sums_read(sub).start())
        squares[...] = squares_in[...]
    else:
        sums[...] = jnp.zeros_like(sums)
        squares[...] = jnp.zeros_like(squares)
    later = [pltpu.make_async_copy(made_in[1], hot, sems.at[3])] if q and cached else []
    for e, e_hbm in enumerate(earlier):
        held = tiles.at[pl.ds(bases[e], e_hbm.shape[0])]
        later.append(pltpu.make_async_copy(e_hbm, held, tile_sems.at[e]))
    for copy in later:
        copy.start()
    products[...] = jnp.zeros_like(products)
    scores[...] = before[...] if q else jnp.zeros_like(scores)
    for held, given, empty in ((mods, mods_in, -1.0), (signed, signed_in, 0.0)):
        held[:none, :] = given[...]
        held[none : none + 1, :] = jnp.full((1, LANES), empty, jnp.float32)
    cluster = lax.broadcasted_iota(jnp.int32, (HALF, LANES), 0).astype(jnp.float32)
    cluster = cluster.astype(jnp.bfloat16).reshape(HALF // 16, 16, LANES)
    one, zero = jnp.ones((), jnp.bfloat16), jnp.zeros((), jnp.bfloat16)
    lane = lax.broadcasted_iota(jnp.int32, (LANES, LANES), 1)

    def column(ref, row):
        return jnp.transpose(jnp.broadcast_to(ref[pl.ds(row, 1), :], (LANES, LANES)))

    def one_hot(row):
        own = column(mods, row).astype(jnp.int32)
        some = [jnp.where(own == lane + g, 1.0, 0.0) for g in range(0, HALF, LANES)]
        return jnp.concatenate(some, axis=1).astype(jnp.bfloat16)

    batch = math.gcd(none + 1, 3)

    def build(c, carry):
        for j in range(batch):
            spread[c * batch + j] = column(signed, c * batch + j)
            if cached:
                hot[c * batch + j] = one_hot(c * batch + j)
        return carry

    if not q:
        lax.fori_loop(0, (none + 1) // batch, build, 0)
    for copy in needed:
        copy.wait()

    def eight(entries, start, end, p):
        at = [start + EIGHT * p + j for j in range(EIGHT)]
        return [(entries[jnp.where(spot < end, spot, start)], spot < end) for spot in at]

    def fold_sub(sub):
        start = fold_bound[q * (TB_OWN + 1) + sub]
        end = fold_bound[q * (TB_OWN + 1) + sub + 1]
        if q:
            sums_read(sub).wait()

        def one_eight(p, carry):
            folded, picks = [], []
            for entry, held in eight(fold_list, start, end, p):
                row = entry >> ROW_SHIFT
                source, slot = (entry >> SOURCE_SHIFT) & SOURCE_MASK, entry & SLOT_MASK
                spot = base + source * width + slot
                raw = x[source, pl.ds(pl.multiple_of(slot * LANES, LANES), LANES), :]
                root = raw.astype(jnp.int32).astype(jnp.float32) + float(CODE_SHIFT)
                scale = spread[row]
                square = root * root
                tile = square * jnp.abs(scale)
                lower = square * jnp.maximum(scale, 0.0)
                tiles[spot] = tile.astype(jnp.bfloat16)
                halves = [lower.astype(jnp.bfloat16), (tile - lower).astype(jnp.bfloat16)]
                folded.append(jnp.concatenate(halves, axis=1))
                own = jnp.broadcast_to(mods[pl.ds(jnp.where(held, row, none), 1), :], (16, LANES))
                own = jnp.where(cluster == own.astype(jnp.bfloat16)[None], one, zero)
                picks.append(own.reshape(HALF, LANES))
            pick = jnp.concatenate(picks, axis=1)
            sums[columns(sub)] += jnp.dot(
                pick, jnp.concatenate(folded, axis=0), preferred_element_type=jnp.float32
            )
            return carry

        lax.fori_loop(0, (end - start + EIGHT - 1) // EIGHT, one_eight, 0)
        sums_write(sub).start()

    each_sub(begin, TB_OWN, fold_sub)
    kept = []
    if not last:
        fresh = tiles.at[pl.ds(base, devices * width)]
        kept.append(pltpu.make_async_copy(fresh, fresh_out, sems.at[2]))
        kept.append(pltpu.make_async_copy(spread, made_out[0], sems.at[4]))
        kept.append(pltpu.make_async_copy(hot, made_out[1], sems.at[5]))
    for copy in kept:
        copy.start()
    for copy in later:
        copy.wait()

    def score_sub(sub):
        start, end = score_bound[sub], score_bound[sub + 1]
        some = sums[columns(sub)]
        narrow[...] = some.astype(jnp.bfloat16)
        squares[...] += some * some

        def one_eight(p, carry):
            listed = eight(score_list, start, end, p)
            rows = [jnp.where(held, entry >> ROW_SHIFT, none) for entry, held in listed]
            spots = [entry & PLACE_MASK for entry, held in listed]
            hots = [hot[row] if cached else one_hot(row) for row in rows]
            chosen = jnp.dot(
                jnp.concatenate(hots, axis=0), narrow[...], preferred_element_type=jnp.float32
            )
            for j in range(EIGHT):
                both = chosen[j * LANES : (j + 1) * LANES]
                own = jnp.where(spread[rows[j]] < 0.0, both[:, LANES:], both[:, :LANES])
                products[rows[j]] += own * tiles[spots[j]].astype(jnp.float32)
            return carry

        lax.fori_loop(0, (end - start + EIGHT - 1) // EIGHT, one_eight, 0)

    each_sub(begin, end, score_sub)
    block_sums(products, scores, none)
    if last:
        own = none // devices
        square = [lane_sums(squares[:, h : h + LANES])[:1] for h in (0, LANES)]
        square = jnp.concatenate(square, axis=1)
        for d in range(devices):
            part[d, :, part.shape[2] - K :] = square
            for b in range(own):
                at = d * own + b
                part[d, :, b * LANES : (b + 1) * LANES] = scores[at : at + 1, :]
    else:
        part[...] = scores[...]
        squares_out[...] = squares[...]
    for copy in kept:
        copy.wait()
    each_sub(begin, TB_OWN, lambda sub: sums_write(sub).wait())


def stage(q, cuts, scalars, mods, signed, x, normed, totals):
    devices = x.shape[0]
    last = q == len(cuts) - 2
    blocks = mods.shape[0]
    cached = blocks <= CACHED_BLOCKS
    width = cuts[q + 1] - cuts[q]
    home = blocks // devices * LANES
    wide = jax.ShapeDtypeStruct((HALF, TB_OWN * 2 * LANES), jnp.float32)
    square = jax.ShapeDtypeStruct((HALF, 2 * LANES), jnp.float32)
    if last:
        out_shape = [jax.ShapeDtypeStruct((devices, 1, home + K), jnp.float32), wide]
    else:
        out_shape = [
            jax.ShapeDtypeStruct((blocks, LANES), jnp.float32),
            wide,
            square,
            jax.ShapeDtypeStruct((blocks + 1, LANES, LANES), jnp.float32),
            jax.ShapeDtypeStruct((blocks + 1 if cached else 1, LANES, HALF), jnp.bfloat16),
            jax.ShapeDtypeStruct((devices * width, LANES, LANES), jnp.bfloat16),
        ]
    slots = devices * cuts[-1]
    operands = [*scalars, mods, signed, x, *normed, *totals]
    return pl.pallas_call(
        functools.partial(stage_kernel, q, [devices * cut for cut in cuts], last, cached),
        in_specs=[SMEM] * len(scalars) + [VMEM] * 2 + [ANY] * (1 + q) + [VMEM, ANY, VMEM, ANY, ANY][: len(totals)],
        out_specs=[VMEM, ANY, VMEM, ANY, ANY, ANY][: len(out_shape)],
        out_shape=out_shape,
        input_output_aliases={len(operands) - len(totals) + 1: 1} if q else {},
        scratch_shapes=[
            pltpu.VMEM((blocks + 1, LANES, LANES), jnp.float32),
            pltpu.VMEM((devices, width * LANES, LANES), jnp.int16),
            pltpu.VMEM((blocks + 1 if cached else 1, LANES, HALF), jnp.bfloat16),
            pltpu.VMEM(wide.shape, jnp.float32),
            pltpu.VMEM(square.shape, jnp.bfloat16),
            pltpu.VMEM((slots, LANES, LANES), jnp.bfloat16),
            pltpu.VMEM((blocks + 1, LANES, LANES), jnp.float32),
            pltpu.VMEM((blocks, LANES), jnp.float32),
            pltpu.VMEM(square.shape, jnp.float32),
            pltpu.VMEM((blocks + 1, LANES), jnp.float32),
            pltpu.VMEM((blocks + 1, LANES), jnp.float32),
            pltpu.SemaphoreType.DMA((6,)),
            pltpu.SemaphoreType.DMA((2, TB_OWN)),
            pltpu.SemaphoreType.DMA((len(cuts),)),
        ],
        compiler_params=params(),
        cost_estimate=pl.CostEstimate(
            flops=devices * width * LANES * LANES * K * 8,
            bytes_accessed=4 * devices * width * LANES * LANES + 8 * K * TB_OWN * LANES,
            transcendentals=0,
        ),
        name="stage",
    )(*operands)


def close_kernel(root, groups, labels_ref, got_ref, sums_hbm, out_hbm, similarity, sums, out, sems):
    width = TB_OWN // groups
    reads, writes = [], []
    for g in range(groups):
        some = (slice(None), pl.ds(g * width * 2 * LANES, width * 2 * LANES))
        reads.append(pltpu.make_async_copy(sums_hbm.at[some], sums.at[some], sems.at[0, g]))
        some = (slice(None), pl.ds(g * width * LANES, width * LANES))
        writes.append(pltpu.make_async_copy(out.at[some], out_hbm.at[some], sems.at[1, g]))
        reads[g].start()
    total = jnp.sum(got_ref[...], axis=0)
    home = total.shape[1] - K
    own = lax.rsqrt(total[:, home:] + EPSILON)
    columns = [
        jnp.transpose(jnp.broadcast_to(own[:, k : k + LANES], (LANES, LANES)))
        for k in range(0, K, LANES)
    ]
    cluster = lax.broadcasted_iota(jnp.int32, (LANES, LANES), 0)
    for b in range(home // LANES):
        found = jnp.zeros((LANES, LANES), jnp.float32)
        for i, column in enumerate(columns):
            found += jnp.where(cluster + i * LANES == labels_ref[b : b + 1, :], column, 0.0)
        found = jnp.sum(found, axis=0, keepdims=True)
        similarity[b : b + 1, :] = total[:, b * LANES : (b + 1) * LANES] * found
    for g in range(groups):
        reads[g].wait()

        def one_sub(sub, carry):
            to = pl.ds(pl.multiple_of(sub * LANES, LANES), LANES)
            for i, column in enumerate(columns):
                half, row = divmod(i * LANES, HALF)
                at = pl.ds(pl.multiple_of((2 * sub + half) * LANES, LANES), LANES)
                done = sums[row : row + LANES, at] * column * root
                out[i * LANES : (i + 1) * LANES, to] = done.astype(jnp.bfloat16)
            return carry

        lax.fori_loop(g * width, (g + 1) * width, one_sub, 0)
        writes[g].start()
    for write in writes:
        write.wait()


def close(labels, got, sums, vocab_size):
    groups = 4
    labels = labels.reshape(-1, LANES)
    wide = jax.ShapeDtypeStruct((K, TB_OWN * LANES), jnp.bfloat16)
    centroids, similarity = pl.pallas_call(
        functools.partial(close_kernel, math.sqrt(vocab_size), groups),
        in_specs=[VMEM, VMEM, ANY],
        out_specs=[ANY, VMEM],
        out_shape=[wide, jax.ShapeDtypeStruct(labels.shape, jnp.float32)],
        scratch_shapes=[
            pltpu.VMEM(sums.shape, jnp.float32),
            pltpu.VMEM(wide.shape, jnp.bfloat16),
            pltpu.SemaphoreType.DMA((2, groups)),
        ],
        compiler_params=params(),
        cost_estimate=pl.CostEstimate(
            flops=2 * sums.size, bytes_accessed=6 * sums.size, transcendentals=0
        ),
        name="close",
    )(labels, got, sums)
    return centroids, similarity.reshape(-1)


def exchange(x):
    return lax.all_to_all(x, "dp", split_axis=0, concat_axis=0, tiled=True)


def after(value, *others):
    return lax.optimization_barrier((value, *others))[0]


def sorted_slots(key, top, entries):
    slots = jnp.arange(key.shape[0], dtype=jnp.int32)
    ahead = (key[None, :] < key[:, None]) | (
        (key[None, :] == key[:, None]) & (slots[None, :] < slots[:, None])
    )
    position = jnp.sum(ahead.astype(jnp.int32), axis=1)
    here = position[None, :] == slots[:, None]
    listed = jnp.sum(jnp.where(here, entries[None, :], 0), axis=1)
    levels = jnp.arange(top + 1, dtype=jnp.int32)
    bounds = jnp.sum((key[None, :] < levels[:, None]).astype(jnp.int32), axis=1)
    return listed, bounds


def ranks(group, sub):
    index = jnp.arange(sub.shape[-1], dtype=jnp.int32)
    before = (sub[..., None, :] < sub[..., :, None]) | (
        (sub[..., None, :] == sub[..., :, None]) & (index[None, :] < index[:, None])
    )
    same = group[..., None, :] == group[..., :, None]
    return jnp.sum((before & same).astype(jnp.int32), axis=-1)


def shards(tile_values, tile_row, tile_owner, tile_sub, labels):
    devices = lax.axis_size("dp")
    tiles = tile_values.shape[0]
    home = labels.shape[0]
    blocks = home // LANES * devices
    cap = max(2, 2 * tiles // devices)
    cuts = tuple(sorted({int(cap * share) for share in PARTS})) if cap >= 8 else (0, cap)
    parts = len(cuts) - 1
    here = lax.axis_index("dp").astype(jnp.int32)
    owner = tile_owner[:, 0]

    told = (labels, owner, tile_row, tile_sub)
    rank = ranks(owner, tile_sub)
    outgoing = pack(tile_values, owner, rank, tile_row, told, devices, blocks, cuts)
    incoming = [exchange(outgoing[0])]
    heard = incoming[0][:, (cuts[1] - cuts[0]) * LANES :].astype(jnp.int32)
    level = heard[:, :blocks]
    partial_sq = jnp.exp2(level.astype(jnp.float32) * (1.0 / LOG_STEPS) + LOG_MIDDLE)
    row_sq = jnp.sum(jnp.where(level > -32768, partial_sq, 0.0), axis=0)
    all_described = heard[:, blocks:].reshape(devices, -1)
    all_labels = all_described[:, :home].reshape(blocks, LANES)
    mine = all_described[:, home : home + tiles] == here
    code = all_described[:, home + tiles : home + 2 * tiles]
    rank = ranks(mine.astype(jnp.int32), code % TB_OWN)
    chosen = mine[:, None, :] & (rank[:, None, :] == jnp.arange(cap)[None, :, None])
    meta = jnp.sum(jnp.where(chosen, code[:, None, :] + 1, 0), axis=2).reshape(-1) - 1
    sub = jnp.where(meta < 0, TB_OWN, meta % TB_OWN)
    slot_rank = np.arange(devices * cap) % cap
    slot_part = np.searchsorted(np.array(cuts), slot_rank, side="right") - 1
    low, high = np.array(cuts)[slot_part], np.array(cuts)[slot_part + 1]
    place = devices * low + np.arange(devices * cap) // cap * (high - low) + slot_rank - low
    fold_key = jnp.asarray(slot_part * (TB_OWN + 1), jnp.int32) + sub
    row = (meta // TB_OWN) << ROW_SHIFT
    from_slot = (np.arange(devices * cap) // cap << SOURCE_SHIFT) + slot_rank - low
    fold_list, fold_bounds = sorted_slots(
        fold_key, parts * (TB_OWN + 1), row + jnp.asarray(from_slot, jnp.int32)
    )
    score_list, score_bounds = sorted_slots(sub, TB_OWN, row + jnp.asarray(place, jnp.int32))
    left = np.arange(parts)[:, None] < slot_part[None, :]
    done = jnp.min(jnp.where(left, sub[None, :], TB_OWN), axis=1)
    scalars = [fold_list, fold_bounds, score_list, score_bounds, done]

    scale = lax.rsqrt(row_sq + EPSILON) * (1.0 / CODE_TOP**2)
    signed = jnp.where(all_labels < HALF, scale, -scale)
    mods = (all_labels % HALF).astype(jnp.float32)
    totals, normed = (), []
    beside = (*scalars, mods, signed)
    for q in range(parts):
        if q + 1 < parts:
            ahead = (incoming[q], *beside) if q else (incoming[q],)
            incoming.append(exchange(after(outgoing[q + 1], *ahead)))
        partial, sums, *more = stage(
            q, cuts, scalars, mods, signed, incoming[q], normed, totals
        )
        beside = (partial, sums)
        totals, normed = (partial, sums, *more[:3]), normed + more[3:]
    return close(labels, exchange(partial), sums, TB_OWN * LANES * devices)


def solution(mesh):
    return jax.shard_map(
        shards,
        mesh=mesh,
        in_specs=(
            P(("groups", "dp"), None, None),
            P(("groups", "dp")),
            P(("groups", "dp"), None),
            P(("groups", "dp")),
            P(("groups", "dp")),
        ),
        out_specs=(P("groups", "dp"), P(("groups", "dp"))),
        check_vma=False,
    )
```

```python
import functools
import math

import jax
import jax.numpy as jnp
import numpy as np
from jax import lax
from jax.experimental import pallas as pl
from jax.experimental.pallas import tpu as pltpu
from jax.sharding import PartitionSpec as P

K = 512
HALF = K // 2
TB_OWN = 16
LANES = 128
EPSILON = 1e-06
CODE_TOP = 65535.0
CODE_SHIFT = 32768
VMEM_BYTES = 60 * 1024 * 1024
STEP_TILES = 16
PARTS = (0.0, 13 / 16, 1.0)
LOG_STEPS = 1800.0
LOG_MIDDLE = -3.0
CACHED_BLOCKS = 64
QUAD = 4
EIGHT = 8
ROW_SHIFT, SOURCE_SHIFT = 16, 8
PLACE_MASK, SOURCE_MASK, SLOT_MASK = 0xFFFF, 0xFF, 0xFF
BATCH = 8
NT = (((1,), (1,)), ((), ()))
SMEM = pl.BlockSpec(memory_space=pltpu.SMEM)
VMEM = pl.BlockSpec(memory_space=pltpu.VMEM)
ANY = pl.BlockSpec(memory_space=pl.ANY)


def lane_sums(values):
    ones = jnp.ones((8, 2 * LANES), jnp.bfloat16)
    high = values.astype(jnp.bfloat16)
    low = (values - high.astype(jnp.float32)).astype(jnp.bfloat16)
    both = jnp.concatenate([high, low], axis=1)
    return lax.dot_general(ones, both, NT, preferred_element_type=jnp.float32)


def block_sums(square, out_ref, count):
    batch = math.gcd(BATCH, count)

    def one_batch(c, carry):
        some = square[pl.ds(c * batch, batch)].reshape((batch * LANES, LANES))
        sums = lane_sums(some)
        for j in range(batch):
            out_ref[pl.ds(c * batch + j, 1), :] += sums[:1, j * LANES : (j + 1) * LANES]
        return carry

    lax.fori_loop(0, count // batch, one_batch, 0)


def params():
    return pltpu.CompilerParams(vmem_limit_bytes=VMEM_BYTES)


def pack_kernel(cuts, owner_ref, rank_ref, row_ref, *refs):
    parts = len(cuts) - 1
    (*told_refs, x_hbm), refs = refs[:5], refs[5:]
    outs = refs[:parts]
    x, coded, square, sums, words, notes, held, sems, x_sems = refs[parts:]
    tiles = x.shape[0]
    devices = held.shape[0]
    blocks = square.shape[0]
    step = math.gcd(STEP_TILES, tiles)

    def read(c):
        some = pl.ds(c * step, step)
        return pltpu.make_async_copy(x_hbm.at[some], x.at[some], x_sems.at[c])

    def clear(d, carry):
        held[d] = 0
        return carry

    for c in range(tiles // step):
        read(c).start()
    lax.fori_loop(0, devices, clear, 0)
    square[...] = jnp.zeros_like(square)

    def some_tiles(i, carry):
        pl.when(i % (step // QUAD) == 0)(lambda: read(i // (step // QUAD)).wait())
        for j in range(QUAD):
            t = i * QUAD + j
            some = x[t]
            root = some * lax.rsqrt(some)
            code = (root * CODE_TOP + 0.5).astype(jnp.int32) - CODE_SHIFT
            owner, rank = owner_ref[t], rank_ref[t]
            at = pl.ds(pl.multiple_of((owner * cuts[-1] + rank) * LANES, LANES), LANES)
            coded[at, :] = code.astype(jnp.int16)
            square[row_ref[t]] += some * some
            held[owner] = jnp.maximum(held[owner], rank + 1)
        return carry

    lax.fori_loop(0, tiles // QUAD, some_tiles, 0)

    def slots(q, d):
        some = pl.ds((d * cuts[-1] + cuts[q]) * LANES, (cuts[q + 1] - cuts[q]) * LANES)
        into = outs[q].at[d, pl.ds(0, (cuts[q + 1] - cuts[q]) * LANES)]
        return pltpu.make_async_copy(coded.at[some], into, sems.at[q, d])

    def note(d):
        into = outs[0].at[d, pl.ds((cuts[1] - cuts[0]) * LANES, notes.shape[0])]
        return pltpu.make_async_copy(notes, into, sems.at[parts, d])

    def each(what):
        def one(d, carry):
            for q in range(parts):
                pl.when(held[d] > cuts[q])(lambda q=q: what(slots(q, d)))
            return carry

        lax.fori_loop(0, devices, one, 0)

    each(lambda copy: copy.start())
    sums[...] = jnp.zeros_like(sums)
    block_sums(square, sums, blocks)
    total = sums[...]
    level = (jnp.log2(jnp.maximum(total, 1e-30)) - LOG_MIDDLE) * LOG_STEPS
    level = jnp.where(total > 0.0, jnp.clip(level, -32700.0, 32700.0), -32768.0)
    level = (level + 32768.5).astype(jnp.int32) - 32768
    labels, owner, row, sub = [ref[...] for ref in told_refs]
    words[...] = jnp.zeros_like(words)
    words[:blocks, :] = level
    at = blocks
    for told in (labels, owner, row * TB_OWN + sub):
        words[at : at + told.shape[0], :] = told
        at += told.shape[0]
    notes[...] = words[...].astype(jnp.int16)

    for d in range(devices):
        note(d).start()
    each(lambda copy: copy.wait())
    for d in range(devices):
        note(d).wait()


def pack(tile_values, owner, rank, tile_row, told, devices, blocks, cuts):
    tiles = tile_values.shape[0]
    told = [x.reshape(-1, LANES) for x in told]
    noted = -(-(blocks + sum(x.shape[0] for x in told[:3])) // 16) * 16
    rows = [(high - low) * LANES for low, high in zip(cuts, cuts[1:])]
    rows[0] += noted
    return pl.pallas_call(
        functools.partial(pack_kernel, cuts),
        in_specs=[SMEM] * 3 + [VMEM] * 4 + [ANY],
        out_specs=[ANY] * len(rows),
        out_shape=[jax.ShapeDtypeStruct((devices, some, LANES), jnp.int16) for some in rows],
        scratch_shapes=[
            pltpu.VMEM(tile_values.shape, jnp.float32),
            pltpu.VMEM((devices * cuts[-1] * LANES, LANES), jnp.int16),
            pltpu.VMEM((blocks, LANES, LANES), jnp.float32),
            pltpu.VMEM((blocks, LANES), jnp.float32),
            pltpu.VMEM((noted, LANES), jnp.int32),
            pltpu.VMEM((noted, LANES), jnp.int16),
            pltpu.SMEM((devices,), jnp.int32),
            pltpu.SemaphoreType.DMA((len(rows) + 1, devices)),
            pltpu.SemaphoreType.DMA((tiles,)),
        ],
        compiler_params=params(),
        cost_estimate=pl.CostEstimate(
            flops=8 * tile_values.size,
            bytes_accessed=6 * tile_values.size,
            transcendentals=tile_values.size,
        ),
        name="pack",
    )(owner, rank, tile_row, *told, tile_values)


def stage_kernel(q, bases, last, cached, fold_list, fold_bound, score_list,
                 mods_in, signed_in, x_hbm, *refs):
    base = bases[q]
    earlier, refs = refs[:q], refs[q:]
    before, sums_in, squares_in, *made_in = refs[:5] if q else (None,) * 5
    refs = refs[5:] if q else refs
    part, sums_out, refs = refs[0], refs[1], refs[2:]
    (squares_out, *made_out, fresh_out), refs = ((None,) * 4, refs) if last else (refs[:4], refs[4:])
    spread, x, hot, sums, narrow, tiles, products, scores, squares, mods, signed, *refs = refs
    sems, sub_sems, tile_sems = refs
    devices, width = x.shape[0], x.shape[1] // LANES
    none = products.shape[0] - 1
    parts = len(bases) - 1

    def bound(p, sub):
        return fold_bound[p * (TB_OWN + 1) + sub]

    def score_bound(sub):
        return sum(bound(p, sub) - bound(p, 0) for p in range(parts))

    def complete(arrived):
        def one(i, least):
            sub = TB_OWN - 1 - i
            waits = [bound(p, sub + 1) > bound(p, sub) for p in range(arrived, parts)]
            return jnp.where(functools.reduce(jnp.logical_or, waits), sub, least)

        return lax.fori_loop(0, TB_OWN, one, TB_OWN) if arrived < parts else TB_OWN

    begin, end = complete(q) if q else 0, complete(q + 1)
    needed = [pltpu.make_async_copy(x_hbm.at[:, pl.ds(0, width * LANES)], x, sems.at[0])]
    if q:
        needed.append(pltpu.make_async_copy(made_in[0], spread, sems.at[1]))
    for copy in needed:
        copy.start()

    def columns(sub):
        return (slice(None), pl.ds(pl.multiple_of(sub * 2 * LANES, 2 * LANES), 2 * LANES))

    def sums_read(sub):
        return pltpu.make_async_copy(
            sums_in.at[columns(sub)], sums.at[columns(sub)], sub_sems.at[0, sub]
        )

    def sums_write(sub):
        return pltpu.make_async_copy(
            sums.at[columns(sub)], sums_out.at[columns(sub)], sub_sems.at[1, sub]
        )

    def each_sub(low, high, what):
        def one(sub, carry):
            what(sub)
            return carry

        lax.fori_loop(low, high, one, 0)

    if q:
        each_sub(begin, TB_OWN, lambda sub: sums_read(sub).start())
        squares[...] = squares_in[...]
    else:
        sums[...] = jnp.zeros_like(sums)
        squares[...] = jnp.zeros_like(squares)
    later = [pltpu.make_async_copy(made_in[1], hot, sems.at[3])] if q and cached else []
    for e, e_hbm in enumerate(earlier):
        held = tiles.at[pl.ds(bases[e], e_hbm.shape[0])]
        later.append(pltpu.make_async_copy(e_hbm, held, tile_sems.at[e]))
    products[...] = jnp.zeros_like(products)
    scores[...] = before[...] if q else jnp.zeros_like(scores)
    for held, given, empty in ((mods, mods_in, -1.0), (signed, signed_in, 0.0)):
        held[:none, :] = given[...]
        held[none : none + 1, :] = jnp.full((1, LANES), empty, jnp.float32)
    cluster = lax.broadcasted_iota(jnp.int32, (HALF, LANES), 0).astype(jnp.float32)
    cluster = cluster.astype(jnp.bfloat16).reshape(HALF // 16, 16, LANES)
    one, zero = jnp.ones((), jnp.bfloat16), jnp.zeros((), jnp.bfloat16)
    lane = lax.broadcasted_iota(jnp.int32, (LANES, LANES), 1)

    def column(ref, row):
        return jnp.transpose(jnp.broadcast_to(ref[pl.ds(row, 1), :], (LANES, LANES)))

    def one_hot(row):
        own = column(mods, row).astype(jnp.int32)
        some = [jnp.where(own == lane + g, 1.0, 0.0) for g in range(0, HALF, LANES)]
        return jnp.concatenate(some, axis=1).astype(jnp.bfloat16)

    batch = math.gcd(none + 1, 3)

    def build(c, carry):
        for j in range(batch):
            spread[c * batch + j] = column(signed, c * batch + j)
            if cached:
                hot[c * batch + j] = one_hot(c * batch + j)
        return carry

    if not q:
        lax.fori_loop(0, (none + 1) // batch, build, 0)
    for copy in needed:
        copy.wait()
    for copy in later:
        copy.start()

    def eight(entries, start, end, p):
        at = [start + EIGHT * p + j for j in range(EIGHT)]
        return [(entries[jnp.where(spot < end, spot, start)], spot < end) for spot in at]

    def fold_sub(sub):
        start, end = bound(q, sub), bound(q, sub + 1)
        if q:
            sums_read(sub).wait()

        def one_eight(p, carry):
            folded, picks = [], []
            for entry, held in eight(fold_list, start, end, p):
                row = entry >> ROW_SHIFT
                source, slot = (entry >> SOURCE_SHIFT) & SOURCE_MASK, entry & SLOT_MASK
                spot = base + source * width + slot
                raw = x[source, pl.ds(pl.multiple_of(slot * LANES, LANES), LANES), :]
                root = raw.astype(jnp.int32).astype(jnp.float32) + float(CODE_SHIFT)
                scale = spread[row]
                square = root * root
                tile = square * jnp.abs(scale)
                lower = square * jnp.maximum(scale, 0.0)
                tiles[spot] = tile.astype(jnp.bfloat16)
                halves = [lower.astype(jnp.bfloat16), (tile - lower).astype(jnp.bfloat16)]
                folded.append(jnp.concatenate(halves, axis=1))
                own = jnp.broadcast_to(mods[pl.ds(jnp.where(held, row, none), 1), :], (16, LANES))
                own = jnp.where(cluster == own.astype(jnp.bfloat16)[None], one, zero)
                picks.append(own.reshape(HALF, LANES))
            pick = jnp.concatenate(picks, axis=1)
            sums[columns(sub)] += jnp.dot(
                pick, jnp.concatenate(folded, axis=0), preferred_element_type=jnp.float32
            )
            return carry

        lax.fori_loop(0, (end - start + EIGHT - 1) // EIGHT, one_eight, 0)
        sums_write(sub).start()

    each_sub(begin, TB_OWN, fold_sub)
    kept = []
    if not last:
        fresh = tiles.at[pl.ds(base, devices * width)]
        kept.append(pltpu.make_async_copy(fresh, fresh_out, sems.at[2]))
        kept.append(pltpu.make_async_copy(spread, made_out[0], sems.at[4]))
        kept.append(pltpu.make_async_copy(hot, made_out[1], sems.at[5]))
    for copy in kept:
        copy.start()
    for copy in later:
        copy.wait()

    def score_sub(sub):
        start, end = score_bound(sub), score_bound(sub + 1)
        some = sums[columns(sub)]
        narrow[...] = some.astype(jnp.bfloat16)
        squares[...] += some * some

        def one_eight(p, carry):
            listed = eight(score_list, start, end, p)
            rows = [jnp.where(held, entry >> ROW_SHIFT, none) for entry, held in listed]
            spots = [entry & PLACE_MASK for entry, held in listed]
            hots = [hot[row] if cached else one_hot(row) for row in rows]
            chosen = jnp.dot(
                jnp.concatenate(hots, axis=0), narrow[...], preferred_element_type=jnp.float32
            )
            for j in range(EIGHT):
                both = chosen[j * LANES : (j + 1) * LANES]
                own = jnp.where(spread[rows[j]] < 0.0, both[:, LANES:], both[:, :LANES])
                products[rows[j]] += own * tiles[spots[j]].astype(jnp.float32)
            return carry

        lax.fori_loop(0, (end - start + EIGHT - 1) // EIGHT, one_eight, 0)

    each_sub(begin, end, score_sub)
    block_sums(products, scores, none)
    if last:
        own = none // devices
        square = [lane_sums(squares[:, h : h + LANES])[:1] for h in (0, LANES)]
        square = jnp.concatenate(square, axis=1)
        for d in range(devices):
            part[d, :, part.shape[2] - K :] = square
            for b in range(own):
                at = d * own + b
                part[d, :, b * LANES : (b + 1) * LANES] = scores[at : at + 1, :]
    else:
        part[...] = scores[...]
        squares_out[...] = squares[...]
    for copy in kept:
        copy.wait()
    each_sub(begin, TB_OWN, lambda sub: sums_write(sub).wait())


def stage(q, cuts, scalars, mods, signed, x, normed, totals):
    devices = x.shape[0]
    last = q == len(cuts) - 2
    blocks = mods.shape[0]
    cached = blocks <= CACHED_BLOCKS
    width = cuts[q + 1] - cuts[q]
    home = blocks // devices * LANES
    wide = jax.ShapeDtypeStruct((HALF, TB_OWN * 2 * LANES), jnp.float32)
    square = jax.ShapeDtypeStruct((HALF, 2 * LANES), jnp.float32)
    if last:
        out_shape = [jax.ShapeDtypeStruct((devices, 1, home + K), jnp.float32), wide]
    else:
        out_shape = [
            jax.ShapeDtypeStruct((blocks, LANES), jnp.float32),
            wide,
            square,
            jax.ShapeDtypeStruct((blocks + 1, LANES, LANES), jnp.float32),
            jax.ShapeDtypeStruct((blocks + 1 if cached else 1, LANES, HALF), jnp.bfloat16),
            jax.ShapeDtypeStruct((devices * width, LANES, LANES), jnp.bfloat16),
        ]
    slots = devices * cuts[-1]
    operands = [*scalars, mods, signed, x, *normed, *totals]
    return pl.pallas_call(
        functools.partial(stage_kernel, q, [devices * cut for cut in cuts], last, cached),
        in_specs=[SMEM] * len(scalars) + [VMEM] * 2 + [ANY] * (1 + q) + [VMEM, ANY, VMEM, ANY, ANY][: len(totals)],
        out_specs=[VMEM, ANY, VMEM, ANY, ANY, ANY][: len(out_shape)],
        out_shape=out_shape,
        input_output_aliases={len(operands) - len(totals) + 1: 1} if q else {},
        scratch_shapes=[
            pltpu.VMEM((blocks + 1, LANES, LANES), jnp.float32),
            pltpu.VMEM((devices, width * LANES, LANES), jnp.int16),
            pltpu.VMEM((blocks + 1 if cached else 1, LANES, HALF), jnp.bfloat16),
            pltpu.VMEM(wide.shape, jnp.float32),
            pltpu.VMEM(square.shape, jnp.bfloat16),
            pltpu.VMEM((slots, LANES, LANES), jnp.bfloat16),
            pltpu.VMEM((blocks + 1, LANES, LANES), jnp.float32),
            pltpu.VMEM((blocks, LANES), jnp.float32),
            pltpu.VMEM(square.shape, jnp.float32),
            pltpu.VMEM((blocks + 1, LANES), jnp.float32),
            pltpu.VMEM((blocks + 1, LANES), jnp.float32),
            pltpu.SemaphoreType.DMA((6,)),
            pltpu.SemaphoreType.DMA((2, TB_OWN)),
            pltpu.SemaphoreType.DMA((len(cuts),)),
        ],
        compiler_params=params(),
        cost_estimate=pl.CostEstimate(
            flops=devices * width * LANES * LANES * K * 8,
            bytes_accessed=4 * devices * width * LANES * LANES + 8 * K * TB_OWN * LANES,
            transcendentals=0,
        ),
        name="stage",
    )(*operands)


def close_kernel(root, groups, labels_ref, got_ref, sums_hbm, out_hbm, similarity, sums, out, sems):
    width = TB_OWN // groups
    reads, writes = [], []
    for g in range(groups):
        some = (slice(None), pl.ds(g * width * 2 * LANES, width * 2 * LANES))
        reads.append(pltpu.make_async_copy(sums_hbm.at[some], sums.at[some], sems.at[0, g]))
        some = (slice(None), pl.ds(g * width * LANES, width * LANES))
        writes.append(pltpu.make_async_copy(out.at[some], out_hbm.at[some], sems.at[1, g]))
        reads[g].start()
    total = jnp.sum(got_ref[...], axis=0)
    home = total.shape[1] - K
    own = lax.rsqrt(total[:, home:] + EPSILON)
    columns = [
        jnp.transpose(jnp.broadcast_to(own[:, k : k + LANES], (LANES, LANES)))
        for k in range(0, K, LANES)
    ]
    cluster = lax.broadcasted_iota(jnp.int32, (LANES, LANES), 0)
    for b in range(home // LANES):
        found = jnp.zeros((LANES, LANES), jnp.float32)
        for i, column in enumerate(columns):
            found += jnp.where(cluster + i * LANES == labels_ref[b : b + 1, :], column, 0.0)
        found = jnp.sum(found, axis=0, keepdims=True)
        similarity[b : b + 1, :] = total[:, b * LANES : (b + 1) * LANES] * found
    for g in range(groups):
        reads[g].wait()

        def one_sub(sub, carry):
            to = pl.ds(pl.multiple_of(sub * LANES, LANES), LANES)
            for i, column in enumerate(columns):
                half, row = divmod(i * LANES, HALF)
                at = pl.ds(pl.multiple_of((2 * sub + half) * LANES, LANES), LANES)
                done = sums[row : row + LANES, at] * column * root
                out[i * LANES : (i + 1) * LANES, to] = done.astype(jnp.bfloat16)
            return carry

        lax.fori_loop(g * width, (g + 1) * width, one_sub, 0)
        writes[g].start()
    for write in writes:
        write.wait()


def close(labels, got, sums, vocab_size):
    groups = 4
    labels = labels.reshape(-1, LANES)
    wide = jax.ShapeDtypeStruct((K, TB_OWN * LANES), jnp.bfloat16)
    centroids, similarity = pl.pallas_call(
        functools.partial(close_kernel, math.sqrt(vocab_size), groups),
        in_specs=[VMEM, VMEM, ANY],
        out_specs=[ANY, VMEM],
        out_shape=[wide, jax.ShapeDtypeStruct(labels.shape, jnp.float32)],
        scratch_shapes=[
            pltpu.VMEM(sums.shape, jnp.float32),
            pltpu.VMEM(wide.shape, jnp.bfloat16),
            pltpu.SemaphoreType.DMA((2, groups)),
        ],
        compiler_params=params(),
        cost_estimate=pl.CostEstimate(
            flops=2 * sums.size, bytes_accessed=6 * sums.size, transcendentals=0
        ),
        name="close",
    )(labels, got, sums)
    return centroids, similarity.reshape(-1)


def exchange(x):
    return lax.all_to_all(x, "dp", split_axis=0, concat_axis=0, tiled=True)


def after(value, *others):
    return lax.optimization_barrier((value, *others))[0]


def sorted_slots(key, top, entries):
    slots = jnp.arange(key.shape[0], dtype=jnp.int32)
    ahead = (key[None, :] < key[:, None]) | (
        (key[None, :] == key[:, None]) & (slots[None, :] < slots[:, None])
    )
    position = jnp.sum(ahead.astype(jnp.int32), axis=1)
    here = position[None, :] == slots[:, None]
    listed = jnp.sum(jnp.where(here, entries[None, :], 0), axis=1)
    levels = jnp.arange(top + 1, dtype=jnp.int32)
    bounds = jnp.sum((key[None, :] < levels[:, None]).astype(jnp.int32), axis=1)
    return listed, bounds


def ranks(group, sub):
    index = jnp.arange(sub.shape[-1], dtype=jnp.int32)
    before = (sub[..., None, :] < sub[..., :, None]) | (
        (sub[..., None, :] == sub[..., :, None]) & (index[None, :] < index[:, None])
    )
    same = group[..., None, :] == group[..., :, None]
    return jnp.sum((before & same).astype(jnp.int32), axis=-1)


def shards(tile_values, tile_row, tile_owner, tile_sub, labels):
    devices = lax.axis_size("dp")
    tiles = tile_values.shape[0]
    home = labels.shape[0]
    blocks = home // LANES * devices
    cap = max(2, 2 * tiles // devices)
    cuts = tuple(sorted({int(cap * share) for share in PARTS})) if cap >= 8 else (0, cap)
    parts = len(cuts) - 1
    here = lax.axis_index("dp").astype(jnp.int32)
    owner = tile_owner[:, 0]

    told = (labels, owner, tile_row, tile_sub)
    rank = ranks(owner, tile_sub)
    outgoing = pack(tile_values, owner, rank, tile_row, told, devices, blocks, cuts)
    incoming = [exchange(outgoing[0])]
    heard = incoming[0][:, (cuts[1] - cuts[0]) * LANES :].astype(jnp.int32)
    level = heard[:, :blocks]
    partial_sq = jnp.exp2(level.astype(jnp.float32) * (1.0 / LOG_STEPS) + LOG_MIDDLE)
    row_sq = jnp.sum(jnp.where(level > -32768, partial_sq, 0.0), axis=0)
    all_described = heard[:, blocks:].reshape(devices, -1)
    all_labels = all_described[:, :home].reshape(blocks, LANES)
    mine = all_described[:, home : home + tiles] == here
    code = all_described[:, home + tiles : home + 2 * tiles]
    rank = ranks(mine.astype(jnp.int32), code % TB_OWN)
    chosen = mine[:, None, :] & (rank[:, None, :] == jnp.arange(cap)[None, :, None])
    meta = jnp.sum(jnp.where(chosen, code[:, None, :] + 1, 0), axis=2).reshape(-1) - 1
    sub = jnp.where(meta < 0, TB_OWN, meta % TB_OWN)
    slot_rank = np.arange(devices * cap) % cap
    slot_part = np.searchsorted(np.array(cuts), slot_rank, side="right") - 1
    low, high = np.array(cuts)[slot_part], np.array(cuts)[slot_part + 1]
    place = devices * low + np.arange(devices * cap) // cap * (high - low) + slot_rank - low
    fold_key = jnp.asarray(slot_part * (TB_OWN + 1), jnp.int32) + sub
    row = (meta // TB_OWN) << ROW_SHIFT
    from_slot = (np.arange(devices * cap) // cap << SOURCE_SHIFT) + slot_rank - low
    fold_list, fold_bounds = sorted_slots(
        fold_key, parts * (TB_OWN + 1), row + jnp.asarray(from_slot, jnp.int32)
    )
    score_list, _ = sorted_slots(sub, TB_OWN, row + jnp.asarray(place, jnp.int32))
    scalars = [fold_list, fold_bounds, score_list]

    scale = lax.rsqrt(row_sq + EPSILON) * (1.0 / CODE_TOP**2)
    signed = jnp.where(all_labels < HALF, scale, -scale)
    mods = (all_labels % HALF).astype(jnp.float32)
    totals, normed = (), []
    beside = (*scalars, mods, signed)
    for q in range(parts):
        if q + 1 < parts:
            ahead = (incoming[q], *beside) if q else (incoming[q],)
            incoming.append(exchange(after(outgoing[q + 1], *ahead)))
        partial, sums, *more = stage(
            q, cuts, scalars, mods, signed, incoming[q], normed, totals
        )
        beside = (partial, sums)
        totals, normed = (partial, sums, *more[:3]), normed + more[3:]
    return close(labels, exchange(partial), sums, TB_OWN * LANES * devices)


def solution(mesh):
    return jax.shard_map(
        shards,
        mesh=mesh,
        in_specs=(
            P(("groups", "dp"), None, None),
            P(("groups", "dp")),
            P(("groups", "dp"), None),
            P(("groups", "dp")),
            P(("groups", "dp")),
        ),
        out_specs=(P("groups", "dp"), P(("groups", "dp"))),
        check_vma=False,
    )
```

```python
import functools
import math

import jax
import jax.numpy as jnp
import numpy as np
from jax import lax
from jax.experimental import pallas as pl
from jax.experimental.pallas import tpu as pltpu
from jax.sharding import PartitionSpec as P

K = 512
HALF = K // 2
TB_OWN = 16
LANES = 128
EPSILON = 1e-06
CODE_TOP = 65535.0
CODE_SHIFT = 32768
VMEM_BYTES = 60 * 1024 * 1024
STEP_TILES = 16
PARTS = (0.0, 13 / 16, 1.0)
LOG_STEPS = 1800.0
LOG_MIDDLE = -3.0
CACHED_BLOCKS = 64
QUAD = 4
EIGHT = 8
CHUNK = 16
ROW_SHIFT, SOURCE_SHIFT = 16, 8
PLACE_MASK, SOURCE_MASK, SLOT_MASK = 0xFFFF, 0xFF, 0xFF
BATCH = 8
NT = (((1,), (1,)), ((), ()))
SMEM = pl.BlockSpec(memory_space=pltpu.SMEM)
VMEM = pl.BlockSpec(memory_space=pltpu.VMEM)
ANY = pl.BlockSpec(memory_space=pl.ANY)


def lane_sums(values):
    ones = jnp.ones((8, 2 * LANES), jnp.bfloat16)
    high = values.astype(jnp.bfloat16)
    low = (values - high.astype(jnp.float32)).astype(jnp.bfloat16)
    both = jnp.concatenate([high, low], axis=1)
    return lax.dot_general(ones, both, NT, preferred_element_type=jnp.float32)


def block_sums(square, out_ref, count):
    batch = math.gcd(BATCH, count)

    def one_batch(c, carry):
        some = square[pl.ds(c * batch, batch)].reshape((batch * LANES, LANES))
        sums = lane_sums(some)
        for j in range(batch):
            out_ref[pl.ds(c * batch + j, 1), :] += sums[:1, j * LANES : (j + 1) * LANES]
        return carry

    lax.fori_loop(0, count // batch, one_batch, 0)


def params():
    return pltpu.CompilerParams(vmem_limit_bytes=VMEM_BYTES)


def pack_kernel(cuts, owner_ref, row_ref, *refs):
    parts = len(cuts) - 1
    (*told_refs, x_hbm), refs = refs[:5], refs[5:]
    outs = refs[:parts]
    x, coded, square, sums, words, notes, held, rank_row, rank_ref, sems, x_sems = refs[parts:]
    tiles = x.shape[0]
    devices = held.shape[0]
    blocks = square.shape[0]
    step = math.gcd(STEP_TILES, tiles)

    def read(c):
        some = pl.ds(c * step, step)
        return pltpu.make_async_copy(x_hbm.at[some], x.at[some], x_sems.at[c])

    def clear(d, carry):
        held[d] = 0
        return carry

    for c in range(tiles // step):
        read(c).start()
    labels, owner, row, sub = [ref[...] for ref in told_refs]
    own, sub_own = [jnp.broadcast_to(v.astype(jnp.float32), (tiles, tiles)) for v in (owner, sub)]
    other, sub_other = jnp.transpose(own), jnp.transpose(sub_own)
    index = [lax.broadcasted_iota(jnp.int32, (tiles, tiles), d) for d in (0, 1)]
    ahead = (sub_other < sub_own) | ((sub_other == sub_own) & (index[0] < index[1]))
    ahead = jnp.where(ahead & (other == own), 1.0, 0.0)
    rank_row[...] = jnp.sum(ahead, axis=0, keepdims=True).astype(jnp.int32)
    pltpu.sync_copy(rank_row, rank_ref)
    lax.fori_loop(0, devices, clear, 0)
    square[...] = jnp.zeros_like(square)

    def some_tiles(i, carry):
        pl.when(i % (step // QUAD) == 0)(lambda: read(i // (step // QUAD)).wait())
        for j in range(QUAD):
            t = i * QUAD + j
            some = x[t]
            root = some * lax.rsqrt(some)
            code = (root * CODE_TOP + 0.5).astype(jnp.int32) - CODE_SHIFT
            owner, rank = owner_ref[t], rank_ref[0, t]
            at = pl.ds(pl.multiple_of((owner * cuts[-1] + rank) * LANES, LANES), LANES)
            coded[at, :] = code.astype(jnp.int16)
            square[row_ref[t]] += some * some
            held[owner] = jnp.maximum(held[owner], rank + 1)
        return carry

    lax.fori_loop(0, tiles // QUAD, some_tiles, 0)

    def slots(q, d):
        some = pl.ds((d * cuts[-1] + cuts[q]) * LANES, (cuts[q + 1] - cuts[q]) * LANES)
        into = outs[q].at[d, pl.ds(0, (cuts[q + 1] - cuts[q]) * LANES)]
        return pltpu.make_async_copy(coded.at[some], into, sems.at[q, d])

    def note(d):
        into = outs[0].at[d, pl.ds((cuts[1] - cuts[0]) * LANES, notes.shape[0])]
        return pltpu.make_async_copy(notes, into, sems.at[parts, d])

    def each(what):
        def one(d, carry):
            for q in range(parts):
                pl.when(held[d] > cuts[q])(lambda q=q: what(slots(q, d)))
            return carry

        lax.fori_loop(0, devices, one, 0)

    each(lambda copy: copy.start())
    sums[...] = jnp.zeros_like(sums)
    block_sums(square, sums, blocks)
    total = sums[...]
    level = (jnp.log2(jnp.maximum(total, 1e-30)) - LOG_MIDDLE) * LOG_STEPS
    level = jnp.where(total > 0.0, jnp.clip(level, -32700.0, 32700.0), -32768.0)
    level = (level + 32768.5).astype(jnp.int32) - 32768
    words[...] = jnp.zeros_like(words)
    words[:blocks, :] = level
    at = blocks
    for told in (labels, owner, row * TB_OWN + sub):
        words[at : at + told.shape[0], :] = told
        at += told.shape[0]
    notes[...] = words[...].astype(jnp.int16)

    for d in range(devices):
        note(d).start()
    each(lambda copy: copy.wait())
    for d in range(devices):
        note(d).wait()


def pack(tile_values, owner, tile_row, told, devices, blocks, cuts):
    tiles = tile_values.shape[0]
    told = [x.reshape(-1, LANES) for x in told]
    noted = -(-(blocks + sum(x.shape[0] for x in told[:3])) // 16) * 16
    rows = [(high - low) * LANES for low, high in zip(cuts, cuts[1:])]
    rows[0] += noted
    return pl.pallas_call(
        functools.partial(pack_kernel, cuts),
        in_specs=[SMEM] * 2 + [VMEM] * 4 + [ANY],
        out_specs=[ANY] * len(rows),
        out_shape=[jax.ShapeDtypeStruct((devices, some, LANES), jnp.int16) for some in rows],
        scratch_shapes=[
            pltpu.VMEM(tile_values.shape, jnp.float32),
            pltpu.VMEM((devices * cuts[-1] * LANES, LANES), jnp.int16),
            pltpu.VMEM((blocks, LANES, LANES), jnp.float32),
            pltpu.VMEM((blocks, LANES), jnp.float32),
            pltpu.VMEM((noted, LANES), jnp.int32),
            pltpu.VMEM((noted, LANES), jnp.int16),
            pltpu.SMEM((devices,), jnp.int32),
            pltpu.VMEM((1, tiles), jnp.int32),
            pltpu.SMEM((1, tiles), jnp.int32),
            pltpu.SemaphoreType.DMA((len(rows) + 1, devices)),
            pltpu.SemaphoreType.DMA((tiles,)),
        ],
        compiler_params=params(),
        cost_estimate=pl.CostEstimate(
            flops=8 * tile_values.size,
            bytes_accessed=6 * tile_values.size,
            transcendentals=tile_values.size,
        ),
        name="pack",
    )(owner, tile_row, *told, tile_values)


def stage_kernel(q, bases, last, cached, fold_list, fold_bound, score_list,
                 mods_in, signed_in, x_hbm, *refs):
    base = bases[q]
    earlier, refs = refs[:q], refs[q:]
    before, sums_in, squares_in, *made_in = refs[:5] if q else (None,) * 5
    refs = refs[5:] if q else refs
    part, sums_out, refs = refs[0], refs[1], refs[2:]
    (squares_out, *made_out, fresh_out), refs = ((None,) * 4, refs) if last else (refs[:4], refs[4:])
    spread, x, hot, sums, narrow, tiles, products, scores, squares, mods, signed, *refs = refs
    sems, sub_sems, tile_sems = refs
    devices, width = x.shape[0], x.shape[1] // LANES
    none = products.shape[0] - 1
    parts = len(bases) - 1

    def bound(p, sub):
        return fold_bound[p * (TB_OWN + 1) + sub]

    def score_bound(sub):
        return sum(bound(p, sub) - bound(p, 0) for p in range(parts))

    def complete(arrived):
        def one(i, least):
            sub = TB_OWN - 1 - i
            waits = [bound(p, sub + 1) > bound(p, sub) for p in range(arrived, parts)]
            return jnp.where(functools.reduce(jnp.logical_or, waits), sub, least)

        return lax.fori_loop(0, TB_OWN, one, TB_OWN) if arrived < parts else TB_OWN

    begin, end = complete(q) if q else 0, complete(q + 1)
    needed = [pltpu.make_async_copy(x_hbm.at[:, pl.ds(0, width * LANES)], x, sems.at[0])]
    if q:
        needed.append(pltpu.make_async_copy(made_in[0], spread, sems.at[1]))
    for copy in needed:
        copy.start()

    def columns(sub):
        return (slice(None), pl.ds(pl.multiple_of(sub * 2 * LANES, 2 * LANES), 2 * LANES))

    def sums_read(sub):
        return pltpu.make_async_copy(
            sums_in.at[columns(sub)], sums.at[columns(sub)], sub_sems.at[0, sub]
        )

    def sums_write(sub):
        return pltpu.make_async_copy(
            sums.at[columns(sub)], sums_out.at[columns(sub)], sub_sems.at[1, sub]
        )

    def each_sub(low, high, what):
        def one(sub, carry):
            what(sub)
            return carry

        lax.fori_loop(low, high, one, 0)

    if q:
        each_sub(begin, TB_OWN, lambda sub: sums_read(sub).start())
        squares[...] = squares_in[...]
    else:
        sums[...] = jnp.zeros_like(sums)
        squares[...] = jnp.zeros_like(squares)
    later = [pltpu.make_async_copy(made_in[1], hot, sems.at[3])] if q and cached else []

    def each_chunk(p, outside, write, sub, what):
        count = math.gcd(CHUNK, bases[p + 1] - bases[p])

        def one(c, carry):
            away, own = outside.at[pl.ds(c * count, count)], tiles.at[pl.ds(bases[p] + c * count, count)]
            some = (own, away) if write else (away, own)
            what(pltpu.make_async_copy(*some, tile_sems.at[p, c]))
            return carry

        first, stop = bound(p, sub) - bases[p], bound(p, TB_OWN) - bases[p]
        lax.fori_loop(first // count, (stop + count - 1) // count, one, 0)

    def each_earlier(what):
        for copy in later:
            what(copy)
        for e, e_hbm in enumerate(earlier):
            each_chunk(e, e_hbm, False, begin, what)

    each_earlier(lambda copy: copy.start())
    products[...] = jnp.zeros_like(products)
    scores[...] = before[...] if q else jnp.zeros_like(scores)
    for held, given, empty in ((mods, mods_in, -1.0), (signed, signed_in, 0.0)):
        held[:none, :] = given[...]
        held[none : none + 1, :] = jnp.full((1, LANES), empty, jnp.float32)
    cluster = lax.broadcasted_iota(jnp.int32, (HALF, LANES), 0).astype(jnp.float32)
    cluster = cluster.astype(jnp.bfloat16).reshape(HALF // 16, 16, LANES)
    one, zero = jnp.ones((), jnp.bfloat16), jnp.zeros((), jnp.bfloat16)
    lane = lax.broadcasted_iota(jnp.int32, (LANES, LANES), 1)

    def column(ref, row):
        return jnp.transpose(jnp.broadcast_to(ref[pl.ds(row, 1), :], (LANES, LANES)))

    def one_hot(row):
        own = column(mods, row).astype(jnp.int32)
        some = [jnp.where(own == lane + g, 1.0, 0.0) for g in range(0, HALF, LANES)]
        return jnp.concatenate(some, axis=1).astype(jnp.bfloat16)

    batch = math.gcd(none + 1, 3)

    def build(c, carry):
        for j in range(batch):
            spread[c * batch + j] = column(signed, c * batch + j)
            if cached:
                hot[c * batch + j] = one_hot(c * batch + j)
        return carry

    if not q:
        lax.fori_loop(0, (none + 1) // batch, build, 0)
    for copy in needed:
        copy.wait()

    def eight(entries, start, end, p):
        at = [start + EIGHT * p + j for j in range(EIGHT)]
        at = [(jnp.where(spot < end, spot, start), spot < end) for spot in at]
        return [(entries[spot], spot, held) for spot, held in at]

    def fold_sub(sub):
        start, end = bound(q, sub), bound(q, sub + 1)
        if q:
            sums_read(sub).wait()

        def one_eight(p, carry):
            folded, picks = [], []
            for entry, spot, held in eight(fold_list, start, end, p):
                row = entry >> ROW_SHIFT
                source, slot = (entry >> SOURCE_SHIFT) & SOURCE_MASK, entry & SLOT_MASK
                raw = x[source, pl.ds(pl.multiple_of(slot * LANES, LANES), LANES), :]
                root = raw.astype(jnp.int32).astype(jnp.float32) + float(CODE_SHIFT)
                scale = spread[row]
                square = root * root
                tile = square * jnp.abs(scale)
                lower = square * jnp.maximum(scale, 0.0)
                tiles[spot] = tile.astype(jnp.bfloat16)
                halves = [lower.astype(jnp.bfloat16), (tile - lower).astype(jnp.bfloat16)]
                folded.append(jnp.concatenate(halves, axis=1))
                own = jnp.broadcast_to(mods[pl.ds(jnp.where(held, row, none), 1), :], (16, LANES))
                own = jnp.where(cluster == own.astype(jnp.bfloat16)[None], one, zero)
                picks.append(own.reshape(HALF, LANES))
            pick = jnp.concatenate(picks, axis=1)
            sums[columns(sub)] += jnp.dot(
                pick, jnp.concatenate(folded, axis=0), preferred_element_type=jnp.float32
            )
            return carry

        lax.fori_loop(0, (end - start + EIGHT - 1) // EIGHT, one_eight, 0)
        sums_write(sub).start()

    each_sub(begin, TB_OWN, fold_sub)
    kept = []
    if not last:
        each_chunk(q, fresh_out, True, end, lambda copy: copy.start())
        kept.append(pltpu.make_async_copy(spread, made_out[0], sems.at[4]))
        kept.append(pltpu.make_async_copy(hot, made_out[1], sems.at[5]))
    for copy in kept:
        copy.start()
    each_earlier(lambda copy: copy.wait())

    def score_sub(sub):
        start, end = score_bound(sub), score_bound(sub + 1)
        some = sums[columns(sub)]
        narrow[...] = some.astype(jnp.bfloat16)
        squares[...] += some * some

        def one_eight(p, carry):
            listed = eight(score_list, start, end, p)
            rows = [jnp.where(held, entry >> ROW_SHIFT, none) for entry, spot, held in listed]
            spots = [entry & PLACE_MASK for entry, spot, held in listed]
            hots = [hot[row] if cached else one_hot(row) for row in rows]
            chosen = jnp.dot(
                jnp.concatenate(hots, axis=0), narrow[...], preferred_element_type=jnp.float32
            )
            for j in range(EIGHT):
                both = chosen[j * LANES : (j + 1) * LANES]
                own = jnp.where(spread[rows[j]] < 0.0, both[:, LANES:], both[:, :LANES])
                products[rows[j]] += own * tiles[spots[j]].astype(jnp.float32)
            return carry

        lax.fori_loop(0, (end - start + EIGHT - 1) // EIGHT, one_eight, 0)

    each_sub(begin, end, score_sub)
    block_sums(products, scores, none)
    if last:
        own = none // devices
        square = [lane_sums(squares[:, h : h + LANES])[:1] for h in (0, LANES)]
        square = jnp.concatenate(square, axis=1)
        for d in range(devices):
            part[d, :, part.shape[2] - K :] = square
            for b in range(own):
                at = d * own + b
                part[d, :, b * LANES : (b + 1) * LANES] = scores[at : at + 1, :]
    else:
        part[...] = scores[...]
        squares_out[...] = squares[...]
    for copy in kept:
        copy.wait()
    if not last:
        each_chunk(q, fresh_out, True, end, lambda copy: copy.wait())
    each_sub(begin, TB_OWN, lambda sub: sums_write(sub).wait())


def stage(q, cuts, scalars, mods, signed, x, normed, totals):
    devices = x.shape[0]
    last = q == len(cuts) - 2
    blocks = mods.shape[0]
    cached = blocks <= CACHED_BLOCKS
    width = cuts[q + 1] - cuts[q]
    home = blocks // devices * LANES
    wide = jax.ShapeDtypeStruct((HALF, TB_OWN * 2 * LANES), jnp.float32)
    square = jax.ShapeDtypeStruct((HALF, 2 * LANES), jnp.float32)
    if last:
        out_shape = [jax.ShapeDtypeStruct((devices, 1, home + K), jnp.float32), wide]
    else:
        out_shape = [
            jax.ShapeDtypeStruct((blocks, LANES), jnp.float32),
            wide,
            square,
            jax.ShapeDtypeStruct((blocks + 1, LANES, LANES), jnp.float32),
            jax.ShapeDtypeStruct((blocks + 1 if cached else 1, LANES, HALF), jnp.bfloat16),
            jax.ShapeDtypeStruct((devices * width, LANES, LANES), jnp.bfloat16),
        ]
    slots = devices * cuts[-1]
    operands = [*scalars, mods, signed, x, *normed, *totals]
    return pl.pallas_call(
        functools.partial(stage_kernel, q, [devices * cut for cut in cuts], last, cached),
        in_specs=[SMEM] * len(scalars) + [VMEM] * 2 + [ANY] * (1 + q) + [VMEM, ANY, VMEM, ANY, ANY][: len(totals)],
        out_specs=[VMEM, ANY, VMEM, ANY, ANY, ANY][: len(out_shape)],
        out_shape=out_shape,
        input_output_aliases={len(operands) - len(totals) + 1: 1} if q else {},
        scratch_shapes=[
            pltpu.VMEM((blocks + 1, LANES, LANES), jnp.float32),
            pltpu.VMEM((devices, width * LANES, LANES), jnp.int16),
            pltpu.VMEM((blocks + 1 if cached else 1, LANES, HALF), jnp.bfloat16),
            pltpu.VMEM(wide.shape, jnp.float32),
            pltpu.VMEM(square.shape, jnp.bfloat16),
            pltpu.VMEM((slots, LANES, LANES), jnp.bfloat16),
            pltpu.VMEM((blocks + 1, LANES, LANES), jnp.float32),
            pltpu.VMEM((blocks, LANES), jnp.float32),
            pltpu.VMEM(square.shape, jnp.float32),
            pltpu.VMEM((blocks + 1, LANES), jnp.float32),
            pltpu.VMEM((blocks + 1, LANES), jnp.float32),
            pltpu.SemaphoreType.DMA((6,)),
            pltpu.SemaphoreType.DMA((2, TB_OWN)),
            pltpu.SemaphoreType.DMA((len(cuts), slots)),
        ],
        compiler_params=params(),
        cost_estimate=pl.CostEstimate(
            flops=devices * width * LANES * LANES * K * 8,
            bytes_accessed=4 * devices * width * LANES * LANES + 8 * K * TB_OWN * LANES,
            transcendentals=0,
        ),
        name="stage",
    )(*operands)


def close_kernel(root, groups, labels_ref, got_ref, sums_hbm, out_hbm, similarity, sums, out, sems):
    width = TB_OWN // groups
    reads, writes = [], []
    for g in range(groups):
        some = (slice(None), pl.ds(g * width * 2 * LANES, width * 2 * LANES))
        reads.append(pltpu.make_async_copy(sums_hbm.at[some], sums.at[some], sems.at[0, g]))
        some = (slice(None), pl.ds(g * width * LANES, width * LANES))
        writes.append(pltpu.make_async_copy(out.at[some], out_hbm.at[some], sems.at[1, g]))
        reads[g].start()
    total = jnp.sum(got_ref[...], axis=0)
    home = total.shape[1] - K
    own = lax.rsqrt(total[:, home:] + EPSILON)
    columns = [
        jnp.transpose(jnp.broadcast_to(own[:, k : k + LANES], (LANES, LANES)))
        for k in range(0, K, LANES)
    ]
    cluster = lax.broadcasted_iota(jnp.int32, (LANES, LANES), 0)
    for b in range(home // LANES):
        found = jnp.zeros((LANES, LANES), jnp.float32)
        for i, column in enumerate(columns):
            found += jnp.where(cluster + i * LANES == labels_ref[b : b + 1, :], column, 0.0)
        found = jnp.sum(found, axis=0, keepdims=True)
        similarity[b : b + 1, :] = total[:, b * LANES : (b + 1) * LANES] * found
    for g in range(groups):
        reads[g].wait()

        def one_sub(sub, carry):
            to = pl.ds(pl.multiple_of(sub * LANES, LANES), LANES)
            for i, column in enumerate(columns):
                half, row = divmod(i * LANES, HALF)
                at = pl.ds(pl.multiple_of((2 * sub + half) * LANES, LANES), LANES)
                done = sums[row : row + LANES, at] * column * root
                out[i * LANES : (i + 1) * LANES, to] = done.astype(jnp.bfloat16)
            return carry

        lax.fori_loop(g * width, (g + 1) * width, one_sub, 0)
        writes[g].start()
    for write in writes:
        write.wait()


def close(labels, got, sums, vocab_size):
    groups = 4
    labels = labels.reshape(-1, LANES)
    wide = jax.ShapeDtypeStruct((K, TB_OWN * LANES), jnp.bfloat16)
    centroids, similarity = pl.pallas_call(
        functools.partial(close_kernel, math.sqrt(vocab_size), groups),
        in_specs=[VMEM, VMEM, ANY],
        out_specs=[ANY, VMEM],
        out_shape=[wide, jax.ShapeDtypeStruct(labels.shape, jnp.float32)],
        scratch_shapes=[
            pltpu.VMEM(sums.shape, jnp.float32),
            pltpu.VMEM(wide.shape, jnp.bfloat16),
            pltpu.SemaphoreType.DMA((2, groups)),
        ],
        compiler_params=params(),
        cost_estimate=pl.CostEstimate(
            flops=2 * sums.size, bytes_accessed=6 * sums.size, transcendentals=0
        ),
        name="close",
    )(labels, got, sums)
    return centroids, similarity.reshape(-1)


def exchange(x):
    return lax.all_to_all(x, "dp", split_axis=0, concat_axis=0, tiled=True)


def after(value, *others):
    return lax.optimization_barrier((value, *others))[0]


def sorted_slots(key, top, entries):
    slots = jnp.arange(key.shape[0], dtype=jnp.int32)
    ahead = (key[None, :] < key[:, None]) | (
        (key[None, :] == key[:, None]) & (slots[None, :] < slots[:, None])
    )
    position = jnp.sum(ahead.astype(jnp.int32), axis=1)
    here = position[None, :] == slots[:, None]
    listed = jnp.sum(jnp.where(here, entries[None, :], 0), axis=1)
    levels = jnp.arange(top + 1, dtype=jnp.int32)
    bounds = jnp.sum((key[None, :] < levels[:, None]).astype(jnp.int32), axis=1)
    return listed, bounds, position


def ranks(group, sub):
    index = jnp.arange(sub.shape[-1], dtype=jnp.int32)
    before = (sub[..., None, :] < sub[..., :, None]) | (
        (sub[..., None, :] == sub[..., :, None]) & (index[None, :] < index[:, None])
    )
    same = group[..., None, :] == group[..., :, None]
    return jnp.sum((before & same).astype(jnp.int32), axis=-1)


def shards(tile_values, tile_row, tile_owner, tile_sub, labels):
    devices = lax.axis_size("dp")
    tiles = tile_values.shape[0]
    home = labels.shape[0]
    blocks = home // LANES * devices
    cap = max(2, 2 * tiles // devices)
    cuts = tuple(sorted({int(cap * share) for share in PARTS})) if cap >= 8 else (0, cap)
    parts = len(cuts) - 1
    here = lax.axis_index("dp").astype(jnp.int32)
    owner = tile_owner[:, 0]

    told = (labels, owner, tile_row, tile_sub)
    outgoing = pack(tile_values, owner, tile_row, told, devices, blocks, cuts)
    incoming = [exchange(outgoing[0])]
    heard = incoming[0][:, (cuts[1] - cuts[0]) * LANES :].astype(jnp.int32)
    level = heard[:, :blocks]
    partial_sq = jnp.exp2(level.astype(jnp.float32) * (1.0 / LOG_STEPS) + LOG_MIDDLE)
    row_sq = jnp.sum(jnp.where(level > -32768, partial_sq, 0.0), axis=0)
    all_described = heard[:, blocks:].reshape(devices, -1)
    all_labels = all_described[:, :home].reshape(blocks, LANES)
    mine = all_described[:, home : home + tiles] == here
    code = all_described[:, home + tiles : home + 2 * tiles]
    rank = ranks(mine.astype(jnp.int32), code % TB_OWN)
    chosen = mine[:, None, :] & (rank[:, None, :] == jnp.arange(cap)[None, :, None])
    meta = jnp.sum(jnp.where(chosen, code[:, None, :] + 1, 0), axis=2).reshape(-1) - 1
    sub = jnp.where(meta < 0, TB_OWN, meta % TB_OWN)
    slot_rank = np.arange(devices * cap) % cap
    slot_part = np.searchsorted(np.array(cuts), slot_rank, side="right") - 1
    low = np.array(cuts)[slot_part]
    fold_key = jnp.asarray(slot_part * (TB_OWN + 1), jnp.int32) + sub
    row = (meta // TB_OWN) << ROW_SHIFT
    from_slot = (np.arange(devices * cap) // cap << SOURCE_SHIFT) + slot_rank - low
    fold_list, fold_bounds, position = sorted_slots(
        fold_key, parts * (TB_OWN + 1), row + jnp.asarray(from_slot, jnp.int32)
    )
    score_list, *_ = sorted_slots(sub, TB_OWN, row + position)
    scalars = [fold_list, fold_bounds, score_list]

    scale = lax.rsqrt(row_sq + EPSILON) * (1.0 / CODE_TOP**2)
    signed = jnp.where(all_labels < HALF, scale, -scale)
    mods = (all_labels % HALF).astype(jnp.float32)
    totals, normed = (), []
    beside = (*scalars, mods, signed)
    for q in range(parts):
        if q + 1 < parts:
            ahead = (incoming[q], *beside) if q else (incoming[q],)
            incoming.append(exchange(after(outgoing[q + 1], *ahead)))
        partial, sums, *more = stage(
            q, cuts, scalars, mods, signed, incoming[q], normed, totals
        )
        beside = (partial, sums)
        totals, normed = (partial, sums, *more[:3]), normed + more[3:]
    return close(labels, exchange(partial), sums, TB_OWN * LANES * devices)


def solution(mesh):
    return jax.shard_map(
        shards,
        mesh=mesh,
        in_specs=(
            P(("groups", "dp"), None, None),
            P(("groups", "dp")),
            P(("groups", "dp"), None),
            P(("groups", "dp")),
            P(("groups", "dp")),
        ),
        out_specs=(P("groups", "dp"), P(("groups", "dp"))),
        check_vma=False,
    )
```

```python
import functools
import math

import jax
import jax.numpy as jnp
import numpy as np
from jax import lax
from jax.experimental import pallas as pl
from jax.experimental.pallas import tpu as pltpu
from jax.sharding import PartitionSpec as P

K = 512
HALF = K // 2
TB_OWN = 16
LANES = 128
EPSILON = 1e-06
CODE_TOP = 65535.0
CODE_SHIFT = 32768
VMEM_BYTES = 60 * 1024 * 1024
STEP_TILES = 16
PARTS = (0.0, 13 / 16, 1.0)
LOG_STEPS = 1800.0
LOG_MIDDLE = -3.0
CACHED_BLOCKS = 64
QUAD = 4
EIGHT = 8
CHUNK = 16
ROW_SHIFT, SOURCE_SHIFT = 16, 8
PLACE_MASK, SOURCE_MASK, SLOT_MASK = 0xFFFF, 0xFF, 0xFF
BATCH = 8
NT = (((1,), (1,)), ((), ()))
SMEM = pl.BlockSpec(memory_space=pltpu.SMEM)
VMEM = pl.BlockSpec(memory_space=pltpu.VMEM)
ANY = pl.BlockSpec(memory_space=pl.ANY)


def lane_sums(values):
    ones = jnp.ones((8, 2 * LANES), jnp.bfloat16)
    high = values.astype(jnp.bfloat16)
    low = (values - high.astype(jnp.float32)).astype(jnp.bfloat16)
    both = jnp.concatenate([high, low], axis=1)
    return lax.dot_general(ones, both, NT, preferred_element_type=jnp.float32)


def block_sums(square, out_ref, count):
    batch = math.gcd(BATCH, count)

    def one_batch(c, carry):
        some = square[pl.ds(c * batch, batch)].reshape((batch * LANES, LANES))
        sums = lane_sums(some)
        for j in range(batch):
            out_ref[pl.ds(c * batch + j, 1), :] += sums[:1, j * LANES : (j + 1) * LANES]
        return carry

    lax.fori_loop(0, count // batch, one_batch, 0)


def params():
    return pltpu.CompilerParams(vmem_limit_bytes=VMEM_BYTES)


def pack_kernel(cuts, owner_ref, row_ref, *refs):
    parts = len(cuts) - 1
    (*told_refs, x_hbm), refs = refs[:5], refs[5:]
    outs = refs[:parts]
    x, coded, square, sums, words, notes, held, rank_row, rank_ref, sems, x_sems = refs[parts:]
    tiles = x.shape[0]
    devices = held.shape[0]
    blocks = square.shape[0]
    step = math.gcd(STEP_TILES, tiles)

    def read(c):
        some = pl.ds(c * step, step)
        return pltpu.make_async_copy(x_hbm.at[some], x.at[some], x_sems.at[c])

    def clear(d, carry):
        held[d] = 0
        return carry

    for c in range(tiles // step):
        read(c).start()
    labels, owner, row, sub = [ref[...] for ref in told_refs]
    own, sub_own = [jnp.broadcast_to(v.astype(jnp.float32), (tiles, tiles)) for v in (owner, sub)]
    other, sub_other = jnp.transpose(own), jnp.transpose(sub_own)
    index = [lax.broadcasted_iota(jnp.int32, (tiles, tiles), d) for d in (0, 1)]
    ahead = (sub_other < sub_own) | ((sub_other == sub_own) & (index[0] < index[1]))
    ahead = jnp.where(ahead & (other == own), 1.0, 0.0)
    rank_row[...] = jnp.sum(ahead, axis=0, keepdims=True).astype(jnp.int32)
    pltpu.sync_copy(rank_row, rank_ref)
    lax.fori_loop(0, devices, clear, 0)
    square[...] = jnp.zeros_like(square)

    def some_tiles(i, carry):
        pl.when(i % (step // QUAD) == 0)(lambda: read(i // (step // QUAD)).wait())
        for j in range(QUAD):
            t = i * QUAD + j
            some = x[t]
            root = some * lax.rsqrt(some)
            code = (root * CODE_TOP + 0.5).astype(jnp.int32) - CODE_SHIFT
            owner, rank = owner_ref[t], rank_ref[0, t]
            at = pl.ds(pl.multiple_of((owner * cuts[-1] + rank) * LANES, LANES), LANES)
            coded[at, :] = code.astype(jnp.int16)
            square[row_ref[t]] += some * some
            held[owner] = jnp.maximum(held[owner], rank + 1)
        return carry

    lax.fori_loop(0, tiles // QUAD, some_tiles, 0)

    def slots(q, d):
        some = pl.ds((d * cuts[-1] + cuts[q]) * LANES, (cuts[q + 1] - cuts[q]) * LANES)
        into = outs[q].at[d, pl.ds(0, (cuts[q + 1] - cuts[q]) * LANES)]
        return pltpu.make_async_copy(coded.at[some], into, sems.at[q, d])

    def note(d):
        into = outs[0].at[d, pl.ds((cuts[1] - cuts[0]) * LANES, notes.shape[0])]
        return pltpu.make_async_copy(notes, into, sems.at[parts, d])

    def each(what):
        def one(d, carry):
            for q in range(parts):
                pl.when(held[d] > cuts[q])(lambda q=q: what(slots(q, d)))
            return carry

        lax.fori_loop(0, devices, one, 0)

    each(lambda copy: copy.start())
    sums[...] = jnp.zeros_like(sums)
    block_sums(square, sums, blocks)
    total = sums[...]
    level = (jnp.log2(jnp.maximum(total, 1e-30)) - LOG_MIDDLE) * LOG_STEPS
    level = jnp.where(total > 0.0, jnp.clip(level, -32700.0, 32700.0), -32768.0)
    level = (level + 32768.5).astype(jnp.int32) - 32768
    words[...] = jnp.zeros_like(words)
    words[:blocks, :] = level
    at = blocks
    for told in (labels, owner, row * TB_OWN + sub):
        words[at : at + told.shape[0], :] = told
        at += told.shape[0]
    notes[...] = words[...].astype(jnp.int16)

    for d in range(devices):
        note(d).start()
    each(lambda copy: copy.wait())
    for d in range(devices):
        note(d).wait()


def pack(tile_values, owner, tile_row, told, devices, blocks, cuts):
    tiles = tile_values.shape[0]
    told = [x.reshape(-1, LANES) for x in told]
    noted = -(-(blocks + sum(x.shape[0] for x in told[:3])) // 16) * 16
    rows = [(high - low) * LANES for low, high in zip(cuts, cuts[1:])]
    rows[0] += noted
    return pl.pallas_call(
        functools.partial(pack_kernel, cuts),
        in_specs=[SMEM] * 2 + [VMEM] * 4 + [ANY],
        out_specs=[ANY] * len(rows),
        out_shape=[jax.ShapeDtypeStruct((devices, some, LANES), jnp.int16) for some in rows],
        scratch_shapes=[
            pltpu.VMEM(tile_values.shape, jnp.float32),
            pltpu.VMEM((devices * cuts[-1] * LANES, LANES), jnp.int16),
            pltpu.VMEM((blocks, LANES, LANES), jnp.float32),
            pltpu.VMEM((blocks, LANES), jnp.float32),
            pltpu.VMEM((noted, LANES), jnp.int32),
            pltpu.VMEM((noted, LANES), jnp.int16),
            pltpu.SMEM((devices,), jnp.int32),
            pltpu.VMEM((1, tiles), jnp.int32),
            pltpu.SMEM((1, tiles), jnp.int32),
            pltpu.SemaphoreType.DMA((len(rows) + 1, devices)),
            pltpu.SemaphoreType.DMA((tiles // math.gcd(STEP_TILES, tiles),)),
        ],
        compiler_params=params(),
        cost_estimate=pl.CostEstimate(
            flops=8 * tile_values.size,
            bytes_accessed=6 * tile_values.size,
            transcendentals=tile_values.size,
        ),
        name="pack",
    )(owner, tile_row, *told, tile_values)


def stage_kernel(q, bases, last, cached, fold_list, fold_bound, score_list,
                 mods_in, signed_in, x_hbm, *refs):
    base = bases[q]
    earlier, refs = refs[:q], refs[q:]
    before, sums_in, squares_in, *made_in = refs[:5] if q else (None,) * 5
    refs = refs[5:] if q else refs
    part, sums_out, refs = refs[0], refs[1], refs[2:]
    (squares_out, *made_out, fresh_out), refs = ((None,) * 4, refs) if last else (refs[:4], refs[4:])
    spread, x, hot, sums, narrow, tiles, products, scores, squares, mods, signed, *refs = refs
    sems, sub_sems, tile_sems = refs
    devices, width = x.shape[0], x.shape[1] // LANES
    none = products.shape[0] - 1
    parts = len(bases) - 1

    def bound(p, sub):
        return fold_bound[p * (TB_OWN + 1) + sub]

    def score_bound(sub):
        return sum(bound(p, sub) - bound(p, 0) for p in range(parts))

    def complete(arrived):
        def one(i, least):
            sub = TB_OWN - 1 - i
            waits = [bound(p, sub + 1) > bound(p, sub) for p in range(arrived, parts)]
            return jnp.where(functools.reduce(jnp.logical_or, waits), sub, least)

        return lax.fori_loop(0, TB_OWN, one, TB_OWN) if arrived < parts else TB_OWN

    begin, end = complete(q) if q else 0, complete(q + 1)
    needed = [pltpu.make_async_copy(x_hbm.at[:, pl.ds(0, width * LANES)], x, sems.at[0])]
    if q:
        needed.append(pltpu.make_async_copy(made_in[0], spread, sems.at[1]))
    for copy in needed:
        copy.start()

    def columns(sub):
        return (slice(None), pl.ds(pl.multiple_of(sub * 2 * LANES, 2 * LANES), 2 * LANES))

    def sums_read(sub):
        return pltpu.make_async_copy(
            sums_in.at[columns(sub)], sums.at[columns(sub)], sub_sems.at[0, sub]
        )

    def sums_write(sub):
        return pltpu.make_async_copy(
            sums.at[columns(sub)], sums_out.at[columns(sub)], sub_sems.at[1, sub]
        )

    def each_sub(low, high, what):
        def one(sub, carry):
            what(sub)
            return carry

        lax.fori_loop(low, high, one, 0)

    if q:
        each_sub(begin, TB_OWN, lambda sub: sums_read(sub).start())
        squares[...] = squares_in[...]
    else:
        sums[...] = jnp.zeros_like(sums)
        squares[...] = jnp.zeros_like(squares)
    later = [pltpu.make_async_copy(made_in[1], hot, sems.at[3])] if q and cached else []

    def each_chunk(p, outside, write, sub, what):
        count = math.gcd(CHUNK, bases[p + 1] - bases[p])

        def one(c, carry):
            away, own = outside.at[pl.ds(c * count, count)], tiles.at[pl.ds(bases[p] + c * count, count)]
            some = (own, away) if write else (away, own)
            what(pltpu.make_async_copy(*some, tile_sems.at[0 if write else p, c]))
            return carry

        first, stop = bound(p, sub) - bases[p], bound(p, TB_OWN) - bases[p]
        lax.fori_loop(first // count, (stop + count - 1) // count, one, 0)

    def each_earlier(what):
        for copy in later:
            what(copy)
        for e, e_hbm in enumerate(earlier):
            each_chunk(e, e_hbm, False, begin, what)

    each_earlier(lambda copy: copy.start())
    products[...] = jnp.zeros_like(products)
    scores[...] = before[...] if q else jnp.zeros_like(scores)
    for held, given, empty in ((mods, mods_in, -1.0), (signed, signed_in, 0.0)):
        held[:none, :] = given[...]
        held[none : none + 1, :] = jnp.full((1, LANES), empty, jnp.float32)
    cluster = lax.broadcasted_iota(jnp.int32, (HALF, LANES), 0).astype(jnp.float32)
    cluster = cluster.astype(jnp.bfloat16).reshape(HALF // 16, 16, LANES)
    one, zero = jnp.ones((), jnp.bfloat16), jnp.zeros((), jnp.bfloat16)
    lane = lax.broadcasted_iota(jnp.int32, (LANES, LANES), 1)

    def column(ref, row):
        return jnp.transpose(jnp.broadcast_to(ref[pl.ds(row, 1), :], (LANES, LANES)))

    def one_hot(row):
        own = column(mods, row).astype(jnp.int32)
        some = [jnp.where(own == lane + g, 1.0, 0.0) for g in range(0, HALF, LANES)]
        return jnp.concatenate(some, axis=1).astype(jnp.bfloat16)

    batch = math.gcd(none + 1, 3)

    def build(c, carry):
        for j in range(batch):
            spread[c * batch + j] = column(signed, c * batch + j)
            if cached:
                hot[c * batch + j] = one_hot(c * batch + j)
        return carry

    if not q:
        lax.fori_loop(0, (none + 1) // batch, build, 0)
    for copy in needed:
        copy.wait()

    def eight(entries, start, end, p):
        at = [start + EIGHT * p + j for j in range(EIGHT)]
        at = [(jnp.where(spot < end, spot, start), spot < end) for spot in at]
        return [(entries[spot], spot, held) for spot, held in at]

    def fold_sub(sub):
        start, end = bound(q, sub), bound(q, sub + 1)
        if q:
            sums_read(sub).wait()

        def one_eight(p, carry):
            folded, picks = [], []
            for entry, spot, held in eight(fold_list, start, end, p):
                row = entry >> ROW_SHIFT
                source, slot = (entry >> SOURCE_SHIFT) & SOURCE_MASK, entry & SLOT_MASK
                raw = x[source, pl.ds(pl.multiple_of(slot * LANES, LANES), LANES), :]
                root = raw.astype(jnp.int32).astype(jnp.float32) + float(CODE_SHIFT)
                scale = spread[row]
                square = root * root
                tile = square * jnp.abs(scale)
                lower = square * jnp.maximum(scale, 0.0)
                tiles[spot] = tile.astype(jnp.bfloat16)
                halves = [lower.astype(jnp.bfloat16), (tile - lower).astype(jnp.bfloat16)]
                folded.append(jnp.concatenate(halves, axis=1))
                own = jnp.broadcast_to(mods[pl.ds(jnp.where(held, row, none), 1), :], (16, LANES))
                own = jnp.where(cluster == own.astype(jnp.bfloat16)[None], one, zero)
                picks.append(own.reshape(HALF, LANES))
            pick = jnp.concatenate(picks, axis=1)
            sums[columns(sub)] += jnp.dot(
                pick, jnp.concatenate(folded, axis=0), preferred_element_type=jnp.float32
            )
            return carry

        lax.fori_loop(0, (end - start + EIGHT - 1) // EIGHT, one_eight, 0)
        sums_write(sub).start()

    each_sub(begin, TB_OWN, fold_sub)
    kept = []
    if not last:
        each_chunk(q, fresh_out, True, end, lambda copy: copy.start())
        kept.append(pltpu.make_async_copy(spread, made_out[0], sems.at[4]))
        kept.append(pltpu.make_async_copy(hot, made_out[1], sems.at[5]))
    for copy in kept:
        copy.start()
    each_earlier(lambda copy: copy.wait())

    def score_sub(sub):
        start, end = score_bound(sub), score_bound(sub + 1)
        some = sums[columns(sub)]
        narrow[...] = some.astype(jnp.bfloat16)
        squares[...] += some * some

        def one_eight(p, carry):
            listed = eight(score_list, start, end, p)
            rows = [jnp.where(held, entry >> ROW_SHIFT, none) for entry, spot, held in listed]
            spots = [entry & PLACE_MASK for entry, spot, held in listed]
            hots = [hot[row] if cached else one_hot(row) for row in rows]
            chosen = jnp.dot(
                jnp.concatenate(hots, axis=0), narrow[...], preferred_element_type=jnp.float32
            )
            for j in range(EIGHT):
                both = chosen[j * LANES : (j + 1) * LANES]
                own = jnp.where(spread[rows[j]] < 0.0, both[:, LANES:], both[:, :LANES])
                products[rows[j]] += own * tiles[spots[j]].astype(jnp.float32)
            return carry

        lax.fori_loop(0, (end - start + EIGHT - 1) // EIGHT, one_eight, 0)

    each_sub(begin, end, score_sub)
    block_sums(products, scores, none)
    if last:
        own = none // devices
        square = [lane_sums(squares[:, h : h + LANES])[:1] for h in (0, LANES)]
        square = jnp.concatenate(square, axis=1)
        for d in range(devices):
            part[d, :, part.shape[2] - K :] = square
            for b in range(own):
                at = d * own + b
                part[d, :, b * LANES : (b + 1) * LANES] = scores[at : at + 1, :]
    else:
        part[...] = scores[...]
        squares_out[...] = squares[...]
    for copy in kept:
        copy.wait()
    if not last:
        each_chunk(q, fresh_out, True, end, lambda copy: copy.wait())
    each_sub(begin, TB_OWN, lambda sub: sums_write(sub).wait())


def stage(q, cuts, scalars, mods, signed, x, normed, totals):
    devices = x.shape[0]
    last = q == len(cuts) - 2
    blocks = mods.shape[0]
    cached = blocks <= CACHED_BLOCKS
    width = cuts[q + 1] - cuts[q]
    home = blocks // devices * LANES
    wide = jax.ShapeDtypeStruct((HALF, TB_OWN * 2 * LANES), jnp.float32)
    square = jax.ShapeDtypeStruct((HALF, 2 * LANES), jnp.float32)
    if last:
        out_shape = [jax.ShapeDtypeStruct((devices, 1, home + K), jnp.float32), wide]
    else:
        out_shape = [
            jax.ShapeDtypeStruct((blocks, LANES), jnp.float32),
            wide,
            square,
            jax.ShapeDtypeStruct((blocks + 1, LANES, LANES), jnp.float32),
            jax.ShapeDtypeStruct((blocks + 1 if cached else 1, LANES, HALF), jnp.bfloat16),
            jax.ShapeDtypeStruct((devices * width, LANES, LANES), jnp.bfloat16),
        ]
    slots = devices * cuts[-1]
    sizes = [devices * (high - low) for low, high in zip(cuts, cuts[1:])]
    chunks = max(size // math.gcd(CHUNK, size) for size in sizes)
    operands = [*scalars, mods, signed, x, *normed, *totals]
    return pl.pallas_call(
        functools.partial(stage_kernel, q, [devices * cut for cut in cuts], last, cached),
        in_specs=[SMEM] * len(scalars) + [VMEM] * 2 + [ANY] * (1 + q) + [VMEM, ANY, VMEM, ANY, ANY][: len(totals)],
        out_specs=[VMEM, ANY, VMEM, ANY, ANY, ANY][: len(out_shape)],
        out_shape=out_shape,
        input_output_aliases={len(operands) - len(totals) + 1: 1} if q else {},
        scratch_shapes=[
            pltpu.VMEM((blocks + 1, LANES, LANES), jnp.float32),
            pltpu.VMEM((devices, width * LANES, LANES), jnp.int16),
            pltpu.VMEM((blocks + 1 if cached else 1, LANES, HALF), jnp.bfloat16),
            pltpu.VMEM(wide.shape, jnp.float32),
            pltpu.VMEM(square.shape, jnp.bfloat16),
            pltpu.VMEM((slots, LANES, LANES), jnp.bfloat16),
            pltpu.VMEM((blocks + 1, LANES, LANES), jnp.float32),
            pltpu.VMEM((blocks, LANES), jnp.float32),
            pltpu.VMEM(square.shape, jnp.float32),
            pltpu.VMEM((blocks + 1, LANES), jnp.float32),
            pltpu.VMEM((blocks + 1, LANES), jnp.float32),
            pltpu.SemaphoreType.DMA((6,)),
            pltpu.SemaphoreType.DMA((2, TB_OWN)),
            pltpu.SemaphoreType.DMA((max(q, 1), chunks)),
        ],
        compiler_params=params(),
        cost_estimate=pl.CostEstimate(
            flops=devices * width * LANES * LANES * K * 8,
            bytes_accessed=4 * devices * width * LANES * LANES + 8 * K * TB_OWN * LANES,
            transcendentals=0,
        ),
        name="stage",
    )(*operands)


def close_kernel(root, groups, labels_ref, got_ref, sums_hbm, out_hbm, similarity, sums, out, sems):
    width = TB_OWN // groups
    reads, writes = [], []
    for g in range(groups):
        some = (slice(None), pl.ds(g * width * 2 * LANES, width * 2 * LANES))
        reads.append(pltpu.make_async_copy(sums_hbm.at[some], sums.at[some], sems.at[0, g]))
        some = (slice(None), pl.ds(g * width * LANES, width * LANES))
        writes.append(pltpu.make_async_copy(out.at[some], out_hbm.at[some], sems.at[1, g]))
        reads[g].start()
    total = jnp.sum(got_ref[...], axis=0)
    home = total.shape[1] - K
    own = lax.rsqrt(total[:, home:] + EPSILON)
    columns = [
        jnp.transpose(jnp.broadcast_to(own[:, k : k + LANES], (LANES, LANES)))
        for k in range(0, K, LANES)
    ]
    cluster = lax.broadcasted_iota(jnp.int32, (LANES, LANES), 0)
    for b in range(home // LANES):
        found = jnp.zeros((LANES, LANES), jnp.float32)
        for i, column in enumerate(columns):
            found += jnp.where(cluster + i * LANES == labels_ref[b : b + 1, :], column, 0.0)
        found = jnp.sum(found, axis=0, keepdims=True)
        similarity[b : b + 1, :] = total[:, b * LANES : (b + 1) * LANES] * found
    for g in range(groups):
        reads[g].wait()

        def one_sub(sub, carry):
            to = pl.ds(pl.multiple_of(sub * LANES, LANES), LANES)
            for i, column in enumerate(columns):
                half, row = divmod(i * LANES, HALF)
                at = pl.ds(pl.multiple_of((2 * sub + half) * LANES, LANES), LANES)
                done = sums[row : row + LANES, at] * column * root
                out[i * LANES : (i + 1) * LANES, to] = done.astype(jnp.bfloat16)
            return carry

        lax.fori_loop(g * width, (g + 1) * width, one_sub, 0)
        writes[g].start()
    for write in writes:
        write.wait()


def close(labels, got, sums, vocab_size):
    groups = 4
    labels = labels.reshape(-1, LANES)
    wide = jax.ShapeDtypeStruct((K, TB_OWN * LANES), jnp.bfloat16)
    centroids, similarity = pl.pallas_call(
        functools.partial(close_kernel, math.sqrt(vocab_size), groups),
        in_specs=[VMEM, VMEM, ANY],
        out_specs=[ANY, VMEM],
        out_shape=[wide, jax.ShapeDtypeStruct(labels.shape, jnp.float32)],
        scratch_shapes=[
            pltpu.VMEM(sums.shape, jnp.float32),
            pltpu.VMEM(wide.shape, jnp.bfloat16),
            pltpu.SemaphoreType.DMA((2, groups)),
        ],
        compiler_params=params(),
        cost_estimate=pl.CostEstimate(
            flops=2 * sums.size, bytes_accessed=6 * sums.size, transcendentals=0
        ),
        name="close",
    )(labels, got, sums)
    return centroids, similarity.reshape(-1)


def exchange(x):
    return lax.all_to_all(x, "dp", split_axis=0, concat_axis=0, tiled=True)


def after(value, *others):
    return lax.optimization_barrier((value, *others))[0]


def sorted_slots(key, top, entries):
    slots = jnp.arange(key.shape[0], dtype=jnp.int32)
    ahead = (key[None, :] < key[:, None]) | (
        (key[None, :] == key[:, None]) & (slots[None, :] < slots[:, None])
    )
    position = jnp.sum(ahead.astype(jnp.int32), axis=1)
    here = position[None, :] == slots[:, None]
    listed = jnp.sum(jnp.where(here, entries[None, :], 0), axis=1)
    levels = jnp.arange(top + 1, dtype=jnp.int32)
    bounds = jnp.sum((key[None, :] < levels[:, None]).astype(jnp.int32), axis=1)
    return listed, bounds, position


def ranks(group, sub):
    index = jnp.arange(sub.shape[-1], dtype=jnp.int32)
    before = (sub[..., None, :] < sub[..., :, None]) | (
        (sub[..., None, :] == sub[..., :, None]) & (index[None, :] < index[:, None])
    )
    same = group[..., None, :] == group[..., :, None]
    return jnp.sum((before & same).astype(jnp.int32), axis=-1)


def shards(tile_values, tile_row, tile_owner, tile_sub, labels):
    devices = lax.axis_size("dp")
    tiles = tile_values.shape[0]
    home = labels.shape[0]
    blocks = home // LANES * devices
    cap = max(2, 2 * tiles // devices)
    cuts = tuple(sorted({int(cap * share) for share in PARTS})) if cap >= 8 else (0, cap)
    parts = len(cuts) - 1
    here = lax.axis_index("dp").astype(jnp.int32)
    owner = tile_owner[:, 0]

    told = (labels, owner, tile_row, tile_sub)
    outgoing = pack(tile_values, owner, tile_row, told, devices, blocks, cuts)
    incoming = [exchange(outgoing[0])]
    heard = incoming[0][:, (cuts[1] - cuts[0]) * LANES :].astype(jnp.int32)
    level = heard[:, :blocks]
    partial_sq = jnp.exp2(level.astype(jnp.float32) * (1.0 / LOG_STEPS) + LOG_MIDDLE)
    row_sq = jnp.sum(jnp.where(level > -32768, partial_sq, 0.0), axis=0)
    all_described = heard[:, blocks:].reshape(devices, -1)
    all_labels = all_described[:, :home].reshape(blocks, LANES)
    mine = all_described[:, home : home + tiles] == here
    code = all_described[:, home + tiles : home + 2 * tiles]
    rank = ranks(mine.astype(jnp.int32), code % TB_OWN)
    chosen = mine[:, None, :] & (rank[:, None, :] == jnp.arange(cap)[None, :, None])
    meta = jnp.sum(jnp.where(chosen, code[:, None, :] + 1, 0), axis=2).reshape(-1) - 1
    sub = jnp.where(meta < 0, TB_OWN, meta % TB_OWN)
    slot_rank = np.arange(devices * cap) % cap
    slot_part = np.searchsorted(np.array(cuts), slot_rank, side="right") - 1
    low = np.array(cuts)[slot_part]
    fold_key = jnp.asarray(slot_part * (TB_OWN + 1), jnp.int32) + sub
    row = (meta // TB_OWN) << ROW_SHIFT
    from_slot = (np.arange(devices * cap) // cap << SOURCE_SHIFT) + slot_rank - low
    fold_list, fold_bounds, position = sorted_slots(
        fold_key, parts * (TB_OWN + 1), row + jnp.asarray(from_slot, jnp.int32)
    )
    score_list, *_ = sorted_slots(sub, TB_OWN, row + position)
    scalars = [fold_list, fold_bounds, score_list]

    scale = lax.rsqrt(row_sq + EPSILON) * (1.0 / CODE_TOP**2)
    signed = jnp.where(all_labels < HALF, scale, -scale)
    mods = (all_labels % HALF).astype(jnp.float32)
    totals, normed = (), []
    beside = (*scalars, mods, signed)
    for q in range(parts):
        if q + 1 < parts:
            ahead = (incoming[q], *beside) if q else (incoming[q],)
            incoming.append(exchange(after(outgoing[q + 1], *ahead)))
        partial, sums, *more = stage(
            q, cuts, scalars, mods, signed, incoming[q], normed, totals
        )
        beside = (partial, sums)
        totals, normed = (partial, sums, *more[:3]), normed + more[3:]
    return close(labels, exchange(partial), sums, TB_OWN * LANES * devices)


def solution(mesh):
    return jax.shard_map(
        shards,
        mesh=mesh,
        in_specs=(
            P(("groups", "dp"), None, None),
            P(("groups", "dp")),
            P(("groups", "dp"), None),
            P(("groups", "dp")),
            P(("groups", "dp")),
        ),
        out_specs=(P("groups", "dp"), P(("groups", "dp"))),
        check_vma=False,
    )
```

```python
import functools
import math

import jax
import jax.numpy as jnp
import numpy as np
from jax import lax
from jax.experimental import pallas as pl
from jax.experimental.pallas import tpu as pltpu
from jax.sharding import PartitionSpec as P

K = 512
HALF = K // 2
TB_OWN = 16
LANES = 128
EPSILON = 1e-06
CODE_TOP = 65535.0
CODE_SHIFT = 32768
VMEM_BYTES = 60 * 1024 * 1024
STEP_TILES = 16
PARTS = (0.0, 13 / 16, 1.0)
LOG_STEPS = 1800.0
LOG_MIDDLE = -3.0
CACHED_BLOCKS = 64
QUAD = 4
EIGHT = 8
CHUNK = 16
BLOCKS = 4
ROW_SHIFT, SOURCE_SHIFT = 16, 8
PLACE_MASK, SOURCE_MASK, SLOT_MASK = 0xFFFF, 0xFF, 0xFF
BATCH = 8
NT = (((1,), (1,)), ((), ()))
SMEM = pl.BlockSpec(memory_space=pltpu.SMEM)
VMEM = pl.BlockSpec(memory_space=pltpu.VMEM)
ANY = pl.BlockSpec(memory_space=pl.ANY)


def lane_sums(values):
    ones = jnp.ones((8, 2 * LANES), jnp.bfloat16)
    high = values.astype(jnp.bfloat16)
    low = (values - high.astype(jnp.float32)).astype(jnp.bfloat16)
    both = jnp.concatenate([high, low], axis=1)
    return lax.dot_general(ones, both, NT, preferred_element_type=jnp.float32)


def block_sums(square, out_ref, count):
    batch = math.gcd(BATCH, count)

    def one_batch(c, carry):
        some = square[pl.ds(c * batch, batch)].reshape((batch * LANES, LANES))
        sums = lane_sums(some)
        for j in range(batch):
            out_ref[pl.ds(c * batch + j, 1), :] += sums[:1, j * LANES : (j + 1) * LANES]
        return carry

    lax.fori_loop(0, count // batch, one_batch, 0)


def params():
    return pltpu.CompilerParams(vmem_limit_bytes=VMEM_BYTES)


def pack_kernel(cuts, owner_ref, row_ref, *refs):
    parts = len(cuts) - 1
    (*told_refs, x_hbm), refs = refs[:5], refs[5:]
    outs = refs[:parts]
    x, coded, square, sums, words, notes, rank_row, rank_ref, sems, x_sems = refs[parts:]
    tiles = x.shape[0]
    devices = coded.shape[0]
    blocks = square.shape[0]
    step = math.gcd(STEP_TILES, tiles)

    def read(c):
        some = pl.ds(c * step, step)
        return pltpu.make_async_copy(x_hbm.at[some], x.at[some], x_sems.at[c])

    for c in range(tiles // step):
        read(c).start()
    labels, owner, row, sub = [ref[...] for ref in told_refs]
    own, sub_own = [jnp.broadcast_to(v.astype(jnp.float32), (tiles, tiles)) for v in (owner, sub)]
    other, sub_other = jnp.transpose(own), jnp.transpose(sub_own)
    index = [lax.broadcasted_iota(jnp.int32, (tiles, tiles), d) for d in (0, 1)]
    ahead = (sub_other < sub_own) | ((sub_other == sub_own) & (index[0] < index[1]))
    ahead = jnp.where(ahead & (other == own), 1.0, 0.0)
    rank_row[...] = jnp.sum(ahead, axis=0, keepdims=True).astype(jnp.int32)
    pltpu.sync_copy(rank_row, rank_ref)
    square[...] = jnp.zeros_like(square)

    def some_tiles(i, carry):
        pl.when(i % (step // QUAD) == 0)(lambda: read(i // (step // QUAD)).wait())
        for j in range(QUAD):
            t = i * QUAD + j
            some = x[t]
            root = some * lax.rsqrt(some)
            code = (root * CODE_TOP + 0.5).astype(jnp.int32) - CODE_SHIFT
            owner, rank = owner_ref[t], rank_ref[0, t]
            at = pl.ds(pl.multiple_of(rank * LANES, LANES), LANES)
            coded[owner, at, :] = code.astype(jnp.int16)
            square[row_ref[t]] += some * some
        return carry

    lax.fori_loop(0, tiles // QUAD, some_tiles, 0)

    copies = []
    for q in range(parts):
        rows, count = (cuts[q + 1] - cuts[q]) * LANES, devices // (1 if q else math.gcd(4, devices))
        for d in range(0, devices, count):
            from_ref = coded.at[pl.ds(d, count), pl.ds(cuts[q] * LANES, rows)]
            into = outs[q].at[pl.ds(d, count), pl.ds(0, rows)]
            copies.append(pltpu.make_async_copy(from_ref, into, sems.at[len(copies)]))
    for copy in copies:
        copy.start()
    sums[...] = jnp.zeros_like(sums)
    block_sums(square, sums, blocks)
    total = sums[...]
    level = (jnp.log2(jnp.maximum(total, 1e-30)) - LOG_MIDDLE) * LOG_STEPS
    level = jnp.where(total > 0.0, jnp.clip(level, -32700.0, 32700.0), -32768.0)
    level = (level + 32768.5).astype(jnp.int32) - 32768
    words[...] = jnp.zeros_like(words)
    words[:blocks, :] = level
    at = blocks
    for told in (labels, owner, row * TB_OWN + sub):
        words[at : at + told.shape[0], :] = told
        at += told.shape[0]
    notes[...] = jnp.broadcast_to(words[...].astype(jnp.int16)[None], notes.shape)
    into = outs[0].at[:, pl.ds((cuts[1] - cuts[0]) * LANES, notes.shape[1])]
    copies.append(pltpu.make_async_copy(notes, into, sems.at[len(copies)]))
    copies[-1].start()
    for copy in copies:
        copy.wait()


def pack(tile_values, owner, tile_row, told, devices, blocks, cuts):
    tiles = tile_values.shape[0]
    told = [x.reshape(-1, LANES) for x in told]
    noted = -(-(blocks + sum(x.shape[0] for x in told[:3])) // 16) * 16
    rows = [(high - low) * LANES for low, high in zip(cuts, cuts[1:])]
    rows[0] += noted
    return pl.pallas_call(
        functools.partial(pack_kernel, cuts),
        in_specs=[SMEM] * 2 + [VMEM] * 4 + [ANY],
        out_specs=[ANY] * len(rows),
        out_shape=[jax.ShapeDtypeStruct((devices, some, LANES), jnp.int16) for some in rows],
        scratch_shapes=[
            pltpu.VMEM(tile_values.shape, jnp.float32),
            pltpu.VMEM((devices, cuts[-1] * LANES, LANES), jnp.int16),
            pltpu.VMEM((blocks, LANES, LANES), jnp.float32),
            pltpu.VMEM((blocks, LANES), jnp.float32),
            pltpu.VMEM((noted, LANES), jnp.int32),
            pltpu.VMEM((devices, noted, LANES), jnp.int16),
            pltpu.VMEM((1, tiles), jnp.int32),
            pltpu.SMEM((1, tiles), jnp.int32),
            pltpu.SemaphoreType.DMA((len(rows) + 4,)),
            pltpu.SemaphoreType.DMA((tiles // math.gcd(STEP_TILES, tiles),)),
        ],
        compiler_params=params(),
        cost_estimate=pl.CostEstimate(
            flops=8 * tile_values.size,
            bytes_accessed=6 * tile_values.size,
            transcendentals=tile_values.size,
        ),
        name="pack",
    )(owner, tile_row, *told, tile_values)


def stage_kernel(q, bases, last, cached, fold_list, fold_bound, score_list,
                 mods_in, signed_in, x_hbm, *refs):
    base = bases[q]
    earlier, refs = refs[:q], refs[q:]
    before, sums_in, squares_in, *made_in = refs[:5] if q else (None,) * 5
    refs = refs[5:] if q else refs
    part, sums_out, refs = refs[0], refs[1], refs[2:]
    (squares_out, *made_out, fresh_out), refs = ((None,) * 4, refs) if last else (refs[:4], refs[4:])
    spread, x, hot, sums, narrow, tiles, products, scores, squares, mods, signed, *refs = refs
    sems, sub_sems, tile_sems = refs
    devices, width = x.shape[0], x.shape[1] // LANES
    none = products.shape[0] - 1
    parts = len(bases) - 1

    def bound(p, sub):
        return fold_bound[p * (TB_OWN + 1) + sub]

    def score_bound(sub):
        return sum(bound(p, sub) - bound(p, 0) for p in range(parts))

    def complete(arrived):
        def one(i, least):
            sub = TB_OWN - 1 - i
            waits = [bound(p, sub + 1) > bound(p, sub) for p in range(arrived, parts)]
            return jnp.where(functools.reduce(jnp.logical_or, waits), sub, least)

        return lax.fori_loop(0, TB_OWN, one, TB_OWN) if arrived < parts else TB_OWN

    begin, end = complete(q) if q else 0, complete(q + 1)
    needed = [pltpu.make_async_copy(x_hbm.at[:, pl.ds(0, width * LANES)], x, sems.at[0])]
    if q:
        needed.append(pltpu.make_async_copy(made_in[0], spread, sems.at[1]))
    for copy in needed:
        copy.start()

    def columns(sub):
        return (slice(None), pl.ds(pl.multiple_of(sub * 2 * LANES, 2 * LANES), 2 * LANES))

    def group(g):
        size = BLOCKS * 2 * LANES
        return (slice(None), pl.ds(pl.multiple_of(g * size, size), size))

    def sums_read(g):
        return pltpu.make_async_copy(sums_in.at[group(g)], sums.at[group(g)], sub_sems.at[0, g])

    def sums_write(g):
        return pltpu.make_async_copy(sums.at[group(g)], sums_out.at[group(g)], sub_sems.at[1, g])

    def each_sub(low, high, what):
        def one(sub, carry):
            what(sub)
            return carry

        lax.fori_loop(low, high, one, 0)

    if q:
        each_sub(begin // BLOCKS, TB_OWN // BLOCKS, lambda g: sums_read(g).start())
        squares[...] = squares_in[...]
    else:
        sums[...] = jnp.zeros_like(sums)
        squares[...] = jnp.zeros_like(squares)
    later = [pltpu.make_async_copy(made_in[1], hot, sems.at[3])] if q and cached else []

    def each_chunk(p, outside, write, sub, what):
        count = math.gcd(CHUNK, bases[p + 1] - bases[p])

        def one(c, carry):
            away, own = outside.at[pl.ds(c * count, count)], tiles.at[pl.ds(bases[p] + c * count, count)]
            some = (own, away) if write else (away, own)
            what(pltpu.make_async_copy(*some, tile_sems.at[0 if write else p, c]))
            return carry

        first, stop = bound(p, sub) - bases[p], bound(p, TB_OWN) - bases[p]
        lax.fori_loop(first // count, (stop + count - 1) // count, one, 0)

    def each_earlier(what):
        for copy in later:
            what(copy)
        for e, e_hbm in enumerate(earlier):
            each_chunk(e, e_hbm, False, begin, what)

    each_earlier(lambda copy: copy.start())
    products[...] = jnp.zeros_like(products)
    scores[...] = before[...] if q else jnp.zeros_like(scores)
    for held, given, empty in ((mods, mods_in, -1.0), (signed, signed_in, 0.0)):
        held[:none, :] = given[...]
        held[none : none + 1, :] = jnp.full((1, LANES), empty, jnp.float32)
    cluster = lax.broadcasted_iota(jnp.int32, (HALF, LANES), 0).astype(jnp.float32)
    cluster = cluster.astype(jnp.bfloat16).reshape(HALF // 16, 16, LANES)
    one, zero = jnp.ones((), jnp.bfloat16), jnp.zeros((), jnp.bfloat16)
    lane = lax.broadcasted_iota(jnp.int32, (LANES, LANES), 1)

    def column(ref, row):
        return jnp.transpose(jnp.broadcast_to(ref[pl.ds(row, 1), :], (LANES, LANES)))

    def one_hot(row):
        own = column(mods, row).astype(jnp.int32)
        some = [jnp.where(own == lane + g, 1.0, 0.0) for g in range(0, HALF, LANES)]
        return jnp.concatenate(some, axis=1).astype(jnp.bfloat16)

    batch = math.gcd(none + 1, 3)

    def build(c, carry):
        for j in range(batch):
            spread[c * batch + j] = column(signed, c * batch + j)
            if cached:
                hot[c * batch + j] = one_hot(c * batch + j)
        return carry

    if not q:
        lax.fori_loop(0, (none + 1) // batch, build, 0)
    for copy in needed:
        copy.wait()
    if q:
        each_sub(begin // BLOCKS, TB_OWN // BLOCKS, lambda g: sums_read(g).wait())

    def eight(entries, start, end, p):
        at = [start + EIGHT * p + j for j in range(EIGHT)]
        at = [(jnp.where(spot < end, spot, start), spot < end) for spot in at]
        return [(entries[spot], spot, held) for spot, held in at]

    def fold_sub(sub):
        start, end = bound(q, sub), bound(q, sub + 1)
        def one_eight(p, carry):
            folded, picks = [], []
            for entry, spot, held in eight(fold_list, start, end, p):
                row = entry >> ROW_SHIFT
                source, slot = (entry >> SOURCE_SHIFT) & SOURCE_MASK, entry & SLOT_MASK
                raw = x[source, pl.ds(pl.multiple_of(slot * LANES, LANES), LANES), :]
                root = raw.astype(jnp.int32).astype(jnp.float32) + float(CODE_SHIFT)
                scale = spread[row]
                square = root * root
                tile = square * jnp.abs(scale)
                lower = square * jnp.maximum(scale, 0.0)
                tiles[spot] = tile.astype(jnp.bfloat16)
                halves = [lower.astype(jnp.bfloat16), (tile - lower).astype(jnp.bfloat16)]
                folded.append(jnp.concatenate(halves, axis=1))
                own = jnp.broadcast_to(mods[pl.ds(jnp.where(held, row, none), 1), :], (16, LANES))
                own = jnp.where(cluster == own.astype(jnp.bfloat16)[None], one, zero)
                picks.append(own.reshape(HALF, LANES))
            pick = jnp.concatenate(picks, axis=1)
            sums[columns(sub)] += jnp.dot(
                pick, jnp.concatenate(folded, axis=0), preferred_element_type=jnp.float32
            )
            return carry

        lax.fori_loop(0, (end - start + EIGHT - 1) // EIGHT, one_eight, 0)

    def fold_group(g):
        each_sub(jnp.maximum(begin, g * BLOCKS), (g + 1) * BLOCKS, fold_sub)
        sums_write(g).start()

    each_sub(begin // BLOCKS, TB_OWN // BLOCKS, fold_group)
    kept = []
    if not last:
        each_chunk(q, fresh_out, True, end, lambda copy: copy.start())
        kept.append(pltpu.make_async_copy(spread, made_out[0], sems.at[4]))
        kept.append(pltpu.make_async_copy(hot, made_out[1], sems.at[5]))
    for copy in kept:
        copy.start()
    each_earlier(lambda copy: copy.wait())

    def score_sub(sub):
        start, end = score_bound(sub), score_bound(sub + 1)
        some = sums[columns(sub)]
        narrow[...] = some.astype(jnp.bfloat16)
        squares[...] += some * some

        def one_eight(p, carry):
            listed = eight(score_list, start, end, p)
            rows = [jnp.where(held, entry >> ROW_SHIFT, none) for entry, spot, held in listed]
            spots = [entry & PLACE_MASK for entry, spot, held in listed]
            hots = [hot[row] if cached else one_hot(row) for row in rows]
            chosen = jnp.dot(
                jnp.concatenate(hots, axis=0), narrow[...], preferred_element_type=jnp.float32
            )
            for j in range(EIGHT):
                both = chosen[j * LANES : (j + 1) * LANES]
                own = jnp.where(spread[rows[j]] < 0.0, both[:, LANES:], both[:, :LANES])
                products[rows[j]] += own * tiles[spots[j]].astype(jnp.float32)
            return carry

        lax.fori_loop(0, (end - start + EIGHT - 1) // EIGHT, one_eight, 0)

    each_sub(begin, end, score_sub)
    block_sums(products, scores, none)
    if last:
        own = none // devices
        square = [lane_sums(squares[:, h : h + LANES])[:1] for h in (0, LANES)]
        square = jnp.concatenate(square, axis=1)
        for d in range(devices):
            part[d, :, part.shape[2] - K :] = square
            for b in range(own):
                at = d * own + b
                part[d, :, b * LANES : (b + 1) * LANES] = scores[at : at + 1, :]
    else:
        part[...] = scores[...]
        squares_out[...] = squares[...]
    for copy in kept:
        copy.wait()
    if not last:
        each_chunk(q, fresh_out, True, end, lambda copy: copy.wait())
    each_sub(begin // BLOCKS, TB_OWN // BLOCKS, lambda g: sums_write(g).wait())


def stage(q, cuts, scalars, mods, signed, x, normed, totals):
    devices = x.shape[0]
    last = q == len(cuts) - 2
    blocks = mods.shape[0]
    cached = blocks <= CACHED_BLOCKS
    width = cuts[q + 1] - cuts[q]
    home = blocks // devices * LANES
    wide = jax.ShapeDtypeStruct((HALF, TB_OWN * 2 * LANES), jnp.float32)
    square = jax.ShapeDtypeStruct((HALF, 2 * LANES), jnp.float32)
    if last:
        out_shape = [jax.ShapeDtypeStruct((devices, 1, home + K), jnp.float32), wide]
    else:
        out_shape = [
            jax.ShapeDtypeStruct((blocks, LANES), jnp.float32),
            wide,
            square,
            jax.ShapeDtypeStruct((blocks + 1, LANES, LANES), jnp.float32),
            jax.ShapeDtypeStruct((blocks + 1 if cached else 1, LANES, HALF), jnp.bfloat16),
            jax.ShapeDtypeStruct((devices * width, LANES, LANES), jnp.bfloat16),
        ]
    slots = devices * cuts[-1]
    sizes = [devices * (high - low) for low, high in zip(cuts, cuts[1:])]
    chunks = max(size // math.gcd(CHUNK, size) for size in sizes)
    operands = [*scalars, mods, signed, x, *normed, *totals]
    return pl.pallas_call(
        functools.partial(stage_kernel, q, [devices * cut for cut in cuts], last, cached),
        in_specs=[SMEM] * len(scalars) + [VMEM] * 2 + [ANY] * (1 + q) + [VMEM, ANY, VMEM, ANY, ANY][: len(totals)],
        out_specs=[VMEM, ANY, VMEM, ANY, ANY, ANY][: len(out_shape)],
        out_shape=out_shape,
        input_output_aliases={len(operands) - len(totals) + 1: 1} if q else {},
        scratch_shapes=[
            pltpu.VMEM((blocks + 1, LANES, LANES), jnp.float32),
            pltpu.VMEM((devices, width * LANES, LANES), jnp.int16),
            pltpu.VMEM((blocks + 1 if cached else 1, LANES, HALF), jnp.bfloat16),
            pltpu.VMEM(wide.shape, jnp.float32),
            pltpu.VMEM(square.shape, jnp.bfloat16),
            pltpu.VMEM((slots, LANES, LANES), jnp.bfloat16),
            pltpu.VMEM((blocks + 1, LANES, LANES), jnp.float32),
            pltpu.VMEM((blocks, LANES), jnp.float32),
            pltpu.VMEM(square.shape, jnp.float32),
            pltpu.VMEM((blocks + 1, LANES), jnp.float32),
            pltpu.VMEM((blocks + 1, LANES), jnp.float32),
            pltpu.SemaphoreType.DMA((6,)),
            pltpu.SemaphoreType.DMA((2, TB_OWN // BLOCKS)),
            pltpu.SemaphoreType.DMA((max(q, 1), chunks)),
        ],
        compiler_params=params(),
        cost_estimate=pl.CostEstimate(
            flops=devices * width * LANES * LANES * K * 8,
            bytes_accessed=4 * devices * width * LANES * LANES + 8 * K * TB_OWN * LANES,
            transcendentals=0,
        ),
        name="stage",
    )(*operands)


def close_kernel(root, groups, labels_ref, got_ref, sums_hbm, out_hbm, similarity, sums, out, sems):
    width = TB_OWN // groups
    reads, writes = [], []
    for g in range(groups):
        some = (slice(None), pl.ds(g * width * 2 * LANES, width * 2 * LANES))
        reads.append(pltpu.make_async_copy(sums_hbm.at[some], sums.at[some], sems.at[0, g]))
        some = (slice(None), pl.ds(g * width * LANES, width * LANES))
        writes.append(pltpu.make_async_copy(out.at[some], out_hbm.at[some], sems.at[1, g]))
        reads[g].start()
    total = jnp.sum(got_ref[...], axis=0)
    home = total.shape[1] - K
    own = lax.rsqrt(total[:, home:] + EPSILON)
    columns = [
        jnp.transpose(jnp.broadcast_to(own[:, k : k + LANES], (LANES, LANES)))
        for k in range(0, K, LANES)
    ]
    cluster = lax.broadcasted_iota(jnp.int32, (LANES, LANES), 0)
    for b in range(home // LANES):
        found = jnp.zeros((LANES, LANES), jnp.float32)
        for i, column in enumerate(columns):
            found += jnp.where(cluster + i * LANES == labels_ref[b : b + 1, :], column, 0.0)
        found = jnp.sum(found, axis=0, keepdims=True)
        similarity[b : b + 1, :] = total[:, b * LANES : (b + 1) * LANES] * found
    for g in range(groups):
        reads[g].wait()

        def one_sub(sub, carry):
            to = pl.ds(pl.multiple_of(sub * LANES, LANES), LANES)
            for i, column in enumerate(columns):
                half, row = divmod(i * LANES, HALF)
                at = pl.ds(pl.multiple_of((2 * sub + half) * LANES, LANES), LANES)
                done = sums[row : row + LANES, at] * column * root
                out[i * LANES : (i + 1) * LANES, to] = done.astype(jnp.bfloat16)
            return carry

        lax.fori_loop(g * width, (g + 1) * width, one_sub, 0)
        writes[g].start()
    for write in writes:
        write.wait()


def close(labels, got, sums, vocab_size):
    groups = 4
    labels = labels.reshape(-1, LANES)
    wide = jax.ShapeDtypeStruct((K, TB_OWN * LANES), jnp.bfloat16)
    centroids, similarity = pl.pallas_call(
        functools.partial(close_kernel, math.sqrt(vocab_size), groups),
        in_specs=[VMEM, VMEM, ANY],
        out_specs=[ANY, VMEM],
        out_shape=[wide, jax.ShapeDtypeStruct(labels.shape, jnp.float32)],
        scratch_shapes=[
            pltpu.VMEM(sums.shape, jnp.float32),
            pltpu.VMEM(wide.shape, jnp.bfloat16),
            pltpu.SemaphoreType.DMA((2, groups)),
        ],
        compiler_params=params(),
        cost_estimate=pl.CostEstimate(
            flops=2 * sums.size, bytes_accessed=6 * sums.size, transcendentals=0
        ),
        name="close",
    )(labels, got, sums)
    return centroids, similarity.reshape(-1)


def exchange(x):
    return lax.all_to_all(x, "dp", split_axis=0, concat_axis=0, tiled=True)


def after(value, *others):
    return lax.optimization_barrier((value, *others))[0]


def sorted_slots(key, top, entries):
    slots = jnp.arange(key.shape[0], dtype=jnp.int32)
    ahead = (key[None, :] < key[:, None]) | (
        (key[None, :] == key[:, None]) & (slots[None, :] < slots[:, None])
    )
    position = jnp.sum(ahead.astype(jnp.int32), axis=1)
    here = position[None, :] == slots[:, None]
    listed = jnp.sum(jnp.where(here, entries[None, :], 0), axis=1)
    levels = jnp.arange(top + 1, dtype=jnp.int32)
    bounds = jnp.sum((key[None, :] < levels[:, None]).astype(jnp.int32), axis=1)
    return listed, bounds, position


def ranks(group, sub):
    index = jnp.arange(sub.shape[-1], dtype=jnp.int32)
    before = (sub[..., None, :] < sub[..., :, None]) | (
        (sub[..., None, :] == sub[..., :, None]) & (index[None, :] < index[:, None])
    )
    same = group[..., None, :] == group[..., :, None]
    return jnp.sum((before & same).astype(jnp.int32), axis=-1)


def shards(tile_values, tile_row, tile_owner, tile_sub, labels):
    devices = lax.axis_size("dp")
    tiles = tile_values.shape[0]
    home = labels.shape[0]
    blocks = home // LANES * devices
    cap = max(2, 2 * tiles // devices)
    cuts = tuple(sorted({int(cap * share) for share in PARTS})) if cap >= 8 else (0, cap)
    parts = len(cuts) - 1
    here = lax.axis_index("dp").astype(jnp.int32)
    owner = tile_owner[:, 0]

    told = (labels, owner, tile_row, tile_sub)
    outgoing = pack(tile_values, owner, tile_row, told, devices, blocks, cuts)
    incoming = [exchange(outgoing[0])]
    heard = incoming[0][:, (cuts[1] - cuts[0]) * LANES :].astype(jnp.int32)
    level = heard[:, :blocks]
    partial_sq = jnp.exp2(level.astype(jnp.float32) * (1.0 / LOG_STEPS) + LOG_MIDDLE)
    row_sq = jnp.sum(jnp.where(level > -32768, partial_sq, 0.0), axis=0)
    all_described = heard[:, blocks:].reshape(devices, -1)
    all_labels = all_described[:, :home].reshape(blocks, LANES)
    mine = all_described[:, home : home + tiles] == here
    code = all_described[:, home + tiles : home + 2 * tiles]
    rank = ranks(mine.astype(jnp.int32), code % TB_OWN)
    chosen = mine[:, None, :] & (rank[:, None, :] == jnp.arange(cap)[None, :, None])
    meta = jnp.sum(jnp.where(chosen, code[:, None, :] + 1, 0), axis=2).reshape(-1) - 1
    sub = jnp.where(meta < 0, TB_OWN, meta % TB_OWN)
    slot_rank = np.arange(devices * cap) % cap
    slot_part = np.searchsorted(np.array(cuts), slot_rank, side="right") - 1
    low = np.array(cuts)[slot_part]
    fold_key = jnp.asarray(slot_part * (TB_OWN + 1), jnp.int32) + sub
    row = (meta // TB_OWN) << ROW_SHIFT
    from_slot = (np.arange(devices * cap) // cap << SOURCE_SHIFT) + slot_rank - low
    fold_list, fold_bounds, position = sorted_slots(
        fold_key, parts * (TB_OWN + 1), row + jnp.asarray(from_slot, jnp.int32)
    )
    score_list, *_ = sorted_slots(sub, TB_OWN, row + position)
    scalars = [fold_list, fold_bounds, score_list]

    scale = lax.rsqrt(row_sq + EPSILON) * (1.0 / CODE_TOP**2)
    signed = jnp.where(all_labels < HALF, scale, -scale)
    mods = (all_labels % HALF).astype(jnp.float32)
    totals, normed = (), []
    beside = (*scalars, mods, signed)
    for q in range(parts):
        if q + 1 < parts:
            ahead = (incoming[q], *beside) if q else (incoming[q],)
            incoming.append(exchange(after(outgoing[q + 1], *ahead)))
        partial, sums, *more = stage(
            q, cuts, scalars, mods, signed, incoming[q], normed, totals
        )
        beside = (partial, sums)
        totals, normed = (partial, sums, *more[:3]), normed + more[3:]
    return close(labels, exchange(partial), sums, TB_OWN * LANES * devices)


def solution(mesh):
    return jax.shard_map(
        shards,
        mesh=mesh,
        in_specs=(
            P(("groups", "dp"), None, None),
            P(("groups", "dp")),
            P(("groups", "dp"), None),
            P(("groups", "dp")),
            P(("groups", "dp")),
        ),
        out_specs=(P("groups", "dp"), P(("groups", "dp"))),
        check_vma=False,
    )
```

```python
import functools
import math

import jax
import jax.numpy as jnp
import numpy as np
from jax import lax
from jax.experimental import pallas as pl
from jax.experimental.pallas import tpu as pltpu
from jax.sharding import PartitionSpec as P

K = 512
HALF = K // 2
TB_OWN = 16
LANES = 128
EPSILON = 1e-06
CODE_TOP = 65535.0
CODE_SHIFT = 32768
VMEM_BYTES = 60 * 1024 * 1024
STEP_TILES = 16
PARTS = (0.0, 13 / 16, 1.0)
LOG_STEPS = 1800.0
LOG_MIDDLE = -3.0
CACHED_BLOCKS = 64
QUAD = 4
EIGHT = 8
WIDE_SHIFT = 4
CHUNK = 16
BLOCKS = 4
ROW_SHIFT, SOURCE_SHIFT = 16, 8
PLACE_MASK, SOURCE_MASK, SLOT_MASK = 0xFFFF, 0xFF, 0xFF
BATCH = 8
NT = (((1,), (1,)), ((), ()))
SMEM = pl.BlockSpec(memory_space=pltpu.SMEM)
VMEM = pl.BlockSpec(memory_space=pltpu.VMEM)
ANY = pl.BlockSpec(memory_space=pl.ANY)


def lane_sums(values):
    ones = jnp.ones((8, 2 * LANES), jnp.bfloat16)
    high = values.astype(jnp.bfloat16)
    low = (values - high.astype(jnp.float32)).astype(jnp.bfloat16)
    both = jnp.concatenate([high, low], axis=1)
    return lax.dot_general(ones, both, NT, preferred_element_type=jnp.float32)


def block_sums(square, out_ref, count):
    batch = math.gcd(BATCH, count)

    def one_batch(c, carry):
        some = square[pl.ds(c * batch, batch)].reshape((batch * LANES, LANES))
        sums = lane_sums(some)
        for j in range(batch):
            out_ref[pl.ds(c * batch + j, 1), :] += sums[:1, j * LANES : (j + 1) * LANES]
        return carry

    lax.fori_loop(0, count // batch, one_batch, 0)


def params():
    return pltpu.CompilerParams(vmem_limit_bytes=VMEM_BYTES)


def pack_kernel(cuts, owner_ref, row_ref, *refs):
    parts = len(cuts) - 1
    (*told_refs, x_hbm), refs = refs[:5], refs[5:]
    outs = refs[:parts]
    x, coded, square, sums, words, notes, rank_row, rank_ref, sems, x_sems = refs[parts:]
    tiles = x.shape[0]
    devices = coded.shape[0]
    blocks = square.shape[0]
    step = math.gcd(STEP_TILES, tiles)

    def read(c):
        some = pl.ds(c * step, step)
        return pltpu.make_async_copy(x_hbm.at[some], x.at[some], x_sems.at[c])

    for c in range(tiles // step):
        read(c).start()
    labels, owner, row, sub = [ref[...] for ref in told_refs]
    own, sub_own = [jnp.broadcast_to(v.astype(jnp.float32), (tiles, tiles)) for v in (owner, sub)]
    other, sub_other = jnp.transpose(own), jnp.transpose(sub_own)
    index = [lax.broadcasted_iota(jnp.int32, (tiles, tiles), d) for d in (0, 1)]
    ahead = (sub_other < sub_own) | ((sub_other == sub_own) & (index[0] < index[1]))
    ahead = jnp.where(ahead & (other == own), 1.0, 0.0)
    rank_row[...] = jnp.sum(ahead, axis=0, keepdims=True).astype(jnp.int32)
    pltpu.sync_copy(rank_row, rank_ref)
    square[...] = jnp.zeros_like(square)

    def some_tiles(i, carry):
        pl.when(i % (step // QUAD) == 0)(lambda: read(i // (step // QUAD)).wait())
        for j in range(QUAD):
            t = i * QUAD + j
            some = x[t]
            root = some * lax.rsqrt(some)
            code = (root * CODE_TOP + 0.5).astype(jnp.int32) - CODE_SHIFT
            owner, rank = owner_ref[t], rank_ref[0, t]
            at = pl.ds(pl.multiple_of(rank * LANES, LANES), LANES)
            coded[owner, at, :] = code.astype(jnp.int16)
            square[row_ref[t]] += some * some
        return carry

    lax.fori_loop(0, tiles // QUAD, some_tiles, 0)

    copies = []
    for q in range(parts):
        rows, count = (cuts[q + 1] - cuts[q]) * LANES, devices // (1 if q else math.gcd(4, devices))
        for d in range(0, devices, count):
            from_ref = coded.at[pl.ds(d, count), pl.ds(cuts[q] * LANES, rows)]
            into = outs[q].at[pl.ds(d, count), pl.ds(0, rows)]
            copies.append(pltpu.make_async_copy(from_ref, into, sems.at[len(copies)]))
    for copy in copies:
        copy.start()
    sums[...] = jnp.zeros_like(sums)
    block_sums(square, sums, blocks)
    total = sums[...]
    level = (jnp.log2(jnp.maximum(total, 1e-30)) - LOG_MIDDLE) * LOG_STEPS
    level = jnp.where(total > 0.0, jnp.clip(level, -32700.0, 32700.0), -32768.0)
    level = (level + 32768.5).astype(jnp.int32) - 32768
    words[...] = jnp.zeros_like(words)
    words[:blocks, :] = level
    at = blocks
    for told in (labels, owner, row * TB_OWN + sub):
        words[at : at + told.shape[0], :] = told
        at += told.shape[0]
    notes[...] = jnp.broadcast_to(words[...].astype(jnp.int16)[None], notes.shape)
    into = outs[0].at[:, pl.ds((cuts[1] - cuts[0]) * LANES, notes.shape[1])]
    copies.append(pltpu.make_async_copy(notes, into, sems.at[len(copies)]))
    copies[-1].start()
    for copy in copies:
        copy.wait()


def pack(tile_values, owner, tile_row, told, devices, blocks, cuts):
    tiles = tile_values.shape[0]
    told = [x.reshape(-1, LANES) for x in told]
    noted = -(-(blocks + sum(x.shape[0] for x in told[:3])) // 16) * 16
    rows = [(high - low) * LANES for low, high in zip(cuts, cuts[1:])]
    rows[0] += noted
    return pl.pallas_call(
        functools.partial(pack_kernel, cuts),
        in_specs=[SMEM] * 2 + [VMEM] * 4 + [ANY],
        out_specs=[ANY] * len(rows),
        out_shape=[jax.ShapeDtypeStruct((devices, some, LANES), jnp.int16) for some in rows],
        scratch_shapes=[
            pltpu.VMEM(tile_values.shape, jnp.float32),
            pltpu.VMEM((devices, cuts[-1] * LANES, LANES), jnp.int16),
            pltpu.VMEM((blocks, LANES, LANES), jnp.float32),
            pltpu.VMEM((blocks, LANES), jnp.float32),
            pltpu.VMEM((noted, LANES), jnp.int32),
            pltpu.VMEM((devices, noted, LANES), jnp.int16),
            pltpu.VMEM((1, tiles), jnp.int32),
            pltpu.SMEM((1, tiles), jnp.int32),
            pltpu.SemaphoreType.DMA((len(rows) + 4,)),
            pltpu.SemaphoreType.DMA((tiles // math.gcd(STEP_TILES, tiles),)),
        ],
        compiler_params=params(),
        cost_estimate=pl.CostEstimate(
            flops=8 * tile_values.size,
            bytes_accessed=6 * tile_values.size,
            transcendentals=tile_values.size,
        ),
        name="pack",
    )(owner, tile_row, *told, tile_values)


def stage_kernel(q, bases, last, cached, fold_list, fold_bound, score_list,
                 mods_in, signed_in, x_hbm, *refs):
    base = bases[q]
    earlier, refs = refs[:q], refs[q:]
    before, sums_in, squares_in, *made_in = refs[:5] if q else (None,) * 5
    refs = refs[5:] if q else refs
    part, sums_out, refs = refs[0], refs[1], refs[2:]
    (squares_out, *made_out, fresh_out), refs = ((None,) * 4, refs) if last else (refs[:4], refs[4:])
    spread, x, hot, sums, narrow, tiles, products, scores, squares, mods, signed, *refs = refs
    sems, sub_sems, tile_sems = refs
    devices, width = x.shape[0], x.shape[1] // LANES
    none = products.shape[0] - 1
    parts = len(bases) - 1

    def bound(p, sub):
        return fold_bound[p * (TB_OWN + 1) + sub]

    def score_bound(sub):
        return sum(bound(p, sub) - bound(p, 0) for p in range(parts))

    def complete(arrived):
        def one(i, least):
            sub = TB_OWN - 1 - i
            waits = [bound(p, sub + 1) > bound(p, sub) for p in range(arrived, parts)]
            return jnp.where(functools.reduce(jnp.logical_or, waits), sub, least)

        return lax.fori_loop(0, TB_OWN, one, TB_OWN) if arrived < parts else TB_OWN

    begin, end = complete(q) if q else 0, complete(q + 1)
    needed = [pltpu.make_async_copy(x_hbm.at[:, pl.ds(0, width * LANES)], x, sems.at[0])]
    if q:
        needed.append(pltpu.make_async_copy(made_in[0], spread, sems.at[1]))
    for copy in needed:
        copy.start()

    def columns(sub):
        return (slice(None), pl.ds(pl.multiple_of(sub * 2 * LANES, 2 * LANES), 2 * LANES))

    def group(g):
        size = BLOCKS * 2 * LANES
        return (slice(None), pl.ds(pl.multiple_of(g * size, size), size))

    def sums_read(g):
        return pltpu.make_async_copy(sums_in.at[group(g)], sums.at[group(g)], sub_sems.at[0, g])

    def sums_write(g):
        return pltpu.make_async_copy(sums.at[group(g)], sums_out.at[group(g)], sub_sems.at[1, g])

    def each_sub(low, high, what):
        def one(sub, carry):
            what(sub)
            return carry

        lax.fori_loop(low, high, one, 0)

    if q:
        each_sub(begin // BLOCKS, TB_OWN // BLOCKS, lambda g: sums_read(g).start())
        squares[...] = squares_in[...]
    else:
        sums[...] = jnp.zeros_like(sums)
        squares[...] = jnp.zeros_like(squares)
    later = [pltpu.make_async_copy(made_in[1], hot, sems.at[3])] if q and cached else []

    def each_chunk(p, outside, write, sub, what):
        count = math.gcd(CHUNK, bases[p + 1] - bases[p])

        def one(c, carry):
            away, own = outside.at[pl.ds(c * count, count)], tiles.at[pl.ds(bases[p] + c * count, count)]
            some = (own, away) if write else (away, own)
            what(pltpu.make_async_copy(*some, tile_sems.at[0 if write else p, c]))
            return carry

        first, stop = bound(p, sub) - bases[p], bound(p, TB_OWN) - bases[p]
        lax.fori_loop(first // count, (stop + count - 1) // count, one, 0)

    def each_earlier(what):
        for copy in later:
            what(copy)
        for e, e_hbm in enumerate(earlier):
            each_chunk(e, e_hbm, False, begin, what)

    each_earlier(lambda copy: copy.start())
    products[...] = jnp.zeros_like(products)
    scores[...] = before[...] if q else jnp.zeros_like(scores)
    for held, given, empty in ((mods, mods_in, -1.0), (signed, signed_in, 0.0)):
        held[:none, :] = given[...]
        held[none : none + 1, :] = jnp.full((1, LANES), empty, jnp.float32)
    cluster = lax.broadcasted_iota(jnp.int32, (HALF, LANES), 0).astype(jnp.float32)
    cluster = cluster.astype(jnp.bfloat16).reshape(HALF // 16, 16, LANES)
    one, zero = jnp.ones((), jnp.bfloat16), jnp.zeros((), jnp.bfloat16)
    lane = lax.broadcasted_iota(jnp.int32, (LANES, LANES), 1)

    def column(ref, row):
        return jnp.transpose(jnp.broadcast_to(ref[pl.ds(row, 1), :], (LANES, LANES)))

    def one_hot(row):
        own = column(mods, row).astype(jnp.int32)
        some = [jnp.where(own == lane + g, 1.0, 0.0) for g in range(0, HALF, LANES)]
        return jnp.concatenate(some, axis=1).astype(jnp.bfloat16)

    batch = math.gcd(none + 1, 3)

    def build(c, carry):
        for j in range(batch):
            spread[c * batch + j] = column(signed, c * batch + j)
            if cached:
                hot[c * batch + j] = one_hot(c * batch + j)
        return carry

    if not q:
        lax.fori_loop(0, (none + 1) // batch, build, 0)
    for copy in needed:
        copy.wait()
    if q:
        each_sub(begin // BLOCKS, TB_OWN // BLOCKS, lambda g: sums_read(g).wait())

    def steps(start, end, work):
        wide = 2 * EIGHT
        count = (end - start + EIGHT - 1) >> WIDE_SHIFT

        def one(p, carry):
            work(start + wide * p, wide)
            return carry

        lax.fori_loop(0, count, one, 0)
        pl.when(start + wide * count < end)(lambda: work(start + wide * count, EIGHT))

    def some(entries, start, end, count):
        at = [start + j for j in range(count)]
        at = [(jnp.where(spot < end, spot, start), spot < end) for spot in at]
        return [(entries[spot], spot, held) for spot, held in at]

    def fold_sub(sub):
        start, end = bound(q, sub), bound(q, sub + 1)
        def fold_some(first, count):
            folded, picks = [], []
            for entry, spot, held in some(fold_list, first, end, count):
                row = entry >> ROW_SHIFT
                source, slot = (entry >> SOURCE_SHIFT) & SOURCE_MASK, entry & SLOT_MASK
                raw = x[source, pl.ds(pl.multiple_of(slot * LANES, LANES), LANES), :]
                root = raw.astype(jnp.int32).astype(jnp.float32) + float(CODE_SHIFT)
                scale = spread[row]
                square = root * root
                tile = square * jnp.abs(scale)
                lower = square * jnp.maximum(scale, 0.0)
                tiles[spot] = tile.astype(jnp.bfloat16)
                halves = [lower.astype(jnp.bfloat16), (tile - lower).astype(jnp.bfloat16)]
                folded.append(jnp.concatenate(halves, axis=1))
                own = jnp.broadcast_to(mods[pl.ds(jnp.where(held, row, none), 1), :], (16, LANES))
                own = jnp.where(cluster == own.astype(jnp.bfloat16)[None], one, zero)
                picks.append(own.reshape(HALF, LANES))
            pick = jnp.concatenate(picks, axis=1)
            sums[columns(sub)] += jnp.dot(
                pick, jnp.concatenate(folded, axis=0), preferred_element_type=jnp.float32
            )

        steps(start, end, fold_some)

    def fold_group(g):
        each_sub(jnp.maximum(begin, g * BLOCKS), (g + 1) * BLOCKS, fold_sub)
        sums_write(g).start()

    each_sub(begin // BLOCKS, TB_OWN // BLOCKS, fold_group)
    kept = []
    if not last:
        each_chunk(q, fresh_out, True, end, lambda copy: copy.start())
        kept.append(pltpu.make_async_copy(spread, made_out[0], sems.at[4]))
        kept.append(pltpu.make_async_copy(hot, made_out[1], sems.at[5]))
    for copy in kept:
        copy.start()
    each_earlier(lambda copy: copy.wait())

    def score_sub(sub):
        start, end = score_bound(sub), score_bound(sub + 1)
        own_sums = sums[columns(sub)]
        narrow[...] = own_sums.astype(jnp.bfloat16)
        squares[...] += own_sums * own_sums

        def score_some(first, count):
            listed = some(score_list, first, end, count)
            rows = [jnp.where(held, entry >> ROW_SHIFT, none) for entry, spot, held in listed]
            spots = [entry & PLACE_MASK for entry, spot, held in listed]
            hots = [hot[row] if cached else one_hot(row) for row in rows]
            chosen = jnp.dot(
                jnp.concatenate(hots, axis=0), narrow[...], preferred_element_type=jnp.float32
            )
            for j in range(count):
                both = chosen[j * LANES : (j + 1) * LANES]
                own = jnp.where(spread[rows[j]] < 0.0, both[:, LANES:], both[:, :LANES])
                products[rows[j]] += own * tiles[spots[j]].astype(jnp.float32)

        steps(start, end, score_some)

    each_sub(begin, end, score_sub)
    block_sums(products, scores, none)
    if last:
        own = none // devices
        square = [lane_sums(squares[:, h : h + LANES])[:1] for h in (0, LANES)]
        square = jnp.concatenate(square, axis=1)
        for d in range(devices):
            part[d, :, part.shape[2] - K :] = square
            for b in range(own):
                at = d * own + b
                part[d, :, b * LANES : (b + 1) * LANES] = scores[at : at + 1, :]
    else:
        part[...] = scores[...]
        squares_out[...] = squares[...]
    for copy in kept:
        copy.wait()
    if not last:
        each_chunk(q, fresh_out, True, end, lambda copy: copy.wait())
    each_sub(begin // BLOCKS, TB_OWN // BLOCKS, lambda g: sums_write(g).wait())


def stage(q, cuts, scalars, mods, signed, x, normed, totals):
    devices = x.shape[0]
    last = q == len(cuts) - 2
    blocks = mods.shape[0]
    cached = blocks <= CACHED_BLOCKS
    width = cuts[q + 1] - cuts[q]
    home = blocks // devices * LANES
    wide = jax.ShapeDtypeStruct((HALF, TB_OWN * 2 * LANES), jnp.float32)
    square = jax.ShapeDtypeStruct((HALF, 2 * LANES), jnp.float32)
    if last:
        out_shape = [jax.ShapeDtypeStruct((devices, 1, home + K), jnp.float32), wide]
    else:
        out_shape = [
            jax.ShapeDtypeStruct((blocks, LANES), jnp.float32),
            wide,
            square,
            jax.ShapeDtypeStruct((blocks + 1, LANES, LANES), jnp.float32),
            jax.ShapeDtypeStruct((blocks + 1 if cached else 1, LANES, HALF), jnp.bfloat16),
            jax.ShapeDtypeStruct((devices * width, LANES, LANES), jnp.bfloat16),
        ]
    slots = devices * cuts[-1]
    sizes = [devices * (high - low) for low, high in zip(cuts, cuts[1:])]
    chunks = max(size // math.gcd(CHUNK, size) for size in sizes)
    operands = [*scalars, mods, signed, x, *normed, *totals]
    return pl.pallas_call(
        functools.partial(stage_kernel, q, [devices * cut for cut in cuts], last, cached),
        in_specs=[SMEM] * len(scalars) + [VMEM] * 2 + [ANY] * (1 + q) + [VMEM, ANY, VMEM, ANY, ANY][: len(totals)],
        out_specs=[VMEM, ANY, VMEM, ANY, ANY, ANY][: len(out_shape)],
        out_shape=out_shape,
        input_output_aliases={len(operands) - len(totals) + 1: 1} if q else {},
        scratch_shapes=[
            pltpu.VMEM((blocks + 1, LANES, LANES), jnp.float32),
            pltpu.VMEM((devices, width * LANES, LANES), jnp.int16),
            pltpu.VMEM((blocks + 1 if cached else 1, LANES, HALF), jnp.bfloat16),
            pltpu.VMEM(wide.shape, jnp.float32),
            pltpu.VMEM(square.shape, jnp.bfloat16),
            pltpu.VMEM((slots, LANES, LANES), jnp.bfloat16),
            pltpu.VMEM((blocks + 1, LANES, LANES), jnp.float32),
            pltpu.VMEM((blocks, LANES), jnp.float32),
            pltpu.VMEM(square.shape, jnp.float32),
            pltpu.VMEM((blocks + 1, LANES), jnp.float32),
            pltpu.VMEM((blocks + 1, LANES), jnp.float32),
            pltpu.SemaphoreType.DMA((6,)),
            pltpu.SemaphoreType.DMA((2, TB_OWN // BLOCKS)),
            pltpu.SemaphoreType.DMA((max(q, 1), chunks)),
        ],
        compiler_params=params(),
        cost_estimate=pl.CostEstimate(
            flops=devices * width * LANES * LANES * K * 8,
            bytes_accessed=4 * devices * width * LANES * LANES + 8 * K * TB_OWN * LANES,
            transcendentals=0,
        ),
        name="stage",
    )(*operands)


def close_kernel(root, groups, labels_ref, got_ref, sums_hbm, out_hbm, similarity, sums, out, sems):
    width = TB_OWN // groups
    reads, writes = [], []
    for g in range(groups):
        some = (slice(None), pl.ds(g * width * 2 * LANES, width * 2 * LANES))
        reads.append(pltpu.make_async_copy(sums_hbm.at[some], sums.at[some], sems.at[0, g]))
        some = (slice(None), pl.ds(g * width * LANES, width * LANES))
        writes.append(pltpu.make_async_copy(out.at[some], out_hbm.at[some], sems.at[1, g]))
        reads[g].start()
    total = jnp.sum(got_ref[...], axis=0)
    home = total.shape[1] - K
    own = lax.rsqrt(total[:, home:] + EPSILON)
    columns = [
        jnp.transpose(jnp.broadcast_to(own[:, k : k + LANES], (LANES, LANES)))
        for k in range(0, K, LANES)
    ]
    cluster = lax.broadcasted_iota(jnp.int32, (LANES, LANES), 0)
    for b in range(home // LANES):
        found = jnp.zeros((LANES, LANES), jnp.float32)
        for i, column in enumerate(columns):
            found += jnp.where(cluster + i * LANES == labels_ref[b : b + 1, :], column, 0.0)
        found = jnp.sum(found, axis=0, keepdims=True)
        similarity[b : b + 1, :] = total[:, b * LANES : (b + 1) * LANES] * found
    for g in range(groups):
        reads[g].wait()

        def one_sub(sub, carry):
            to = pl.ds(pl.multiple_of(sub * LANES, LANES), LANES)
            for i, column in enumerate(columns):
                half, row = divmod(i * LANES, HALF)
                at = pl.ds(pl.multiple_of((2 * sub + half) * LANES, LANES), LANES)
                done = sums[row : row + LANES, at] * column * root
                out[i * LANES : (i + 1) * LANES, to] = done.astype(jnp.bfloat16)
            return carry

        lax.fori_loop(g * width, (g + 1) * width, one_sub, 0)
        writes[g].start()
    for write in writes:
        write.wait()


def close(labels, got, sums, vocab_size):
    groups = 4
    labels = labels.reshape(-1, LANES)
    wide = jax.ShapeDtypeStruct((K, TB_OWN * LANES), jnp.bfloat16)
    centroids, similarity = pl.pallas_call(
        functools.partial(close_kernel, math.sqrt(vocab_size), groups),
        in_specs=[VMEM, VMEM, ANY],
        out_specs=[ANY, VMEM],
        out_shape=[wide, jax.ShapeDtypeStruct(labels.shape, jnp.float32)],
        scratch_shapes=[
            pltpu.VMEM(sums.shape, jnp.float32),
            pltpu.VMEM(wide.shape, jnp.bfloat16),
            pltpu.SemaphoreType.DMA((2, groups)),
        ],
        compiler_params=params(),
        cost_estimate=pl.CostEstimate(
            flops=2 * sums.size, bytes_accessed=6 * sums.size, transcendentals=0
        ),
        name="close",
    )(labels, got, sums)
    return centroids, similarity.reshape(-1)


def exchange(x):
    return lax.all_to_all(x, "dp", split_axis=0, concat_axis=0, tiled=True)


def after(value, *others):
    return lax.optimization_barrier((value, *others))[0]


def sorted_slots(key, top, entries):
    slots = jnp.arange(key.shape[0], dtype=jnp.int32)
    ahead = (key[None, :] < key[:, None]) | (
        (key[None, :] == key[:, None]) & (slots[None, :] < slots[:, None])
    )
    position = jnp.sum(ahead.astype(jnp.int32), axis=1)
    here = position[None, :] == slots[:, None]
    listed = jnp.sum(jnp.where(here, entries[None, :], 0), axis=1)
    levels = jnp.arange(top + 1, dtype=jnp.int32)
    bounds = jnp.sum((key[None, :] < levels[:, None]).astype(jnp.int32), axis=1)
    return listed, bounds, position


def ranks(group, sub):
    index = jnp.arange(sub.shape[-1], dtype=jnp.int32)
    before = (sub[..., None, :] < sub[..., :, None]) | (
        (sub[..., None, :] == sub[..., :, None]) & (index[None, :] < index[:, None])
    )
    same = group[..., None, :] == group[..., :, None]
    return jnp.sum((before & same).astype(jnp.int32), axis=-1)


def shards(tile_values, tile_row, tile_owner, tile_sub, labels):
    devices = lax.axis_size("dp")
    tiles = tile_values.shape[0]
    home = labels.shape[0]
    blocks = home // LANES * devices
    cap = max(2, 2 * tiles // devices)
    cuts = tuple(sorted({int(cap * share) for share in PARTS})) if cap >= 8 else (0, cap)
    parts = len(cuts) - 1
    here = lax.axis_index("dp").astype(jnp.int32)
    owner = tile_owner[:, 0]

    told = (labels, owner, tile_row, tile_sub)
    outgoing = pack(tile_values, owner, tile_row, told, devices, blocks, cuts)
    incoming = [exchange(outgoing[0])]
    heard = incoming[0][:, (cuts[1] - cuts[0]) * LANES :].astype(jnp.int32)
    level = heard[:, :blocks]
    partial_sq = jnp.exp2(level.astype(jnp.float32) * (1.0 / LOG_STEPS) + LOG_MIDDLE)
    row_sq = jnp.sum(jnp.where(level > -32768, partial_sq, 0.0), axis=0)
    all_described = heard[:, blocks:].reshape(devices, -1)
    all_labels = all_described[:, :home].reshape(blocks, LANES)
    mine = all_described[:, home : home + tiles] == here
    code = all_described[:, home + tiles : home + 2 * tiles]
    rank = ranks(mine.astype(jnp.int32), code % TB_OWN)
    chosen = mine[:, None, :] & (rank[:, None, :] == jnp.arange(cap)[None, :, None])
    meta = jnp.sum(jnp.where(chosen, code[:, None, :] + 1, 0), axis=2).reshape(-1) - 1
    sub = jnp.where(meta < 0, TB_OWN, meta % TB_OWN)
    slot_rank = np.arange(devices * cap) % cap
    slot_part = np.searchsorted(np.array(cuts), slot_rank, side="right") - 1
    low = np.array(cuts)[slot_part]
    fold_key = jnp.asarray(slot_part * (TB_OWN + 1), jnp.int32) + sub
    row = (meta // TB_OWN) << ROW_SHIFT
    from_slot = (np.arange(devices * cap) // cap << SOURCE_SHIFT) + slot_rank - low
    fold_list, fold_bounds, position = sorted_slots(
        fold_key, parts * (TB_OWN + 1), row + jnp.asarray(from_slot, jnp.int32)
    )
    score_list, *_ = sorted_slots(sub, TB_OWN, row + position)
    scalars = [fold_list, fold_bounds, score_list]

    scale = lax.rsqrt(row_sq + EPSILON) * (1.0 / CODE_TOP**2)
    signed = jnp.where(all_labels < HALF, scale, -scale)
    mods = (all_labels % HALF).astype(jnp.float32)
    totals, normed = (), []
    beside = (*scalars, mods, signed)
    for q in range(parts):
        if q + 1 < parts:
            ahead = (incoming[q], *beside) if q else (incoming[q],)
            incoming.append(exchange(after(outgoing[q + 1], *ahead)))
        partial, sums, *more = stage(
            q, cuts, scalars, mods, signed, incoming[q], normed, totals
        )
        beside = (partial, sums)
        totals, normed = (partial, sums, *more[:3]), normed + more[3:]
    return close(labels, exchange(partial), sums, TB_OWN * LANES * devices)


def solution(mesh):
    return jax.shard_map(
        shards,
        mesh=mesh,
        in_specs=(
            P(("groups", "dp"), None, None),
            P(("groups", "dp")),
            P(("groups", "dp"), None),
            P(("groups", "dp")),
            P(("groups", "dp")),
        ),
        out_specs=(P("groups", "dp"), P(("groups", "dp"))),
        check_vma=False,
    )
```

```python
import functools
import math

import jax
import jax.numpy as jnp
import numpy as np
from jax import lax
from jax.experimental import pallas as pl
from jax.experimental.pallas import tpu as pltpu
from jax.sharding import PartitionSpec as P

K = 512
HALF = K // 2
TB_OWN = 16
LANES = 128
EPSILON = 1e-06
CODE_TOP = 65535.0
CODE_SHIFT = 32768
VMEM_BYTES = 60 * 1024 * 1024
STEP_TILES = 16
PARTS = (0.0, 13 / 16, 1.0)
LOG_STEPS = 1800.0
LOG_MIDDLE = -3.0
CACHED_BLOCKS = 64
QUAD = 4
EIGHT = 8
WIDE_SHIFT = 4
CHUNK = 16
BLOCKS = 4
ROW_SHIFT, SOURCE_SHIFT = 16, 8
PLACE_MASK, SOURCE_MASK, SLOT_MASK = 0xFFFF, 0xFF, 0xFF
BATCH = 8
NT = (((1,), (1,)), ((), ()))
SMEM = pl.BlockSpec(memory_space=pltpu.SMEM)
VMEM = pl.BlockSpec(memory_space=pltpu.VMEM)
ANY = pl.BlockSpec(memory_space=pl.ANY)


def lane_sums(values):
    ones = jnp.ones((8, 2 * LANES), jnp.bfloat16)
    high = values.astype(jnp.bfloat16)
    low = (values - high.astype(jnp.float32)).astype(jnp.bfloat16)
    both = jnp.concatenate([high, low], axis=1)
    return lax.dot_general(ones, both, NT, preferred_element_type=jnp.float32)


def block_sums(square, out_ref, count):
    batch = math.gcd(BATCH, count)

    def one_batch(c, carry):
        some = square[pl.ds(c * batch, batch)].reshape((batch * LANES, LANES))
        sums = lane_sums(some)
        for j in range(batch):
            out_ref[pl.ds(c * batch + j, 1), :] += sums[:1, j * LANES : (j + 1) * LANES]
        return carry

    lax.fori_loop(0, count // batch, one_batch, 0)


def params():
    return pltpu.CompilerParams(vmem_limit_bytes=VMEM_BYTES)


def pack_kernel(cuts, owner_ref, row_ref, *refs):
    parts = len(cuts) - 1
    (*told_refs, x_hbm), refs = refs[:5], refs[5:]
    outs = refs[:parts]
    x, coded, square, sums, words, notes, rank_row, rank_ref, sems, x_sems = refs[parts:]
    tiles = x.shape[0]
    devices = coded.shape[0]
    blocks = square.shape[0]
    step = math.gcd(STEP_TILES, tiles)

    def read(c):
        some = pl.ds(c * step, step)
        return pltpu.make_async_copy(x_hbm.at[some], x.at[some], x_sems.at[c])

    for c in range(tiles // step):
        read(c).start()
    labels, owner, row, sub = [ref[...] for ref in told_refs]
    own, sub_own = [jnp.broadcast_to(v.astype(jnp.float32), (tiles, tiles)) for v in (owner, sub)]
    other, sub_other = jnp.transpose(own), jnp.transpose(sub_own)
    index = [lax.broadcasted_iota(jnp.int32, (tiles, tiles), d) for d in (0, 1)]
    ahead = (sub_other < sub_own) | ((sub_other == sub_own) & (index[0] < index[1]))
    ahead = jnp.where(ahead & (other == own), 1.0, 0.0)
    rank_row[...] = jnp.sum(ahead, axis=0, keepdims=True).astype(jnp.int32)
    pltpu.sync_copy(rank_row, rank_ref)
    square[...] = jnp.zeros_like(square)

    def some_tiles(i, carry):
        pl.when(i % (step // QUAD) == 0)(lambda: read(i // (step // QUAD)).wait())
        for j in range(QUAD):
            t = i * QUAD + j
            some = x[t]
            root = some * lax.rsqrt(some)
            code = (root * CODE_TOP + 0.5).astype(jnp.int32) - CODE_SHIFT
            owner, rank = owner_ref[t], rank_ref[0, t]
            at = pl.ds(pl.multiple_of(rank * LANES, LANES), LANES)
            coded[owner, at, :] = code.astype(jnp.int16)
            square[row_ref[t]] += some * some
        return carry

    lax.fori_loop(0, tiles // QUAD, some_tiles, 0)

    copies = []
    for q in range(parts):
        rows, count = (cuts[q + 1] - cuts[q]) * LANES, devices // (1 if q else math.gcd(4, devices))
        for d in range(0, devices, count):
            from_ref = coded.at[pl.ds(d, count), pl.ds(cuts[q] * LANES, rows)]
            into = outs[q].at[pl.ds(d, count), pl.ds(0, rows)]
            copies.append(pltpu.make_async_copy(from_ref, into, sems.at[len(copies)]))
    for copy in copies:
        copy.start()
    sums[...] = jnp.zeros_like(sums)
    block_sums(square, sums, blocks)
    total = sums[...]
    level = (jnp.log2(jnp.maximum(total, 1e-30)) - LOG_MIDDLE) * LOG_STEPS
    level = jnp.where(total > 0.0, jnp.clip(level, -32700.0, 32700.0), -32768.0)
    level = (level + 32768.5).astype(jnp.int32) - 32768
    words[...] = jnp.zeros_like(words)
    words[:blocks, :] = level
    at = blocks
    for told in (labels, owner, row * TB_OWN + sub):
        words[at : at + told.shape[0], :] = told
        at += told.shape[0]
    notes[...] = jnp.broadcast_to(words[...].astype(jnp.int16)[None], notes.shape)
    into = outs[0].at[:, pl.ds((cuts[1] - cuts[0]) * LANES, notes.shape[1])]
    copies.append(pltpu.make_async_copy(notes, into, sems.at[len(copies)]))
    copies[-1].start()
    for copy in copies:
        copy.wait()


def pack(tile_values, owner, tile_row, told, devices, blocks, cuts):
    tiles = tile_values.shape[0]
    told = [x.reshape(-1, LANES) for x in told]
    noted = -(-(blocks + sum(x.shape[0] for x in told[:3])) // 16) * 16
    rows = [(high - low) * LANES for low, high in zip(cuts, cuts[1:])]
    rows[0] += noted
    return pl.pallas_call(
        functools.partial(pack_kernel, cuts),
        in_specs=[SMEM] * 2 + [VMEM] * 4 + [ANY],
        out_specs=[ANY] * len(rows),
        out_shape=[jax.ShapeDtypeStruct((devices, some, LANES), jnp.int16) for some in rows],
        scratch_shapes=[
            pltpu.VMEM(tile_values.shape, jnp.float32),
            pltpu.VMEM((devices, cuts[-1] * LANES, LANES), jnp.int16),
            pltpu.VMEM((blocks, LANES, LANES), jnp.float32),
            pltpu.VMEM((blocks, LANES), jnp.float32),
            pltpu.VMEM((noted, LANES), jnp.int32),
            pltpu.VMEM((devices, noted, LANES), jnp.int16),
            pltpu.VMEM((1, tiles), jnp.int32),
            pltpu.SMEM((1, tiles), jnp.int32),
            pltpu.SemaphoreType.DMA((len(rows) + 4,)),
            pltpu.SemaphoreType.DMA((tiles // math.gcd(STEP_TILES, tiles),)),
        ],
        compiler_params=params(),
        cost_estimate=pl.CostEstimate(
            flops=8 * tile_values.size,
            bytes_accessed=6 * tile_values.size,
            transcendentals=tile_values.size,
        ),
        name="pack",
    )(owner, tile_row, *told, tile_values)


def stage_kernel(q, bases, last, cached, fold_list, fold_bound, score_list,
                 mods_in, signed_in, x_hbm, *refs):
    base = bases[q]
    earlier, refs = refs[:q], refs[q:]
    before, sums_in, squares_in, *made_in = refs[:5] if q else (None,) * 5
    refs = refs[5:] if q else refs
    part, sums_out, refs = refs[0], refs[1], refs[2:]
    (squares_out, *made_out, fresh_out), refs = ((None,) * 4, refs) if last else (refs[:4], refs[4:])
    spread, x, hot, sums, narrow, tiles, products, scores, squares, mods, signed, *refs = refs
    sems, sub_sems, tile_sems = refs
    devices, width = x.shape[0], x.shape[1] // LANES
    none = products.shape[0] - 1
    parts = len(bases) - 1

    def bound(p, sub):
        return fold_bound[p * (TB_OWN + 1) + sub]

    def score_bound(sub):
        return sum(bound(p, sub) - bound(p, 0) for p in range(parts))

    def complete(arrived):
        def one(i, least):
            sub = TB_OWN - 1 - i
            waits = [bound(p, sub + 1) > bound(p, sub) for p in range(arrived, parts)]
            return jnp.where(functools.reduce(jnp.logical_or, waits), sub, least)

        return lax.fori_loop(0, TB_OWN, one, TB_OWN) if arrived < parts else TB_OWN

    begin, end = complete(q) if q else 0, complete(q + 1)
    needed = [pltpu.make_async_copy(x_hbm.at[:, pl.ds(0, width * LANES)], x, sems.at[0])]
    if q:
        needed.append(pltpu.make_async_copy(made_in[0], spread, sems.at[1]))
    for copy in needed:
        copy.start()

    def columns(sub):
        return (slice(None), pl.ds(pl.multiple_of(sub * 2 * LANES, 2 * LANES), 2 * LANES))

    def group(g):
        size = BLOCKS * 2 * LANES
        return (slice(None), pl.ds(pl.multiple_of(g * size, size), size))

    def sums_read(g):
        return pltpu.make_async_copy(sums_in.at[group(g)], sums.at[group(g)], sub_sems.at[0, g])

    def sums_write(g):
        return pltpu.make_async_copy(sums.at[group(g)], sums_out.at[group(g)], sub_sems.at[1, g])

    def each_sub(low, high, what):
        def one(sub, carry):
            what(sub)
            return carry

        lax.fori_loop(low, high, one, 0)

    if q:
        each_sub(begin // BLOCKS, TB_OWN // BLOCKS, lambda g: sums_read(g).start())
        squares[...] = squares_in[...]
    else:
        sums[...] = jnp.zeros_like(sums)
        squares[...] = jnp.zeros_like(squares)
    later = [pltpu.make_async_copy(made_in[1], hot, sems.at[3])] if q and cached else []

    def each_chunk(p, outside, write, sub, what):
        count = math.gcd(CHUNK, bases[p + 1] - bases[p])

        def one(c, carry):
            away, own = outside.at[pl.ds(c * count, count)], tiles.at[pl.ds(bases[p] + c * count, count)]
            some = (own, away) if write else (away, own)
            what(pltpu.make_async_copy(*some, tile_sems.at[0 if write else p, c]))
            return carry

        first, stop = bound(p, sub) - bases[p], bound(p, TB_OWN) - bases[p]
        lax.fori_loop(first // count, (stop + count - 1) // count, one, 0)

    def each_earlier(what):
        for copy in later:
            what(copy)
        for e, e_hbm in enumerate(earlier):
            each_chunk(e, e_hbm, False, begin, what)

    each_earlier(lambda copy: copy.start())
    products[...] = jnp.zeros_like(products)
    scores[...] = before[...] if q else jnp.zeros_like(scores)
    for held, given, empty in ((mods, mods_in, -1.0), (signed, signed_in, 0.0)):
        held[:none, :] = given[...]
        held[none : none + 1, :] = jnp.full((1, LANES), empty, jnp.float32)
    cluster = lax.broadcasted_iota(jnp.int32, (HALF, LANES), 0).astype(jnp.float32)
    cluster = cluster.astype(jnp.bfloat16).reshape(HALF // 16, 16, LANES)
    one, zero = jnp.ones((), jnp.bfloat16), jnp.zeros((), jnp.bfloat16)
    lane = lax.broadcasted_iota(jnp.int32, (LANES, LANES), 1)

    def column(ref, row):
        return jnp.transpose(jnp.broadcast_to(ref[pl.ds(row, 1), :], (LANES, LANES)))

    def one_hot(row):
        own = column(mods, row).astype(jnp.int32)
        some = [jnp.where(own == lane + g, 1.0, 0.0) for g in range(0, HALF, LANES)]
        return jnp.concatenate(some, axis=1).astype(jnp.bfloat16)

    batch = math.gcd(none + 1, 3)

    def build(c, carry):
        for j in range(batch):
            spread[c * batch + j] = column(signed, c * batch + j)
            if cached:
                hot[c * batch + j] = one_hot(c * batch + j)
        return carry

    if not q:
        lax.fori_loop(0, (none + 1) // batch, build, 0)
    for copy in needed:
        copy.wait()
    if q:
        each_sub(begin // BLOCKS, TB_OWN // BLOCKS, lambda g: sums_read(g).wait())

    def steps(start, end, work):
        wide = 2 * EIGHT
        count = (end - start + EIGHT - 1) >> WIDE_SHIFT

        def one(p, carry):
            work(start + wide * p, wide)
            return carry

        lax.fori_loop(0, count, one, 0)
        pl.when(start + wide * count < end)(lambda: work(start + wide * count, EIGHT))

    def some(entries, start, end, count):
        at = [start + j for j in range(count)]
        at = [(jnp.where(spot < end, spot, start), spot < end) for spot in at]
        return [(entries[spot], spot, held) for spot, held in at]

    def fold_sub(sub):
        start, end = bound(q, sub), bound(q, sub + 1)
        def fold_some(first, count):
            folded, picks = [], []
            for entry, spot, held in some(fold_list, first, end, count):
                row = entry >> ROW_SHIFT
                source, slot = (entry >> SOURCE_SHIFT) & SOURCE_MASK, entry & SLOT_MASK
                raw = x[source, pl.ds(pl.multiple_of(slot * LANES, LANES), LANES), :]
                root = raw.astype(jnp.int32).astype(jnp.float32) + float(CODE_SHIFT)
                scale = spread[row]
                square = root * root
                tile = square * jnp.abs(scale)
                lower = square * jnp.maximum(scale, 0.0)
                tiles[spot] = tile.astype(jnp.bfloat16)
                halves = [lower.astype(jnp.bfloat16), (tile - lower).astype(jnp.bfloat16)]
                folded.append(jnp.concatenate(halves, axis=1))
                own = jnp.broadcast_to(mods[pl.ds(jnp.where(held, row, none), 1), :], (16, LANES))
                own = jnp.where(cluster == own.astype(jnp.bfloat16)[None], one, zero)
                picks.append(own.reshape(HALF, LANES))
            pick = jnp.concatenate(picks, axis=1)
            sums[columns(sub)] += jnp.dot(
                pick, jnp.concatenate(folded, axis=0), preferred_element_type=jnp.float32
            )

        steps(start, end, fold_some)

    def fold_group(g):
        each_sub(jnp.maximum(begin, g * BLOCKS), (g + 1) * BLOCKS, fold_sub)
        sums_write(g).start()

    each_sub(begin // BLOCKS, TB_OWN // BLOCKS, fold_group)
    kept = []
    if not last:
        each_chunk(q, fresh_out, True, end, lambda copy: copy.start())
        kept.append(pltpu.make_async_copy(spread, made_out[0], sems.at[4]))
        kept.append(pltpu.make_async_copy(hot, made_out[1], sems.at[5]))
    for copy in kept:
        copy.start()
    each_earlier(lambda copy: copy.wait())

    def score_sub(sub):
        start, end = score_bound(sub), score_bound(sub + 1)
        own_sums = sums[columns(sub)]
        narrow[...] = own_sums.astype(jnp.bfloat16)
        squares[...] += own_sums * own_sums

        def score_some(first, count):
            listed = some(score_list, first, end, count)
            rows = [jnp.where(held, entry >> ROW_SHIFT, none) for entry, spot, held in listed]
            spots = [entry & PLACE_MASK for entry, spot, held in listed]
            hots = [hot[row] if cached else one_hot(row) for row in rows]
            chosen = jnp.dot(
                jnp.concatenate(hots, axis=0), narrow[...], preferred_element_type=jnp.float32
            )
            for j in range(count):
                both = chosen[j * LANES : (j + 1) * LANES]
                own = jnp.where(spread[rows[j]] < 0.0, both[:, LANES:], both[:, :LANES])
                products[rows[j]] += own * tiles[spots[j]].astype(jnp.float32)

        steps(start, end, score_some)

    each_sub(begin, end, score_sub)
    block_sums(products, scores, none)
    if last:
        own = none // devices
        square = [lane_sums(squares[:, h : h + LANES])[:1] for h in (0, LANES)]
        square = jnp.concatenate(square, axis=1)
        for d in range(devices):
            part[d, :, part.shape[2] - K :] = square
            for b in range(own):
                at = d * own + b
                part[d, :, b * LANES : (b + 1) * LANES] = scores[at : at + 1, :]
    else:
        part[...] = scores[...]
        squares_out[...] = squares[...]
    for copy in kept:
        copy.wait()
    if not last:
        each_chunk(q, fresh_out, True, end, lambda copy: copy.wait())
    each_sub(begin // BLOCKS, TB_OWN // BLOCKS, lambda g: sums_write(g).wait())


def stage(q, cuts, scalars, mods, signed, x, normed, totals):
    devices = x.shape[0]
    last = q == len(cuts) - 2
    blocks = mods.shape[0]
    cached = blocks <= CACHED_BLOCKS
    width = cuts[q + 1] - cuts[q]
    home = blocks // devices * LANES
    wide = jax.ShapeDtypeStruct((HALF, TB_OWN * 2 * LANES), jnp.float32)
    square = jax.ShapeDtypeStruct((HALF, 2 * LANES), jnp.float32)
    if last:
        out_shape = [jax.ShapeDtypeStruct((devices, 1, home + K), jnp.float32), wide]
    else:
        out_shape = [
            jax.ShapeDtypeStruct((blocks, LANES), jnp.float32),
            wide,
            square,
            jax.ShapeDtypeStruct((blocks + 1, LANES, LANES), jnp.float32),
            jax.ShapeDtypeStruct((blocks + 1 if cached else 1, LANES, HALF), jnp.bfloat16),
            jax.ShapeDtypeStruct((devices * width, LANES, LANES), jnp.bfloat16),
        ]
    slots = devices * cuts[-1]
    sizes = [devices * (high - low) for low, high in zip(cuts, cuts[1:])]
    chunks = max(size // math.gcd(CHUNK, size) for size in sizes)
    operands = [*scalars, mods, signed, x, *normed, *totals]
    return pl.pallas_call(
        functools.partial(stage_kernel, q, [devices * cut for cut in cuts], last, cached),
        in_specs=[SMEM] * len(scalars) + [VMEM] * 2 + [ANY] * (1 + q) + [VMEM, ANY, VMEM, ANY, ANY][: len(totals)],
        out_specs=[VMEM, ANY, VMEM, ANY, ANY, ANY][: len(out_shape)],
        out_shape=out_shape,
        input_output_aliases={len(operands) - len(totals) + 1: 1} if q else {},
        scratch_shapes=[
            pltpu.VMEM((blocks + 1, LANES, LANES), jnp.float32),
            pltpu.VMEM((devices, width * LANES, LANES), jnp.int16),
            pltpu.VMEM((blocks + 1 if cached else 1, LANES, HALF), jnp.bfloat16),
            pltpu.VMEM(wide.shape, jnp.float32),
            pltpu.VMEM(square.shape, jnp.bfloat16),
            pltpu.VMEM((slots, LANES, LANES), jnp.bfloat16),
            pltpu.VMEM((blocks + 1, LANES, LANES), jnp.float32),
            pltpu.VMEM((blocks, LANES), jnp.float32),
            pltpu.VMEM(square.shape, jnp.float32),
            pltpu.VMEM((blocks + 1, LANES), jnp.float32),
            pltpu.VMEM((blocks + 1, LANES), jnp.float32),
            pltpu.SemaphoreType.DMA((6,)),
            pltpu.SemaphoreType.DMA((2, TB_OWN // BLOCKS)),
            pltpu.SemaphoreType.DMA((max(q, 1), chunks)),
        ],
        compiler_params=params(),
        cost_estimate=pl.CostEstimate(
            flops=devices * width * LANES * LANES * K, bytes_accessed=wide.size, transcendentals=0
        ),
        name="stage",
    )(*operands)


def close_kernel(root, groups, labels_ref, got_ref, sums_hbm, out_hbm, similarity, sums, out, sems):
    width = TB_OWN // groups
    reads, writes = [], []
    for g in range(groups):
        some = (slice(None), pl.ds(g * width * 2 * LANES, width * 2 * LANES))
        reads.append(pltpu.make_async_copy(sums_hbm.at[some], sums.at[some], sems.at[0, g]))
        some = (slice(None), pl.ds(g * width * LANES, width * LANES))
        writes.append(pltpu.make_async_copy(out.at[some], out_hbm.at[some], sems.at[1, g]))
        reads[g].start()
    total = jnp.sum(got_ref[...], axis=0)
    home = total.shape[1] - K
    own = lax.rsqrt(total[:, home:] + EPSILON)
    columns = [
        jnp.transpose(jnp.broadcast_to(own[:, k : k + LANES], (LANES, LANES)))
        for k in range(0, K, LANES)
    ]
    cluster = lax.broadcasted_iota(jnp.int32, (LANES, LANES), 0)
    for b in range(home // LANES):
        found = jnp.zeros((LANES, LANES), jnp.float32)
        for i, column in enumerate(columns):
            found += jnp.where(cluster + i * LANES == labels_ref[b : b + 1, :], column, 0.0)
        found = jnp.sum(found, axis=0, keepdims=True)
        similarity[b : b + 1, :] = total[:, b * LANES : (b + 1) * LANES] * found
    for g in range(groups):
        reads[g].wait()

        def one_sub(sub, carry):
            to = pl.ds(pl.multiple_of(sub * LANES, LANES), LANES)
            for i, column in enumerate(columns):
                half, row = divmod(i * LANES, HALF)
                at = pl.ds(pl.multiple_of((2 * sub + half) * LANES, LANES), LANES)
                done = sums[row : row + LANES, at] * column * root
                out[i * LANES : (i + 1) * LANES, to] = done.astype(jnp.bfloat16)
            return carry

        lax.fori_loop(g * width, (g + 1) * width, one_sub, 0)
        writes[g].start()
    for write in writes:
        write.wait()


def close(labels, got, sums, vocab_size):
    groups = 8
    labels = labels.reshape(-1, LANES)
    wide = jax.ShapeDtypeStruct((K, TB_OWN * LANES), jnp.bfloat16)
    centroids, similarity = pl.pallas_call(
        functools.partial(close_kernel, math.sqrt(vocab_size), groups),
        in_specs=[VMEM, VMEM, ANY],
        out_specs=[ANY, VMEM],
        out_shape=[wide, jax.ShapeDtypeStruct(labels.shape, jnp.float32)],
        scratch_shapes=[
            pltpu.VMEM(sums.shape, jnp.float32),
            pltpu.VMEM(wide.shape, jnp.bfloat16),
            pltpu.SemaphoreType.DMA((2, groups)),
        ],
        compiler_params=params(),
        cost_estimate=pl.CostEstimate(
            flops=2 * sums.size, bytes_accessed=6 * sums.size, transcendentals=0
        ),
        name="close",
    )(labels, got, sums)
    return centroids, similarity.reshape(-1)


def exchange(x):
    return lax.all_to_all(x, "dp", split_axis=0, concat_axis=0, tiled=True)


def after(value, *others):
    return lax.optimization_barrier((value, *others))[0]


def sorted_slots(key, top, entries):
    slots = jnp.arange(key.shape[0], dtype=jnp.int32)
    ahead = (key[None, :] < key[:, None]) | (
        (key[None, :] == key[:, None]) & (slots[None, :] < slots[:, None])
    )
    position = jnp.sum(ahead.astype(jnp.int32), axis=1)
    here = position[None, :] == slots[:, None]
    listed = jnp.sum(jnp.where(here, entries[None, :], 0), axis=1)
    levels = jnp.arange(top + 1, dtype=jnp.int32)
    bounds = jnp.sum((key[None, :] < levels[:, None]).astype(jnp.int32), axis=1)
    return listed, bounds, position


def ranks(group, sub):
    index = jnp.arange(sub.shape[-1], dtype=jnp.int32)
    before = (sub[..., None, :] < sub[..., :, None]) | (
        (sub[..., None, :] == sub[..., :, None]) & (index[None, :] < index[:, None])
    )
    same = group[..., None, :] == group[..., :, None]
    return jnp.sum((before & same).astype(jnp.int32), axis=-1)


def shards(tile_values, tile_row, tile_owner, tile_sub, labels):
    devices = lax.axis_size("dp")
    tiles = tile_values.shape[0]
    home = labels.shape[0]
    blocks = home // LANES * devices
    cap = max(2, 2 * tiles // devices)
    cuts = tuple(sorted({int(cap * share) for share in PARTS})) if cap >= 8 else (0, cap)
    parts = len(cuts) - 1
    here = lax.axis_index("dp").astype(jnp.int32)
    owner = tile_owner[:, 0]

    told = (labels, owner, tile_row, tile_sub)
    outgoing = pack(tile_values, owner, tile_row, told, devices, blocks, cuts)
    incoming = [exchange(outgoing[0])]
    heard = incoming[0][:, (cuts[1] - cuts[0]) * LANES :].astype(jnp.int32)
    level = heard[:, :blocks]
    partial_sq = jnp.exp2(level.astype(jnp.float32) * (1.0 / LOG_STEPS) + LOG_MIDDLE)
    row_sq = jnp.sum(jnp.where(level > -32768, partial_sq, 0.0), axis=0)
    all_described = heard[:, blocks:].reshape(devices, -1)
    all_labels = all_described[:, :home].reshape(blocks, LANES)
    mine = all_described[:, home : home + tiles] == here
    code = all_described[:, home + tiles : home + 2 * tiles]
    rank = ranks(mine.astype(jnp.int32), code % TB_OWN)
    chosen = mine[:, None, :] & (rank[:, None, :] == jnp.arange(cap)[None, :, None])
    meta = jnp.sum(jnp.where(chosen, code[:, None, :] + 1, 0), axis=2).reshape(-1) - 1
    sub = jnp.where(meta < 0, TB_OWN, meta % TB_OWN)
    slot_rank = np.arange(devices * cap) % cap
    slot_part = np.searchsorted(np.array(cuts), slot_rank, side="right") - 1
    low = np.array(cuts)[slot_part]
    fold_key = jnp.asarray(slot_part * (TB_OWN + 1), jnp.int32) + sub
    row = (meta // TB_OWN) << ROW_SHIFT
    from_slot = (np.arange(devices * cap) // cap << SOURCE_SHIFT) + slot_rank - low
    fold_list, fold_bounds, position = sorted_slots(
        fold_key, parts * (TB_OWN + 1), row + jnp.asarray(from_slot, jnp.int32)
    )
    score_list, *_ = sorted_slots(sub, TB_OWN, row + position)
    scalars = [fold_list, fold_bounds, score_list]

    scale = lax.rsqrt(row_sq + EPSILON) * (1.0 / CODE_TOP**2)
    signed = jnp.where(all_labels < HALF, scale, -scale)
    mods = (all_labels % HALF).astype(jnp.float32)
    totals, normed = (), []
    beside = (*scalars, mods, signed)
    for q in range(parts):
        if q + 1 < parts:
            ahead = (incoming[q], *beside) if q else (incoming[q],)
            incoming.append(exchange(after(outgoing[q + 1], *ahead)))
        partial, sums, *more = stage(
            q, cuts, scalars, mods, signed, incoming[q], normed, totals
        )
        beside = (partial, sums)
        totals, normed = (partial, sums, *more[:3]), normed + more[3:]
    return close(labels, exchange(partial), sums, TB_OWN * LANES * devices)


def solution(mesh):
    return jax.shard_map(
        shards,
        mesh=mesh,
        in_specs=(
            P(("groups", "dp"), None, None),
            P(("groups", "dp")),
            P(("groups", "dp"), None),
            P(("groups", "dp")),
            P(("groups", "dp")),
        ),
        out_specs=(P("groups", "dp"), P(("groups", "dp"))),
        check_vma=False,
    )
```

```python
import functools
import math

import jax
import jax.numpy as jnp
import numpy as np
from jax import lax
from jax.experimental import pallas as pl
from jax.experimental.pallas import tpu as pltpu
from jax.sharding import PartitionSpec as P

K = 512
HALF = K // 2
TB_OWN = 16
LANES = 128
EPSILON = 1e-06
CODE_TOP = 65535.0
CODE_SHIFT = 32768
VMEM_BYTES = 60 * 1024 * 1024
STEP_TILES = 16
PARTS = (0.0, 13 / 16, 1.0)
LOG_STEPS = 1800.0
LOG_MIDDLE = -3.0
CACHED_BLOCKS = 64
QUAD = 4
EIGHT = 8
WIDE_SHIFT = 4
CHUNK = 16
BLOCKS = 4
ROW_SHIFT, SOURCE_SHIFT = 16, 8
PLACE_MASK, SOURCE_MASK, SLOT_MASK = 0xFFFF, 0xFF, 0xFF
BATCH = 8
NT = (((1,), (1,)), ((), ()))
SMEM = pl.BlockSpec(memory_space=pltpu.SMEM)
VMEM = pl.BlockSpec(memory_space=pltpu.VMEM)
ANY = pl.BlockSpec(memory_space=pl.ANY)


def lane_sums(values):
    ones = jnp.ones((8, 2 * LANES), jnp.bfloat16)
    high = values.astype(jnp.bfloat16)
    low = (values - high.astype(jnp.float32)).astype(jnp.bfloat16)
    both = jnp.concatenate([high, low], axis=1)
    return lax.dot_general(ones, both, NT, preferred_element_type=jnp.float32)


def block_sums(square, out_ref, count):
    batch = math.gcd(BATCH, count)

    def one_batch(c, carry):
        some = square[pl.ds(c * batch, batch)].reshape((batch * LANES, LANES))
        sums = lane_sums(some)
        for j in range(batch):
            out_ref[pl.ds(c * batch + j, 1), :] += sums[:1, j * LANES : (j + 1) * LANES]
        return carry

    lax.fori_loop(0, count // batch, one_batch, 0)


def params():
    return pltpu.CompilerParams(vmem_limit_bytes=VMEM_BYTES)


def pack_kernel(cuts, owner_hbm, row_hbm, *refs):
    parts = len(cuts) - 1
    (*told_hbms, x_hbm), refs = refs[:5], refs[5:]
    outs = refs[:parts]
    x, coded, square, sums, words, notes, rank_row, rank_ref, *refs = refs[parts:]
    owner_ref, row_ref, *told_refs, sems, x_sems, small_sems = refs
    tiles = x.shape[0]
    devices = coded.shape[0]
    blocks = square.shape[0]
    step = math.gcd(STEP_TILES, tiles)

    def read(c):
        some = pl.ds(c * step, step)
        return pltpu.make_async_copy(x_hbm.at[some], x.at[some], x_sems.at[c])

    for c in range(tiles // step):
        read(c).start()
    pairs = zip((owner_hbm, row_hbm, *told_hbms), (owner_ref, row_ref, *told_refs))
    small = [pltpu.make_async_copy(*pair, small_sems.at[i]) for i, pair in enumerate(pairs)]
    for copy in small:
        copy.start()
    for copy in small:
        copy.wait()
    labels, owner, row, sub = [ref[...] for ref in told_refs]
    own, sub_own = [jnp.broadcast_to(v.astype(jnp.float32), (tiles, tiles)) for v in (owner, sub)]
    other, sub_other = jnp.transpose(own), jnp.transpose(sub_own)
    index = [lax.broadcasted_iota(jnp.int32, (tiles, tiles), d) for d in (0, 1)]
    ahead = (sub_other < sub_own) | ((sub_other == sub_own) & (index[0] < index[1]))
    ahead = jnp.where(ahead & (other == own), 1.0, 0.0)
    rank_row[...] = jnp.sum(ahead, axis=0, keepdims=True).astype(jnp.int32)
    pltpu.sync_copy(rank_row, rank_ref)
    square[...] = jnp.zeros_like(square)

    def some_tiles(i, carry):
        pl.when(i % (step // QUAD) == 0)(lambda: read(i // (step // QUAD)).wait())
        for j in range(QUAD):
            t = i * QUAD + j
            some = x[t]
            root = some * lax.rsqrt(some)
            code = (root * CODE_TOP + 0.5).astype(jnp.int32) - CODE_SHIFT
            owner, rank = owner_ref[t], rank_ref[0, t]
            at = pl.ds(pl.multiple_of(rank * LANES, LANES), LANES)
            coded[owner, at, :] = code.astype(jnp.int16)
            square[row_ref[t]] += some * some
        return carry

    lax.fori_loop(0, tiles // QUAD, some_tiles, 0)

    copies = []
    for q in range(parts):
        rows, count = (cuts[q + 1] - cuts[q]) * LANES, devices // (1 if q else math.gcd(4, devices))
        for d in range(0, devices, count):
            from_ref = coded.at[pl.ds(d, count), pl.ds(cuts[q] * LANES, rows)]
            into = outs[q].at[pl.ds(d, count), pl.ds(0, rows)]
            copies.append(pltpu.make_async_copy(from_ref, into, sems.at[len(copies)]))
    for copy in copies:
        copy.start()
    sums[...] = jnp.zeros_like(sums)
    block_sums(square, sums, blocks)
    total = sums[...]
    level = (jnp.log2(jnp.maximum(total, 1e-30)) - LOG_MIDDLE) * LOG_STEPS
    level = jnp.where(total > 0.0, jnp.clip(level, -32700.0, 32700.0), -32768.0)
    level = (level + 32768.5).astype(jnp.int32) - 32768
    words[...] = jnp.zeros_like(words)
    words[:blocks, :] = level
    at = blocks
    for told in (labels, owner, row * TB_OWN + sub):
        words[at : at + told.shape[0], :] = told
        at += told.shape[0]
    notes[...] = jnp.broadcast_to(words[...].astype(jnp.int16)[None], notes.shape)
    into = outs[0].at[:, pl.ds((cuts[1] - cuts[0]) * LANES, notes.shape[1])]
    copies.append(pltpu.make_async_copy(notes, into, sems.at[len(copies)]))
    copies[-1].start()
    for copy in copies:
        copy.wait()


def pack(tile_values, owner, tile_row, told, devices, blocks, cuts):
    tiles = tile_values.shape[0]
    told = [x.reshape(-1, LANES) for x in told]
    noted = -(-(blocks + sum(x.shape[0] for x in told[:3])) // 16) * 16
    rows = [(high - low) * LANES for low, high in zip(cuts, cuts[1:])]
    rows[0] += noted
    return pl.pallas_call(
        functools.partial(pack_kernel, cuts),
        in_specs=[ANY] * 7,
        out_specs=[ANY] * len(rows),
        out_shape=[jax.ShapeDtypeStruct((devices, some, LANES), jnp.int16) for some in rows],
        scratch_shapes=[
            pltpu.VMEM(tile_values.shape, jnp.float32),
            pltpu.VMEM((devices, cuts[-1] * LANES, LANES), jnp.int16),
            pltpu.VMEM((blocks, LANES, LANES), jnp.float32),
            pltpu.VMEM((blocks, LANES), jnp.float32),
            pltpu.VMEM((noted, LANES), jnp.int32),
            pltpu.VMEM((devices, noted, LANES), jnp.int16),
            pltpu.VMEM((1, tiles), jnp.int32),
            pltpu.SMEM((1, tiles), jnp.int32),
            pltpu.SMEM((tiles,), jnp.int32),
            pltpu.SMEM((tiles,), jnp.int32),
            *[pltpu.VMEM(some.shape, jnp.int32) for some in told],
            pltpu.SemaphoreType.DMA((len(rows) + 4,)),
            pltpu.SemaphoreType.DMA((tiles // math.gcd(STEP_TILES, tiles),)),
            pltpu.SemaphoreType.DMA((6,)),
        ],
        compiler_params=params(),
        cost_estimate=pl.CostEstimate(
            flops=8 * tile_values.size,
            bytes_accessed=6 * tile_values.size,
            transcendentals=tile_values.size,
        ),
        name="pack",
    )(owner, tile_row, *told, tile_values)


def stage_kernel(q, bases, last, cached, fold_list_in, fold_bound_in, score_list_in,
                 mods_in, signed_in, x_hbm, *refs):
    base = bases[q]
    earlier, refs = refs[:q], refs[q:]
    before, sums_in, squares_in, *made_in = refs[:5] if q else (None,) * 5
    refs = refs[5:] if q else refs
    part, sums_out, refs = refs[0], refs[1], refs[2:]
    (squares_out, *made_out, fresh_out), refs = ((None,) * 4, refs) if last else (refs[:4], refs[4:])
    spread, x, hot, sums, narrow, tiles, products, scores, squares, mods, signed, *refs = refs
    fold_list, fold_bound, score_list, sems, sub_sems, tile_sems, small_sems = refs
    devices, width = x.shape[0], x.shape[1] // LANES
    none = products.shape[0] - 1
    needed = [pltpu.make_async_copy(x_hbm.at[:, pl.ds(0, width * LANES)], x, sems.at[0])]
    if q:
        needed.append(pltpu.make_async_copy(made_in[0], spread, sems.at[1]))
    for copy in needed:
        copy.start()
    for held, empty in ((mods, -1.0), (signed, 0.0)):
        held[none : none + 1, :] = jnp.full((1, LANES), empty, jnp.float32)
    pairs = [(fold_list_in, fold_list), (fold_bound_in, fold_bound), (score_list_in, score_list)]
    pairs += [(mods_in, mods.at[pl.ds(0, none)]), (signed_in, signed.at[pl.ds(0, none)])]
    pairs += [(before, scores), (squares_in, squares)] if q else []
    small = [pltpu.make_async_copy(*pair, small_sems.at[i]) for i, pair in enumerate(pairs)]
    for copy in small:
        copy.start()
    for copy in small:
        copy.wait()
    parts = len(bases) - 1

    def bound(p, sub):
        return fold_bound[p * (TB_OWN + 1) + sub]

    def score_bound(sub):
        return sum(bound(p, sub) - bound(p, 0) for p in range(parts))

    def complete(arrived):
        def one(i, least):
            sub = TB_OWN - 1 - i
            waits = [bound(p, sub + 1) > bound(p, sub) for p in range(arrived, parts)]
            return jnp.where(functools.reduce(jnp.logical_or, waits), sub, least)

        return lax.fori_loop(0, TB_OWN, one, TB_OWN) if arrived < parts else TB_OWN

    begin, end = complete(q) if q else 0, complete(q + 1)

    def columns(sub):
        return (slice(None), pl.ds(pl.multiple_of(sub * 2 * LANES, 2 * LANES), 2 * LANES))

    def group(g):
        size = BLOCKS * 2 * LANES
        return (slice(None), pl.ds(pl.multiple_of(g * size, size), size))

    def sums_read(g):
        return pltpu.make_async_copy(sums_in.at[group(g)], sums.at[group(g)], sub_sems.at[0, g])

    def sums_write(g):
        return pltpu.make_async_copy(sums.at[group(g)], sums_out.at[group(g)], sub_sems.at[1, g])

    def each_sub(low, high, what):
        def one(sub, carry):
            what(sub)
            return carry

        lax.fori_loop(low, high, one, 0)

    if q:
        each_sub(begin // BLOCKS, TB_OWN // BLOCKS, lambda g: sums_read(g).start())
    else:
        scores[...] = jnp.zeros_like(scores)
        sums[...] = jnp.zeros_like(sums)
        squares[...] = jnp.zeros_like(squares)
    later = [pltpu.make_async_copy(made_in[1], hot, sems.at[3])] if q and cached else []

    def each_chunk(p, outside, write, sub, what):
        count = math.gcd(CHUNK, bases[p + 1] - bases[p])

        def one(c, carry):
            away, own = outside.at[pl.ds(c * count, count)], tiles.at[pl.ds(bases[p] + c * count, count)]
            some = (own, away) if write else (away, own)
            what(pltpu.make_async_copy(*some, tile_sems.at[0 if write else p, c]))
            return carry

        first, stop = bound(p, sub) - bases[p], bound(p, TB_OWN) - bases[p]
        lax.fori_loop(first // count, (stop + count - 1) // count, one, 0)

    def each_earlier(what):
        for copy in later:
            what(copy)
        for e, e_hbm in enumerate(earlier):
            each_chunk(e, e_hbm, False, begin, what)

    each_earlier(lambda copy: copy.start())
    products[...] = jnp.zeros_like(products)
    cluster = lax.broadcasted_iota(jnp.int32, (HALF, LANES), 0).astype(jnp.float32)
    cluster = cluster.astype(jnp.bfloat16).reshape(HALF // 16, 16, LANES)
    one, zero = jnp.ones((), jnp.bfloat16), jnp.zeros((), jnp.bfloat16)
    lane = lax.broadcasted_iota(jnp.int32, (LANES, LANES), 1)

    def column(ref, row):
        return jnp.transpose(jnp.broadcast_to(ref[pl.ds(row, 1), :], (LANES, LANES)))

    def one_hot(row):
        own = column(mods, row).astype(jnp.int32)
        some = [jnp.where(own == lane + g, 1.0, 0.0) for g in range(0, HALF, LANES)]
        return jnp.concatenate(some, axis=1).astype(jnp.bfloat16)

    batch = math.gcd(none + 1, 3)

    def build(c, carry):
        for j in range(batch):
            spread[c * batch + j] = column(signed, c * batch + j)
            if cached:
                hot[c * batch + j] = one_hot(c * batch + j)
        return carry

    if not q:
        lax.fori_loop(0, (none + 1) // batch, build, 0)
    for copy in needed:
        copy.wait()
    if q:
        each_sub(begin // BLOCKS, TB_OWN // BLOCKS, lambda g: sums_read(g).wait())

    def steps(start, end, work):
        wide = 2 * EIGHT
        count = (end - start + EIGHT - 1) >> WIDE_SHIFT

        def one(p, carry):
            work(start + wide * p, wide)
            return carry

        lax.fori_loop(0, count, one, 0)
        pl.when(start + wide * count < end)(lambda: work(start + wide * count, EIGHT))

    def some(entries, start, end, count):
        at = [start + j for j in range(count)]
        at = [(jnp.where(spot < end, spot, start), spot < end) for spot in at]
        return [(entries[spot], spot, held) for spot, held in at]

    def fold_sub(sub):
        start, end = bound(q, sub), bound(q, sub + 1)
        def fold_some(first, count):
            folded, picks = [], []
            for entry, spot, held in some(fold_list, first, end, count):
                row = entry >> ROW_SHIFT
                source, slot = (entry >> SOURCE_SHIFT) & SOURCE_MASK, entry & SLOT_MASK
                raw = x[source, pl.ds(pl.multiple_of(slot * LANES, LANES), LANES), :]
                root = raw.astype(jnp.int32).astype(jnp.float32) + float(CODE_SHIFT)
                scale = spread[row]
                square = root * root
                tile = square * jnp.abs(scale)
                lower = square * jnp.maximum(scale, 0.0)
                tiles[spot] = tile.astype(jnp.bfloat16)
                halves = [lower.astype(jnp.bfloat16), (tile - lower).astype(jnp.bfloat16)]
                folded.append(jnp.concatenate(halves, axis=1))
                own = jnp.broadcast_to(mods[pl.ds(jnp.where(held, row, none), 1), :], (16, LANES))
                own = jnp.where(cluster == own.astype(jnp.bfloat16)[None], one, zero)
                picks.append(own.reshape(HALF, LANES))
            pick = jnp.concatenate(picks, axis=1)
            sums[columns(sub)] += jnp.dot(
                pick, jnp.concatenate(folded, axis=0), preferred_element_type=jnp.float32
            )

        steps(start, end, fold_some)

    def fold_group(g):
        each_sub(jnp.maximum(begin, g * BLOCKS), (g + 1) * BLOCKS, fold_sub)
        sums_write(g).start()

    each_sub(begin // BLOCKS, TB_OWN // BLOCKS, fold_group)
    kept = []
    if not last:
        each_chunk(q, fresh_out, True, end, lambda copy: copy.start())
        kept.append(pltpu.make_async_copy(spread, made_out[0], sems.at[4]))
        kept.append(pltpu.make_async_copy(hot, made_out[1], sems.at[5]))
    for copy in kept:
        copy.start()
    each_earlier(lambda copy: copy.wait())

    def score_sub(sub):
        start, end = score_bound(sub), score_bound(sub + 1)
        own_sums = sums[columns(sub)]
        narrow[...] = own_sums.astype(jnp.bfloat16)
        squares[...] += own_sums * own_sums

        def score_some(first, count):
            listed = some(score_list, first, end, count)
            rows = [jnp.where(held, entry >> ROW_SHIFT, none) for entry, spot, held in listed]
            spots = [entry & PLACE_MASK for entry, spot, held in listed]
            hots = [hot[row] if cached else one_hot(row) for row in rows]
            chosen = jnp.dot(
                jnp.concatenate(hots, axis=0), narrow[...], preferred_element_type=jnp.float32
            )
            for j in range(count):
                both = chosen[j * LANES : (j + 1) * LANES]
                own = jnp.where(spread[rows[j]] < 0.0, both[:, LANES:], both[:, :LANES])
                products[rows[j]] += own * tiles[spots[j]].astype(jnp.float32)

        steps(start, end, score_some)

    each_sub(begin, end, score_sub)
    block_sums(products, scores, none)
    if last:
        own = none // devices
        square = [lane_sums(squares[:, h : h + LANES])[:1] for h in (0, LANES)]
        square = jnp.concatenate(square, axis=1)
        for d in range(devices):
            part[d, :, part.shape[2] - K :] = square
            for b in range(own):
                at = d * own + b
                part[d, :, b * LANES : (b + 1) * LANES] = scores[at : at + 1, :]
    else:
        part[...] = scores[...]
        squares_out[...] = squares[...]
    for copy in kept:
        copy.wait()
    if not last:
        each_chunk(q, fresh_out, True, end, lambda copy: copy.wait())
    each_sub(begin // BLOCKS, TB_OWN // BLOCKS, lambda g: sums_write(g).wait())


def stage(q, cuts, scalars, mods, signed, x, normed, totals):
    devices = x.shape[0]
    last = q == len(cuts) - 2
    blocks = mods.shape[0]
    cached = blocks <= CACHED_BLOCKS
    width = cuts[q + 1] - cuts[q]
    home = blocks // devices * LANES
    wide = jax.ShapeDtypeStruct((HALF, TB_OWN * 2 * LANES), jnp.float32)
    square = jax.ShapeDtypeStruct((HALF, 2 * LANES), jnp.float32)
    if last:
        out_shape = [jax.ShapeDtypeStruct((devices, 1, home + K), jnp.float32), wide]
    else:
        out_shape = [
            jax.ShapeDtypeStruct((blocks, LANES), jnp.float32),
            wide,
            square,
            jax.ShapeDtypeStruct((blocks + 1, LANES, LANES), jnp.float32),
            jax.ShapeDtypeStruct((blocks + 1 if cached else 1, LANES, HALF), jnp.bfloat16),
            jax.ShapeDtypeStruct((devices * width, LANES, LANES), jnp.bfloat16),
        ]
    slots = devices * cuts[-1]
    sizes = [devices * (high - low) for low, high in zip(cuts, cuts[1:])]
    chunks = max(size // math.gcd(CHUNK, size) for size in sizes)
    operands = [*scalars, mods, signed, x, *normed, *totals]
    return pl.pallas_call(
        functools.partial(stage_kernel, q, [devices * cut for cut in cuts], last, cached),
        in_specs=[ANY] * len(operands),
        out_specs=[VMEM, ANY, VMEM, ANY, ANY, ANY][: len(out_shape)],
        out_shape=out_shape,
        input_output_aliases={len(operands) - len(totals) + 1: 1} if q else {},
        scratch_shapes=[
            pltpu.VMEM((blocks + 1, LANES, LANES), jnp.float32),
            pltpu.VMEM((devices, width * LANES, LANES), jnp.int16),
            pltpu.VMEM((blocks + 1 if cached else 1, LANES, HALF), jnp.bfloat16),
            pltpu.VMEM(wide.shape, jnp.float32),
            pltpu.VMEM(square.shape, jnp.bfloat16),
            pltpu.VMEM((slots, LANES, LANES), jnp.bfloat16),
            pltpu.VMEM((blocks + 1, LANES, LANES), jnp.float32),
            pltpu.VMEM((blocks, LANES), jnp.float32),
            pltpu.VMEM(square.shape, jnp.float32),
            pltpu.VMEM((blocks + 1, LANES), jnp.float32),
            pltpu.VMEM((blocks + 1, LANES), jnp.float32),
            *[pltpu.SMEM(some.shape, jnp.int32) for some in scalars],
            pltpu.SemaphoreType.DMA((6,)),
            pltpu.SemaphoreType.DMA((2, TB_OWN // BLOCKS)),
            pltpu.SemaphoreType.DMA((max(q, 1), chunks)),
            pltpu.SemaphoreType.DMA((7,)),
        ],
        compiler_params=params(),
        cost_estimate=pl.CostEstimate(
            flops=devices * width * LANES * LANES * K, bytes_accessed=wide.size, transcendentals=0
        ),
        name="stage",
    )(*operands)


def close_kernel(root, groups, labels_hbm, got_hbm, sums_hbm, out_hbm, similarity_hbm, labels_ref,
                 got_ref, similarity, sums, out, sems, small_sems):
    width = TB_OWN // groups
    reads, writes = [], []
    small = [
        pltpu.make_async_copy(got_hbm, got_ref, small_sems.at[0]),
        pltpu.make_async_copy(labels_hbm, labels_ref, small_sems.at[1]),
    ]
    for copy in small:
        copy.start()
    for g in range(groups):
        some = (slice(None), pl.ds(g * width * 2 * LANES, width * 2 * LANES))
        reads.append(pltpu.make_async_copy(sums_hbm.at[some], sums.at[some], sems.at[0, g]))
        some = (slice(None), pl.ds(g * width * LANES, width * LANES))
        writes.append(pltpu.make_async_copy(out.at[some], out_hbm.at[some], sems.at[1, g]))
        reads[g].start()
    for copy in small:
        copy.wait()
    total = jnp.sum(got_ref[...], axis=0)
    home = total.shape[1] - K
    own = lax.rsqrt(total[:, home:] + EPSILON)
    columns = [
        jnp.transpose(jnp.broadcast_to(own[:, k : k + LANES], (LANES, LANES)))
        for k in range(0, K, LANES)
    ]
    cluster = lax.broadcasted_iota(jnp.int32, (LANES, LANES), 0)
    for b in range(home // LANES):
        found = jnp.zeros((LANES, LANES), jnp.float32)
        for i, column in enumerate(columns):
            found += jnp.where(cluster + i * LANES == labels_ref[b : b + 1, :], column, 0.0)
        found = jnp.sum(found, axis=0, keepdims=True)
        similarity[b : b + 1, :] = total[:, b * LANES : (b + 1) * LANES] * found
    writes.append(pltpu.make_async_copy(similarity, similarity_hbm, small_sems.at[2]))
    writes[-1].start()
    for g in range(groups):
        reads[g].wait()

        def one_sub(sub, carry):
            to = pl.ds(pl.multiple_of(sub * LANES, LANES), LANES)
            for i, column in enumerate(columns):
                half, row = divmod(i * LANES, HALF)
                at = pl.ds(pl.multiple_of((2 * sub + half) * LANES, LANES), LANES)
                done = sums[row : row + LANES, at] * column * root
                out[i * LANES : (i + 1) * LANES, to] = done.astype(jnp.bfloat16)
            return carry

        lax.fori_loop(g * width, (g + 1) * width, one_sub, 0)
        writes[g].start()
    for write in writes:
        write.wait()


def close(labels, got, sums, vocab_size):
    groups = 4
    labels = labels.reshape(-1, LANES)
    wide = jax.ShapeDtypeStruct((K, TB_OWN * LANES), jnp.bfloat16)
    centroids, similarity = pl.pallas_call(
        functools.partial(close_kernel, math.sqrt(vocab_size), groups),
        in_specs=[ANY] * 3,
        out_specs=[ANY] * 2,
        out_shape=[wide, jax.ShapeDtypeStruct(labels.shape, jnp.float32)],
        scratch_shapes=[
            pltpu.VMEM(labels.shape, jnp.int32),
            pltpu.VMEM(got.shape, jnp.float32),
            pltpu.VMEM(labels.shape, jnp.float32),
            pltpu.VMEM(sums.shape, jnp.float32),
            pltpu.VMEM(wide.shape, jnp.bfloat16),
            pltpu.SemaphoreType.DMA((2, groups)),
            pltpu.SemaphoreType.DMA((3,)),
        ],
        compiler_params=params(),
        cost_estimate=pl.CostEstimate(
            flops=2 * sums.size, bytes_accessed=6 * sums.size, transcendentals=0
        ),
        name="close",
    )(labels, got, sums)
    return centroids, similarity.reshape(-1)


def exchange(x):
    return lax.all_to_all(x, "dp", split_axis=0, concat_axis=0, tiled=True)


def after(value, *others):
    return lax.optimization_barrier((value, *others))[0]


def sorted_slots(key, top, entries):
    slots = jnp.arange(key.shape[0], dtype=jnp.int32)
    ahead = (key[None, :] < key[:, None]) | (
        (key[None, :] == key[:, None]) & (slots[None, :] < slots[:, None])
    )
    position = jnp.sum(ahead.astype(jnp.int32), axis=1)
    here = position[None, :] == slots[:, None]
    listed = jnp.sum(jnp.where(here, entries[None, :], 0), axis=1)
    levels = jnp.arange(-(-(top + 1) // LANES) * LANES, dtype=jnp.int32)
    bounds = jnp.sum((key[None, :] < levels[:, None]).astype(jnp.int32), axis=1)
    return listed, bounds, position


def ranks(group, sub):
    index = jnp.arange(sub.shape[-1], dtype=jnp.int32)
    before = (sub[..., None, :] < sub[..., :, None]) | (
        (sub[..., None, :] == sub[..., :, None]) & (index[None, :] < index[:, None])
    )
    same = group[..., None, :] == group[..., :, None]
    return jnp.sum((before & same).astype(jnp.int32), axis=-1)


def shards(tile_values, tile_row, tile_owner, tile_sub, labels):
    devices = lax.axis_size("dp")
    tiles = tile_values.shape[0]
    home = labels.shape[0]
    blocks = home // LANES * devices
    cap = max(2, 2 * tiles // devices)
    cuts = tuple(sorted({int(cap * share) for share in PARTS})) if cap >= 8 else (0, cap)
    parts = len(cuts) - 1
    here = lax.axis_index("dp").astype(jnp.int32)
    owner = tile_owner[:, 0]

    told = (labels, owner, tile_row, tile_sub)
    outgoing = pack(tile_values, owner, tile_row, told, devices, blocks, cuts)
    incoming = [exchange(outgoing[0])]
    heard = incoming[0][:, (cuts[1] - cuts[0]) * LANES :].astype(jnp.int32)
    level = heard[:, :blocks]
    partial_sq = jnp.exp2(level.astype(jnp.float32) * (1.0 / LOG_STEPS) + LOG_MIDDLE)
    row_sq = jnp.sum(jnp.where(level > -32768, partial_sq, 0.0), axis=0)
    all_described = heard[:, blocks:].reshape(devices, -1)
    all_labels = all_described[:, :home].reshape(blocks, LANES)
    mine = all_described[:, home : home + tiles] == here
    code = all_described[:, home + tiles : home + 2 * tiles]
    rank = ranks(mine.astype(jnp.int32), code % TB_OWN)
    chosen = mine[:, None, :] & (rank[:, None, :] == jnp.arange(cap)[None, :, None])
    meta = jnp.sum(jnp.where(chosen, code[:, None, :] + 1, 0), axis=2).reshape(-1) - 1
    sub = jnp.where(meta < 0, TB_OWN, meta % TB_OWN)
    slot_rank = np.arange(devices * cap) % cap
    slot_part = np.searchsorted(np.array(cuts), slot_rank, side="right") - 1
    low = np.array(cuts)[slot_part]
    fold_key = jnp.asarray(slot_part * (TB_OWN + 1), jnp.int32) + sub
    row = (meta // TB_OWN) << ROW_SHIFT
    from_slot = (np.arange(devices * cap) // cap << SOURCE_SHIFT) + slot_rank - low
    fold_list, fold_bounds, position = sorted_slots(
        fold_key, parts * (TB_OWN + 1), row + jnp.asarray(from_slot, jnp.int32)
    )
    score_list, *_ = sorted_slots(sub, TB_OWN, row + position)
    scalars = [fold_list, fold_bounds, score_list]

    scale = lax.rsqrt(row_sq + EPSILON) * (1.0 / CODE_TOP**2)
    signed = jnp.where(all_labels < HALF, scale, -scale)
    mods = (all_labels % HALF).astype(jnp.float32)
    totals, normed = (), []
    beside = (*scalars, mods, signed)
    for q in range(parts):
        if q + 1 < parts:
            ahead = (incoming[q], *beside) if q else (incoming[q],)
            incoming.append(exchange(after(outgoing[q + 1], *ahead)))
        partial, sums, *more = stage(
            q, cuts, scalars, mods, signed, incoming[q], normed, totals
        )
        beside = (partial, sums)
        totals, normed = (partial, sums, *more[:3]), normed + more[3:]
    return close(labels, exchange(partial), sums, TB_OWN * LANES * devices)


def solution(mesh):
    return jax.shard_map(
        shards,
        mesh=mesh,
        in_specs=(
            P(("groups", "dp"), None, None),
            P(("groups", "dp")),
            P(("groups", "dp"), None),
            P(("groups", "dp")),
            P(("groups", "dp")),
        ),
        out_specs=(P("groups", "dp"), P(("groups", "dp"))),
        check_vma=False,
    )
```

```python
import functools
import math

import jax
import jax.numpy as jnp
import numpy as np
from jax import lax
from jax.experimental import pallas as pl
from jax.experimental.pallas import tpu as pltpu
from jax.sharding import PartitionSpec as P

K = 512
HALF = K // 2
TB_OWN = 16
LANES = 128
EPSILON = 1e-06
CODE_TOP = 65535.0
CODE_SHIFT = 32768
VMEM_BYTES = 60 * 1024 * 1024
STEP_TILES = 16
PARTS = (0.0, 13 / 16, 1.0)
LOG_STEPS = 1800.0
LOG_MIDDLE = -3.0
CACHED_BLOCKS = 64
QUAD = 4
EIGHT = 8
WIDE_SHIFT = 4
CHUNK = 16
BLOCKS = 4
ROW_SHIFT, SOURCE_SHIFT = 16, 8
PLACE_MASK, SOURCE_MASK, SLOT_MASK = 0xFFFF, 0xFF, 0xFF
BATCH = 8
NT = (((1,), (1,)), ((), ()))
SMEM = pl.BlockSpec(memory_space=pltpu.SMEM)
VMEM = pl.BlockSpec(memory_space=pltpu.VMEM)
ANY = pl.BlockSpec(memory_space=pl.ANY)


def lane_sums(values):
    ones = jnp.ones((8, 2 * LANES), jnp.bfloat16)
    high = values.astype(jnp.bfloat16)
    low = (values - high.astype(jnp.float32)).astype(jnp.bfloat16)
    both = jnp.concatenate([high, low], axis=1)
    return lax.dot_general(ones, both, NT, preferred_element_type=jnp.float32)


def block_sums(square, out_ref, count):
    batch = math.gcd(BATCH, count)

    def one_batch(c, carry):
        some = square[pl.ds(c * batch, batch)].reshape((batch * LANES, LANES))
        sums = lane_sums(some)
        for j in range(batch):
            out_ref[pl.ds(c * batch + j, 1), :] += sums[:1, j * LANES : (j + 1) * LANES]
        return carry

    lax.fori_loop(0, count // batch, one_batch, 0)


def params():
    return pltpu.CompilerParams(vmem_limit_bytes=VMEM_BYTES)


def pack_kernel(cuts, owner_ref, row_ref, *refs):
    parts = len(cuts) - 1
    (*told_refs, x_hbm), refs = refs[:5], refs[5:]
    outs = refs[:parts]
    x, coded, square, sums, words, notes, rank_row, rank_ref, sems, x_sems = refs[parts:]
    tiles = x.shape[0]
    devices = coded.shape[0]
    blocks = square.shape[0]
    step = math.gcd(STEP_TILES, tiles)

    def read(c):
        some = pl.ds(c * step, step)
        return pltpu.make_async_copy(x_hbm.at[some], x.at[some], x_sems.at[c])

    for c in range(tiles // step):
        read(c).start()
    labels, owner, row, sub = [ref[...] for ref in told_refs]
    own, sub_own = [jnp.broadcast_to(v.astype(jnp.float32), (tiles, tiles)) for v in (owner, sub)]
    other, sub_other = jnp.transpose(own), jnp.transpose(sub_own)
    index = [lax.broadcasted_iota(jnp.int32, (tiles, tiles), d) for d in (0, 1)]
    ahead = (sub_other < sub_own) | ((sub_other == sub_own) & (index[0] < index[1]))
    ahead = jnp.where(ahead & (other == own), 1.0, 0.0)
    rank_row[...] = jnp.sum(ahead, axis=0, keepdims=True).astype(jnp.int32)
    pltpu.sync_copy(rank_row, rank_ref)
    square[...] = jnp.zeros_like(square)

    def some_tiles(i, carry):
        pl.when(i % (step // QUAD) == 0)(lambda: read(i // (step // QUAD)).wait())
        for j in range(QUAD):
            t = i * QUAD + j
            some = x[t]
            root = some * lax.rsqrt(some)
            code = (root * CODE_TOP + 0.5).astype(jnp.int32) - CODE_SHIFT
            owner, rank = owner_ref[t], rank_ref[0, t]
            at = pl.ds(pl.multiple_of(rank * LANES, LANES), LANES)
            coded[owner, at, :] = code.astype(jnp.int16)
            square[row_ref[t]] += some * some
        return carry

    lax.fori_loop(0, tiles // QUAD, some_tiles, 0)

    copies = []
    for q in range(parts):
        rows, count = (cuts[q + 1] - cuts[q]) * LANES, devices // (1 if q else math.gcd(4, devices))
        for d in range(0, devices, count):
            from_ref = coded.at[pl.ds(d, count), pl.ds(cuts[q] * LANES, rows)]
            into = outs[q].at[pl.ds(d, count), pl.ds(0, rows)]
            copies.append(pltpu.make_async_copy(from_ref, into, sems.at[len(copies)]))
    for copy in copies:
        copy.start()
    sums[...] = jnp.zeros_like(sums)
    block_sums(square, sums, blocks)
    total = sums[...]
    level = (jnp.log2(jnp.maximum(total, 1e-30)) - LOG_MIDDLE) * LOG_STEPS
    level = jnp.where(total > 0.0, jnp.clip(level, -32700.0, 32700.0), -32768.0)
    level = (level + 32768.5).astype(jnp.int32) - 32768
    words[...] = jnp.zeros_like(words)
    words[:blocks, :] = level
    at = blocks
    for told in (labels, owner, row * TB_OWN + sub):
        words[at : at + told.shape[0], :] = told
        at += told.shape[0]
    notes[...] = jnp.broadcast_to(words[...].astype(jnp.int16)[None], notes.shape)
    into = outs[0].at[:, pl.ds((cuts[1] - cuts[0]) * LANES, notes.shape[1])]
    copies.append(pltpu.make_async_copy(notes, into, sems.at[len(copies)]))
    copies[-1].start()
    for copy in copies:
        copy.wait()


def pack(tile_values, owner, tile_row, told, devices, blocks, cuts):
    tiles = tile_values.shape[0]
    told = [x.reshape(-1, LANES) for x in told]
    noted = -(-(blocks + sum(x.shape[0] for x in told[:3])) // 16) * 16
    rows = [(high - low) * LANES for low, high in zip(cuts, cuts[1:])]
    rows[0] += noted
    return pl.pallas_call(
        functools.partial(pack_kernel, cuts),
        in_specs=[SMEM] * 2 + [VMEM] * 4 + [ANY],
        out_specs=[ANY] * len(rows),
        out_shape=[jax.ShapeDtypeStruct((devices, some, LANES), jnp.int16) for some in rows],
        scratch_shapes=[
            pltpu.VMEM(tile_values.shape, jnp.float32),
            pltpu.VMEM((devices, cuts[-1] * LANES, LANES), jnp.int16),
            pltpu.VMEM((blocks, LANES, LANES), jnp.float32),
            pltpu.VMEM((blocks, LANES), jnp.float32),
            pltpu.VMEM((noted, LANES), jnp.int32),
            pltpu.VMEM((devices, noted, LANES), jnp.int16),
            pltpu.VMEM((1, tiles), jnp.int32),
            pltpu.SMEM((1, tiles), jnp.int32),
            pltpu.SemaphoreType.DMA((len(rows) + 4,)),
            pltpu.SemaphoreType.DMA((tiles // math.gcd(STEP_TILES, tiles),)),
        ],
        compiler_params=params(),
        cost_estimate=pl.CostEstimate(
            flops=8 * tile_values.size,
            bytes_accessed=6 * tile_values.size,
            transcendentals=tile_values.size,
        ),
        name="pack",
    )(owner, tile_row, *told, tile_values)


def stage_kernel(q, bases, last, cached, fold_list, fold_bound, score_list,
                 mods_in, signed_in, x_hbm, *refs):
    base = bases[q]
    earlier, refs = refs[:q], refs[q:]
    before, sums_in, squares_in, *made_in = refs[:5] if q else (None,) * 5
    refs = refs[5:] if q else refs
    part, sums_out, refs = refs[0], refs[1], refs[2:]
    (squares_out, *made_out, fresh_out), refs = ((None,) * 4, refs) if last else (refs[:4], refs[4:])
    spread, x, hot, sums, narrow, tiles, products, scores, squares, mods, signed, *refs = refs
    sems, sub_sems, tile_sems = refs
    devices, width = x.shape[0], x.shape[1] // LANES
    none = products.shape[0] - 1
    parts = len(bases) - 1

    def bound(p, sub):
        return fold_bound[p * (TB_OWN + 1) + sub]

    def score_bound(sub):
        return sum(bound(p, sub) - bound(p, 0) for p in range(parts))

    def complete(arrived):
        def one(i, least):
            sub = TB_OWN - 1 - i
            waits = [bound(p, sub + 1) > bound(p, sub) for p in range(arrived, parts)]
            return jnp.where(functools.reduce(jnp.logical_or, waits), sub, least)

        return lax.fori_loop(0, TB_OWN, one, TB_OWN) if arrived < parts else TB_OWN

    begin, end = complete(q) if q else 0, complete(q + 1)
    needed = [pltpu.make_async_copy(x_hbm.at[:, pl.ds(0, width * LANES)], x, sems.at[0])]
    if q:
        needed.append(pltpu.make_async_copy(made_in[0], spread, sems.at[1]))
    for copy in needed:
        copy.start()

    def columns(sub):
        return (slice(None), pl.ds(pl.multiple_of(sub * 2 * LANES, 2 * LANES), 2 * LANES))

    def group(g):
        size = BLOCKS * 2 * LANES
        return (slice(None), pl.ds(pl.multiple_of(g * size, size), size))

    def sums_read(g):
        return pltpu.make_async_copy(sums_in.at[group(g)], sums.at[group(g)], sub_sems.at[0, g])

    def sums_write(g):
        return pltpu.make_async_copy(sums.at[group(g)], sums_out.at[group(g)], sub_sems.at[1, g])

    def each_sub(low, high, what):
        def one(sub, carry):
            what(sub)
            return carry

        lax.fori_loop(low, high, one, 0)

    if q:
        each_sub(begin // BLOCKS, TB_OWN // BLOCKS, lambda g: sums_read(g).start())
        squares[...] = squares_in[...]
    else:
        sums[...] = jnp.zeros_like(sums)
        squares[...] = jnp.zeros_like(squares)
    later = [pltpu.make_async_copy(made_in[1], hot, sems.at[3])] if q and cached else []

    def each_chunk(p, outside, write, sub, what):
        count = math.gcd(CHUNK, bases[p + 1] - bases[p])

        def one(c, carry):
            away, own = outside.at[pl.ds(c * count, count)], tiles.at[pl.ds(bases[p] + c * count, count)]
            some = (own, away) if write else (away, own)
            what(pltpu.make_async_copy(*some, tile_sems.at[0 if write else p, c]))
            return carry

        first, stop = bound(p, sub) - bases[p], bound(p, TB_OWN) - bases[p]
        lax.fori_loop(first // count, (stop + count - 1) // count, one, 0)

    def each_earlier(what):
        for copy in later:
            what(copy)
        for e, e_hbm in enumerate(earlier):
            each_chunk(e, e_hbm, False, begin, what)

    each_earlier(lambda copy: copy.start())
    products[...] = jnp.zeros_like(products)
    scores[...] = before[...] if q else jnp.zeros_like(scores)
    for held, given, empty in ((mods, mods_in, -1.0), (signed, signed_in, 0.0)):
        held[:none, :] = given[...]
        held[none : none + 1, :] = jnp.full((1, LANES), empty, jnp.float32)
    cluster = lax.broadcasted_iota(jnp.int32, (HALF, LANES), 0).astype(jnp.float32)
    cluster = cluster.astype(jnp.bfloat16).reshape(HALF // 16, 16, LANES)
    one, zero = jnp.ones((), jnp.bfloat16), jnp.zeros((), jnp.bfloat16)
    lane = lax.broadcasted_iota(jnp.int32, (LANES, LANES), 1)

    def column(ref, row):
        return jnp.transpose(jnp.broadcast_to(ref[pl.ds(row, 1), :], (LANES, LANES)))

    def one_hot(row):
        own = column(mods, row).astype(jnp.int32)
        some = [jnp.where(own == lane + g, 1.0, 0.0) for g in range(0, HALF, LANES)]
        return jnp.concatenate(some, axis=1).astype(jnp.bfloat16)

    batch = math.gcd(none + 1, 3)

    def build(c, carry):
        for j in range(batch):
            spread[c * batch + j] = column(signed, c * batch + j)
            if cached:
                hot[c * batch + j] = one_hot(c * batch + j)
        return carry

    if not q:
        lax.fori_loop(0, (none + 1) // batch, build, 0)
    for copy in needed:
        copy.wait()
    if q:
        each_sub(begin // BLOCKS, TB_OWN // BLOCKS, lambda g: sums_read(g).wait())

    def steps(start, end, work):
        wide = 2 * EIGHT
        count = (end - start + EIGHT - 1) >> WIDE_SHIFT

        def one(p, carry):
            work(start + wide * p, wide)
            return carry

        lax.fori_loop(0, count, one, 0)
        pl.when(start + wide * count < end)(lambda: work(start + wide * count, EIGHT))

    def some(entries, start, end, count):
        at = [start + j for j in range(count)]
        at = [(jnp.where(spot < end, spot, start), spot < end) for spot in at]
        return [(entries[spot], spot, held) for spot, held in at]

    def fold_sub(sub):
        start, end = bound(q, sub), bound(q, sub + 1)
        def fold_some(first, count):
            folded, picks = [], []
            for entry, spot, held in some(fold_list, first, end, count):
                row = entry >> ROW_SHIFT
                source, slot = (entry >> SOURCE_SHIFT) & SOURCE_MASK, entry & SLOT_MASK
                raw = x[source, pl.ds(pl.multiple_of(slot * LANES, LANES), LANES), :]
                root = raw.astype(jnp.int32).astype(jnp.float32) + float(CODE_SHIFT)
                scale = spread[row]
                square = root * root
                tile = square * jnp.abs(scale)
                lower = square * jnp.maximum(scale, 0.0)
                tiles[spot] = tile.astype(jnp.bfloat16)
                halves = [lower.astype(jnp.bfloat16), (tile - lower).astype(jnp.bfloat16)]
                folded.append(jnp.concatenate(halves, axis=1))
                own = jnp.broadcast_to(mods[pl.ds(jnp.where(held, row, none), 1), :], (16, LANES))
                own = jnp.where(cluster == own.astype(jnp.bfloat16)[None], one, zero)
                picks.append(own.reshape(HALF, LANES))
            pick = jnp.concatenate(picks, axis=1)
            sums[columns(sub)] += jnp.dot(
                pick, jnp.concatenate(folded, axis=0), preferred_element_type=jnp.float32
            )

        steps(start, end, fold_some)

    def fold_group(g):
        each_sub(jnp.maximum(begin, g * BLOCKS), (g + 1) * BLOCKS, fold_sub)
        sums_write(g).start()

    each_sub(begin // BLOCKS, TB_OWN // BLOCKS, fold_group)
    kept = []
    if not last:
        each_chunk(q, fresh_out, True, end, lambda copy: copy.start())
        kept.append(pltpu.make_async_copy(spread, made_out[0], sems.at[4]))
        kept.append(pltpu.make_async_copy(hot, made_out[1], sems.at[5]))
    for copy in kept:
        copy.start()
    each_earlier(lambda copy: copy.wait())

    def score_sub(sub):
        start, end = score_bound(sub), score_bound(sub + 1)
        own_sums = sums[columns(sub)]
        narrow[...] = own_sums.astype(jnp.bfloat16)
        squares[...] += own_sums * own_sums

        def score_some(first, count):
            listed = some(score_list, first, end, count)
            rows = [jnp.where(held, entry >> ROW_SHIFT, none) for entry, spot, held in listed]
            spots = [entry & PLACE_MASK for entry, spot, held in listed]
            hots = [hot[row] if cached else one_hot(row) for row in rows]
            chosen = jnp.dot(
                jnp.concatenate(hots, axis=0), narrow[...], preferred_element_type=jnp.float32
            )
            for j in range(count):
                both = chosen[j * LANES : (j + 1) * LANES]
                own = jnp.where(spread[rows[j]] < 0.0, both[:, LANES:], both[:, :LANES])
                products[rows[j]] += own * tiles[spots[j]].astype(jnp.float32)

        steps(start, end, score_some)

    each_sub(begin, end, score_sub)
    block_sums(products, scores, none)
    if last:
        own = none // devices
        square = [lane_sums(squares[:, h : h + LANES])[:1] for h in (0, LANES)]
        square = jnp.concatenate(square, axis=1)
        for d in range(devices):
            part[d, :, part.shape[2] - K :] = square
            for b in range(own):
                at = d * own + b
                part[d, :, b * LANES : (b + 1) * LANES] = scores[at : at + 1, :]
    else:
        part[...] = scores[...]
        squares_out[...] = squares[...]
    for copy in kept:
        copy.wait()
    if not last:
        each_chunk(q, fresh_out, True, end, lambda copy: copy.wait())
    each_sub(begin // BLOCKS, TB_OWN // BLOCKS, lambda g: sums_write(g).wait())


def stage(q, cuts, scalars, mods, signed, x, normed, totals):
    devices = x.shape[0]
    last = q == len(cuts) - 2
    blocks = mods.shape[0]
    cached = blocks <= CACHED_BLOCKS
    width = cuts[q + 1] - cuts[q]
    home = blocks // devices * LANES
    wide = jax.ShapeDtypeStruct((HALF, TB_OWN * 2 * LANES), jnp.float32)
    square = jax.ShapeDtypeStruct((HALF, 2 * LANES), jnp.float32)
    if last:
        out_shape = [jax.ShapeDtypeStruct((devices, 1, home + K), jnp.float32), wide]
    else:
        out_shape = [
            jax.ShapeDtypeStruct((blocks, LANES), jnp.float32),
            wide,
            square,
            jax.ShapeDtypeStruct((blocks + 1, LANES, LANES), jnp.float32),
            jax.ShapeDtypeStruct((blocks + 1 if cached else 1, LANES, HALF), jnp.bfloat16),
            jax.ShapeDtypeStruct((devices * width, LANES, LANES), jnp.bfloat16),
        ]
    slots = devices * cuts[-1]
    sizes = [devices * (high - low) for low, high in zip(cuts, cuts[1:])]
    chunks = max(size // math.gcd(CHUNK, size) for size in sizes)
    operands = [*scalars, mods, signed, x, *normed, *totals]
    return pl.pallas_call(
        functools.partial(stage_kernel, q, [devices * cut for cut in cuts], last, cached),
        in_specs=[SMEM] * len(scalars) + [VMEM] * 2 + [ANY] * (1 + q) + [VMEM, ANY, VMEM, ANY, ANY][: len(totals)],
        out_specs=[VMEM, ANY, VMEM, ANY, ANY, ANY][: len(out_shape)],
        out_shape=out_shape,
        input_output_aliases={len(operands) - len(totals) + 1: 1} if q else {},
        scratch_shapes=[
            pltpu.VMEM((blocks + 1, LANES, LANES), jnp.float32),
            pltpu.VMEM((devices, width * LANES, LANES), jnp.int16),
            pltpu.VMEM((blocks + 1 if cached else 1, LANES, HALF), jnp.bfloat16),
            pltpu.VMEM(wide.shape, jnp.float32),
            pltpu.VMEM(square.shape, jnp.bfloat16),
            pltpu.VMEM((slots, LANES, LANES), jnp.bfloat16),
            pltpu.VMEM((blocks + 1, LANES, LANES), jnp.float32),
            pltpu.VMEM((blocks, LANES), jnp.float32),
            pltpu.VMEM(square.shape, jnp.float32),
            pltpu.VMEM((blocks + 1, LANES), jnp.float32),
            pltpu.VMEM((blocks + 1, LANES), jnp.float32),
            pltpu.SemaphoreType.DMA((6,)),
            pltpu.SemaphoreType.DMA((2, TB_OWN // BLOCKS)),
            pltpu.SemaphoreType.DMA((max(q, 1), chunks)),
        ],
        compiler_params=params(),
        cost_estimate=pl.CostEstimate(
            flops=devices * width * LANES * LANES * K, bytes_accessed=wide.size, transcendentals=0
        ),
        name="stage",
    )(*operands)


def close_kernel(root, groups, labels_hbm, got_hbm, sums_hbm, out_hbm, similarity_hbm, labels_ref,
                 got_ref, similarity, sums, out, sems, small_sems):
    width = TB_OWN // groups
    reads, writes = [], []
    small = [
        pltpu.make_async_copy(got_hbm, got_ref, small_sems.at[0]),
        pltpu.make_async_copy(labels_hbm, labels_ref, small_sems.at[1]),
    ]
    for copy in small:
        copy.start()
    for g in range(groups):
        some = (slice(None), pl.ds(g * width * 2 * LANES, width * 2 * LANES))
        reads.append(pltpu.make_async_copy(sums_hbm.at[some], sums.at[some], sems.at[0, g]))
        some = (slice(None), pl.ds(g * width * LANES, width * LANES))
        writes.append(pltpu.make_async_copy(out.at[some], out_hbm.at[some], sems.at[1, g]))
        reads[g].start()
    for copy in small:
        copy.wait()
    total = jnp.sum(got_ref[...], axis=0)
    home = total.shape[1] - K
    own = lax.rsqrt(total[:, home:] + EPSILON)
    columns = [
        jnp.transpose(jnp.broadcast_to(own[:, k : k + LANES], (LANES, LANES)))
        for k in range(0, K, LANES)
    ]
    cluster = lax.broadcasted_iota(jnp.int32, (LANES, LANES), 0)
    for b in range(home // LANES):
        found = jnp.zeros((LANES, LANES), jnp.float32)
        for i, column in enumerate(columns):
            found += jnp.where(cluster + i * LANES == labels_ref[b : b + 1, :], column, 0.0)
        found = jnp.sum(found, axis=0, keepdims=True)
        similarity[b : b + 1, :] = total[:, b * LANES : (b + 1) * LANES] * found
    writes.append(pltpu.make_async_copy(similarity, similarity_hbm, small_sems.at[2]))
    writes[-1].start()
    for g in range(groups):
        reads[g].wait()

        def one_sub(sub, carry):
            to = pl.ds(pl.multiple_of(sub * LANES, LANES), LANES)
            for i, column in enumerate(columns):
                half, row = divmod(i * LANES, HALF)
                at = pl.ds(pl.multiple_of((2 * sub + half) * LANES, LANES), LANES)
                done = sums[row : row + LANES, at] * column * root
                out[i * LANES : (i + 1) * LANES, to] = done.astype(jnp.bfloat16)
            return carry

        lax.fori_loop(g * width, (g + 1) * width, one_sub, 0)
        writes[g].start()
    for write in writes:
        write.wait()


def close(labels, got, sums, vocab_size):
    groups = 4
    labels = labels.reshape(-1, LANES)
    wide = jax.ShapeDtypeStruct((K, TB_OWN * LANES), jnp.bfloat16)
    centroids, similarity = pl.pallas_call(
        functools.partial(close_kernel, math.sqrt(vocab_size), groups),
        in_specs=[ANY] * 3,
        out_specs=[ANY] * 2,
        out_shape=[wide, jax.ShapeDtypeStruct(labels.shape, jnp.float32)],
        scratch_shapes=[
            pltpu.VMEM(labels.shape, jnp.int32),
            pltpu.VMEM(got.shape, jnp.float32),
            pltpu.VMEM(labels.shape, jnp.float32),
            pltpu.VMEM(sums.shape, jnp.float32),
            pltpu.VMEM(wide.shape, jnp.bfloat16),
            pltpu.SemaphoreType.DMA((2, groups)),
            pltpu.SemaphoreType.DMA((3,)),
        ],
        compiler_params=params(),
        cost_estimate=pl.CostEstimate(
            flops=2 * sums.size, bytes_accessed=6 * sums.size, transcendentals=0
        ),
        name="close",
    )(labels, got, sums)
    return centroids, similarity.reshape(-1)


def exchange(x):
    return lax.all_to_all(x, "dp", split_axis=0, concat_axis=0, tiled=True)


def after(value, *others):
    return lax.optimization_barrier((value, *others))[0]


def sorted_slots(key, top, entries):
    slots = jnp.arange(key.shape[0], dtype=jnp.int32)
    ahead = (key[None, :] < key[:, None]) | (
        (key[None, :] == key[:, None]) & (slots[None, :] < slots[:, None])
    )
    position = jnp.sum(ahead.astype(jnp.int32), axis=1)
    here = position[None, :] == slots[:, None]
    listed = jnp.sum(jnp.where(here, entries[None, :], 0), axis=1)
    levels = jnp.arange(top + 1, dtype=jnp.int32)
    bounds = jnp.sum((key[None, :] < levels[:, None]).astype(jnp.int32), axis=1)
    return listed, bounds, position


def ranks(group, sub):
    index = jnp.arange(sub.shape[-1], dtype=jnp.int32)
    before = (sub[..., None, :] < sub[..., :, None]) | (
        (sub[..., None, :] == sub[..., :, None]) & (index[None, :] < index[:, None])
    )
    same = group[..., None, :] == group[..., :, None]
    return jnp.sum((before & same).astype(jnp.int32), axis=-1)


def shards(tile_values, tile_row, tile_owner, tile_sub, labels):
    devices = lax.axis_size("dp")
    tiles = tile_values.shape[0]
    home = labels.shape[0]
    blocks = home // LANES * devices
    cap = max(2, 2 * tiles // devices)
    cuts = tuple(sorted({int(cap * share) for share in PARTS})) if cap >= 8 else (0, cap)
    parts = len(cuts) - 1
    here = lax.axis_index("dp").astype(jnp.int32)
    owner = tile_owner[:, 0]

    told = (labels, owner, tile_row, tile_sub)
    outgoing = pack(tile_values, owner, tile_row, told, devices, blocks, cuts)
    incoming = [exchange(outgoing[0])]
    heard = incoming[0][:, (cuts[1] - cuts[0]) * LANES :].astype(jnp.int32)
    level = heard[:, :blocks]
    partial_sq = jnp.exp2(level.astype(jnp.float32) * (1.0 / LOG_STEPS) + LOG_MIDDLE)
    row_sq = jnp.sum(jnp.where(level > -32768, partial_sq, 0.0), axis=0)
    all_described = heard[:, blocks:].reshape(devices, -1)
    all_labels = all_described[:, :home].reshape(blocks, LANES)
    mine = all_described[:, home : home + tiles] == here
    code = all_described[:, home + tiles : home + 2 * tiles]
    rank = ranks(mine.astype(jnp.int32), code % TB_OWN)
    chosen = mine[:, None, :] & (rank[:, None, :] == jnp.arange(cap)[None, :, None])
    meta = jnp.sum(jnp.where(chosen, code[:, None, :] + 1, 0), axis=2).reshape(-1) - 1
    sub = jnp.where(meta < 0, TB_OWN, meta % TB_OWN)
    slot_rank = np.arange(devices * cap) % cap
    slot_part = np.searchsorted(np.array(cuts), slot_rank, side="right") - 1
    low = np.array(cuts)[slot_part]
    fold_key = jnp.asarray(slot_part * (TB_OWN + 1), jnp.int32) + sub
    row = (meta // TB_OWN) << ROW_SHIFT
    from_slot = (np.arange(devices * cap) // cap << SOURCE_SHIFT) + slot_rank - low
    fold_list, fold_bounds, position = sorted_slots(
        fold_key, parts * (TB_OWN + 1), row + jnp.asarray(from_slot, jnp.int32)
    )
    score_list, *_ = sorted_slots(sub, TB_OWN, row + position)
    scalars = [fold_list, fold_bounds, score_list]

    scale = lax.rsqrt(row_sq + EPSILON) * (1.0 / CODE_TOP**2)
    signed = jnp.where(all_labels < HALF, scale, -scale)
    mods = (all_labels % HALF).astype(jnp.float32)
    totals, normed = (), []
    beside = (*scalars, mods, signed)
    for q in range(parts):
        if q + 1 < parts:
            ahead = (incoming[q], *beside) if q else (incoming[q],)
            incoming.append(exchange(after(outgoing[q + 1], *ahead)))
        partial, sums, *more = stage(
            q, cuts, scalars, mods, signed, incoming[q], normed, totals
        )
        beside = (partial, sums)
        totals, normed = (partial, sums, *more[:3]), normed + more[3:]
    return close(labels, exchange(partial), sums, TB_OWN * LANES * devices)


def solution(mesh):
    return jax.shard_map(
        shards,
        mesh=mesh,
        in_specs=(
            P(("groups", "dp"), None, None),
            P(("groups", "dp")),
            P(("groups", "dp"), None),
            P(("groups", "dp")),
            P(("groups", "dp")),
        ),
        out_specs=(P("groups", "dp"), P(("groups", "dp"))),
        check_vma=False,
    )
```

```python
import functools
import math

import jax
import jax.numpy as jnp
import numpy as np
from jax import lax
from jax.experimental import pallas as pl
from jax.experimental.pallas import tpu as pltpu
from jax.sharding import PartitionSpec as P

K = 512
HALF = K // 2
TB_OWN = 16
LANES = 128
EPSILON = 1e-06
CODE_TOP = 65535.0
CODE_SHIFT = 32768
VMEM_BYTES = 60 * 1024 * 1024
STEP_TILES = 16
PARTS = (0.0, 13 / 16, 1.0)
LOG_STEPS = 1800.0
LOG_MIDDLE = -3.0
CACHED_BLOCKS = 64
QUAD = 4
EIGHT = 8
WIDE_SHIFT = 4
CHUNK = 16
BLOCKS = 4
ROW_SHIFT, SOURCE_SHIFT = 16, 8
PLACE_MASK, SOURCE_MASK, SLOT_MASK = 0xFFFF, 0xFF, 0xFF
BATCH = 8
NT = (((1,), (1,)), ((), ()))
SMEM = pl.BlockSpec(memory_space=pltpu.SMEM)
VMEM = pl.BlockSpec(memory_space=pltpu.VMEM)
ANY = pl.BlockSpec(memory_space=pl.ANY)


def lane_sums(values):
    ones = jnp.ones((8, 2 * LANES), jnp.bfloat16)
    high = values.astype(jnp.bfloat16)
    low = (values - high.astype(jnp.float32)).astype(jnp.bfloat16)
    both = jnp.concatenate([high, low], axis=1)
    return lax.dot_general(ones, both, NT, preferred_element_type=jnp.float32)


def block_sums(square, out_ref, count):
    batch = math.gcd(BATCH, count)

    def one_batch(c, carry):
        some = square[pl.ds(c * batch, batch)].reshape((batch * LANES, LANES))
        sums = lane_sums(some)
        for j in range(batch):
            out_ref[pl.ds(c * batch + j, 1), :] += sums[:1, j * LANES : (j + 1) * LANES]
        return carry

    lax.fori_loop(0, count // batch, one_batch, 0)


def params():
    return pltpu.CompilerParams(vmem_limit_bytes=VMEM_BYTES)


def pack_kernel(cuts, owner_hbm, row_hbm, *refs):
    parts = len(cuts) - 1
    (*told_hbms, x_hbm), refs = refs[:5], refs[5:]
    outs = refs[:parts]
    x, coded, square, sums, words, notes, rank_row, rank_ref, *refs = refs[parts:]
    owner_ref, row_ref, *told_refs, sems, x_sems, small_sems = refs
    tiles = x.shape[0]
    devices = coded.shape[0]
    blocks = square.shape[0]
    step = math.gcd(STEP_TILES, tiles)

    def read(c):
        some = pl.ds(c * step, step)
        return pltpu.make_async_copy(x_hbm.at[some], x.at[some], x_sems.at[c])

    pairs = zip((owner_hbm, row_hbm, *told_hbms), (owner_ref, row_ref, *told_refs))
    small = [pltpu.make_async_copy(*pair, small_sems.at[i]) for i, pair in enumerate(pairs)]
    for copy in small:
        copy.start()
    for c in range(tiles // step):
        read(c).start()
    for copy in small:
        copy.wait()
    labels, owner, row, sub = [ref[...] for ref in told_refs]
    own, sub_own = [jnp.broadcast_to(v.astype(jnp.float32), (tiles, tiles)) for v in (owner, sub)]
    other, sub_other = jnp.transpose(own), jnp.transpose(sub_own)
    index = [lax.broadcasted_iota(jnp.int32, (tiles, tiles), d) for d in (0, 1)]
    ahead = (sub_other < sub_own) | ((sub_other == sub_own) & (index[0] < index[1]))
    ahead = jnp.where(ahead & (other == own), 1.0, 0.0)
    rank_row[...] = jnp.sum(ahead, axis=0, keepdims=True).astype(jnp.int32)
    pltpu.sync_copy(rank_row, rank_ref)
    square[...] = jnp.zeros_like(square)

    def some_tiles(i, carry):
        pl.when(i % (step // QUAD) == 0)(lambda: read(i // (step // QUAD)).wait())
        for j in range(QUAD):
            t = i * QUAD + j
            some = x[t]
            root = some * lax.rsqrt(some)
            code = (root * CODE_TOP + 0.5).astype(jnp.int32) - CODE_SHIFT
            owner, rank = owner_ref[t], rank_ref[0, t]
            at = pl.ds(pl.multiple_of(rank * LANES, LANES), LANES)
            coded[owner, at, :] = code.astype(jnp.int16)
            square[row_ref[t]] += some * some
        return carry

    lax.fori_loop(0, tiles // QUAD, some_tiles, 0)

    copies = []
    for q in range(parts):
        rows, count = (cuts[q + 1] - cuts[q]) * LANES, devices // (1 if q else math.gcd(4, devices))
        for d in range(0, devices, count):
            from_ref = coded.at[pl.ds(d, count), pl.ds(cuts[q] * LANES, rows)]
            into = outs[q].at[pl.ds(d, count), pl.ds(0, rows)]
            copies.append(pltpu.make_async_copy(from_ref, into, sems.at[len(copies)]))
    for copy in copies:
        copy.start()
    sums[...] = jnp.zeros_like(sums)
    block_sums(square, sums, blocks)
    total = sums[...]
    level = (jnp.log2(jnp.maximum(total, 1e-30)) - LOG_MIDDLE) * LOG_STEPS
    level = jnp.where(total > 0.0, jnp.clip(level, -32700.0, 32700.0), -32768.0)
    level = (level + 32768.5).astype(jnp.int32) - 32768
    words[...] = jnp.zeros_like(words)
    words[:blocks, :] = level
    at = blocks
    for told in (labels, owner, row * TB_OWN + sub):
        words[at : at + told.shape[0], :] = told
        at += told.shape[0]
    notes[...] = jnp.broadcast_to(words[...].astype(jnp.int16)[None], notes.shape)
    into = outs[0].at[:, pl.ds((cuts[1] - cuts[0]) * LANES, notes.shape[1])]
    copies.append(pltpu.make_async_copy(notes, into, sems.at[len(copies)]))
    copies[-1].start()
    for copy in copies:
        copy.wait()


def pack(tile_values, owner, tile_row, told, devices, blocks, cuts):
    tiles = tile_values.shape[0]
    told = [x.reshape(-1, LANES) for x in told]
    noted = -(-(blocks + sum(x.shape[0] for x in told[:3])) // 16) * 16
    rows = [(high - low) * LANES for low, high in zip(cuts, cuts[1:])]
    rows[0] += noted
    return pl.pallas_call(
        functools.partial(pack_kernel, cuts),
        in_specs=[ANY] * 7,
        out_specs=[ANY] * len(rows),
        out_shape=[jax.ShapeDtypeStruct((devices, some, LANES), jnp.int16) for some in rows],
        scratch_shapes=[
            pltpu.VMEM(tile_values.shape, jnp.float32),
            pltpu.VMEM((devices, cuts[-1] * LANES, LANES), jnp.int16),
            pltpu.VMEM((blocks, LANES, LANES), jnp.float32),
            pltpu.VMEM((blocks, LANES), jnp.float32),
            pltpu.VMEM((noted, LANES), jnp.int32),
            pltpu.VMEM((devices, noted, LANES), jnp.int16),
            pltpu.VMEM((1, tiles), jnp.int32),
            pltpu.SMEM((1, tiles), jnp.int32),
            pltpu.SMEM((tiles,), jnp.int32),
            pltpu.SMEM((tiles,), jnp.int32),
            *[pltpu.VMEM(some.shape, jnp.int32) for some in told],
            pltpu.SemaphoreType.DMA((len(rows) + 4,)),
            pltpu.SemaphoreType.DMA((tiles // math.gcd(STEP_TILES, tiles),)),
            pltpu.SemaphoreType.DMA((6,)),
        ],
        compiler_params=params(),
        cost_estimate=pl.CostEstimate(
            flops=8 * tile_values.size,
            bytes_accessed=6 * tile_values.size,
            transcendentals=tile_values.size,
        ),
        name="pack",
    )(owner, tile_row, *told, tile_values)


def stage_kernel(q, bases, last, cached, fold_list_in, fold_bound_in, score_list_in,
                 mods_in, signed_in, x_hbm, *refs):
    base = bases[q]
    earlier, refs = refs[:q], refs[q:]
    before, sums_in, squares_in, *made_in = refs[:5] if q else (None,) * 5
    refs = refs[5:] if q else refs
    part, sums_out, refs = refs[0], refs[1], refs[2:]
    (squares_out, *made_out, fresh_out), refs = ((None,) * 4, refs) if last else (refs[:4], refs[4:])
    spread, x, hot, sums, narrow, tiles, products, scores, squares, mods, signed, *refs = refs
    fold_list, fold_bound, score_list, sems, sub_sems, tile_sems, small_sems = refs
    devices, width = x.shape[0], x.shape[1] // LANES
    none = products.shape[0] - 1
    needed = [pltpu.make_async_copy(x_hbm.at[:, pl.ds(0, width * LANES)], x, sems.at[0])]
    if q:
        needed.append(pltpu.make_async_copy(made_in[0], spread, sems.at[1]))
    for held, empty in ((mods, -1.0), (signed, 0.0)):
        held[none : none + 1, :] = jnp.full((1, LANES), empty, jnp.float32)
    pairs = [(fold_list_in, fold_list), (fold_bound_in, fold_bound), (score_list_in, score_list)]
    pairs += [(mods_in, mods.at[pl.ds(0, none)]), (signed_in, signed.at[pl.ds(0, none)])]
    pairs += [(before, scores), (squares_in, squares)] if q else []
    small = [pltpu.make_async_copy(*pair, small_sems.at[i]) for i, pair in enumerate(pairs)]
    for copy in small + needed:
        copy.start()
    for copy in small:
        copy.wait()
    parts = len(bases) - 1

    def bound(p, sub):
        return fold_bound[p * (TB_OWN + 1) + sub]

    def score_bound(sub):
        return sum(bound(p, sub) - bound(p, 0) for p in range(parts))

    def complete(arrived):
        def one(i, least):
            sub = TB_OWN - 1 - i
            waits = [bound(p, sub + 1) > bound(p, sub) for p in range(arrived, parts)]
            return jnp.where(functools.reduce(jnp.logical_or, waits), sub, least)

        return lax.fori_loop(0, TB_OWN, one, TB_OWN) if arrived < parts else TB_OWN

    begin, end = complete(q) if q else 0, complete(q + 1)

    def columns(sub):
        return (slice(None), pl.ds(pl.multiple_of(sub * 2 * LANES, 2 * LANES), 2 * LANES))

    def group(g):
        size = BLOCKS * 2 * LANES
        return (slice(None), pl.ds(pl.multiple_of(g * size, size), size))

    def sums_read(g):
        return pltpu.make_async_copy(sums_in.at[group(g)], sums.at[group(g)], sub_sems.at[0, g])

    def sums_write(g):
        return pltpu.make_async_copy(sums.at[group(g)], sums_out.at[group(g)], sub_sems.at[1, g])

    def each_sub(low, high, what):
        def one(sub, carry):
            what(sub)
            return carry

        lax.fori_loop(low, high, one, 0)

    if q:
        each_sub(begin // BLOCKS, TB_OWN // BLOCKS, lambda g: sums_read(g).start())
    else:
        scores[...] = jnp.zeros_like(scores)
        sums[...] = jnp.zeros_like(sums)
        squares[...] = jnp.zeros_like(squares)
    later = [pltpu.make_async_copy(made_in[1], hot, sems.at[3])] if q and cached else []

    def each_chunk(p, outside, write, sub, what):
        count = math.gcd(CHUNK, bases[p + 1] - bases[p])

        def one(c, carry):
            away, own = outside.at[pl.ds(c * count, count)], tiles.at[pl.ds(bases[p] + c * count, count)]
            some = (own, away) if write else (away, own)
            what(pltpu.make_async_copy(*some, tile_sems.at[0 if write else p, c]))
            return carry

        first, stop = bound(p, sub) - bases[p], bound(p, TB_OWN) - bases[p]
        lax.fori_loop(first // count, (stop + count - 1) // count, one, 0)

    def each_earlier(what):
        for copy in later:
            what(copy)
        for e, e_hbm in enumerate(earlier):
            each_chunk(e, e_hbm, False, begin, what)

    each_earlier(lambda copy: copy.start())
    products[...] = jnp.zeros_like(products)
    cluster = lax.broadcasted_iota(jnp.int32, (HALF, LANES), 0).astype(jnp.float32)
    cluster = cluster.astype(jnp.bfloat16).reshape(HALF // 16, 16, LANES)
    one, zero = jnp.ones((), jnp.bfloat16), jnp.zeros((), jnp.bfloat16)
    lane = lax.broadcasted_iota(jnp.int32, (LANES, LANES), 1)

    def column(ref, row):
        return jnp.transpose(jnp.broadcast_to(ref[pl.ds(row, 1), :], (LANES, LANES)))

    def one_hot(row):
        own = column(mods, row).astype(jnp.int32)
        some = [jnp.where(own == lane + g, 1.0, 0.0) for g in range(0, HALF, LANES)]
        return jnp.concatenate(some, axis=1).astype(jnp.bfloat16)

    batch = math.gcd(none + 1, 3)

    def build(c, carry):
        for j in range(batch):
            spread[c * batch + j] = column(signed, c * batch + j)
            if cached:
                hot[c * batch + j] = one_hot(c * batch + j)
        return carry

    if not q:
        lax.fori_loop(0, (none + 1) // batch, build, 0)
    for copy in needed:
        copy.wait()
    if q:
        each_sub(begin // BLOCKS, TB_OWN // BLOCKS, lambda g: sums_read(g).wait())

    def steps(start, end, work):
        wide = 2 * EIGHT
        count = (end - start + EIGHT - 1) >> WIDE_SHIFT

        def one(p, carry):
            work(start + wide * p, wide)
            return carry

        lax.fori_loop(0, count, one, 0)
        pl.when(start + wide * count < end)(lambda: work(start + wide * count, EIGHT))

    def some(entries, start, end, count):
        at = [start + j for j in range(count)]
        at = [(jnp.where(spot < end, spot, start), spot < end) for spot in at]
        return [(entries[spot], spot, held) for spot, held in at]

    def fold_sub(sub):
        start, end = bound(q, sub), bound(q, sub + 1)
        def fold_some(first, count):
            folded, picks = [], []
            for entry, spot, held in some(fold_list, first, end, count):
                row = entry >> ROW_SHIFT
                source, slot = (entry >> SOURCE_SHIFT) & SOURCE_MASK, entry & SLOT_MASK
                raw = x[source, pl.ds(pl.multiple_of(slot * LANES, LANES), LANES), :]
                root = raw.astype(jnp.int32).astype(jnp.float32) + float(CODE_SHIFT)
                scale = spread[row]
                square = root * root
                tile = square * jnp.abs(scale)
                lower = square * jnp.maximum(scale, 0.0)
                tiles[spot] = tile.astype(jnp.bfloat16)
                halves = [lower.astype(jnp.bfloat16), (tile - lower).astype(jnp.bfloat16)]
                folded.append(jnp.concatenate(halves, axis=1))
                own = jnp.broadcast_to(mods[pl.ds(jnp.where(held, row, none), 1), :], (16, LANES))
                own = jnp.where(cluster == own.astype(jnp.bfloat16)[None], one, zero)
                picks.append(own.reshape(HALF, LANES))
            pick = jnp.concatenate(picks, axis=1)
            sums[columns(sub)] += jnp.dot(
                pick, jnp.concatenate(folded, axis=0), preferred_element_type=jnp.float32
            )

        steps(start, end, fold_some)

    def fold_group(g):
        each_sub(jnp.maximum(begin, g * BLOCKS), (g + 1) * BLOCKS, fold_sub)
        sums_write(g).start()

    each_sub(begin // BLOCKS, TB_OWN // BLOCKS, fold_group)
    kept = []
    if not last:
        each_chunk(q, fresh_out, True, end, lambda copy: copy.start())
        kept.append(pltpu.make_async_copy(spread, made_out[0], sems.at[4]))
        kept.append(pltpu.make_async_copy(hot, made_out[1], sems.at[5]))
    for copy in kept:
        copy.start()
    each_earlier(lambda copy: copy.wait())

    def score_sub(sub):
        start, end = score_bound(sub), score_bound(sub + 1)
        own_sums = sums[columns(sub)]
        narrow[...] = own_sums.astype(jnp.bfloat16)
        squares[...] += own_sums * own_sums

        def score_some(first, count):
            listed = some(score_list, first, end, count)
            rows = [jnp.where(held, entry >> ROW_SHIFT, none) for entry, spot, held in listed]
            spots = [entry & PLACE_MASK for entry, spot, held in listed]
            hots = [hot[row] if cached else one_hot(row) for row in rows]
            chosen = jnp.dot(
                jnp.concatenate(hots, axis=0), narrow[...], preferred_element_type=jnp.float32
            )
            for j in range(count):
                both = chosen[j * LANES : (j + 1) * LANES]
                own = jnp.where(spread[rows[j]] < 0.0, both[:, LANES:], both[:, :LANES])
                products[rows[j]] += own * tiles[spots[j]].astype(jnp.float32)

        steps(start, end, score_some)

    each_sub(begin, end, score_sub)
    block_sums(products, scores, none)
    if last:
        own = none // devices
        square = [lane_sums(squares[:, h : h + LANES])[:1] for h in (0, LANES)]
        square = jnp.concatenate(square, axis=1)
        for d in range(devices):
            part[d, :, part.shape[2] - K :] = square
            for b in range(own):
                at = d * own + b
                part[d, :, b * LANES : (b + 1) * LANES] = scores[at : at + 1, :]
    else:
        part[...] = scores[...]
        squares_out[...] = squares[...]
    for copy in kept:
        copy.wait()
    if not last:
        each_chunk(q, fresh_out, True, end, lambda copy: copy.wait())
    each_sub(begin // BLOCKS, TB_OWN // BLOCKS, lambda g: sums_write(g).wait())


def stage(q, cuts, scalars, mods, signed, x, normed, totals):
    devices = x.shape[0]
    last = q == len(cuts) - 2
    blocks = mods.shape[0]
    cached = blocks <= CACHED_BLOCKS
    width = cuts[q + 1] - cuts[q]
    home = blocks // devices * LANES
    wide = jax.ShapeDtypeStruct((HALF, TB_OWN * 2 * LANES), jnp.float32)
    square = jax.ShapeDtypeStruct((HALF, 2 * LANES), jnp.float32)
    if last:
        out_shape = [jax.ShapeDtypeStruct((devices, 1, home + K), jnp.float32), wide]
    else:
        out_shape = [
            jax.ShapeDtypeStruct((blocks, LANES), jnp.float32),
            wide,
            square,
            jax.ShapeDtypeStruct((blocks + 1, LANES, LANES), jnp.float32),
            jax.ShapeDtypeStruct((blocks + 1 if cached else 1, LANES, HALF), jnp.bfloat16),
            jax.ShapeDtypeStruct((devices * width, LANES, LANES), jnp.bfloat16),
        ]
    slots = devices * cuts[-1]
    sizes = [devices * (high - low) for low, high in zip(cuts, cuts[1:])]
    chunks = max(size // math.gcd(CHUNK, size) for size in sizes)
    operands = [*scalars, mods, signed, x, *normed, *totals]
    return pl.pallas_call(
        functools.partial(stage_kernel, q, [devices * cut for cut in cuts], last, cached),
        in_specs=[ANY] * len(operands),
        out_specs=[VMEM, ANY, VMEM, ANY, ANY, ANY][: len(out_shape)],
        out_shape=out_shape,
        input_output_aliases={len(operands) - len(totals) + 1: 1} if q else {},
        scratch_shapes=[
            pltpu.VMEM((blocks + 1, LANES, LANES), jnp.float32),
            pltpu.VMEM((devices, width * LANES, LANES), jnp.int16),
            pltpu.VMEM((blocks + 1 if cached else 1, LANES, HALF), jnp.bfloat16),
            pltpu.VMEM(wide.shape, jnp.float32),
            pltpu.VMEM(square.shape, jnp.bfloat16),
            pltpu.VMEM((slots, LANES, LANES), jnp.bfloat16),
            pltpu.VMEM((blocks + 1, LANES, LANES), jnp.float32),
            pltpu.VMEM((blocks, LANES), jnp.float32),
            pltpu.VMEM(square.shape, jnp.float32),
            pltpu.VMEM((blocks + 1, LANES), jnp.float32),
            pltpu.VMEM((blocks + 1, LANES), jnp.float32),
            *[pltpu.SMEM(some.shape, jnp.int32) for some in scalars],
            pltpu.SemaphoreType.DMA((6,)),
            pltpu.SemaphoreType.DMA((2, TB_OWN // BLOCKS)),
            pltpu.SemaphoreType.DMA((max(q, 1), chunks)),
            pltpu.SemaphoreType.DMA((7,)),
        ],
        compiler_params=params(),
        cost_estimate=pl.CostEstimate(
            flops=devices * width * LANES * LANES * K, bytes_accessed=wide.size, transcendentals=0
        ),
        name="stage",
    )(*operands)


def close_kernel(root, groups, labels_hbm, got_hbm, sums_hbm, out_hbm, similarity_hbm, labels_ref,
                 got_ref, similarity, sums, out, sems, small_sems):
    width = TB_OWN // groups
    reads, writes = [], []
    small = [
        pltpu.make_async_copy(got_hbm, got_ref, small_sems.at[0]),
        pltpu.make_async_copy(labels_hbm, labels_ref, small_sems.at[1]),
    ]
    for copy in small:
        copy.start()
    for g in range(groups):
        some = (slice(None), pl.ds(g * width * 2 * LANES, width * 2 * LANES))
        reads.append(pltpu.make_async_copy(sums_hbm.at[some], sums.at[some], sems.at[0, g]))
        some = (slice(None), pl.ds(g * width * LANES, width * LANES))
        writes.append(pltpu.make_async_copy(out.at[some], out_hbm.at[some], sems.at[1, g]))
        reads[g].start()
    for copy in small:
        copy.wait()
    total = jnp.sum(got_ref[...], axis=0)
    home = total.shape[1] - K
    own = lax.rsqrt(total[:, home:] + EPSILON)
    columns = [
        jnp.transpose(jnp.broadcast_to(own[:, k : k + LANES], (LANES, LANES)))
        for k in range(0, K, LANES)
    ]
    cluster = lax.broadcasted_iota(jnp.int32, (LANES, LANES), 0)
    for b in range(home // LANES):
        found = jnp.zeros((LANES, LANES), jnp.float32)
        for i, column in enumerate(columns):
            found += jnp.where(cluster + i * LANES == labels_ref[b : b + 1, :], column, 0.0)
        found = jnp.sum(found, axis=0, keepdims=True)
        similarity[b : b + 1, :] = total[:, b * LANES : (b + 1) * LANES] * found
    writes.append(pltpu.make_async_copy(similarity, similarity_hbm, small_sems.at[2]))
    writes[-1].start()
    for g in range(groups):
        reads[g].wait()

        def one_sub(sub, carry):
            to = pl.ds(pl.multiple_of(sub * LANES, LANES), LANES)
            for i, column in enumerate(columns):
                half, row = divmod(i * LANES, HALF)
                at = pl.ds(pl.multiple_of((2 * sub + half) * LANES, LANES), LANES)
                done = sums[row : row + LANES, at] * column * root
                out[i * LANES : (i + 1) * LANES, to] = done.astype(jnp.bfloat16)
            return carry

        lax.fori_loop(g * width, (g + 1) * width, one_sub, 0)
        writes[g].start()
    for write in writes:
        write.wait()


def close(labels, got, sums, vocab_size):
    groups = 4
    labels = labels.reshape(-1, LANES)
    wide = jax.ShapeDtypeStruct((K, TB_OWN * LANES), jnp.bfloat16)
    centroids, similarity = pl.pallas_call(
        functools.partial(close_kernel, math.sqrt(vocab_size), groups),
        in_specs=[ANY] * 3,
        out_specs=[ANY] * 2,
        out_shape=[wide, jax.ShapeDtypeStruct(labels.shape, jnp.float32)],
        scratch_shapes=[
            pltpu.VMEM(labels.shape, jnp.int32),
            pltpu.VMEM(got.shape, jnp.float32),
            pltpu.VMEM(labels.shape, jnp.float32),
            pltpu.VMEM(sums.shape, jnp.float32),
            pltpu.VMEM(wide.shape, jnp.bfloat16),
            pltpu.SemaphoreType.DMA((2, groups)),
            pltpu.SemaphoreType.DMA((3,)),
        ],
        compiler_params=params(),
        cost_estimate=pl.CostEstimate(
            flops=2 * sums.size, bytes_accessed=6 * sums.size, transcendentals=0
        ),
        name="close",
    )(labels, got, sums)
    return centroids, similarity.reshape(-1)


def exchange(x):
    return lax.all_to_all(x, "dp", split_axis=0, concat_axis=0, tiled=True)


def after(value, *others):
    return lax.optimization_barrier((value, *others))[0]


def sorted_slots(key, top, entries):
    slots = jnp.arange(key.shape[0], dtype=jnp.int32)
    ahead = (key[None, :] < key[:, None]) | (
        (key[None, :] == key[:, None]) & (slots[None, :] < slots[:, None])
    )
    position = jnp.sum(ahead.astype(jnp.int32), axis=1)
    here = position[None, :] == slots[:, None]
    listed = jnp.sum(jnp.where(here, entries[None, :], 0), axis=1)
    levels = jnp.arange(-(-(top + 1) // LANES) * LANES, dtype=jnp.int32)
    bounds = jnp.sum((key[None, :] < levels[:, None]).astype(jnp.int32), axis=1)
    return listed, bounds, position


def ranks(group, sub):
    index = jnp.arange(sub.shape[-1], dtype=jnp.int32)
    before = (sub[..., None, :] < sub[..., :, None]) | (
        (sub[..., None, :] == sub[..., :, None]) & (index[None, :] < index[:, None])
    )
    same = group[..., None, :] == group[..., :, None]
    return jnp.sum((before & same).astype(jnp.int32), axis=-1)


def shards(tile_values, tile_row, tile_owner, tile_sub, labels):
    devices = lax.axis_size("dp")
    tiles = tile_values.shape[0]
    home = labels.shape[0]
    blocks = home // LANES * devices
    cap = max(2, 2 * tiles // devices)
    cuts = tuple(sorted({int(cap * share) for share in PARTS})) if cap >= 8 else (0, cap)
    parts = len(cuts) - 1
    here = lax.axis_index("dp").astype(jnp.int32)
    owner = tile_owner[:, 0]

    told = (labels, owner, tile_row, tile_sub)
    outgoing = pack(tile_values, owner, tile_row, told, devices, blocks, cuts)
    incoming = [exchange(outgoing[0])]
    heard = incoming[0][:, (cuts[1] - cuts[0]) * LANES :].astype(jnp.int32)
    level = heard[:, :blocks]
    partial_sq = jnp.exp2(level.astype(jnp.float32) * (1.0 / LOG_STEPS) + LOG_MIDDLE)
    row_sq = jnp.sum(jnp.where(level > -32768, partial_sq, 0.0), axis=0)
    all_described = heard[:, blocks:].reshape(devices, -1)
    all_labels = all_described[:, :home].reshape(blocks, LANES)
    mine = all_described[:, home : home + tiles] == here
    code = all_described[:, home + tiles : home + 2 * tiles]
    rank = ranks(mine.astype(jnp.int32), code % TB_OWN)
    chosen = mine[:, None, :] & (rank[:, None, :] == jnp.arange(cap)[None, :, None])
    meta = jnp.sum(jnp.where(chosen, code[:, None, :] + 1, 0), axis=2).reshape(-1) - 1
    sub = jnp.where(meta < 0, TB_OWN, meta % TB_OWN)
    slot_rank = np.arange(devices * cap) % cap
    slot_part = np.searchsorted(np.array(cuts), slot_rank, side="right") - 1
    low = np.array(cuts)[slot_part]
    fold_key = jnp.asarray(slot_part * (TB_OWN + 1), jnp.int32) + sub
    row = (meta // TB_OWN) << ROW_SHIFT
    from_slot = (np.arange(devices * cap) // cap << SOURCE_SHIFT) + slot_rank - low
    fold_list, fold_bounds, position = sorted_slots(
        fold_key, parts * (TB_OWN + 1), row + jnp.asarray(from_slot, jnp.int32)
    )
    score_list, *_ = sorted_slots(sub, TB_OWN, row + position)
    scalars = [fold_list, fold_bounds, score_list]

    scale = lax.rsqrt(row_sq + EPSILON) * (1.0 / CODE_TOP**2)
    signed = jnp.where(all_labels < HALF, scale, -scale)
    mods = (all_labels % HALF).astype(jnp.float32)
    totals, normed = (), []
    beside = (*scalars, mods, signed)
    for q in range(parts):
        if q + 1 < parts:
            ahead = (incoming[q], *beside) if q else (incoming[q],)
            incoming.append(exchange(after(outgoing[q + 1], *ahead)))
        partial, sums, *more = stage(
            q, cuts, scalars, mods, signed, incoming[q], normed, totals
        )
        beside = (partial, sums)
        totals, normed = (partial, sums, *more[:3]), normed + more[3:]
    return close(labels, exchange(partial), sums, TB_OWN * LANES * devices)


def solution(mesh):
    return jax.shard_map(
        shards,
        mesh=mesh,
        in_specs=(
            P(("groups", "dp"), None, None),
            P(("groups", "dp")),
            P(("groups", "dp"), None),
            P(("groups", "dp")),
            P(("groups", "dp")),
        ),
        out_specs=(P("groups", "dp"), P(("groups", "dp"))),
        check_vma=False,
    )
```

```python
import functools
import math

import jax
import jax.numpy as jnp
import numpy as np
from jax import lax
from jax.experimental import pallas as pl
from jax.experimental.pallas import tpu as pltpu
from jax.sharding import PartitionSpec as P

K = 512
HALF = K // 2
TB_OWN = 16
LANES = 128
EPSILON = 1e-06
CODE_TOP = 65535.0
CODE_SHIFT = 32768
VMEM_BYTES = 60 * 1024 * 1024
STEP_TILES = 16
PARTS = (0.0, 13 / 16, 1.0)
LOG_STEPS = 1800.0
LOG_MIDDLE = -3.0
CACHED_BLOCKS = 64
QUAD = 4
EIGHT = 8
WIDE_SHIFT = 4
CHUNK = 16
BLOCKS = 4
ROW_SHIFT, SOURCE_SHIFT = 16, 8
PLACE_MASK, SOURCE_MASK, SLOT_MASK = 0xFFFF, 0xFF, 0xFF
BATCH = 8
NT = (((1,), (1,)), ((), ()))
SMEM = pl.BlockSpec(memory_space=pltpu.SMEM)
VMEM = pl.BlockSpec(memory_space=pltpu.VMEM)
ANY = pl.BlockSpec(memory_space=pl.ANY)


def lane_sums(values):
    ones = jnp.ones((8, 2 * LANES), jnp.bfloat16)
    high = values.astype(jnp.bfloat16)
    low = (values - high.astype(jnp.float32)).astype(jnp.bfloat16)
    both = jnp.concatenate([high, low], axis=1)
    return lax.dot_general(ones, both, NT, preferred_element_type=jnp.float32)


def block_sums(square, out_ref, count):
    batch = math.gcd(BATCH, count)

    def one_batch(c, carry):
        some = square[pl.ds(c * batch, batch)].reshape((batch * LANES, LANES))
        sums = lane_sums(some)
        for j in range(batch):
            out_ref[pl.ds(c * batch + j, 1), :] += sums[:1, j * LANES : (j + 1) * LANES]
        return carry

    lax.fori_loop(0, count // batch, one_batch, 0)


def params():
    return pltpu.CompilerParams(vmem_limit_bytes=VMEM_BYTES)


def pack_kernel(cuts, owner_ref, row_ref, *refs):
    parts = len(cuts) - 1
    (*told_refs, x_hbm), refs = refs[:5], refs[5:]
    outs = refs[:parts]
    x, coded, square, sums, words, notes, rank_row, rank_ref, sems, x_sems = refs[parts:]
    tiles = x.shape[0]
    devices = coded.shape[0]
    blocks = square.shape[0]
    step = math.gcd(STEP_TILES, tiles)

    def read(c):
        some = pl.ds(c * step, step)
        return pltpu.make_async_copy(x_hbm.at[some], x.at[some], x_sems.at[c])

    for c in range(tiles // step):
        read(c).start()
    labels, owner, row, sub = [ref[...] for ref in told_refs]
    own, sub_own = [jnp.broadcast_to(v.astype(jnp.float32), (tiles, tiles)) for v in (owner, sub)]
    other, sub_other = jnp.transpose(own), jnp.transpose(sub_own)
    index = [lax.broadcasted_iota(jnp.int32, (tiles, tiles), d) for d in (0, 1)]
    ahead = (sub_other < sub_own) | ((sub_other == sub_own) & (index[0] < index[1]))
    ahead = jnp.where(ahead & (other == own), 1.0, 0.0)
    rank_row[...] = jnp.sum(ahead, axis=0, keepdims=True).astype(jnp.int32)
    pltpu.sync_copy(rank_row, rank_ref)
    square[...] = jnp.zeros_like(square)

    def some_tiles(i, carry):
        pl.when(i % (step // QUAD) == 0)(lambda: read(i // (step // QUAD)).wait())
        for j in range(QUAD):
            t = i * QUAD + j
            some = x[t]
            root = some * lax.rsqrt(some)
            code = (root * CODE_TOP + 0.5).astype(jnp.int32) - CODE_SHIFT
            owner, rank = owner_ref[t], rank_ref[0, t]
            at = pl.ds(pl.multiple_of(rank * LANES, LANES), LANES)
            coded[owner, at, :] = code.astype(jnp.int16)
            square[row_ref[t]] += some * some
        return carry

    lax.fori_loop(0, tiles // QUAD, some_tiles, 0)

    copies = []
    for q in range(parts):
        rows, count = (cuts[q + 1] - cuts[q]) * LANES, devices // (1 if q else math.gcd(4, devices))
        for d in range(0, devices, count):
            from_ref = coded.at[pl.ds(d, count), pl.ds(cuts[q] * LANES, rows)]
            into = outs[q].at[pl.ds(d, count), pl.ds(0, rows)]
            copies.append(pltpu.make_async_copy(from_ref, into, sems.at[len(copies)]))
    for copy in copies:
        copy.start()
    sums[...] = jnp.zeros_like(sums)
    block_sums(square, sums, blocks)
    total = sums[...]
    level = (jnp.log2(jnp.maximum(total, 1e-30)) - LOG_MIDDLE) * LOG_STEPS
    level = jnp.where(total > 0.0, jnp.clip(level, -32700.0, 32700.0), -32768.0)
    level = (level + 32768.5).astype(jnp.int32) - 32768
    words[...] = jnp.zeros_like(words)
    words[:blocks, :] = level
    at = blocks
    for told in (labels, owner, row * TB_OWN + sub):
        words[at : at + told.shape[0], :] = told
        at += told.shape[0]
    notes[...] = jnp.broadcast_to(words[...].astype(jnp.int16)[None], notes.shape)
    into = outs[0].at[:, pl.ds((cuts[1] - cuts[0]) * LANES, notes.shape[1])]
    copies.append(pltpu.make_async_copy(notes, into, sems.at[len(copies)]))
    copies[-1].start()
    for copy in copies:
        copy.wait()


def pack(tile_values, owner, tile_row, told, devices, blocks, cuts):
    tiles = tile_values.shape[0]
    told = [x.reshape(-1, LANES) for x in told]
    noted = -(-(blocks + sum(x.shape[0] for x in told[:3])) // 16) * 16
    rows = [(high - low) * LANES for low, high in zip(cuts, cuts[1:])]
    rows[0] += noted
    return pl.pallas_call(
        functools.partial(pack_kernel, cuts),
        in_specs=[SMEM] * 2 + [VMEM] * 4 + [ANY],
        out_specs=[ANY] * len(rows),
        out_shape=[jax.ShapeDtypeStruct((devices, some, LANES), jnp.int16) for some in rows],
        scratch_shapes=[
            pltpu.VMEM(tile_values.shape, jnp.float32),
            pltpu.VMEM((devices, cuts[-1] * LANES, LANES), jnp.int16),
            pltpu.VMEM((blocks, LANES, LANES), jnp.float32),
            pltpu.VMEM((blocks, LANES), jnp.float32),
            pltpu.VMEM((noted, LANES), jnp.int32),
            pltpu.VMEM((devices, noted, LANES), jnp.int16),
            pltpu.VMEM((1, tiles), jnp.int32),
            pltpu.SMEM((1, tiles), jnp.int32),
            pltpu.SemaphoreType.DMA((len(rows) + 4,)),
            pltpu.SemaphoreType.DMA((tiles // math.gcd(STEP_TILES, tiles),)),
        ],
        compiler_params=params(),
        cost_estimate=pl.CostEstimate(
            flops=8 * tile_values.size,
            bytes_accessed=6 * tile_values.size,
            transcendentals=tile_values.size,
        ),
        name="pack",
    )(owner, tile_row, *told, tile_values)


def stage_kernel(q, bases, last, cached, fold_list_in, fold_bound_in, score_list_in,
                 mods_in, signed_in, x_hbm, *refs):
    base = bases[q]
    earlier, refs = refs[:q], refs[q:]
    before, sums_in, squares_in, *made_in = refs[:5] if q else (None,) * 5
    refs = refs[5:] if q else refs
    part, sums_out, refs = refs[0], refs[1], refs[2:]
    (squares_out, *made_out, fresh_out), refs = ((None,) * 4, refs) if last else (refs[:4], refs[4:])
    spread, x, hot, sums, narrow, tiles, products, scores, squares, mods, signed, *refs = refs
    fold_list, fold_bound, score_list, sems, sub_sems, tile_sems, small_sems = refs
    devices, width = x.shape[0], x.shape[1] // LANES
    none = products.shape[0] - 1
    needed = [pltpu.make_async_copy(x_hbm.at[:, pl.ds(0, width * LANES)], x, sems.at[0])]
    if q:
        needed.append(pltpu.make_async_copy(made_in[0], spread, sems.at[1]))
    for held, empty in ((mods, -1.0), (signed, 0.0)):
        held[none : none + 1, :] = jnp.full((1, LANES), empty, jnp.float32)
    pairs = [(fold_list_in, fold_list), (fold_bound_in, fold_bound), (score_list_in, score_list)]
    pairs += [(mods_in, mods.at[pl.ds(0, none)]), (signed_in, signed.at[pl.ds(0, none)])]
    pairs += [(before, scores), (squares_in, squares)] if q else []
    small = [pltpu.make_async_copy(*pair, small_sems.at[i]) for i, pair in enumerate(pairs)]
    for copy in small + needed:
        copy.start()
    for copy in small:
        copy.wait()
    parts = len(bases) - 1

    def bound(p, sub):
        return fold_bound[p * (TB_OWN + 1) + sub]

    def score_bound(sub):
        return sum(bound(p, sub) - bound(p, 0) for p in range(parts))

    def complete(arrived):
        def one(i, least):
            sub = TB_OWN - 1 - i
            waits = [bound(p, sub + 1) > bound(p, sub) for p in range(arrived, parts)]
            return jnp.where(functools.reduce(jnp.logical_or, waits), sub, least)

        return lax.fori_loop(0, TB_OWN, one, TB_OWN) if arrived < parts else TB_OWN

    begin, end = complete(q) if q else 0, complete(q + 1)

    def columns(sub):
        return (slice(None), pl.ds(pl.multiple_of(sub * 2 * LANES, 2 * LANES), 2 * LANES))

    def group(g):
        size = BLOCKS * 2 * LANES
        return (slice(None), pl.ds(pl.multiple_of(g * size, size), size))

    def sums_read(g):
        return pltpu.make_async_copy(sums_in.at[group(g)], sums.at[group(g)], sub_sems.at[0, g])

    def sums_write(g):
        return pltpu.make_async_copy(sums.at[group(g)], sums_out.at[group(g)], sub_sems.at[1, g])

    def each_sub(low, high, what):
        def one(sub, carry):
            what(sub)
            return carry

        lax.fori_loop(low, high, one, 0)

    if q:
        each_sub(begin // BLOCKS, TB_OWN // BLOCKS, lambda g: sums_read(g).start())
    else:
        scores[...] = jnp.zeros_like(scores)
        sums[...] = jnp.zeros_like(sums)
        squares[...] = jnp.zeros_like(squares)
    later = [pltpu.make_async_copy(made_in[1], hot, sems.at[3])] if q and cached else []

    def each_chunk(p, outside, write, sub, what):
        count = math.gcd(CHUNK, bases[p + 1] - bases[p])

        def one(c, carry):
            away, own = outside.at[pl.ds(c * count, count)], tiles.at[pl.ds(bases[p] + c * count, count)]
            some = (own, away) if write else (away, own)
            what(pltpu.make_async_copy(*some, tile_sems.at[0 if write else p, c]))
            return carry

        first, stop = bound(p, sub) - bases[p], bound(p, TB_OWN) - bases[p]
        lax.fori_loop(first // count, (stop + count - 1) // count, one, 0)

    def each_earlier(what):
        for copy in later:
            what(copy)
        for e, e_hbm in enumerate(earlier):
            each_chunk(e, e_hbm, False, begin, what)

    each_earlier(lambda copy: copy.start())
    products[...] = jnp.zeros_like(products)
    cluster = lax.broadcasted_iota(jnp.int32, (HALF, LANES), 0).astype(jnp.float32)
    cluster = cluster.astype(jnp.bfloat16).reshape(HALF // 16, 16, LANES)
    one, zero = jnp.ones((), jnp.bfloat16), jnp.zeros((), jnp.bfloat16)
    lane = lax.broadcasted_iota(jnp.int32, (LANES, LANES), 1)

    def column(ref, row):
        return jnp.transpose(jnp.broadcast_to(ref[pl.ds(row, 1), :], (LANES, LANES)))

    def one_hot(row):
        own = column(mods, row).astype(jnp.int32)
        some = [jnp.where(own == lane + g, 1.0, 0.0) for g in range(0, HALF, LANES)]
        return jnp.concatenate(some, axis=1).astype(jnp.bfloat16)

    batch = math.gcd(none + 1, 3)

    def build(c, carry):
        for j in range(batch):
            spread[c * batch + j] = column(signed, c * batch + j)
            if cached:
                hot[c * batch + j] = one_hot(c * batch + j)
        return carry

    if not q:
        lax.fori_loop(0, (none + 1) // batch, build, 0)
    for copy in needed:
        copy.wait()
    if q:
        each_sub(begin // BLOCKS, TB_OWN // BLOCKS, lambda g: sums_read(g).wait())

    def steps(start, end, work):
        wide = 2 * EIGHT
        count = (end - start + EIGHT - 1) >> WIDE_SHIFT

        def one(p, carry):
            work(start + wide * p, wide)
            return carry

        lax.fori_loop(0, count, one, 0)
        pl.when(start + wide * count < end)(lambda: work(start + wide * count, EIGHT))

    def some(entries, start, end, count):
        at = [start + j for j in range(count)]
        at = [(jnp.where(spot < end, spot, start), spot < end) for spot in at]
        return [(entries[spot], spot, held) for spot, held in at]

    def fold_sub(sub):
        start, end = bound(q, sub), bound(q, sub + 1)
        def fold_some(first, count):
            folded, picks = [], []
            for entry, spot, held in some(fold_list, first, end, count):
                row = entry >> ROW_SHIFT
                source, slot = (entry >> SOURCE_SHIFT) & SOURCE_MASK, entry & SLOT_MASK
                raw = x[source, pl.ds(pl.multiple_of(slot * LANES, LANES), LANES), :]
                root = raw.astype(jnp.int32).astype(jnp.float32) + float(CODE_SHIFT)
                scale = spread[row]
                square = root * root
                tile = square * jnp.abs(scale)
                lower = square * jnp.maximum(scale, 0.0)
                tiles[spot] = tile.astype(jnp.bfloat16)
                halves = [lower.astype(jnp.bfloat16), (tile - lower).astype(jnp.bfloat16)]
                folded.append(jnp.concatenate(halves, axis=1))
                own = jnp.broadcast_to(mods[pl.ds(jnp.where(held, row, none), 1), :], (16, LANES))
                own = jnp.where(cluster == own.astype(jnp.bfloat16)[None], one, zero)
                picks.append(own.reshape(HALF, LANES))
            pick = jnp.concatenate(picks, axis=1)
            sums[columns(sub)] += jnp.dot(
                pick, jnp.concatenate(folded, axis=0), preferred_element_type=jnp.float32
            )

        steps(start, end, fold_some)

    def fold_group(g):
        each_sub(jnp.maximum(begin, g * BLOCKS), (g + 1) * BLOCKS, fold_sub)
        sums_write(g).start()

    each_sub(begin // BLOCKS, TB_OWN // BLOCKS, fold_group)
    kept = []
    if not last:
        each_chunk(q, fresh_out, True, end, lambda copy: copy.start())
        kept.append(pltpu.make_async_copy(spread, made_out[0], sems.at[4]))
        kept.append(pltpu.make_async_copy(hot, made_out[1], sems.at[5]))
    for copy in kept:
        copy.start()
    each_earlier(lambda copy: copy.wait())

    def score_sub(sub):
        start, end = score_bound(sub), score_bound(sub + 1)
        own_sums = sums[columns(sub)]
        narrow[...] = own_sums.astype(jnp.bfloat16)
        squares[...] += own_sums * own_sums

        def score_some(first, count):
            listed = some(score_list, first, end, count)
            rows = [jnp.where(held, entry >> ROW_SHIFT, none) for entry, spot, held in listed]
            spots = [entry & PLACE_MASK for entry, spot, held in listed]
            hots = [hot[row] if cached else one_hot(row) for row in rows]
            chosen = jnp.dot(
                jnp.concatenate(hots, axis=0), narrow[...], preferred_element_type=jnp.float32
            )
            for j in range(count):
                both = chosen[j * LANES : (j + 1) * LANES]
                own = jnp.where(spread[rows[j]] < 0.0, both[:, LANES:], both[:, :LANES])
                products[rows[j]] += own * tiles[spots[j]].astype(jnp.float32)

        steps(start, end, score_some)

    each_sub(begin, end, score_sub)
    block_sums(products, scores, none)
    if last:
        own = none // devices
        square = [lane_sums(squares[:, h : h + LANES])[:1] for h in (0, LANES)]
        square = jnp.concatenate(square, axis=1)
        for d in range(devices):
            part[d, :, part.shape[2] - K :] = square
            for b in range(own):
                at = d * own + b
                part[d, :, b * LANES : (b + 1) * LANES] = scores[at : at + 1, :]
    else:
        part[...] = scores[...]
        squares_out[...] = squares[...]
    for copy in kept:
        copy.wait()
    if not last:
        each_chunk(q, fresh_out, True, end, lambda copy: copy.wait())
    each_sub(begin // BLOCKS, TB_OWN // BLOCKS, lambda g: sums_write(g).wait())


def stage(q, cuts, scalars, mods, signed, x, normed, totals):
    devices = x.shape[0]
    last = q == len(cuts) - 2
    blocks = mods.shape[0]
    cached = blocks <= CACHED_BLOCKS
    width = cuts[q + 1] - cuts[q]
    home = blocks // devices * LANES
    wide = jax.ShapeDtypeStruct((HALF, TB_OWN * 2 * LANES), jnp.float32)
    square = jax.ShapeDtypeStruct((HALF, 2 * LANES), jnp.float32)
    if last:
        out_shape = [jax.ShapeDtypeStruct((devices, 1, home + K), jnp.float32), wide]
    else:
        out_shape = [
            jax.ShapeDtypeStruct((blocks, LANES), jnp.float32),
            wide,
            square,
            jax.ShapeDtypeStruct((blocks + 1, LANES, LANES), jnp.float32),
            jax.ShapeDtypeStruct((blocks + 1 if cached else 1, LANES, HALF), jnp.bfloat16),
            jax.ShapeDtypeStruct((devices * width, LANES, LANES), jnp.bfloat16),
        ]
    slots = devices * cuts[-1]
    sizes = [devices * (high - low) for low, high in zip(cuts, cuts[1:])]
    chunks = max(size // math.gcd(CHUNK, size) for size in sizes)
    operands = [*scalars, mods, signed, x, *normed, *totals]
    return pl.pallas_call(
        functools.partial(stage_kernel, q, [devices * cut for cut in cuts], last, cached),
        in_specs=[ANY] * len(operands),
        out_specs=[VMEM, ANY, VMEM, ANY, ANY, ANY][: len(out_shape)],
        out_shape=out_shape,
        input_output_aliases={len(operands) - len(totals) + 1: 1} if q else {},
        scratch_shapes=[
            pltpu.VMEM((blocks + 1, LANES, LANES), jnp.float32),
            pltpu.VMEM((devices, width * LANES, LANES), jnp.int16),
            pltpu.VMEM((blocks + 1 if cached else 1, LANES, HALF), jnp.bfloat16),
            pltpu.VMEM(wide.shape, jnp.float32),
            pltpu.VMEM(square.shape, jnp.bfloat16),
            pltpu.VMEM((slots, LANES, LANES), jnp.bfloat16),
            pltpu.VMEM((blocks + 1, LANES, LANES), jnp.float32),
            pltpu.VMEM((blocks, LANES), jnp.float32),
            pltpu.VMEM(square.shape, jnp.float32),
            pltpu.VMEM((blocks + 1, LANES), jnp.float32),
            pltpu.VMEM((blocks + 1, LANES), jnp.float32),
            *[pltpu.SMEM(some.shape, jnp.int32) for some in scalars],
            pltpu.SemaphoreType.DMA((6,)),
            pltpu.SemaphoreType.DMA((2, TB_OWN // BLOCKS)),
            pltpu.SemaphoreType.DMA((max(q, 1), chunks)),
            pltpu.SemaphoreType.DMA((7,)),
        ],
        compiler_params=params(),
        cost_estimate=pl.CostEstimate(
            flops=devices * width * LANES * LANES * K, bytes_accessed=wide.size, transcendentals=0
        ),
        name="stage",
    )(*operands)


def close_kernel(root, groups, labels_hbm, got_hbm, sums_hbm, out_hbm, similarity_hbm, labels_ref,
                 got_ref, similarity, sums, out, sems, small_sems):
    width = TB_OWN // groups
    reads, writes = [], []
    small = [
        pltpu.make_async_copy(got_hbm, got_ref, small_sems.at[0]),
        pltpu.make_async_copy(labels_hbm, labels_ref, small_sems.at[1]),
    ]
    for copy in small:
        copy.start()
    for g in range(groups):
        some = (slice(None), pl.ds(g * width * 2 * LANES, width * 2 * LANES))
        reads.append(pltpu.make_async_copy(sums_hbm.at[some], sums.at[some], sems.at[0, g]))
        some = (slice(None), pl.ds(g * width * LANES, width * LANES))
        writes.append(pltpu.make_async_copy(out.at[some], out_hbm.at[some], sems.at[1, g]))
        reads[g].start()
    for copy in small:
        copy.wait()
    total = jnp.sum(got_ref[...], axis=0)
    home = total.shape[1] - K
    own = lax.rsqrt(total[:, home:] + EPSILON)
    columns = [
        jnp.transpose(jnp.broadcast_to(own[:, k : k + LANES], (LANES, LANES)))
        for k in range(0, K, LANES)
    ]
    cluster = lax.broadcasted_iota(jnp.int32, (LANES, LANES), 0)
    for b in range(home // LANES):
        found = jnp.zeros((LANES, LANES), jnp.float32)
        for i, column in enumerate(columns):
            found += jnp.where(cluster + i * LANES == labels_ref[b : b + 1, :], column, 0.0)
        found = jnp.sum(found, axis=0, keepdims=True)
        similarity[b : b + 1, :] = total[:, b * LANES : (b + 1) * LANES] * found
    writes.append(pltpu.make_async_copy(similarity, similarity_hbm, small_sems.at[2]))
    writes[-1].start()
    for g in range(groups):
        reads[g].wait()

        def one_sub(sub, carry):
            to = pl.ds(pl.multiple_of(sub * LANES, LANES), LANES)
            for i, column in enumerate(columns):
                half, row = divmod(i * LANES, HALF)
                at = pl.ds(pl.multiple_of((2 * sub + half) * LANES, LANES), LANES)
                done = sums[row : row + LANES, at] * column * root
                out[i * LANES : (i + 1) * LANES, to] = done.astype(jnp.bfloat16)
            return carry

        lax.fori_loop(g * width, (g + 1) * width, one_sub, 0)
        writes[g].start()
    for write in writes:
        write.wait()


def close(labels, got, sums, vocab_size):
    groups = 4
    labels = labels.reshape(-1, LANES)
    wide = jax.ShapeDtypeStruct((K, TB_OWN * LANES), jnp.bfloat16)
    centroids, similarity = pl.pallas_call(
        functools.partial(close_kernel, math.sqrt(vocab_size), groups),
        in_specs=[ANY] * 3,
        out_specs=[ANY] * 2,
        out_shape=[wide, jax.ShapeDtypeStruct(labels.shape, jnp.float32)],
        scratch_shapes=[
            pltpu.VMEM(labels.shape, jnp.int32),
            pltpu.VMEM(got.shape, jnp.float32),
            pltpu.VMEM(labels.shape, jnp.float32),
            pltpu.VMEM(sums.shape, jnp.float32),
            pltpu.VMEM(wide.shape, jnp.bfloat16),
            pltpu.SemaphoreType.DMA((2, groups)),
            pltpu.SemaphoreType.DMA((3,)),
        ],
        compiler_params=params(),
        cost_estimate=pl.CostEstimate(
            flops=2 * sums.size, bytes_accessed=6 * sums.size, transcendentals=0
        ),
        name="close",
    )(labels, got, sums)
    return centroids, similarity.reshape(-1)


def exchange(x):
    return lax.all_to_all(x, "dp", split_axis=0, concat_axis=0, tiled=True)


def after(value, *others):
    return lax.optimization_barrier((value, *others))[0]


def sorted_slots(key, top, entries):
    slots = jnp.arange(key.shape[0], dtype=jnp.int32)
    ahead = (key[None, :] < key[:, None]) | (
        (key[None, :] == key[:, None]) & (slots[None, :] < slots[:, None])
    )
    position = jnp.sum(ahead.astype(jnp.int32), axis=1)
    here = position[None, :] == slots[:, None]
    listed = jnp.sum(jnp.where(here, entries[None, :], 0), axis=1)
    levels = jnp.arange(-(-(top + 1) // LANES) * LANES, dtype=jnp.int32)
    bounds = jnp.sum((key[None, :] < levels[:, None]).astype(jnp.int32), axis=1)
    return listed, bounds, position


def ranks(group, sub):
    index = jnp.arange(sub.shape[-1], dtype=jnp.int32)
    before = (sub[..., None, :] < sub[..., :, None]) | (
        (sub[..., None, :] == sub[..., :, None]) & (index[None, :] < index[:, None])
    )
    same = group[..., None, :] == group[..., :, None]
    return jnp.sum((before & same).astype(jnp.int32), axis=-1)


def shards(tile_values, tile_row, tile_owner, tile_sub, labels):
    devices = lax.axis_size("dp")
    tiles = tile_values.shape[0]
    home = labels.shape[0]
    blocks = home // LANES * devices
    cap = max(2, 2 * tiles // devices)
    cuts = tuple(sorted({int(cap * share) for share in PARTS})) if cap >= 8 else (0, cap)
    parts = len(cuts) - 1
    here = lax.axis_index("dp").astype(jnp.int32)
    owner = tile_owner[:, 0]

    told = (labels, owner, tile_row, tile_sub)
    outgoing = pack(tile_values, owner, tile_row, told, devices, blocks, cuts)
    incoming = [exchange(outgoing[0])]
    heard = incoming[0][:, (cuts[1] - cuts[0]) * LANES :].astype(jnp.int32)
    level = heard[:, :blocks]
    partial_sq = jnp.exp2(level.astype(jnp.float32) * (1.0 / LOG_STEPS) + LOG_MIDDLE)
    row_sq = jnp.sum(jnp.where(level > -32768, partial_sq, 0.0), axis=0)
    all_described = heard[:, blocks:].reshape(devices, -1)
    all_labels = all_described[:, :home].reshape(blocks, LANES)
    mine = all_described[:, home : home + tiles] == here
    code = all_described[:, home + tiles : home + 2 * tiles]
    rank = ranks(mine.astype(jnp.int32), code % TB_OWN)
    chosen = mine[:, None, :] & (rank[:, None, :] == jnp.arange(cap)[None, :, None])
    meta = jnp.sum(jnp.where(chosen, code[:, None, :] + 1, 0), axis=2).reshape(-1) - 1
    sub = jnp.where(meta < 0, TB_OWN, meta % TB_OWN)
    slot_rank = np.arange(devices * cap) % cap
    slot_part = np.searchsorted(np.array(cuts), slot_rank, side="right") - 1
    low = np.array(cuts)[slot_part]
    fold_key = jnp.asarray(slot_part * (TB_OWN + 1), jnp.int32) + sub
    row = (meta // TB_OWN) << ROW_SHIFT
    from_slot = (np.arange(devices * cap) // cap << SOURCE_SHIFT) + slot_rank - low
    fold_list, fold_bounds, position = sorted_slots(
        fold_key, parts * (TB_OWN + 1), row + jnp.asarray(from_slot, jnp.int32)
    )
    score_list, *_ = sorted_slots(sub, TB_OWN, row + position)
    scalars = [fold_list, fold_bounds, score_list]

    scale = lax.rsqrt(row_sq + EPSILON) * (1.0 / CODE_TOP**2)
    signed = jnp.where(all_labels < HALF, scale, -scale)
    mods = (all_labels % HALF).astype(jnp.float32)
    totals, normed = (), []
    beside = (*scalars, mods, signed)
    for q in range(parts):
        if q + 1 < parts:
            ahead = (incoming[q], *beside) if q else (incoming[q],)
            incoming.append(exchange(after(outgoing[q + 1], *ahead)))
        partial, sums, *more = stage(
            q, cuts, scalars, mods, signed, incoming[q], normed, totals
        )
        beside = (partial, sums)
        totals, normed = (partial, sums, *more[:3]), normed + more[3:]
    return close(labels, exchange(partial), sums, TB_OWN * LANES * devices)


def solution(mesh):
    return jax.shard_map(
        shards,
        mesh=mesh,
        in_specs=(
            P(("groups", "dp"), None, None),
            P(("groups", "dp")),
            P(("groups", "dp"), None),
            P(("groups", "dp")),
            P(("groups", "dp")),
        ),
        out_specs=(P("groups", "dp"), P(("groups", "dp"))),
        check_vma=False,
    )
```

```python
import functools
import math

import jax
import jax.numpy as jnp
import numpy as np
from jax import lax
from jax.experimental import pallas as pl
from jax.experimental.pallas import tpu as pltpu
from jax.sharding import PartitionSpec as P

K = 512
HALF = K // 2
TB_OWN = 16
LANES = 128
EPSILON = 1e-06
CODE_TOP = 65535.0
CODE_SHIFT = 32768
VMEM_BYTES = 60 * 1024 * 1024
STEP_TILES = 16
PARTS = (0.0, 13 / 16, 1.0)
LOG_STEPS = 1800.0
LOG_MIDDLE = -3.0
CACHED_BLOCKS = 64
QUAD = 4
EIGHT = 8
WIDE_SHIFT = 4
CHUNK = 16
BLOCKS = 4
ROW_SHIFT, SOURCE_SHIFT = 16, 8
PLACE_MASK, SOURCE_MASK, SLOT_MASK = 0xFFFF, 0xFF, 0xFF
BATCH = 32
NT = (((1,), (1,)), ((), ()))
SMEM = pl.BlockSpec(memory_space=pltpu.SMEM)
VMEM = pl.BlockSpec(memory_space=pltpu.VMEM)
ANY = pl.BlockSpec(memory_space=pl.ANY)


def lane_sums(values):
    ones = jnp.ones((8, 2 * LANES), jnp.bfloat16)
    high = values.astype(jnp.bfloat16)
    low = (values - high.astype(jnp.float32)).astype(jnp.bfloat16)
    both = jnp.concatenate([high, low], axis=1)
    return lax.dot_general(ones, both, NT, preferred_element_type=jnp.float32)


def block_sums(square, out_ref, count):
    batch = math.gcd(BATCH, count)

    def one_batch(c, carry):
        some = square[pl.ds(c * batch, batch)].reshape((batch * LANES, LANES))
        sums = lane_sums(some)
        for j in range(batch):
            out_ref[pl.ds(c * batch + j, 1), :] += sums[:1, j * LANES : (j + 1) * LANES]
        return carry

    lax.fori_loop(0, count // batch, one_batch, 0)


def params():
    return pltpu.CompilerParams(vmem_limit_bytes=VMEM_BYTES)


def pack_kernel(cuts, owner_ref, row_ref, *refs):
    parts = len(cuts) - 1
    (*told_refs, x_hbm), refs = refs[:5], refs[5:]
    outs = refs[:parts]
    x, coded, square, sums, words, notes, rank_row, rank_ref, sems, x_sems = refs[parts:]
    tiles = x.shape[0]
    devices = coded.shape[0]
    blocks = square.shape[0]
    step = math.gcd(STEP_TILES, tiles)

    def read(c):
        some = pl.ds(c * step, step)
        return pltpu.make_async_copy(x_hbm.at[some], x.at[some], x_sems.at[c])

    for c in range(tiles // step):
        read(c).start()
    labels, owner, row, sub = [ref[...] for ref in told_refs]
    own, sub_own = [jnp.broadcast_to(v.astype(jnp.float32), (tiles, tiles)) for v in (owner, sub)]
    other, sub_other = jnp.transpose(own), jnp.transpose(sub_own)
    index = [lax.broadcasted_iota(jnp.int32, (tiles, tiles), d) for d in (0, 1)]
    ahead = (sub_other < sub_own) | ((sub_other == sub_own) & (index[0] < index[1]))
    ahead = jnp.where(ahead & (other == own), 1.0, 0.0)
    rank_row[...] = jnp.sum(ahead, axis=0, keepdims=True).astype(jnp.int32)
    pltpu.sync_copy(rank_row, rank_ref)
    square[...] = jnp.zeros_like(square)

    def some_tiles(i, carry):
        pl.when(i % (step // QUAD) == 0)(lambda: read(i // (step // QUAD)).wait())
        for j in range(QUAD):
            t = i * QUAD + j
            some = x[t]
            root = some * lax.rsqrt(some)
            code = (root * CODE_TOP + 0.5).astype(jnp.int32) - CODE_SHIFT
            owner, rank = owner_ref[t], rank_ref[0, t]
            at = pl.ds(pl.multiple_of(rank * LANES, LANES), LANES)
            coded[owner, at, :] = code.astype(jnp.int16)
            square[row_ref[t]] += some * some
        return carry

    lax.fori_loop(0, tiles // QUAD, some_tiles, 0)

    copies = []
    for q in range(parts):
        rows, count = (cuts[q + 1] - cuts[q]) * LANES, devices // (1 if q else math.gcd(4, devices))
        for d in range(0, devices, count):
            from_ref = coded.at[pl.ds(d, count), pl.ds(cuts[q] * LANES, rows)]
            into = outs[q].at[pl.ds(d, count), pl.ds(0, rows)]
            copies.append(pltpu.make_async_copy(from_ref, into, sems.at[len(copies)]))
    for copy in copies:
        copy.start()
    sums[...] = jnp.zeros_like(sums)
    block_sums(square, sums, blocks)
    total = sums[...]
    level = (jnp.log2(jnp.maximum(total, 1e-30)) - LOG_MIDDLE) * LOG_STEPS
    level = jnp.where(total > 0.0, jnp.clip(level, -32700.0, 32700.0), -32768.0)
    level = (level + 32768.5).astype(jnp.int32) - 32768
    words[...] = jnp.zeros_like(words)
    words[:blocks, :] = level
    at = blocks
    for told in (labels, owner, row * TB_OWN + sub):
        words[at : at + told.shape[0], :] = told
        at += told.shape[0]
    notes[...] = jnp.broadcast_to(words[...].astype(jnp.int16)[None], notes.shape)
    into = outs[0].at[:, pl.ds((cuts[1] - cuts[0]) * LANES, notes.shape[1])]
    copies.append(pltpu.make_async_copy(notes, into, sems.at[len(copies)]))
    copies[-1].start()
    for copy in copies:
        copy.wait()


def pack(tile_values, owner, tile_row, told, devices, blocks, cuts):
    tiles = tile_values.shape[0]
    told = [x.reshape(-1, LANES) for x in told]
    noted = -(-(blocks + sum(x.shape[0] for x in told[:3])) // 16) * 16
    rows = [(high - low) * LANES for low, high in zip(cuts, cuts[1:])]
    rows[0] += noted
    return pl.pallas_call(
        functools.partial(pack_kernel, cuts),
        in_specs=[SMEM] * 2 + [VMEM] * 4 + [ANY],
        out_specs=[ANY] * len(rows),
        out_shape=[jax.ShapeDtypeStruct((devices, some, LANES), jnp.int16) for some in rows],
        scratch_shapes=[
            pltpu.VMEM(tile_values.shape, jnp.float32),
            pltpu.VMEM((devices, cuts[-1] * LANES, LANES), jnp.int16),
            pltpu.VMEM((blocks, LANES, LANES), jnp.float32),
            pltpu.VMEM((blocks, LANES), jnp.float32),
            pltpu.VMEM((noted, LANES), jnp.int32),
            pltpu.VMEM((devices, noted, LANES), jnp.int16),
            pltpu.VMEM((1, tiles), jnp.int32),
            pltpu.SMEM((1, tiles), jnp.int32),
            pltpu.SemaphoreType.DMA((len(rows) + 4,)),
            pltpu.SemaphoreType.DMA((tiles // math.gcd(STEP_TILES, tiles),)),
        ],
        compiler_params=params(),
        cost_estimate=pl.CostEstimate(
            flops=8 * tile_values.size,
            bytes_accessed=6 * tile_values.size,
            transcendentals=tile_values.size,
        ),
        name="pack",
    )(owner, tile_row, *told, tile_values)


def stage_kernel(q, bases, last, cached, fold_list_in, fold_bound_in, score_list_in,
                 mods_in, signed_in, x_hbm, *refs):
    base = bases[q]
    earlier, refs = refs[:q], refs[q:]
    before, sums_in, squares_in, *made_in = refs[:5] if q else (None,) * 5
    refs = refs[5:] if q else refs
    part, sums_out, refs = refs[0], refs[1], refs[2:]
    (squares_out, *made_out, fresh_out), refs = ((None,) * 4, refs) if last else (refs[:4], refs[4:])
    spread, x, hot, sums, narrow, tiles, products, scores, squares, mods, signed, *refs = refs
    fold_list, fold_bound, score_list, sems, sub_sems, tile_sems, small_sems = refs
    devices, width = x.shape[0], x.shape[1] // LANES
    none = products.shape[0] - 1
    needed = [pltpu.make_async_copy(x_hbm.at[:, pl.ds(0, width * LANES)], x, sems.at[0])]
    if q:
        needed.append(pltpu.make_async_copy(made_in[0], spread, sems.at[1]))
    for held, empty in ((mods, -1.0), (signed, 0.0)):
        held[none : none + 1, :] = jnp.full((1, LANES), empty, jnp.float32)
    pairs = [(fold_list_in, fold_list), (fold_bound_in, fold_bound), (score_list_in, score_list)]
    pairs += [(mods_in, mods.at[pl.ds(0, none)]), (signed_in, signed.at[pl.ds(0, none)])]
    pairs += [(before, scores), (squares_in, squares)] if q else []
    small = [pltpu.make_async_copy(*pair, small_sems.at[i]) for i, pair in enumerate(pairs)]
    for copy in small + needed:
        copy.start()
    for copy in small:
        copy.wait()
    parts = len(bases) - 1

    def bound(p, sub):
        return fold_bound[p * (TB_OWN + 1) + sub]

    def score_bound(sub):
        return sum(bound(p, sub) - bound(p, 0) for p in range(parts))

    def complete(arrived):
        def one(i, least):
            sub = TB_OWN - 1 - i
            waits = [bound(p, sub + 1) > bound(p, sub) for p in range(arrived, parts)]
            return jnp.where(functools.reduce(jnp.logical_or, waits), sub, least)

        return lax.fori_loop(0, TB_OWN, one, TB_OWN) if arrived < parts else TB_OWN

    begin, end = complete(q) if q else 0, complete(q + 1)

    def columns(sub):
        return (slice(None), pl.ds(pl.multiple_of(sub * 2 * LANES, 2 * LANES), 2 * LANES))

    def group(g):
        size = BLOCKS * 2 * LANES
        return (slice(None), pl.ds(pl.multiple_of(g * size, size), size))

    def sums_read(g):
        return pltpu.make_async_copy(sums_in.at[group(g)], sums.at[group(g)], sub_sems.at[0, g])

    def sums_write(g):
        return pltpu.make_async_copy(sums.at[group(g)], sums_out.at[group(g)], sub_sems.at[1, g])

    def each_sub(low, high, what):
        def one(sub, carry):
            what(sub)
            return carry

        lax.fori_loop(low, high, one, 0)

    if q:
        each_sub(begin // BLOCKS, TB_OWN // BLOCKS, lambda g: sums_read(g).start())
    else:
        scores[...] = jnp.zeros_like(scores)
        sums[...] = jnp.zeros_like(sums)
        squares[...] = jnp.zeros_like(squares)
    later = [pltpu.make_async_copy(made_in[1], hot, sems.at[3])] if q and cached else []

    def each_chunk(p, outside, write, sub, what):
        count = math.gcd(CHUNK, bases[p + 1] - bases[p])

        def one(c, carry):
            away, own = outside.at[pl.ds(c * count, count)], tiles.at[pl.ds(bases[p] + c * count, count)]
            some = (own, away) if write else (away, own)
            what(pltpu.make_async_copy(*some, tile_sems.at[0 if write else p, c]))
            return carry

        first, stop = bound(p, sub) - bases[p], bound(p, TB_OWN) - bases[p]
        lax.fori_loop(first // count, (stop + count - 1) // count, one, 0)

    def each_earlier(what):
        for copy in later:
            what(copy)
        for e, e_hbm in enumerate(earlier):
            each_chunk(e, e_hbm, False, begin, what)

    each_earlier(lambda copy: copy.start())
    products[...] = jnp.zeros_like(products)
    cluster = lax.broadcasted_iota(jnp.int32, (HALF, LANES), 0).astype(jnp.float32)
    cluster = cluster.astype(jnp.bfloat16).reshape(HALF // 16, 16, LANES)
    one, zero = jnp.ones((), jnp.bfloat16), jnp.zeros((), jnp.bfloat16)
    lane = lax.broadcasted_iota(jnp.int32, (LANES, LANES), 1)

    def column(ref, row):
        return jnp.transpose(jnp.broadcast_to(ref[pl.ds(row, 1), :], (LANES, LANES)))

    def one_hot(row):
        own = column(mods, row).astype(jnp.int32)
        some = [jnp.where(own == lane + g, 1.0, 0.0) for g in range(0, HALF, LANES)]
        return jnp.concatenate(some, axis=1).astype(jnp.bfloat16)

    batch = math.gcd(none + 1, 3)

    def build(c, carry):
        for j in range(batch):
            spread[c * batch + j] = column(signed, c * batch + j)
            if cached:
                hot[c * batch + j] = one_hot(c * batch + j)
        return carry

    if not q:
        lax.fori_loop(0, (none + 1) // batch, build, 0)
    for copy in needed:
        copy.wait()
    if q:
        each_sub(begin // BLOCKS, TB_OWN // BLOCKS, lambda g: sums_read(g).wait())

    def steps(start, end, work):
        wide = 2 * EIGHT
        count = (end - start + EIGHT - 1) >> WIDE_SHIFT

        def one(p, carry):
            work(start + wide * p, wide)
            return carry

        lax.fori_loop(0, count, one, 0)
        pl.when(start + wide * count < end)(lambda: work(start + wide * count, EIGHT))

    def some(entries, start, end, count):
        at = [start + j for j in range(count)]
        at = [(jnp.where(spot < end, spot, start), spot < end) for spot in at]
        return [(entries[spot], spot, held) for spot, held in at]

    def fold_sub(sub):
        start, end = bound(q, sub), bound(q, sub + 1)
        def fold_some(first, count):
            folded, picks = [], []
            for entry, spot, held in some(fold_list, first, end, count):
                row = entry >> ROW_SHIFT
                source, slot = (entry >> SOURCE_SHIFT) & SOURCE_MASK, entry & SLOT_MASK
                raw = x[source, pl.ds(pl.multiple_of(slot * LANES, LANES), LANES), :]
                root = raw.astype(jnp.int32).astype(jnp.float32) + float(CODE_SHIFT)
                scale = spread[row]
                square = root * root
                tile = square * jnp.abs(scale)
                lower = square * jnp.maximum(scale, 0.0)
                tiles[spot] = tile.astype(jnp.bfloat16)
                halves = [lower.astype(jnp.bfloat16), (tile - lower).astype(jnp.bfloat16)]
                folded.append(jnp.concatenate(halves, axis=1))
                own = jnp.broadcast_to(mods[pl.ds(jnp.where(held, row, none), 1), :], (16, LANES))
                own = jnp.where(cluster == own.astype(jnp.bfloat16)[None], one, zero)
                picks.append(own.reshape(HALF, LANES))
            pick = jnp.concatenate(picks, axis=1)
            sums[columns(sub)] += jnp.dot(
                pick, jnp.concatenate(folded, axis=0), preferred_element_type=jnp.float32
            )

        steps(start, end, fold_some)

    def fold_group(g):
        each_sub(jnp.maximum(begin, g * BLOCKS), (g + 1) * BLOCKS, fold_sub)
        sums_write(g).start()

    each_sub(begin // BLOCKS, TB_OWN // BLOCKS, fold_group)
    kept = []
    if not last:
        each_chunk(q, fresh_out, True, end, lambda copy: copy.start())
        kept.append(pltpu.make_async_copy(spread, made_out[0], sems.at[4]))
        kept.append(pltpu.make_async_copy(hot, made_out[1], sems.at[5]))
    for copy in kept:
        copy.start()
    each_earlier(lambda copy: copy.wait())

    def score_sub(sub):
        start, end = score_bound(sub), score_bound(sub + 1)
        own_sums = sums[columns(sub)]
        narrow[...] = own_sums.astype(jnp.bfloat16)
        squares[...] += own_sums * own_sums

        def score_some(first, count):
            listed = some(score_list, first, end, count)
            rows = [jnp.where(held, entry >> ROW_SHIFT, none) for entry, spot, held in listed]
            spots = [entry & PLACE_MASK for entry, spot, held in listed]
            hots = [hot[row] if cached else one_hot(row) for row in rows]
            chosen = jnp.dot(
                jnp.concatenate(hots, axis=0), narrow[...], preferred_element_type=jnp.float32
            )
            for j in range(count):
                both = chosen[j * LANES : (j + 1) * LANES]
                own = jnp.where(spread[rows[j]] < 0.0, both[:, LANES:], both[:, :LANES])
                products[rows[j]] += own * tiles[spots[j]].astype(jnp.float32)

        steps(start, end, score_some)

    each_sub(begin, end, score_sub)
    block_sums(products, scores, none)
    if last:
        own = none // devices
        square = [lane_sums(squares[:, h : h + LANES])[:1] for h in (0, LANES)]
        square = jnp.concatenate(square, axis=1)
        for d in range(devices):
            part[d, :, part.shape[2] - K :] = square
            for b in range(own):
                at = d * own + b
                part[d, :, b * LANES : (b + 1) * LANES] = scores[at : at + 1, :]
    else:
        part[...] = scores[...]
        squares_out[...] = squares[...]
    for copy in kept:
        copy.wait()
    if not last:
        each_chunk(q, fresh_out, True, end, lambda copy: copy.wait())
    each_sub(begin // BLOCKS, TB_OWN // BLOCKS, lambda g: sums_write(g).wait())


def stage(q, cuts, scalars, mods, signed, x, normed, totals):
    devices = x.shape[0]
    last = q == len(cuts) - 2
    blocks = mods.shape[0]
    cached = blocks <= CACHED_BLOCKS
    width = cuts[q + 1] - cuts[q]
    home = blocks // devices * LANES
    wide = jax.ShapeDtypeStruct((HALF, TB_OWN * 2 * LANES), jnp.float32)
    square = jax.ShapeDtypeStruct((HALF, 2 * LANES), jnp.float32)
    if last:
        out_shape = [jax.ShapeDtypeStruct((devices, 1, home + K), jnp.float32), wide]
    else:
        out_shape = [
            jax.ShapeDtypeStruct((blocks, LANES), jnp.float32),
            wide,
            square,
            jax.ShapeDtypeStruct((blocks + 1, LANES, LANES), jnp.float32),
            jax.ShapeDtypeStruct((blocks + 1 if cached else 1, LANES, HALF), jnp.bfloat16),
            jax.ShapeDtypeStruct((devices * width, LANES, LANES), jnp.bfloat16),
        ]
    slots = devices * cuts[-1]
    sizes = [devices * (high - low) for low, high in zip(cuts, cuts[1:])]
    chunks = max(size // math.gcd(CHUNK, size) for size in sizes)
    operands = [*scalars, mods, signed, x, *normed, *totals]
    return pl.pallas_call(
        functools.partial(stage_kernel, q, [devices * cut for cut in cuts], last, cached),
        in_specs=[ANY] * len(operands),
        out_specs=[VMEM, ANY, VMEM, ANY, ANY, ANY][: len(out_shape)],
        out_shape=out_shape,
        input_output_aliases={len(operands) - len(totals) + 1: 1} if q else {},
        scratch_shapes=[
            pltpu.VMEM((blocks + 1, LANES, LANES), jnp.float32),
            pltpu.VMEM((devices, width * LANES, LANES), jnp.int16),
            pltpu.VMEM((blocks + 1 if cached else 1, LANES, HALF), jnp.bfloat16),
            pltpu.VMEM(wide.shape, jnp.float32),
            pltpu.VMEM(square.shape, jnp.bfloat16),
            pltpu.VMEM((slots, LANES, LANES), jnp.bfloat16),
            pltpu.VMEM((blocks + 1, LANES, LANES), jnp.float32),
            pltpu.VMEM((blocks, LANES), jnp.float32),
            pltpu.VMEM(square.shape, jnp.float32),
            pltpu.VMEM((blocks + 1, LANES), jnp.float32),
            pltpu.VMEM((blocks + 1, LANES), jnp.float32),
            *[pltpu.SMEM(some.shape, jnp.int32) for some in scalars],
            pltpu.SemaphoreType.DMA((6,)),
            pltpu.SemaphoreType.DMA((2, TB_OWN // BLOCKS)),
            pltpu.SemaphoreType.DMA((max(q, 1), chunks)),
            pltpu.SemaphoreType.DMA((7,)),
        ],
        compiler_params=params(),
        cost_estimate=pl.CostEstimate(
            flops=devices * width * LANES * LANES * K, bytes_accessed=wide.size, transcendentals=0
        ),
        name="stage",
    )(*operands)


def close_kernel(root, groups, labels_hbm, got_hbm, sums_hbm, out_hbm, similarity_hbm, labels_ref,
                 got_ref, similarity, sums, out, sems, small_sems):
    width = TB_OWN // groups
    reads, writes = [], []
    small = [
        pltpu.make_async_copy(got_hbm, got_ref, small_sems.at[0]),
        pltpu.make_async_copy(labels_hbm, labels_ref, small_sems.at[1]),
    ]
    for copy in small:
        copy.start()
    for g in range(groups):
        some = (slice(None), pl.ds(g * width * 2 * LANES, width * 2 * LANES))
        reads.append(pltpu.make_async_copy(sums_hbm.at[some], sums.at[some], sems.at[0, g]))
        some = (slice(None), pl.ds(g * width * LANES, width * LANES))
        writes.append(pltpu.make_async_copy(out.at[some], out_hbm.at[some], sems.at[1, g]))
        reads[g].start()
    for copy in small:
        copy.wait()
    total = jnp.sum(got_ref[...], axis=0)
    home = total.shape[1] - K
    own = lax.rsqrt(total[:, home:] + EPSILON)
    columns = [
        jnp.transpose(jnp.broadcast_to(own[:, k : k + LANES], (LANES, LANES)))
        for k in range(0, K, LANES)
    ]
    cluster = lax.broadcasted_iota(jnp.int32, (LANES, LANES), 0)
    for b in range(home // LANES):
        found = jnp.zeros((LANES, LANES), jnp.float32)
        for i, column in enumerate(columns):
            found += jnp.where(cluster + i * LANES == labels_ref[b : b + 1, :], column, 0.0)
        found = jnp.sum(found, axis=0, keepdims=True)
        similarity[b : b + 1, :] = total[:, b * LANES : (b + 1) * LANES] * found
    writes.append(pltpu.make_async_copy(similarity, similarity_hbm, small_sems.at[2]))
    writes[-1].start()
    for g in range(groups):
        reads[g].wait()

        def one_sub(sub, carry):
            to = pl.ds(pl.multiple_of(sub * LANES, LANES), LANES)
            for i, column in enumerate(columns):
                half, row = divmod(i * LANES, HALF)
                at = pl.ds(pl.multiple_of((2 * sub + half) * LANES, LANES), LANES)
                done = sums[row : row + LANES, at] * column * root
                out[i * LANES : (i + 1) * LANES, to] = done.astype(jnp.bfloat16)
            return carry

        lax.fori_loop(g * width, (g + 1) * width, one_sub, 0)
        writes[g].start()
    for write in writes:
        write.wait()


def close(labels, got, sums, vocab_size):
    groups = 4
    labels = labels.reshape(-1, LANES)
    wide = jax.ShapeDtypeStruct((K, TB_OWN * LANES), jnp.bfloat16)
    centroids, similarity = pl.pallas_call(
        functools.partial(close_kernel, math.sqrt(vocab_size), groups),
        in_specs=[ANY] * 3,
        out_specs=[ANY] * 2,
        out_shape=[wide, jax.ShapeDtypeStruct(labels.shape, jnp.float32)],
        scratch_shapes=[
            pltpu.VMEM(labels.shape, jnp.int32),
            pltpu.VMEM(got.shape, jnp.float32),
            pltpu.VMEM(labels.shape, jnp.float32),
            pltpu.VMEM(sums.shape, jnp.float32),
            pltpu.VMEM(wide.shape, jnp.bfloat16),
            pltpu.SemaphoreType.DMA((2, groups)),
            pltpu.SemaphoreType.DMA((3,)),
        ],
        compiler_params=params(),
        cost_estimate=pl.CostEstimate(
            flops=2 * sums.size, bytes_accessed=6 * sums.size, transcendentals=0
        ),
        name="close",
    )(labels, got, sums)
    return centroids, similarity.reshape(-1)


def exchange(x):
    return lax.all_to_all(x, "dp", split_axis=0, concat_axis=0, tiled=True)


def after(value, *others):
    return lax.optimization_barrier((value, *others))[0]


def sorted_slots(key, top, entries):
    slots = jnp.arange(key.shape[0], dtype=jnp.int32)
    ahead = (key[None, :] < key[:, None]) | (
        (key[None, :] == key[:, None]) & (slots[None, :] < slots[:, None])
    )
    position = jnp.sum(ahead.astype(jnp.int32), axis=1)
    here = position[None, :] == slots[:, None]
    listed = jnp.sum(jnp.where(here, entries[None, :], 0), axis=1)
    levels = jnp.arange(-(-(top + 1) // LANES) * LANES, dtype=jnp.int32)
    bounds = jnp.sum((key[None, :] < levels[:, None]).astype(jnp.int32), axis=1)
    return listed, bounds, position


def ranks(group, sub):
    index = jnp.arange(sub.shape[-1], dtype=jnp.int32)
    before = (sub[..., None, :] < sub[..., :, None]) | (
        (sub[..., None, :] == sub[..., :, None]) & (index[None, :] < index[:, None])
    )
    same = group[..., None, :] == group[..., :, None]
    return jnp.sum((before & same).astype(jnp.int32), axis=-1)


def shards(tile_values, tile_row, tile_owner, tile_sub, labels):
    devices = lax.axis_size("dp")
    tiles = tile_values.shape[0]
    home = labels.shape[0]
    blocks = home // LANES * devices
    cap = max(2, 2 * tiles // devices)
    cuts = tuple(sorted({int(cap * share) for share in PARTS})) if cap >= 8 else (0, cap)
    parts = len(cuts) - 1
    here = lax.axis_index("dp").astype(jnp.int32)
    owner = tile_owner[:, 0]

    told = (labels, owner, tile_row, tile_sub)
    outgoing = pack(tile_values, owner, tile_row, told, devices, blocks, cuts)
    incoming = [exchange(outgoing[0])]
    heard = incoming[0][:, (cuts[1] - cuts[0]) * LANES :].astype(jnp.int32)
    level = heard[:, :blocks]
    partial_sq = jnp.exp2(level.astype(jnp.float32) * (1.0 / LOG_STEPS) + LOG_MIDDLE)
    row_sq = jnp.sum(jnp.where(level > -32768, partial_sq, 0.0), axis=0)
    all_described = heard[:, blocks:].reshape(devices, -1)
    all_labels = all_described[:, :home].reshape(blocks, LANES)
    mine = all_described[:, home : home + tiles] == here
    code = all_described[:, home + tiles : home + 2 * tiles]
    rank = ranks(mine.astype(jnp.int32), code % TB_OWN)
    chosen = mine[:, None, :] & (rank[:, None, :] == jnp.arange(cap)[None, :, None])
    meta = jnp.sum(jnp.where(chosen, code[:, None, :] + 1, 0), axis=2).reshape(-1) - 1
    sub = jnp.where(meta < 0, TB_OWN, meta % TB_OWN)
    slot_rank = np.arange(devices * cap) % cap
    slot_part = np.searchsorted(np.array(cuts), slot_rank, side="right") - 1
    low = np.array(cuts)[slot_part]
    fold_key = jnp.asarray(slot_part * (TB_OWN + 1), jnp.int32) + sub
    row = (meta // TB_OWN) << ROW_SHIFT
    from_slot = (np.arange(devices * cap) // cap << SOURCE_SHIFT) + slot_rank - low
    fold_list, fold_bounds, position = sorted_slots(
        fold_key, parts * (TB_OWN + 1), row + jnp.asarray(from_slot, jnp.int32)
    )
    score_list, *_ = sorted_slots(sub, TB_OWN, row + position)
    scalars = [fold_list, fold_bounds, score_list]

    scale = lax.rsqrt(row_sq + EPSILON) * (1.0 / CODE_TOP**2)
    signed = jnp.where(all_labels < HALF, scale, -scale)
    mods = (all_labels % HALF).astype(jnp.float32)
    totals, normed = (), []
    beside = (*scalars, mods, signed)
    for q in range(parts):
        if q + 1 < parts:
            ahead = (incoming[q], *beside) if q else (incoming[q],)
            incoming.append(exchange(after(outgoing[q + 1], *ahead)))
        partial, sums, *more = stage(
            q, cuts, scalars, mods, signed, incoming[q], normed, totals
        )
        beside = (partial, sums)
        totals, normed = (partial, sums, *more[:3]), normed + more[3:]
    return close(labels, exchange(partial), sums, TB_OWN * LANES * devices)


def solution(mesh):
    return jax.shard_map(
        shards,
        mesh=mesh,
        in_specs=(
            P(("groups", "dp"), None, None),
            P(("groups", "dp")),
            P(("groups", "dp"), None),
            P(("groups", "dp")),
            P(("groups", "dp")),
        ),
        out_specs=(P("groups", "dp"), P(("groups", "dp"))),
        check_vma=False,
    )
```
